32 devices in a mesh: dp: 4 (over z), seq: 4 (over y, x), tensor: 2 (over core).
Axes of the slice: x: 2, y: 2, z: 4, core: 2. Of those that a mesh axis runs over, the one named last changes fastest.
Arguments:
- inputs: bfloat16 [2, 8, 1024, 1536], P(None, 'dp', 'seq', 'tensor'), may hold values from -6 to 6
- segments: int32 [2, 8, 1024], P(None, 'dp'), may hold values from 0 to 5, as said below
- cotangent: bfloat16 [2, 8, 1024, 1536], P(None, 'dp', 'seq', 'tensor'), may hold values from -6 to 6
- prenorm: float32 [1536], replicated, may hold values from 0.5 to 1.5
- inproj: bfloat16 [2, 1536, 3072], P(None, 'dp', 'tensor'), may hold values from -0.15625 to 0.15625
- statproj: bfloat16 [1536, 256], P('dp'), may hold values from -0.15625 to 0.15625
- stepproj: bfloat16 [1536, 48], P('dp', 'tensor'), may hold values from -0.15625 to 0.15625
- outproj: bfloat16 [3072, 1536], P('tensor', 'dp'), may hold values from -0.109375 to 0.109375
- convinner: float32 [5, 3072], P(None, 'tensor'), may hold values from -0.5 to 0.5
- convstate: float32 [5, 256], replicated, may hold values from -0.5 to 0.5
- headparam: float32 [3, 48], P(None, 'tensor'), may hold values from -9 to 5, as said below
- gatenorm: float32 [3072], P('tensor'), may hold values from 0.5 to 1.5
- prenorm_moment: float32 [1536], P('tensor'), may hold values from -1.5 to 1.5
- inproj_moment: float32 [2, 1536, 3072], P(None, ('dp', 'seq'), 'tensor'), may hold values from -1.5 to 1.5
- statproj_moment: float32 [1536, 256], P(('dp', 'seq'), 'tensor'), may hold values from -1.5 to 1.5
- stepproj_moment: float32 [1536, 48], P(('dp', 'seq'), 'tensor'), may hold values from -1.5 to 1.5
- outproj_moment: float32 [3072, 1536], P('tensor', ('dp', 'seq')), may hold values from -1.5 to 1.5
- convinner_moment: float32 [5, 3072], P(None, 'tensor'), may hold values from -1.5 to 1.5
- convstate_moment: float32 [5, 256], P(None, 'tensor'), may hold values from -1.5 to 1.5
- headparam_moment: float32 [3, 48], P(None, 'tensor'), may hold values from -1.5 to 1.5
- gatenorm_moment: float32 [3072], P('tensor'), may hold values from -1.5 to 1.5
Outputs:
- layer_out: bfloat16 [2, 8, 1024, 1536], P(None, 'dp', 'seq', 'tensor')
- input_grad: bfloat16 [2, 8, 1024, 1536], P(None, 'dp', 'seq', 'tensor')
- grad_norm: float32 [], replicated
- prenorm_newmoment: float32 [1536], P('tensor')
- inproj_newmoment: float32 [2, 1536, 3072], P(None, ('dp', 'seq'), 'tensor')
- statproj_newmoment: float32 [1536, 256], P(('dp', 'seq'), 'tensor')
- stepproj_newmoment: float32 [1536, 48], P(('dp', 'seq'), 'tensor')
- outproj_newmoment: float32 [3072, 1536], P('tensor', ('dp', 'seq'))
- convinner_newmoment: float32 [5, 3072], P(None, 'tensor')
- convstate_newmoment: float32 [5, 256], P(None, 'tensor')
- headparam_newmoment: float32 [3, 48], P(None, 'tensor')
- gatenorm_newmoment: float32 [3072], P('tensor')
- inproj_new: bfloat16 [2, 1536, 3072], P(None, ('dp', 'seq'), 'tensor')
- statproj_new: bfloat16 [1536, 256], P(('dp', 'seq'), 'tensor')
- stepproj_new: bfloat16 [1536, 48], P(('dp', 'seq'), 'tensor')
- outproj_new: bfloat16 [3072, 1536], P('tensor', ('dp', 'seq'))
- convinner_new: float32 [5, 3072], P(None, 'tensor')
- convstate_new: float32 [5, 256], P(None, 'tensor')
The draws below stay inside these ranges and needn't reach their ends.
Inputs may be any that keep to these rules, and one draw needn't show every extreme that they name: `segments`: along each sequence the document numbers start at 0 and never fall; a document has 200 tokens or more, except the last one of a sequence. `headparam`: row 0 is added to a head's step before the softplus, row 1 is the logarithm of its decay rate, row 2 the weight of its skip term.
All inputs are finite; a program needn't handle non-finite values.
Results may differ from the reference program's by a relative error of at most 0.0093.
Values may be sent and summed in bfloat16 or wider, within the bound.
No kernel may reach another device: no remote copies, remote signals or barrier semaphores. Data moves between devices by JAX's collectives and lax.ppermute only.
A program may use at most 256 MiB of HBM per device.

```python
import math
import jax
import jax.numpy as jnp
from jax import lax

D = 1536
INNER = 3072
HEADDIM = 64
STATE = 128
CONV = 4
SPAN = 256
MB = 2
SEQ_MB = 2
DOC_MIN = 200
DOC_MAX = 2000
HEADS = 48
LEN = 1024
BATCH = 8


def draw_segments(key, part):
    key = jax.random.fold_in(key, 11)
    first_key, second_key, third_key = jax.random.split(key, 3)
    doc_slots = LEN // DOC_MIN + 2
    lengths = jax.random.randint(first_key, (MB, BATCH, doc_slots), DOC_MIN, DOC_MAX + 1)
    ends = jnp.cumsum(lengths, axis=-1)
    places = jnp.arange(LEN, dtype=jnp.int32)
    numbers = jnp.sum((ends[:, :, :, None] <= places[None, None, None, :]).astype(jnp.int32), axis=2)
    groups = BATCH // SEQ_MB
    local_count = MB * SEQ_MB
    picked = jax.random.randint(second_key, (groups,), 0, local_count)
    shift_by = jax.random.randint(third_key, (), 0, max(local_count - 1, 1))
    densest = (picked[0] + 1 + shift_by) % local_count
    batch_ids = jnp.arange(BATCH, dtype=jnp.int32)
    micro_ids = jnp.arange(MB, dtype=jnp.int32)
    local_ids = micro_ids[:, None] * SEQ_MB + (batch_ids % SEQ_MB)[None, :]
    whole = local_ids == picked[batch_ids // SEQ_MB][None, :]
    dense = (local_ids == densest) & (batch_ids // SEQ_MB == 0)[None, :] & jnp.logical_not(whole)
    regular = (places // DOC_MIN).astype(jnp.int32)
    numbers = jnp.where(dense[:, :, None], regular[None, None, :], numbers)
    return jnp.where(whole[:, :, None], 0, numbers).astype(jnp.int32)


def draw_headparam(key, part):
    key = jax.random.fold_in(key, 5)
    first_key, second_key, third_key, fourth_key = jax.random.split(key, 4)
    share = 0.5
    slow = jax.random.uniform(first_key, (HEADS,)) < share
    offset = jax.random.uniform(second_key, (HEADS,))
    spread_draw = jax.random.uniform(third_key, (HEADS,))
    bias = jnp.where(slow, -8.5 + offset, -3.0 + offset)
    level = jnp.where(slow, (0.5 + spread_draw) / (LEN * jnp.exp(bias + 0.5)), 0.15 + 0.15 * spread_draw)
    skip = 0.5 + jax.random.uniform(fourth_key, (HEADS,))
    return jnp.stack([bias, jnp.log(level), skip]).astype(jnp.float32)


def block_scale(stream_key, shape, shards, low, largest):
    factor_of = 1.0
    for axis_at, shards_of in shards:
        steps = jax.random.uniform(jax.random.fold_in(jax.random.fold_in(stream_key, 6), axis_at), (shards_of,), jnp.float32, low / len(shards), largest / len(shards))
        factor_of = factor_of * jnp.repeat(jnp.exp(steps), shape[axis_at] // shards_of).reshape((-1,) + (1,) * (len(shape) - 1 - axis_at))
    return factor_of


def normal_values(stream_key, extent, scale, reach, shards=(), held_as=jnp.bfloat16):
    level = block_scale(stream_key, extent, shards, -0.22, 0.18) if shards else 1.0
    drawn = jax.random.normal(stream_key, extent, jnp.float32) * scale * level
    return jnp.minimum(jnp.maximum(drawn, -reach), reach).astype(held_as)


def setup_inputs(seed: int = 0) -> dict:
    keys = jax.random.split(jax.random.key(seed), 22)
    return {
        "inputs": normal_values(keys[0], (MB, BATCH, LEN, D), 1.0, 6.0, ((1, 4), (2, 4), (3, 2))),
        "segments": draw_segments(jax.random.fold_in(keys[21], 71), 0),
        "cotangent": normal_values(keys[2], (MB, BATCH, LEN, D), 1.0, 6.0, ((1, 4), (2, 4), (3, 2))),
        "prenorm": jnp.clip(1.0 + 0.1 * jax.random.normal(keys[3], (D,), jnp.float32), 0.5, 1.5),
        "inproj": normal_values(keys[4], (2, D, INNER), D ** -0.5, 0.15625, ((1, 4), (2, 2))),
        "statproj": normal_values(keys[5], (D, 2 * STATE), D ** -0.5, 0.15625, ((0, 4),)),
        "stepproj": normal_values(keys[6], (D, HEADS), D ** -0.5, 0.15625, ((0, 4), (1, 2))),
        "outproj": normal_values(keys[7], (INNER, D), INNER ** -0.5, 0.109375, ((0, 2), (1, 4))),
        "convinner": jnp.clip(jax.random.uniform(keys[8], (CONV + 1, INNER), jnp.float32, -0.5, 0.5) * block_scale(keys[8], (CONV + 1, INNER), ((1, 2),), -0.4, 0.0), -0.5, 0.5),
        "convstate": jnp.clip(jax.random.uniform(keys[9], (CONV + 1, 2 * STATE), jnp.float32, -0.5, 0.5), -0.5, 0.5),
        "headparam": draw_headparam(jax.random.fold_in(keys[21], 71), 0),
        "gatenorm": jnp.clip(1.0 + 0.1 * jax.random.normal(keys[11], (INNER,), jnp.float32), 0.5, 1.5),
        "prenorm_moment": normal_values(keys[12], (D,), 0.25, 1.5, ((0, 2),), jnp.float32),
        "inproj_moment": normal_values(keys[13], (2, D, INNER), 0.25, 1.5, ((1, 16), (2, 2)), jnp.float32),
        "statproj_moment": normal_values(keys[14], (D, 2 * STATE), 0.25, 1.5, ((0, 16), (1, 2)), jnp.float32),
        "stepproj_moment": normal_values(keys[15], (D, HEADS), 0.25, 1.5, ((0, 16), (1, 2)), jnp.float32),
        "outproj_moment": normal_values(keys[16], (INNER, D), 0.25, 1.5, ((0, 2), (1, 16)), jnp.float32),
        "convinner_moment": normal_values(keys[17], (CONV + 1, INNER), 0.25, 1.5, ((1, 2),), jnp.float32),
        "convstate_moment": normal_values(keys[18], (CONV + 1, 2 * STATE), 0.25, 1.5, ((1, 2),), jnp.float32),
        "headparam_moment": normal_values(keys[19], (3, HEADS), 0.25, 1.5, ((1, 2),), jnp.float32),
        "gatenorm_moment": normal_values(keys[20], (INNER,), 0.25, 1.5, ((0, 2),), jnp.float32),
    }


EPS = 1e-05
LEARN = 0.05
CLIP_RMS = 0.25
HIGH = lax.Precision.HIGHEST

@jax.custom_vjp
def low(v):
    return lax.optimization_barrier(v.astype(jnp.bfloat16)).astype(jnp.float32)

@jax.custom_vjp
def low_back(v):
    return v

def low_keep(v):
    return (low(v), None)

def low_pass(kept, grad):
    return (grad,)

def back_keep(v):
    return (v, None)

def back_low(kept, grad):
    return (low(grad),)
low.defvjp(low_keep, low_pass)
low_back.defvjp(back_keep, back_low)

def matmul(operand, matrix):
    return jnp.dot(operand, matrix, precision=HIGH, preferred_element_type=jnp.float32)

def rms_scale(values, weight):
    return values * lax.rsqrt(lax.optimization_barrier(jnp.mean(values * values, axis=-1, keepdims=True)) + EPS) * weight

def conv_block(padded, seg_pad, kernel):
    length = padded.shape[0] - (CONV - 1)
    own_seg = seg_pad[CONV - 1:]
    summed = jnp.broadcast_to(kernel[CONV], (length, kernel.shape[1]))
    for offset in range(CONV):
        window = padded[offset:offset + length]
        same_doc = (seg_pad[offset:offset + length] == own_seg)[:, None]
        summed = summed + kernel[offset] * jnp.where(same_doc, window, 0.0)
    return jax.nn.silu(summed)

def decay_table(cumulative, segids):
    row_count = segids.shape[0]
    places = jnp.arange(row_count)
    allowed = (segids[:, None] == segids[None, :]) & (places[:, None] >= places[None, :])
    allowed = allowed[:, :, None]
    gap_values = cumulative[:, None, :] - cumulative[None, :, :]
    return jnp.where(allowed, jnp.exp(jnp.where(allowed, gap_values, -60.0)), 0.0)

def head_rates(raw_step, params):
    step_sizes = jax.nn.softplus(raw_step + params[0])
    return (step_sizes, jnp.cumsum(-step_sizes * jnp.exp(params[1]), axis=0))

def mix_out(values, b_proj, c_proj, raw_step, params, segids, before, carry_in):
    step_sizes, cumulative = head_rates(raw_step, params)
    scores = jnp.dot(c_proj, b_proj.T, precision=HIGH)
    weights = scores[:, :, None] * decay_table(cumulative, segids) * step_sizes[None, :, :]
    result = jnp.einsum('tsh,shp->thp', weights, values, precision=HIGH)
    entering = jnp.where((segids == before)[:, None], jnp.exp(cumulative), 0.0)
    carried = jnp.einsum('tn,hpn->thp', c_proj, carry_in, precision=HIGH)
    return result + entering[:, :, None] * carried + params[2][None, :, None] * values

def mix_state(values, b_proj, raw_step, params, segids, before):
    step_sizes, cumulative = head_rates(raw_step, params)
    tail_weight = jnp.where((segids == segids[-1])[:, None], jnp.exp(cumulative[-1][None, :] - cumulative), 0.0) * step_sizes
    summary = jnp.einsum('sh,shp,sn->hpn', tail_weight, values, b_proj, precision=HIGH)
    passing = jnp.where(segids[-1] == before, jnp.exp(cumulative[-1]), 0.0)
    return (summary, passing)

def mix_all(values, b_proj, c_proj, raw_step, params, segids):
    blocks = LEN // SPAN
    before = jnp.concatenate([jnp.full((1,), -1, jnp.int32), segids[SPAN - 1::SPAN][:-1].astype(jnp.int32)])

    def advance(carry_in, item):
        part_vals, part_b, part_c, part_raw, part_seg, part_before = item
        output = mix_out(part_vals, part_b, part_c, part_raw, params, part_seg, part_before, carry_in)
        summary, passing = mix_state(part_vals, part_b, part_raw, params, part_seg, part_before)
        return (summary + passing[:, None, None] * carry_in, output)
    start = jnp.zeros((HEADS, HEADDIM, STATE), jnp.float32)
    items = (values.reshape(blocks, SPAN, HEADS, HEADDIM), b_proj.reshape(blocks, SPAN, STATE), c_proj.reshape(blocks, SPAN, STATE), raw_step.reshape(blocks, SPAN, HEADS), segids.reshape(blocks, SPAN), before)
    _, outputs = lax.scan(jax.checkpoint(advance), start, items)
    return outputs.reshape(LEN, HEADS * HEADDIM)

def layer(params, rows, segids):
    prenorm, inproj, statproj, stepproj, outproj, convinner, convstate, headparam, gatenorm = params
    normed = low(rms_scale(rows, prenorm))
    gate_pre = low_back(matmul(normed, inproj[0]))
    mixed = low(low_back(jnp.concatenate([matmul(normed, inproj[1]), matmul(normed, statproj)], axis=1)))
    raw_step = low_back(matmul(normed, stepproj))
    padded = jnp.pad(mixed, ((CONV - 1, 0), (0, 0)))
    seg_pad = jnp.pad(segids, (CONV - 1, 0), constant_values=-1)
    conv_out = conv_block(padded, seg_pad, jnp.concatenate([convinner, convstate], axis=1))
    values = conv_out[:, :INNER].reshape(LEN, HEADS, HEADDIM)
    b_proj = conv_out[:, INNER:INNER + STATE]
    c_proj = conv_out[:, INNER + STATE:]
    mixer = mix_all(values, b_proj, c_proj, raw_step, headparam, segids)
    gated_in = mixer * jax.nn.silu(gate_pre)
    gated = low(rms_scale(gated_in, gatenorm))
    return rows + matmul(gated, outproj)

def reference(inputs, segments, cotangent, prenorm, inproj, statproj, stepproj, outproj, convinner, convstate, headparam, gatenorm, prenorm_moment, inproj_moment, statproj_moment, stepproj_moment, outproj_moment, convinner_moment, convstate_moment, headparam_moment, gatenorm_moment):
    weights = (prenorm, inproj, statproj, stepproj, outproj, convinner, convstate, headparam, gatenorm)
    moments = (prenorm_moment, inproj_moment, statproj_moment, stepproj_moment, outproj_moment, convinner_moment, convstate_moment, headparam_moment, gatenorm_moment)
    params = tuple((weight_item.astype(jnp.float32) for weight_item in weights))
    rows_all = inputs.reshape(MB * BATCH, LEN, D)
    segs_all = segments.reshape(MB * BATCH, LEN)
    cot_all = cotangent.reshape(MB * BATCH, LEN, D)

    def one_sequence(totals, item):
        rows, segids, grad_rows = item
        output, back = jax.vjp(lambda param_set, row_vals: layer(param_set, row_vals, segids), params, rows.astype(jnp.float32))
        grad_params, grad_input = back(grad_rows.astype(jnp.float32))
        totals = jax.tree.map(jnp.add, totals, grad_params)
        return (totals, (output.astype(jnp.bfloat16), grad_input.astype(jnp.bfloat16)))
    zero_grads = jax.tree.map(jnp.zeros_like, params)
    grads, (outputs, input_grads) = lax.scan(one_sequence, zero_grads, (rows_all, segs_all, cot_all))
    squares = jnp.sum(jnp.stack([jnp.sum(grad_item * grad_item) for grad_item in grads]))
    grad_norm = jnp.sqrt(squares)
    entries = 0
    for weight_item in weights:
        entries = entries + weight_item.size
    limit = CLIP_RMS * math.sqrt(entries)
    factor = limit / jnp.maximum(grad_norm, limit)
    new_moments = [0.5 * moment_item + 0.5 * factor * grad_item for moment_item, grad_item in zip(moments, grads)]
    new_weights = [(params[index] - LEARN * new_moments[index]).astype(weights[index].dtype) for index in range(1, 7)]
    return (outputs.reshape(MB, BATCH, LEN, D), input_grads.reshape(MB, BATCH, LEN, D), grad_norm, new_moments[0], new_moments[1], new_moments[2], new_moments[3], new_moments[4], new_moments[5], new_moments[6], new_moments[7], new_moments[8], new_weights[0], new_weights[1], new_weights[2], new_weights[3], new_weights[4], new_weights[5])
```

```python
import math

import jax
import jax.numpy as jnp
from jax import lax
from jax.experimental import pallas as pl
from jax.experimental.pallas import tpu as pltpu
from jax.sharding import PartitionSpec as P

D = 1536
INNER = 3072
HEADDIM = 64
STATE = 128
CONV = 4
MB = 2


EPS = 1e-05
LEARN = 0.05
CLIP_RMS = 0.25
HIGH = lax.Precision.HIGHEST


def shifted(block, axis, distance):
    devices = range(lax.axis_size(axis))
    route = [(i - distance, i) for i in devices if i - distance in devices]
    return lax.ppermute(block, axis, route)


def prefix(array, axis, combine, identity):
    size, position = (lax.axis_size(axis), lax.axis_index(axis))
    everything = jax.tree.map(
        lambda part, kind: lax.all_gather(part.astype(kind), axis),
        array,
        (jnp.bfloat16, jnp.bfloat16),
    )
    start = jax.tree.map(
        lambda part, zero: jnp.broadcast_to(jnp.asarray(zero, part.dtype), part.shape),
        array,
        identity,
    )

    def prefix_step(k, before):
        reached = k < position
        new = combine(
            before, jax.tree.map(lambda part, own: part[k].astype(own.dtype), everything, array)
        )
        return jax.tree.map(lambda a, b: jnp.where(reached, a, b), new, before)

    return lax.fori_loop(0, size, prefix_step, start)


def entering_2(array, axis, combine, identity):
    size, position = (lax.axis_size(axis), lax.axis_index(axis))
    everything = jax.tree.map(lambda part: lax.all_gather(part, axis), array)
    start = jax.tree.map(
        lambda part, zero: jnp.broadcast_to(jnp.asarray(zero, part.dtype), part.shape),
        array,
        identity,
    )

    def entering_step(k, before):
        at = size - 1 - k
        reached = at > position
        new = combine(before, jax.tree.map(lambda part: part[at], everything))
        return jax.tree.map(lambda a, b: jnp.where(reached, a, b), new, before)

    return lax.fori_loop(0, size, entering_step, start)


def rms_scale(values, weight):
    return values * lax.rsqrt(jnp.mean(values * values, axis=-1, keepdims=True) + EPS) * weight


def conv_block(padded, seg_pad, kernel):
    length = padded.shape[0] - (CONV - 1)
    own_seg = seg_pad[CONV - 1 :]
    summed = jnp.broadcast_to(kernel[CONV], (length, kernel.shape[1]))
    for offset in range(CONV):
        window = padded[offset : offset + length]
        same_doc = (seg_pad[offset : offset + length] == own_seg)[:, None]
        summed = summed + kernel[offset] * jnp.where(same_doc, window, 0.0)
    return jax.nn.silu(summed)


def decay_table(cumulative, segids):
    row_count = segids.shape[0]
    places = jnp.arange(row_count)
    allowed = (segids[:, None] == segids[None, :]) & (places[:, None] >= places[None, :])
    allowed = allowed[:, :, None]
    gap_values = cumulative[:, None, :] - cumulative[None, :, :]
    return jnp.where(allowed, jnp.exp(jnp.where(allowed, gap_values, -60.0)), 0.0)


def head_rates(raw_step, params):
    step_sizes = jax.nn.softplus(raw_step + params[0])
    return (step_sizes, jnp.cumsum(-step_sizes * jnp.exp(params[1]), axis=0))


def mix_out(values, b_proj, c_proj, raw_step, params, segids, before, carry_in):
    step_sizes, cumulative = head_rates(raw_step, params)
    scores = jnp.dot(c_proj, b_proj.T, precision=HIGH)
    weights = scores[:, :, None] * decay_table(cumulative, segids) * step_sizes[None, :, :]
    result = jnp.einsum("tsh,shp->thp", weights, values, precision=HIGH)
    entering = jnp.where((segids == before)[:, None], jnp.exp(cumulative), 0.0)
    carried = jnp.einsum("tn,hpn->thp", c_proj, carry_in, precision=HIGH)
    return result + entering[:, :, None] * carried + params[2][None, :, None] * values


def mix_state(values, b_proj, raw_step, params, segids, before):
    step_sizes, cumulative = head_rates(raw_step, params)
    tail_weight = (
        jnp.where(
            (segids == segids[-1])[:, None], jnp.exp(cumulative[-1][None, :] - cumulative), 0.0
        )
        * step_sizes
    )
    summary = jnp.einsum("sh,shp,sn->hpn", tail_weight, values, b_proj, precision=HIGH)
    passing = jnp.where(segids[-1] == before, jnp.exp(cumulative[-1]), 0.0)
    return (summary, passing)


def chain(earlier, later):
    return (earlier[0] * later[0], later[0][..., None, None] * earlier[1] + later[1])


def add_tree(totals, terms):
    if totals is None:
        return terms
    return jax.tree.map(jnp.add, totals, terms)


def project(left_rows, matrix):
    return jnp.einsum("bld,dk->blk", left_rows, matrix, preferred_element_type=jnp.float32)


def weight_grad(left_rows, right_rows):
    return jnp.einsum("bld,blk->dk", left_rows, right_rows, preferred_element_type=jnp.float32)


def back_project(grad_rows, matrix):
    return jnp.einsum("blk,dk->bld", grad_rows, matrix, preferred_element_type=jnp.float32)


def general_body(
    inputs,
    segments,
    cotangent,
    prenorm,
    inproj,
    statproj,
    stepproj,
    outproj,
    convinner,
    convstate,
    headparam,
    gatenorm,
    prenorm_moment,
    inproj_moment,
    statproj_moment,
    stepproj_moment,
    outproj_moment,
    convinner_moment,
    convstate_moment,
    headparam_moment,
    gatenorm_moment,
):
    tensor_at = lax.axis_index("tensor")
    seq_at = lax.axis_index("seq")
    data_at = lax.axis_index("dp")
    tensor_count = lax.axis_size("tensor")
    batch_count = inputs.shape[1]
    span_len = inputs.shape[2]
    inner_local = convinner.shape[1]
    heads_local = headparam.shape[1]
    state_half = 2 * STATE // tensor_count
    model_half = D // tensor_count
    rows_full, grads_full = (
        lax.all_gather(inputs, "tensor", axis=3, tiled=True),
        lax.all_gather(cotangent, "tensor", axis=3, tiled=True),
    )
    seg_padded = jnp.pad(segments, ((0, 0), (0, 0), (CONV - 1, 0)), constant_values=-1)
    seg_local = lax.dynamic_slice_in_dim(seg_padded, seq_at * span_len, span_len + CONV - 1, 2)
    kernel = jnp.concatenate([convinner, convstate], axis=1)
    shares = None
    smalls = None
    outputs = []
    input_grads = []
    for batch in range(MB):
        inproj_all, statproj_all, stepproj_all, outproj_all = (
            lax.all_gather(inproj, "dp", axis=1, tiled=True),
            lax.all_gather(statproj, "dp", axis=0, tiled=True),
            lax.all_gather(stepproj, "dp", axis=0, tiled=True),
            lax.all_gather(outproj, "dp", axis=1, tiled=True),
        )
        rows = rows_full[batch].astype(jnp.float32)
        normed, norm_back = jax.vjp(rms_scale, rows, prenorm)
        normed_low = normed.astype(jnp.bfloat16)
        gate_pre = project(normed_low, inproj_all[0])
        inner_pre = project(normed_low, inproj_all[1])
        state_pre = project(normed_low, statproj_all)
        raw_step = project(normed_low, stepproj_all)
        mixed = jnp.concatenate([inner_pre, state_pre], axis=2).astype(jnp.bfloat16)
        edge_in = shifted(mixed[:, span_len - (CONV - 1) :, :], "seq", 1)
        padded = jnp.concatenate([edge_in, mixed], axis=1).astype(jnp.float32)
        seg_now = seg_local[batch]
        own_seg = seg_now[:, CONV - 1 :]
        before = seg_now[:, CONV - 2]
        conv_out, conv_back = jax.vjp(
            lambda pad_vals, kernel_in: jax.vmap(conv_block, in_axes=(0, 0, None))(
                pad_vals, seg_now, kernel_in
            ),
            padded,
            kernel,
        )
        values = conv_out[..., :inner_local].reshape(batch_count, span_len, heads_local, HEADDIM)
        b_proj = conv_out[..., inner_local : inner_local + STATE]
        c_proj = conv_out[..., inner_local + STATE :]
        (summary, passing), state_back = jax.vjp(
            lambda value_in, b_part, raw_part, param_in: jax.vmap(
                mix_state, in_axes=(0, 0, 0, None, 0, 0)
            )(value_in, b_part, raw_part, param_in, own_seg, before),
            values,
            b_proj,
            raw_step,
            headparam,
        )
        identity = (jnp.ones_like(passing), jnp.zeros_like(summary))
        _, carry_in = prefix((passing, summary), "seq", chain, identity)
        mixer, out_back = jax.vjp(
            lambda value_in, b_part, c_part, raw_part, param_in, state_in: jax.vmap(
                mix_out, in_axes=(0, 0, 0, 0, None, 0, 0, 0)
            )(value_in, b_part, c_part, raw_part, param_in, own_seg, before, state_in),
            values,
            b_proj,
            c_proj,
            raw_step,
            headparam,
            carry_in,
        )
        flat_mixer = mixer.reshape(batch_count, span_len, inner_local)
        gate_act = jax.nn.silu(gate_pre)
        gated_in = flat_mixer * gate_act
        total_sq = lax.psum(jnp.sum(gated_in * gated_in, axis=-1), "tensor")
        scale = lax.rsqrt(total_sq / INNER + EPS)[..., None]
        gated_low = (gated_in * scale * gatenorm).astype(jnp.bfloat16)
        branch_part = project(gated_low, outproj_all)
        branch_own = lax.psum_scatter(branch_part, "tensor", scatter_dimension=2, tiled=True)
        outputs.append((inputs[batch].astype(jnp.float32) + branch_own).astype(jnp.bfloat16))
        grad_rows = grads_full[batch]
        d_gated = back_project(grad_rows, outproj_all)
        g_outproj = jnp.einsum(
            "blk,bld->kd", gated_low, grad_rows, preferred_element_type=jnp.float32
        )
        g_gatenorm = jnp.sum(d_gated * gated_in * scale, axis=(0, 1))
        weighted = d_gated * gatenorm
        cross = lax.psum(jnp.sum(weighted * gated_in, axis=-1), "tensor")
        d_in = weighted * scale - gated_in * scale**3 * (cross / INNER)[..., None]
        d_mixer = d_in * gate_act
        sigma = jax.nn.sigmoid(gate_pre)
        d_gate = d_in * flat_mixer * sigma * (1.0 + gate_pre * (1.0 - sigma))
        d_values, d_bproj, d_cproj, d_raw, d_param, d_carry = out_back(
            d_mixer.reshape(batch_count, span_len, heads_local, HEADDIM)
        )
        _, d_after = entering_2((passing, d_carry), "seq", chain, identity)
        d_passing = jnp.sum(d_after * carry_in, axis=(2, 3))
        d_values_tail, d_bproj_tail, d_raw_tail, d_param_tail = state_back((d_after, d_passing))
        d_state = lax.psum(jnp.concatenate([d_bproj + d_bproj_tail, d_cproj], axis=2), "tensor")
        d_conv = jnp.concatenate(
            [(d_values + d_values_tail).reshape(batch_count, span_len, inner_local), d_state],
            axis=2,
        )
        d_padded, d_kernel = conv_back(d_conv)
        edge_back = shifted(d_padded[:, : CONV - 1, :].astype(jnp.bfloat16), "seq", -1).astype(
            jnp.float32
        )
        d_mixed = d_padded[:, CONV - 1 :, :] + jnp.pad(
            edge_back, ((0, 0), (span_len - (CONV - 1), 0), (0, 0))
        )
        d_mixed_low = d_mixed.astype(jnp.bfloat16)
        d_gate_low = d_gate.astype(jnp.bfloat16)
        d_raw_low = (d_raw + d_raw_tail).astype(jnp.bfloat16)
        d_inner_low = d_mixed_low[..., :inner_local]
        d_state_low = lax.dynamic_slice_in_dim(
            d_mixed_low[..., inner_local:], tensor_at * state_half, state_half, 2
        )
        statproj_own = lax.dynamic_slice_in_dim(statproj_all, tensor_at * state_half, state_half, 1)
        g_inproj = jnp.stack(
            [weight_grad(normed_low, d_gate_low), weight_grad(normed_low, d_inner_low)]
        )
        g_statproj = weight_grad(normed_low, d_state_low)
        g_stepproj = weight_grad(normed_low, d_raw_low)
        d_normed_part = (
            back_project(d_gate_low, inproj_all[0])
            + back_project(d_inner_low, inproj_all[1])
            + back_project(d_state_low, statproj_own)
            + back_project(d_raw_low, stepproj_all)
        )
        d_normed = lax.psum(d_normed_part, "tensor")
        d_rows, d_prenorm = norm_back(d_normed)
        own_rows = lax.dynamic_slice_in_dim(d_rows, tensor_at * model_half, model_half, 2)
        input_grads.append((own_rows + cotangent[batch].astype(jnp.float32)).astype(jnp.bfloat16))
        big_terms = (g_inproj, g_outproj, g_statproj, g_stepproj)
        small_terms = (
            lax.dynamic_slice_in_dim(d_prenorm, tensor_at * model_half, model_half, 0),
            d_kernel[:, :inner_local],
            lax.dynamic_slice_in_dim(
                d_kernel[:, inner_local:], tensor_at * state_half, state_half, 1
            ),
            d_param + d_param_tail,
            g_gatenorm,
        )
        shares = add_tree(
            shares,
            (
                lax.psum_scatter(big_terms[0], ("dp", "seq"), scatter_dimension=1, tiled=True),
                lax.psum_scatter(big_terms[1], ("dp", "seq"), scatter_dimension=1, tiled=True),
                lax.psum_scatter(big_terms[2], ("dp", "seq"), scatter_dimension=0, tiled=True),
                lax.psum_scatter(big_terms[3], ("dp", "seq"), scatter_dimension=0, tiled=True),
            ),
        )
        smalls = add_tree(
            smalls,
            lax.psum(
                (small_terms[0], small_terms[1], small_terms[2], small_terms[3], small_terms[4]),
                ("dp", "seq"),
            ),
        )
    big_sq = jnp.sum(jnp.stack([jnp.sum(term * term) for term in shares]))
    small_sq = jnp.sum(jnp.stack([jnp.sum(term * term) for term in smalls]))
    first_owner = jnp.where((data_at == 0) & (seq_at == 0), 1.0, 0.0)
    norm_sq = lax.psum(big_sq + first_owner * small_sq, ("dp", "seq", "tensor"))
    grad_norm = jnp.sqrt(norm_sq)
    heads_all = INNER // HEADDIM
    entries = (
        2 * D * INNER
        + 2 * D * STATE
        + D * heads_all
        + INNER * D
        + (CONV + 1) * (INNER + 2 * STATE)
        + 3 * heads_all
        + INNER
        + D
    )
    limit = CLIP_RMS * math.sqrt(entries)
    factor = limit / jnp.maximum(grad_norm, limit)
    shard_rows = shares[0].shape[1]
    row_start = seq_at * shard_rows
    big_current = (
        lax.dynamic_slice_in_dim(inproj, row_start, shard_rows, 1),
        lax.dynamic_slice_in_dim(outproj, row_start, shard_rows, 1),
        lax.dynamic_slice_in_dim(
            lax.dynamic_slice_in_dim(statproj, row_start, shard_rows, 0),
            tensor_at * state_half,
            state_half,
            1,
        ),
        lax.dynamic_slice_in_dim(stepproj, row_start, shard_rows, 0),
    )
    conv_current = (
        convinner,
        lax.dynamic_slice_in_dim(convstate, tensor_at * state_half, state_half, 1),
    )
    big_moments = (inproj_moment, outproj_moment, statproj_moment, stepproj_moment)
    small_moments = (
        prenorm_moment,
        convinner_moment,
        convstate_moment,
        headparam_moment,
        gatenorm_moment,
    )
    big_new_moments = [
        0.5 * moment_item + 0.5 * factor * grad_item
        for moment_item, grad_item in zip(big_moments, shares)
    ]
    small_new_moments = [
        0.5 * moment_item + 0.5 * factor * grad_item
        for moment_item, grad_item in zip(small_moments, smalls)
    ]
    big_new = [
        (weight_item.astype(jnp.float32) - LEARN * moment_item).astype(weight_item.dtype)
        for weight_item, moment_item in zip(big_current, big_new_moments)
    ]
    conv_new = [
        (weight_item - LEARN * moment_item).astype(weight_item.dtype)
        for weight_item, moment_item in zip(conv_current, small_new_moments[1:3])
    ]
    return (
        jnp.stack(outputs),
        jnp.stack(input_grads),
        grad_norm,
        small_new_moments[0],
        big_new_moments[0],
        big_new_moments[2],
        big_new_moments[3],
        big_new_moments[1],
        small_new_moments[1],
        small_new_moments[2],
        small_new_moments[3],
        small_new_moments[4],
        big_new[0],
        big_new[2],
        big_new[3],
        big_new[1],
        conv_new[0],
        conv_new[1],
    )


BLOCKS = 4
SPAN = 256
QUARTER = 384
QHEADS = 6
BF = jnp.bfloat16
F32 = jnp.float32
ROUTE_X = [(i, i ^ 1) for i in range(BLOCKS)]
ROUTE_Y = [(i, i ^ 2) for i in range(BLOCKS)]
ROUTE_D = [(i, i ^ 3) for i in range(BLOCKS)]
SWAP = [(0, 1), (1, 0)]
VMEM_LIMIT = 56 * 1024 * 1024


def dot_nn(a, b):
    return lax.dot_general(a, b, (((1,), (0,)), ((), ())), preferred_element_type=F32)


def dot_nt(a, b):
    return lax.dot_general(a, b, (((1,), (1,)), ((), ())), preferred_element_type=F32)


def dot_tn(a, b):
    return lax.dot_general(a, b, (((0,), (0,)), ((), ())), preferred_element_type=F32)


def dot_exact(a, b):
    return lax.dot_general(
        a, b, (((1,), (0,)), ((), ())), precision=HIGH, preferred_element_type=F32
    )


def sigmoid(v):
    return 1.0 / (1.0 + jnp.exp(-v))


def pair_cols(table, k, low_half):
    return jnp.where(low_half, table[:, 2 * k : 2 * k + 1], table[:, 2 * k + 1 : 2 * k + 2])


def rates(raw, head):
    shifted_raw = raw + head[0:1]
    step = jnp.maximum(shifted_raw, 0.0) + jnp.log1p(jnp.exp(-jnp.abs(shifted_raw)))
    return shifted_raw, step


def block_terms(raw, head, cols):
    shifted_raw, step = rates(raw, head)
    rows_at = lax.broadcasted_iota(jnp.int32, (SPAN, SPAN), 0)
    cols_at = lax.broadcasted_iota(jnp.int32, (SPAN, SPAN), 1)
    lower = jnp.where(rows_at >= cols_at, 1.0, 0.0)
    cum = dot_exact(lower, -step * head[1:2])
    last = cum[SPAN - 1 : SPAN]
    enter = jnp.exp(cum) * cols[:, 4:5]
    leave = jnp.exp(last - cum) * cols[:, 5:6]
    passing = jnp.exp(last) * cols[SPAN - 1 : SPAN, 4:5]
    return shifted_raw, step, cum, enter, leave, passing, rows_at >= cols_at


def fwd_kernel(
    place_ref, mixed_ref, gate_ref, raw_ref, cols_ref, segr_ref, taps_ref, head_ref, chan_ref,
    pre_ref, y_ref, hin_ref, gun_ref, sq_ref, buf, state,
):
    @pl.when(pl.program_id(1) == 0)
    def _():
        buf[0:8] = jnp.zeros((8, buf.shape[1]), F32)
        state[...] = jnp.zeros_like(state)

    mixed = mixed_ref[0, 0].astype(F32)
    buf[8 : 8 + SPAN] = mixed
    cols = cols_ref[0, 0]
    taps = taps_ref[...]
    pre = jnp.broadcast_to(taps[CONV : CONV + 1], mixed.shape)
    for j in range(CONV):
        window = mixed if j == CONV - 1 else buf[5 + j : 5 + j + SPAN]
        pre = pre + taps[j : j + 1] * (window * cols[:, j : j + 1])
    buf[0:8] = mixed[SPAN - 8 :]
    pre_ref[0, 0] = pre
    act = pre * sigmoid(pre)
    values = act[:, :QUARTER]
    b_low = act[:, QUARTER : QUARTER + STATE].astype(BF)
    c_low = act[:, QUARTER + STATE :].astype(BF)
    _, step, cum, enter, leave, passing, lower = block_terms(raw_ref[0, 0], head_ref[...], cols)
    cum_t = cum.T
    scores = dot_nt(c_low, b_low)
    allowed = lower & (cols[:, 6:7] == segr_ref[0, 0, 0:1])
    block_out = jnp.where(allowed, 0.0, -1e30)
    low_half = lax.broadcasted_iota(jnp.int32, (SPAN, 128), 1) < HEADDIM
    held = state[...].astype(BF)
    hin_ref[0, 0] = held
    carried = dot_nt(c_low, held)
    skip = chan_ref[1:2]
    tails = []
    outs = []
    for k in range(QHEADS // 2):
        at = slice(128 * k, 128 * (k + 1))
        scaled = (pair_cols(step, k, low_half) * values[:, at]).astype(BF)
        parts = []
        for h in (2 * k, 2 * k + 1):
            decay = jnp.exp(cum[:, h : h + 1] - cum_t[h : h + 1] + block_out)
            parts.append(dot_nn((scores * decay).astype(BF), scaled))
        own = jnp.where(low_half, parts[0], parts[1])
        outs.append(
            own + pair_cols(enter, k, low_half) * carried[:, at] + skip[:, at] * values[:, at]
        )
        tails.append((pair_cols(leave, k, low_half) * scaled.astype(F32)).astype(BF))
    y = jnp.concatenate(outs, axis=1)
    y_ref[0, 0] = y
    added = dot_tn(jnp.concatenate(tails, axis=1), b_low)
    for h in range(QHEADS):
        at = slice(HEADDIM * h, HEADDIM * (h + 1))
        state[at] = passing[:, h : h + 1] * state[at] + added[at]
    gate = gate_ref[0, 0]
    gated_in = y * (gate * sigmoid(gate))
    sq_ref[0, 0] = jnp.sum(gated_in * gated_in, axis=1, keepdims=True)
    gun_ref[0, 0] = (gated_in * chan_ref[0:1]).astype(BF)


def bwd_kernel(
    place_ref, mixed_ref, pre_ref, raw_ref, y_ref, hin_ref, dy_ref, cols_ref, segr_ref, taps_ref,
    head_ref, chan_ref, dcat_ref, dbc_ref, slope_ref, gtap_ref, ghead_ref,
    buf, d_state, bc_edge, slope_edge,
):
    @pl.when(pl.program_id(1) == 0)
    def _():
        buf[SPAN:] = jnp.zeros((8, QUARTER), F32)
        d_state[...] = jnp.zeros_like(d_state)
        bc_edge[...] = jnp.zeros_like(bc_edge)
        slope_edge[...] = jnp.zeros_like(slope_edge)

    @pl.when((pl.program_id(0) == 0) & (pl.program_id(1) == 0))
    def _():
        gtap_ref[...] = jnp.zeros_like(gtap_ref)
        ghead_ref[...] = jnp.zeros_like(ghead_ref)

    cols = cols_ref[0, 0]
    head = head_ref[...]
    taps = taps_ref[...]
    pre = pre_ref[0, 0]
    sigma = sigmoid(pre)
    act = pre * sigma
    slope = sigma * (1.0 + pre * (1.0 - sigma))
    values = act[:, :QUARTER]
    b_low = act[:, QUARTER : QUARTER + STATE].astype(BF)
    c_low = act[:, QUARTER + STATE :].astype(BF)
    shifted_raw, step, cum, enter, leave, passing, lower = block_terms(raw_ref[0, 0], head, cols)
    cum_t = cum.T
    scores = dot_nt(c_low, b_low)
    allowed = lower & (cols[:, 6:7] == segr_ref[0, 0, 0:1])
    block_out = jnp.where(allowed, 0.0, -1e30)
    low_half = lax.broadcasted_iota(jnp.int32, (SPAN, 128), 1) < HEADDIM
    held = hin_ref[0, 0]
    dy_low = dy_ref[0, 0]
    dy = dy_low.astype(F32)
    d_after = d_state[...]
    d_after_low = d_after.astype(BF)
    from_after = dot_nt(b_low, d_after_low)
    skip = chan_ref[1:2]
    zero_low = jnp.zeros((SPAN, 128), BF)
    d_scores = jnp.zeros((SPAN, SPAN), F32)
    d_values = []
    d_scaled_all = []
    scaled_all = []
    tail_terms = []
    tails = []
    entering = []
    for k in range(QHEADS // 2):
        at = slice(128 * k, 128 * (k + 1))
        step_k = pair_cols(step, k, low_half)
        scaled = (step_k * values[:, at]).astype(BF)
        scaled_f = scaled.astype(F32)
        dy_k = dy_low[:, at]
        parts = []
        for h in (2 * k, 2 * k + 1):
            decay = jnp.exp(cum[:, h : h + 1] - cum_t[h : h + 1] + block_out)
            weights = (scores * decay).astype(BF)
            parts.append(dot_tn(weights, dy_k))
            mine = low_half if h % 2 == 0 else jnp.logical_not(low_half)
            d_weights = dot_nt(jnp.where(mine, dy_k, zero_low), scaled)
            d_scores = d_scores + d_weights * decay
        leave_k = pair_cols(leave, k, low_half)
        tail_part = leave_k * from_after[:, at]
        d_scaled = jnp.where(low_half, parts[0], parts[1]) + tail_part
        d_scaled_all.append(d_scaled)
        scaled_all.append(scaled_f)
        tail_terms.append(scaled_f * tail_part)
        tails.append((leave_k * scaled_f).astype(BF))
        entering.append((pair_cols(enter, k, low_half) * dy[:, at]).astype(BF))
        d_values.append(step_k * d_scaled + skip[:, at] * dy[:, at])
    d_scaled = jnp.concatenate(d_scaled_all, axis=1)
    scaled = jnp.concatenate(scaled_all, axis=1)
    enter_dy = jnp.concatenate(entering, axis=1)
    d_scores_low = d_scores.astype(BF)
    d_c = dot_nn(d_scores_low, b_low) + dot_nn(enter_dy, held)
    d_b = dot_tn(d_scores_low, c_low) + dot_nn(jnp.concatenate(tails, axis=1), d_after_low)
    d_bc = jnp.concatenate([d_b, d_c], axis=1)
    dbc_ref[0, 0, 0:SPAN] = d_bc.astype(BF)
    dbc_ref[0, 0, SPAN : SPAN + 16] = bc_edge[...].astype(BF)
    bc_edge[...] = d_bc[0:16]
    slope_ref[0, 0, 0:SPAN] = slope[:, QUARTER:]
    slope_ref[0, 0, SPAN : SPAN + 16] = slope_edge[...]
    slope_edge[...] = slope[0:16, QUARTER:]
    chan_at = lax.broadcasted_iota(jnp.int32, (QUARTER, 128), 0)
    head_at = lax.broadcasted_iota(jnp.int32, (QUARTER, 128), 1)
    gather = jnp.where(
        (chan_at >= head_at * HEADDIM) & (chan_at < (head_at + 1) * HEADDIM), 1.0, 0.0
    )
    by_values = dot_exact(values * d_scaled, gather)
    by_skip = dot_exact(values * dy, gather)
    tail_sum = dot_exact(jnp.concatenate(tail_terms, axis=1), gather)
    d_cum = dot_exact(dy * (y_ref[0, 0] - skip * values) - scaled * d_scaled, gather)
    state_dot = jnp.sum(d_after * held.astype(F32), axis=1, keepdims=True)
    state_terms = jnp.sum(state_dot * gather, axis=0, keepdims=True)
    at_last = jnp.sum(tail_sum, axis=0, keepdims=True) + passing * state_terms
    rows_at = lax.broadcasted_iota(jnp.int32, (SPAN, SPAN), 0)
    cols_at = lax.broadcasted_iota(jnp.int32, (SPAN, SPAN), 1)
    upper = jnp.where(rows_at <= cols_at, 1.0, 0.0)
    d_rate = dot_exact(upper, d_cum) + at_last
    d_step = by_values - head[1:2] * d_rate
    d_raw = d_step * sigmoid(shifted_raw)
    ghead_ref[0:1] += jnp.sum(d_raw, axis=0, keepdims=True)
    ghead_ref[1:2] += jnp.sum(-step * head[1:2] * d_rate, axis=0, keepdims=True)
    ghead_ref[2:3] += jnp.sum(by_skip, axis=0, keepdims=True)
    dcat_ref[0, 0, :, QUARTER:] = d_raw.astype(BF)
    new_state = dot_tn(enter_dy, c_low)
    for h in range(QHEADS):
        at = slice(HEADDIM * h, HEADDIM * (h + 1))
        d_state[at] = passing[:, h : h + 1] * d_after[at] + new_state[at]
    d_pre = jnp.concatenate(d_values, axis=1) * slope[:, :QUARTER]
    buf[0:SPAN] = d_pre
    mixed = mixed_ref[0, 0, :, :QUARTER].astype(F32)
    d_mixed = jnp.zeros((SPAN, QUARTER), F32)
    for j in range(CONV):
        ahead = CONV - 1 - j
        window = (d_pre if ahead == 0 else buf[ahead : ahead + SPAN]) * cols[:, 8 + j : 9 + j]
        d_mixed = d_mixed + taps[j : j + 1, :QUARTER] * window
        gtap_ref[j : j + 1] += jnp.sum(mixed * window, axis=0, keepdims=True)
    gtap_ref[CONV : CONV + 1] += jnp.sum(d_pre, axis=0, keepdims=True)
    buf[SPAN:] = d_pre[0:8]
    dcat_ref[0, 0, :, :QUARTER] = d_mixed.astype(BF)


def slot_spec(rows, width, order):
    return pl.BlockSpec((1, 1, rows, width), lambda q, j, place: (q, order(j) ^ place[0], 0, 0))


def place_spec(rows, width, order):
    return pl.BlockSpec((1, 1, rows, width), lambda q, j, place: (q, order(j), 0, 0))


def fixed_spec(rows, width):
    return pl.BlockSpec((rows, width), lambda q, j, place: (0, 0))


def run_fwd(place, mixed, gate, raw, cols, segr, taps, head, chan):
    width = mixed.shape[-1]

    def order(j):
        return j

    def out(rows, cols_of, kind):
        return jax.ShapeDtypeStruct((2, BLOCKS, rows, cols_of), kind)

    return pl.pallas_call(
        fwd_kernel,
        grid_spec=pltpu.PrefetchScalarGridSpec(
            num_scalar_prefetch=1,
            grid=(2, BLOCKS),
            in_specs=[
                slot_spec(SPAN, width, order),
                slot_spec(SPAN, QUARTER, order),
                slot_spec(SPAN, 128, order),
                place_spec(SPAN, 128, order),
                place_spec(8, SPAN, order),
                fixed_spec(8, width),
                fixed_spec(8, 128),
                fixed_spec(8, QUARTER),
            ],
            out_specs=[
                slot_spec(SPAN, width, order),
                slot_spec(SPAN, QUARTER, order),
                slot_spec(QUARTER, STATE, order),
                slot_spec(SPAN, QUARTER, order),
                slot_spec(SPAN, 1, order),
            ],
            scratch_shapes=[
                pltpu.VMEM((SPAN + 8, width), F32),
                pltpu.VMEM((QUARTER, STATE), F32),
            ],
        ),
        out_shape=[
            out(SPAN, width, F32),
            out(SPAN, QUARTER, F32),
            out(QUARTER, STATE, BF),
            out(SPAN, QUARTER, BF),
            out(SPAN, 1, F32),
        ],
        compiler_params=pltpu.CompilerParams(vmem_limit_bytes=VMEM_LIMIT),
        name="mix_forward",
    )(place, mixed, gate, raw, cols, segr, taps, head, chan)


def run_bwd(place, mixed, pre, raw, y, hin, dy, cols, segr, taps, head, chan):
    width = mixed.shape[-1]
    states = 2 * STATE

    def order(j):
        return BLOCKS - 1 - j

    def out(rows, cols_of, kind):
        return jax.ShapeDtypeStruct((2, BLOCKS, rows, cols_of), kind)

    return pl.pallas_call(
        bwd_kernel,
        grid_spec=pltpu.PrefetchScalarGridSpec(
            num_scalar_prefetch=1,
            grid=(2, BLOCKS),
            in_specs=[
                slot_spec(SPAN, width, order),
                slot_spec(SPAN, width, order),
                slot_spec(SPAN, 128, order),
                slot_spec(SPAN, QUARTER, order),
                slot_spec(QUARTER, STATE, order),
                slot_spec(SPAN, QUARTER, order),
                place_spec(SPAN, 128, order),
                place_spec(8, SPAN, order),
                fixed_spec(8, width),
                fixed_spec(8, 128),
                fixed_spec(8, QUARTER),
            ],
            out_specs=[
                slot_spec(SPAN, QUARTER + 128, order),
                slot_spec(SPAN + 16, states, order),
                slot_spec(SPAN + 16, states, order),
                fixed_spec(8, QUARTER),
                fixed_spec(8, 128),
            ],
            scratch_shapes=[
                pltpu.VMEM((SPAN + 8, QUARTER), F32),
                pltpu.VMEM((QUARTER, STATE), F32),
                pltpu.VMEM((16, states), F32),
                pltpu.VMEM((16, states), F32),
            ],
        ),
        out_shape=[
            out(SPAN, QUARTER + 128, BF),
            out(SPAN + 16, states, BF),
            out(SPAN + 16, states, F32),
            jax.ShapeDtypeStruct((8, QUARTER), F32),
            jax.ShapeDtypeStruct((8, 128), F32),
        ],
        compiler_params=pltpu.CompilerParams(vmem_limit_bytes=VMEM_LIMIT),
        name="mix_backward",
    )(place, mixed, pre, raw, y, hin, dy, cols, segr, taps, head, chan)


def swap_cores(block):
    return lax.ppermute(block, "tensor", SWAP)


def over_x(block):
    return lax.ppermute(block, "seq", ROUTE_X)


def over_y(block):
    return lax.ppermute(block, "seq", ROUTE_Y)


def over_d(block):
    return lax.ppermute(block, "seq", ROUTE_D)


def gather_plane(piece):
    half = piece.shape[0] // 2
    by_x = over_x(piece)
    by_y = over_y(piece)
    far_a = over_x(by_y[:half])
    far_b = over_y(by_x[half:])
    return piece, by_x, by_y, far_a, far_b


def gather_tokens(piece):
    own, by_x, by_y, far_a, far_b = gather_plane(piece)
    others = [swap_cores(part) for part in (own, by_x, by_y, far_a, far_b)]
    rows = jnp.concatenate([own, by_x, by_y, far_a, far_b] + others, axis=0)
    return rows.reshape(2, BLOCKS, SPAN, D)


def add_low(a, b):
    return (a.astype(F32) + b.astype(F32)).astype(BF)


def scatter_plane(slots):
    half = slots[0].shape[0] // 2
    far_a = over_x(slots[3][:half])
    far_b = over_y(slots[3][half:])
    first_x = over_x(slots[1][:half])
    first_y = over_y(slots[2][half:])
    second_x = over_x(add_low(slots[1][half:], far_b))
    second_y = over_y(add_low(slots[2][:half], far_a))
    lower = slots[0][:half].astype(F32) + first_x.astype(F32) + second_y.astype(F32)
    upper = slots[0][half:].astype(F32) + second_x.astype(F32) + first_y.astype(F32)
    return jnp.concatenate([lower, upper], axis=0)


def sum_plane_slots(table):
    table = table + swap_cores(table)[:, ::-1]
    shape = table.shape
    pairs = table.reshape(shape[:2] + (2, 2) + shape[3:])
    pairs = pairs + over_x(pairs)[:, :, :, ::-1]
    pairs = pairs + over_y(pairs)[:, :, ::-1]
    return pairs.reshape(shape)


def fast_body(
    inputs,
    segments,
    cotangent,
    prenorm,
    inproj,
    statproj,
    stepproj,
    outproj,
    convinner,
    convstate,
    headparam,
    gatenorm,
    prenorm_moment,
    inproj_moment,
    statproj_moment,
    stepproj_moment,
    outproj_moment,
    convinner_moment,
    convstate_moment,
    headparam_moment,
    gatenorm_moment,
):
    core = lax.axis_index("tensor")
    chip = lax.axis_index("seq")
    data_at = lax.axis_index("dp")
    dp_count = lax.axis_size("dp")
    heads_local = headparam.shape[1]
    rows_local = inproj.shape[1]
    shard = rows_local // BLOCKS
    half_d = D // 2
    place = chip.astype(jnp.int32).reshape(1)

    def by_core(first, second):
        return jnp.where(core == 0, first, second)

    def quarter(array, axis, width):
        return lax.dynamic_slice_in_dim(array, chip * width, width, axis)

    step_flat = stepproj.reshape(-1, 512)
    pad_rows = -step_flat.shape[0] % 16
    first_block = jnp.concatenate(
        [
            jnp.concatenate(
                [
                    quarter(inproj[1], 1, QUARTER),
                    lax.dynamic_slice_in_dim(statproj, core * STATE, STATE, 1),
                ],
                axis=1,
            ),
            step_flat,
            jnp.zeros((pad_rows, 512), BF),
        ],
        axis=0,
    )
    first_all = lax.all_gather(first_block, "dp", axis=0)
    second_block = jnp.concatenate(
        [quarter(inproj[0], 1, QUARTER), quarter(outproj, 0, QUARTER).T], axis=1
    )
    second_all = lax.all_gather(second_block, "dp", axis=0, tiled=True)

    def whole_rows(array):
        mine = lax.dynamic_index_in_dim(array, core, 1, keepdims=False)
        theirs = lax.dynamic_index_in_dim(array, 1 - core, 1, keepdims=False)
        got = swap_cores(theirs)
        return by_core(
            jnp.concatenate([mine, got], axis=2), jnp.concatenate([got, mine], axis=2)
        )

    rows_whole = whole_rows(inputs)
    normed_own = rms_scale(rows_whole.astype(F32), prenorm).astype(BF)
    normed = [gather_tokens(normed_own[m]) for m in range(MB)]
    cot_own = whole_rows(cotangent)
    cots = [gather_tokens(cot_own[m]) for m in range(MB)]

    w_first = first_all[:, :rows_local].reshape(D, 512)
    state_got = swap_cores(w_first[:, QUARTER:])
    w_state = by_core(
        jnp.concatenate([w_first[:, QUARTER:], state_got], axis=1),
        jnp.concatenate([state_got, w_first[:, QUARTER:]], axis=1),
    )
    w_inner = w_first[:, :QUARTER]
    w_mixed = jnp.concatenate([w_inner, w_state], axis=1)
    w_step_all = first_all[:, rows_local : rows_local + step_flat.shape[0]].reshape(D, heads_local)
    w_step = jnp.pad(quarter(w_step_all, 1, QHEADS), ((0, 0), (0, 128 - QHEADS)))
    w_gate = second_all[:, :QUARTER]
    w_out = second_all[:, QUARTER:]

    seg_mine = jnp.concatenate(
        [
            lax.dynamic_index_in_dim(segments, core, 1),
            lax.dynamic_index_in_dim(segments, 1 - core, 1),
        ],
        axis=1,
    )
    length = segments.shape[2]
    seg_pad = jnp.pad(seg_mine, ((0, 0), (0, 0), (8, 8)), constant_values=-1)

    def seen(offset):
        return lax.slice_in_dim(seg_pad, 8 + offset, 8 + offset + length, axis=2)

    blocked = seg_mine.reshape(MB, 2, BLOCKS, SPAN)
    before = jnp.concatenate(
        [jnp.full((MB, 2, 1), -1, jnp.int32), blocked[:, :, :-1, -1]], axis=2
    )[..., None]
    flags = [(seen(j - (CONV - 1)) == seg_mine).reshape(blocked.shape) for j in range(CONV)]
    flags.append(blocked == before)
    flags.append(blocked == blocked[..., -1:])
    flags.append(blocked)
    flags.append(jnp.zeros_like(blocked))
    for j in range(CONV):
        flags.append((seen(CONV - 1 - j) == seg_mine).reshape(blocked.shape))
    cols = jnp.stack([flag.astype(F32) for flag in flags], axis=-1)
    cols = jnp.pad(cols, ((0, 0),) * 4 + ((0, 128 - len(flags)),))
    segr = jnp.broadcast_to(
        blocked.astype(F32)[:, :, :, None, :], (MB, 2, BLOCKS, 8, SPAN)
    )

    taps_inner = quarter(convinner, 1, QUARTER)
    taps = jnp.pad(jnp.concatenate([taps_inner, convstate], axis=1), ((0, 3), (0, 0)))
    head_own = quarter(headparam, 1, QHEADS)
    head = jnp.pad(
        jnp.stack([head_own[0], jnp.exp(head_own[1]), head_own[2]]),
        ((0, 5), (0, 128 - QHEADS)),
    )
    gain = quarter(gatenorm, 0, QUARTER)
    chan = jnp.pad(jnp.stack([gain, jnp.repeat(head_own[2], HEADDIM)]), ((0, 6), (0, 0)))

    def rows_dot(left, right):
        return lax.dot_general(left, right, (((3,), (0,)), ((), ())), preferred_element_type=F32)

    def rows_dot_t(left, right):
        return lax.dot_general(left, right, (((3,), (1,)), ((), ())), preferred_element_type=F32)

    def over_tokens(left, right):
        return lax.dot_general(
            left, right, (((0, 1, 2), (0, 1, 2)), ((), ())), preferred_element_type=F32
        )

    def half_rows(matrix, at):
        return lax.dynamic_slice_in_dim(matrix, at * half_d, half_d, 0)

    def to_owner(mine, theirs):
        got = swap_cores(theirs)
        total = [add_low(mine[:, s], got[::-1, s]).reshape(2 * SPAN, -1) for s in range(BLOCKS)]
        return scatter_plane(total).reshape(2, SPAN, -1)

    kept = []
    for m in range(MB):
        mixed = rows_dot(normed[m], w_mixed).astype(BF)
        raw = rows_dot(normed[m], w_step)
        gate = rows_dot(normed[m], w_gate)
        pre, y, hin, gun, sq = run_fwd(
            place, mixed, gate, raw, cols[m], segr[m], taps, head, chan
        )
        kept.append((mixed, raw, gate, pre, y, hin, gun, sq))

    layer_out = []
    g_out = None
    g_gate = None
    g_late = None
    g_gain = 0.0
    smalls = None
    d_tokens = []
    state_parts = []
    for m in range(MB):
        mixed, raw, gate, pre, y, hin, gun, sq = kept[m]
        d_gated = rows_dot(cots[m], w_out)
        cross = jnp.sum(d_gated * gun.astype(F32), axis=-1)
        sums = sum_plane_slots(jnp.stack([sq[..., 0], cross]))
        scale = lax.rsqrt(sums[0] / INNER + EPS)[..., None]
        pull = (sums[1] / INNER)[..., None] * scale * scale * scale
        mine = rows_dot_t(gun, half_rows(w_out, core)).astype(BF)
        theirs = rows_dot_t(gun, half_rows(w_out, 1 - core)).astype(BF)
        branch = to_owner(mine, theirs) * scale[:, 0]
        layer_out.append(branch)
        sigma = jax.nn.sigmoid(gate)
        gate_act = gate * sigma
        gated_in = y * gate_act
        d_in = d_gated * gain * scale - gated_in * pull
        dy = (d_in * gate_act).astype(BF)
        d_gate = (d_in * y * sigma * (1.0 + gate * (1.0 - sigma))).astype(BF)
        g_gain = g_gain + jnp.sum(d_gated * gated_in * scale, axis=(0, 1, 2))
        gated = (gun.astype(F32) * scale).astype(BF)
        g_out = add_tree(g_out, over_tokens(cots[m], gated))
        g_gate = add_tree(g_gate, over_tokens(normed[m], d_gate))
        d_late, d_bc, slope, g_taps, g_head = run_bwd(
            place, mixed, pre, raw, y, hin, dy, cols[m], segr[m], taps, head, chan
        )
        g_late = add_tree(g_late, over_tokens(normed[m], d_late))
        smalls = add_tree(smalls, (g_taps, g_head))
        w_late = jnp.concatenate([w_inner, w_step], axis=1)

        def back(at):
            total = rows_dot_t(d_gate, half_rows(w_gate, at))
            return (total + rows_dot_t(d_late, half_rows(w_late, at))).astype(BF)

        d_tokens.append(to_owner(back(core), back(1 - core)))
        keep = by_core(d_bc[..., :STATE], d_bc[..., STATE:])
        give = by_core(d_bc[..., STATE:], d_bc[..., :STATE])
        total = add_low(keep, swap_cores(give)[::-1])
        d_conv = (
            total[:, 0].astype(F32)
            + over_x(total[:, 1]).astype(F32)
            + over_y(total[:, 2]).astype(F32)
            + over_d(total[:, 3]).astype(F32)
        )
        d_pre = d_conv * by_core(slope[:, 0, :, :STATE], slope[:, 0, :, STATE:])
        state_parts.append((d_pre, by_core(
            mixed[:, 0, :, QUARTER : QUARTER + STATE], mixed[:, 0, :, QUARTER + STATE :]
        )))

    d_pre = jnp.concatenate([part[0] for part in state_parts], axis=0)
    mixed_state = jnp.concatenate([part[1] for part in state_parts], axis=0).astype(F32)
    cols_own = lax.dynamic_index_in_dim(cols, chip, 2, keepdims=False).reshape(
        2 * MB, SPAN, 128
    )
    taps_state = lax.dynamic_slice_in_dim(convstate, core * STATE, STATE, 1)
    d_mixed_state = 0.0
    g_state_taps = []
    for j in range(CONV):
        ahead = CONV - 1 - j
        window = d_pre[:, ahead : ahead + SPAN] * cols_own[:, :, 8 + j : 9 + j]
        d_mixed_state = d_mixed_state + taps_state[j] * window
        g_state_taps.append(jnp.sum(mixed_state * window, axis=(0, 1)))
    g_state_taps.append(jnp.sum(d_pre[:, :SPAN], axis=(0, 1)))
    g_state_taps = jnp.stack(g_state_taps)
    d_mixed_state = d_mixed_state.astype(BF)
    normed_block = jnp.concatenate([block[:, 0] for block in normed], axis=0)
    g_state = lax.dot_general(
        normed_block, d_mixed_state, (((0, 1), (0, 1)), ((), ())), preferred_element_type=F32
    )
    state_other = swap_cores(d_mixed_state.reshape(MB, 2, SPAN, STATE)[:, ::-1])
    state_mine = d_mixed_state.reshape(MB, 2, SPAN, STATE)
    d_state_both = by_core(
        jnp.concatenate([state_mine, state_other], axis=3),
        jnp.concatenate([state_other, state_mine], axis=3),
    )
    from_state = rows_dot_t(d_state_both, half_rows(w_state, core))

    def in_order(block):
        return by_core(block, block[:, ::-1])

    layer_out = in_order(jnp.stack(layer_out))
    outputs = (inputs.astype(F32) + layer_out).astype(BF)
    d_normed = in_order(jnp.stack(d_tokens) + from_state)
    rows_own = inputs.astype(F32)
    gain_own = lax.dynamic_slice_in_dim(prenorm, core * half_d, half_d, 0)
    weighted = d_normed * gain_own
    pair_sums = jnp.stack(
        [jnp.sum(rows_own * rows_own, axis=-1), jnp.sum(weighted * rows_own, axis=-1)]
    )
    pair_sums = pair_sums + swap_cores(pair_sums)
    root = lax.rsqrt(pair_sums[0] / D + EPS)[..., None]
    input_grads = (
        cotangent.astype(F32)
        + weighted * root
        - rows_own * root * root * root * (pair_sums[1] / D)[..., None]
    ).astype(BF)

    def over_dp(grad):
        return lax.psum_scatter(grad.astype(BF), "dp", scatter_dimension=0, tiled=True)

    g_mid = over_dp(jnp.concatenate([g_out, g_gate], axis=1))
    g_end = over_dp(jnp.concatenate([g_late, g_state], axis=1))
    columns = jnp.concatenate([g_mid, g_end], axis=1).reshape(BLOCKS, shard, -1)

    def for_slot(s):
        return lax.dynamic_index_in_dim(columns, chip ^ s, 0, keepdims=False)

    got = [for_slot(0), over_x(for_slot(1)), over_y(for_slot(2)), over_d(for_slot(3))]

    def spread(first, width, total):
        base = jnp.zeros((shard, total), F32)
        for s in range(BLOCKS):
            base = lax.dynamic_update_slice_in_dim(
                base, got[s][:, first : first + width].astype(F32), (chip ^ s) * width, 1
            )
        return base

    inner_local = BLOCKS * QUARTER
    share_out = spread(0, QUARTER, inner_local).T
    share_in = jnp.stack(
        [spread(QUARTER, QUARTER, inner_local), spread(2 * QUARTER, QUARTER, inner_local)]
    )
    share_step = spread(3 * QUARTER, QHEADS, heads_local)
    at_state = 3 * QUARTER + 128
    share_state = sum(part[:, at_state : at_state + STATE].astype(F32) for part in got)

    row_start = chip * shard
    inproj_own = lax.dynamic_slice_in_dim(inproj, row_start, shard, 1)
    outproj_own = lax.dynamic_slice_in_dim(outproj, row_start, shard, 1)
    statproj_own = lax.dynamic_slice_in_dim(
        lax.dynamic_slice_in_dim(statproj, row_start, shard, 0), core * STATE, STATE, 1
    )
    stepproj_own = lax.dynamic_slice_in_dim(stepproj, row_start, shard, 0)
    gain_part = (
        jnp.sum(inproj_own.astype(F32) * share_in, axis=(0, 2))
        + jnp.sum(statproj_own.astype(F32) * share_state, axis=1)
        + jnp.sum(stepproj_own.astype(F32) * share_step, axis=1)
    )
    gain_part = gain_part + swap_cores(gain_part)
    gain_at = data_at * rows_local + row_start
    g_prenorm = gain_part / lax.dynamic_slice_in_dim(prenorm, gain_at, shard, 0)

    g_taps, g_head = smalls

    def put(values, width, total):
        base = jnp.zeros(values.shape[:-1] + (total,), F32)
        return lax.dynamic_update_slice_in_dim(base, values, chip * width, values.ndim - 1)

    small_parts = [
        put(g_taps[: CONV + 1], QUARTER, inner_local),
        put(g_gain, QUARTER, inner_local),
        put(g_head[:3, :QHEADS], QHEADS, heads_local),
        g_state_taps,
    ]
    sizes = [part.size for part in small_parts]
    vector = jnp.concatenate([part.reshape(-1) for part in small_parts])
    vector = jnp.pad(vector, (0, -vector.size % 1024)).reshape(-1, 128)

    def sum_all(value):
        value = value + over_x(value)
        value = value + over_y(value)
        hop = 1
        while hop < dp_count:
            value = value + lax.ppermute(value, "dp", [(i, i ^ hop) for i in range(dp_count)])
            hop *= 2
        return value

    vector = sum_all(vector).reshape(-1)
    small_sums = []
    start = 0
    for part, size in zip(small_parts, sizes):
        small_sums.append(vector[start : start + size].reshape(part.shape))
        start += size
    s_taps, s_gain, s_head, s_state_taps = small_sums

    big = (share_in, share_out, share_state, share_step)
    owner_sq = sum(jnp.sum(term * term) for term in big)
    small_sq = sum(jnp.sum(term * term) for term in small_sums)
    first_owner = jnp.where((data_at == 0) & (chip == 0), 1.0, 0.0)
    local_sq = owner_sq + first_owner * small_sq
    local_sq = local_sq + swap_cores(local_sq) + jnp.sum(g_prenorm * g_prenorm)
    last = jnp.zeros((D + 128,), F32)
    last = lax.dynamic_update_slice_in_dim(last, g_prenorm, gain_at, 0)
    last = last.at[D].set(local_sq)
    last = sum_all(last)
    grad_norm = jnp.sqrt(last[D])
    s_prenorm = lax.dynamic_slice_in_dim(last, core * half_d, half_d, 0)

    entries = (
        2 * D * INNER
        + 2 * D * STATE
        + D * (INNER // HEADDIM)
        + INNER * D
        + (CONV + 1) * (INNER + 2 * STATE)
        + 3 * (INNER // HEADDIM)
        + INNER
        + D
    )
    limit = CLIP_RMS * math.sqrt(entries)
    factor = limit / jnp.maximum(grad_norm, limit)

    def moved(moment, grad):
        return 0.5 * moment + 0.5 * factor * grad

    def stepped(weight, moment):
        return (weight.astype(F32) - LEARN * moment).astype(weight.dtype)

    new_prenorm = moved(prenorm_moment, s_prenorm)
    new_in = moved(inproj_moment, share_in)
    new_state = moved(statproj_moment, share_state)
    new_step = moved(stepproj_moment, share_step)
    new_out = moved(outproj_moment, share_out)
    new_taps = moved(convinner_moment, s_taps)
    new_state_taps = moved(convstate_moment, s_state_taps)
    new_head = moved(headparam_moment, s_head)
    new_gain = moved(gatenorm_moment, s_gain)
    return (
        outputs,
        input_grads,
        grad_norm,
        new_prenorm,
        new_in,
        new_state,
        new_step,
        new_out,
        new_taps,
        new_state_taps,
        new_head,
        new_gain,
        stepped(inproj_own, new_in),
        stepped(statproj_own, new_state),
        stepped(stepproj_own, new_step),
        stepped(outproj_own, new_out),
        stepped(convinner, new_taps),
        stepped(lax.dynamic_slice_in_dim(convstate, core * STATE, STATE, 1), new_state_taps),
    )


def solution(mesh):
    fast = mesh.shape["seq"] == BLOCKS and mesh.shape["tensor"] == 2
    return jax.shard_map(
        fast_body if fast else general_body,
        mesh=mesh,
        in_specs=(
            P(None, "dp", "seq", "tensor"),
            P(None, "dp", None),
            P(None, "dp", "seq", "tensor"),
            P(),
            P(None, "dp", "tensor"),
            P("dp", None),
            P("dp", "tensor"),
            P("tensor", "dp"),
            P(None, "tensor"),
            P(),
            P(None, "tensor"),
            P("tensor"),
            P("tensor"),
            P(None, ("dp", "seq"), "tensor"),
            P(("dp", "seq"), "tensor"),
            P(("dp", "seq"), "tensor"),
            P("tensor", ("dp", "seq")),
            P(None, "tensor"),
            P(None, "tensor"),
            P(None, "tensor"),
            P("tensor"),
        ),
        out_specs=(
            P(None, "dp", "seq", "tensor"),
            P(None, "dp", "seq", "tensor"),
            P(),
            P("tensor"),
            P(None, ("dp", "seq"), "tensor"),
            P(("dp", "seq"), "tensor"),
            P(("dp", "seq"), "tensor"),
            P("tensor", ("dp", "seq")),
            P(None, "tensor"),
            P(None, "tensor"),
            P(None, "tensor"),
            P("tensor"),
            P(None, ("dp", "seq"), "tensor"),
            P(("dp", "seq"), "tensor"),
            P(("dp", "seq"), "tensor"),
            P("tensor", ("dp", "seq")),
            P(None, "tensor"),
            P(None, "tensor"),
        ),
        check_vma=False,
    )
```

```python
import math

import jax
import jax.numpy as jnp
from jax import lax
from jax.experimental import pallas as pl
from jax.experimental.pallas import tpu as pltpu
from jax.sharding import PartitionSpec as P

D = 1536
INNER = 3072
HEADDIM = 64
STATE = 128
CONV = 4
MB = 2


EPS = 1e-05
LEARN = 0.05
CLIP_RMS = 0.25
HIGH = lax.Precision.HIGHEST


def shifted(block, axis, distance):
    devices = range(lax.axis_size(axis))
    route = [(i - distance, i) for i in devices if i - distance in devices]
    return lax.ppermute(block, axis, route)


def prefix(array, axis, combine, identity):
    size, position = (lax.axis_size(axis), lax.axis_index(axis))
    everything = jax.tree.map(
        lambda part, kind: lax.all_gather(part.astype(kind), axis),
        array,
        (jnp.bfloat16, jnp.bfloat16),
    )
    start = jax.tree.map(
        lambda part, zero: jnp.broadcast_to(jnp.asarray(zero, part.dtype), part.shape),
        array,
        identity,
    )

    def prefix_step(k, before):
        reached = k < position
        new = combine(
            before, jax.tree.map(lambda part, own: part[k].astype(own.dtype), everything, array)
        )
        return jax.tree.map(lambda a, b: jnp.where(reached, a, b), new, before)

    return lax.fori_loop(0, size, prefix_step, start)


def entering_2(array, axis, combine, identity):
    size, position = (lax.axis_size(axis), lax.axis_index(axis))
    everything = jax.tree.map(lambda part: lax.all_gather(part, axis), array)
    start = jax.tree.map(
        lambda part, zero: jnp.broadcast_to(jnp.asarray(zero, part.dtype), part.shape),
        array,
        identity,
    )

    def entering_step(k, before):
        at = size - 1 - k
        reached = at > position
        new = combine(before, jax.tree.map(lambda part: part[at], everything))
        return jax.tree.map(lambda a, b: jnp.where(reached, a, b), new, before)

    return lax.fori_loop(0, size, entering_step, start)


def rms_scale(values, weight):
    return values * lax.rsqrt(jnp.mean(values * values, axis=-1, keepdims=True) + EPS) * weight


def conv_block(padded, seg_pad, kernel):
    length = padded.shape[0] - (CONV - 1)
    own_seg = seg_pad[CONV - 1 :]
    summed = jnp.broadcast_to(kernel[CONV], (length, kernel.shape[1]))
    for offset in range(CONV):
        window = padded[offset : offset + length]
        same_doc = (seg_pad[offset : offset + length] == own_seg)[:, None]
        summed = summed + kernel[offset] * jnp.where(same_doc, window, 0.0)
    return jax.nn.silu(summed)


def decay_table(cumulative, segids):
    row_count = segids.shape[0]
    places = jnp.arange(row_count)
    allowed = (segids[:, None] == segids[None, :]) & (places[:, None] >= places[None, :])
    allowed = allowed[:, :, None]
    gap_values = cumulative[:, None, :] - cumulative[None, :, :]
    return jnp.where(allowed, jnp.exp(jnp.where(allowed, gap_values, -60.0)), 0.0)


def head_rates(raw_step, params):
    step_sizes = jax.nn.softplus(raw_step + params[0])
    return (step_sizes, jnp.cumsum(-step_sizes * jnp.exp(params[1]), axis=0))


def mix_out(values, b_proj, c_proj, raw_step, params, segids, before, carry_in):
    step_sizes, cumulative = head_rates(raw_step, params)
    scores = jnp.dot(c_proj, b_proj.T, precision=HIGH)
    weights = scores[:, :, None] * decay_table(cumulative, segids) * step_sizes[None, :, :]
    result = jnp.einsum("tsh,shp->thp", weights, values, precision=HIGH)
    entering = jnp.where((segids == before)[:, None], jnp.exp(cumulative), 0.0)
    carried = jnp.einsum("tn,hpn->thp", c_proj, carry_in, precision=HIGH)
    return result + entering[:, :, None] * carried + params[2][None, :, None] * values


def mix_state(values, b_proj, raw_step, params, segids, before):
    step_sizes, cumulative = head_rates(raw_step, params)
    tail_weight = (
        jnp.where(
            (segids == segids[-1])[:, None], jnp.exp(cumulative[-1][None, :] - cumulative), 0.0
        )
        * step_sizes
    )
    summary = jnp.einsum("sh,shp,sn->hpn", tail_weight, values, b_proj, precision=HIGH)
    passing = jnp.where(segids[-1] == before, jnp.exp(cumulative[-1]), 0.0)
    return (summary, passing)


def chain(earlier, later):
    return (earlier[0] * later[0], later[0][..., None, None] * earlier[1] + later[1])


def add_tree(totals, terms):
    if totals is None:
        return terms
    return jax.tree.map(jnp.add, totals, terms)


def project(left_rows, matrix):
    return jnp.einsum("bld,dk->blk", left_rows, matrix, preferred_element_type=jnp.float32)


def weight_grad(left_rows, right_rows):
    return jnp.einsum("bld,blk->dk", left_rows, right_rows, preferred_element_type=jnp.float32)


def back_project(grad_rows, matrix):
    return jnp.einsum("blk,dk->bld", grad_rows, matrix, preferred_element_type=jnp.float32)


def general_body(
    inputs,
    segments,
    cotangent,
    prenorm,
    inproj,
    statproj,
    stepproj,
    outproj,
    convinner,
    convstate,
    headparam,
    gatenorm,
    prenorm_moment,
    inproj_moment,
    statproj_moment,
    stepproj_moment,
    outproj_moment,
    convinner_moment,
    convstate_moment,
    headparam_moment,
    gatenorm_moment,
):
    tensor_at = lax.axis_index("tensor")
    seq_at = lax.axis_index("seq")
    data_at = lax.axis_index("dp")
    tensor_count = lax.axis_size("tensor")
    batch_count = inputs.shape[1]
    span_len = inputs.shape[2]
    inner_local = convinner.shape[1]
    heads_local = headparam.shape[1]
    state_half = 2 * STATE // tensor_count
    model_half = D // tensor_count
    rows_full, grads_full = (
        lax.all_gather(inputs, "tensor", axis=3, tiled=True),
        lax.all_gather(cotangent, "tensor", axis=3, tiled=True),
    )
    seg_padded = jnp.pad(segments, ((0, 0), (0, 0), (CONV - 1, 0)), constant_values=-1)
    seg_local = lax.dynamic_slice_in_dim(seg_padded, seq_at * span_len, span_len + CONV - 1, 2)
    kernel = jnp.concatenate([convinner, convstate], axis=1)
    shares = None
    smalls = None
    outputs = []
    input_grads = []
    for batch in range(MB):
        inproj_all, statproj_all, stepproj_all, outproj_all = (
            lax.all_gather(inproj, "dp", axis=1, tiled=True),
            lax.all_gather(statproj, "dp", axis=0, tiled=True),
            lax.all_gather(stepproj, "dp", axis=0, tiled=True),
            lax.all_gather(outproj, "dp", axis=1, tiled=True),
        )
        rows = rows_full[batch].astype(jnp.float32)
        normed, norm_back = jax.vjp(rms_scale, rows, prenorm)
        normed_low = normed.astype(jnp.bfloat16)
        gate_pre = project(normed_low, inproj_all[0])
        inner_pre = project(normed_low, inproj_all[1])
        state_pre = project(normed_low, statproj_all)
        raw_step = project(normed_low, stepproj_all)
        mixed = jnp.concatenate([inner_pre, state_pre], axis=2).astype(jnp.bfloat16)
        edge_in = shifted(mixed[:, span_len - (CONV - 1) :, :], "seq", 1)
        padded = jnp.concatenate([edge_in, mixed], axis=1).astype(jnp.float32)
        seg_now = seg_local[batch]
        own_seg = seg_now[:, CONV - 1 :]
        before = seg_now[:, CONV - 2]
        conv_out, conv_back = jax.vjp(
            lambda pad_vals, kernel_in: jax.vmap(conv_block, in_axes=(0, 0, None))(
                pad_vals, seg_now, kernel_in
            ),
            padded,
            kernel,
        )
        values = conv_out[..., :inner_local].reshape(batch_count, span_len, heads_local, HEADDIM)
        b_proj = conv_out[..., inner_local : inner_local + STATE]
        c_proj = conv_out[..., inner_local + STATE :]
        (summary, passing), state_back = jax.vjp(
            lambda value_in, b_part, raw_part, param_in: jax.vmap(
                mix_state, in_axes=(0, 0, 0, None, 0, 0)
            )(value_in, b_part, raw_part, param_in, own_seg, before),
            values,
            b_proj,
            raw_step,
            headparam,
        )
        identity = (jnp.ones_like(passing), jnp.zeros_like(summary))
        _, carry_in = prefix((passing, summary), "seq", chain, identity)
        mixer, out_back = jax.vjp(
            lambda value_in, b_part, c_part, raw_part, param_in, state_in: jax.vmap(
                mix_out, in_axes=(0, 0, 0, 0, None, 0, 0, 0)
            )(value_in, b_part, c_part, raw_part, param_in, own_seg, before, state_in),
            values,
            b_proj,
            c_proj,
            raw_step,
            headparam,
            carry_in,
        )
        flat_mixer = mixer.reshape(batch_count, span_len, inner_local)
        gate_act = jax.nn.silu(gate_pre)
        gated_in = flat_mixer * gate_act
        total_sq = lax.psum(jnp.sum(gated_in * gated_in, axis=-1), "tensor")
        scale = lax.rsqrt(total_sq / INNER + EPS)[..., None]
        gated_low = (gated_in * scale * gatenorm).astype(jnp.bfloat16)
        branch_part = project(gated_low, outproj_all)
        branch_own = lax.psum_scatter(branch_part, "tensor", scatter_dimension=2, tiled=True)
        outputs.append((inputs[batch].astype(jnp.float32) + branch_own).astype(jnp.bfloat16))
        grad_rows = grads_full[batch]
        d_gated = back_project(grad_rows, outproj_all)
        g_outproj = jnp.einsum(
            "blk,bld->kd", gated_low, grad_rows, preferred_element_type=jnp.float32
        )
        g_gatenorm = jnp.sum(d_gated * gated_in * scale, axis=(0, 1))
        weighted = d_gated * gatenorm
        cross = lax.psum(jnp.sum(weighted * gated_in, axis=-1), "tensor")
        d_in = weighted * scale - gated_in * scale**3 * (cross / INNER)[..., None]
        d_mixer = d_in * gate_act
        sigma = jax.nn.sigmoid(gate_pre)
        d_gate = d_in * flat_mixer * sigma * (1.0 + gate_pre * (1.0 - sigma))
        d_values, d_bproj, d_cproj, d_raw, d_param, d_carry = out_back(
            d_mixer.reshape(batch_count, span_len, heads_local, HEADDIM)
        )
        _, d_after = entering_2((passing, d_carry), "seq", chain, identity)
        d_passing = jnp.sum(d_after * carry_in, axis=(2, 3))
        d_values_tail, d_bproj_tail, d_raw_tail, d_param_tail = state_back((d_after, d_passing))
        d_state = lax.psum(jnp.concatenate([d_bproj + d_bproj_tail, d_cproj], axis=2), "tensor")
        d_conv = jnp.concatenate(
            [(d_values + d_values_tail).reshape(batch_count, span_len, inner_local), d_state],
            axis=2,
        )
        d_padded, d_kernel = conv_back(d_conv)
        edge_back = shifted(d_padded[:, : CONV - 1, :].astype(jnp.bfloat16), "seq", -1).astype(
            jnp.float32
        )
        d_mixed = d_padded[:, CONV - 1 :, :] + jnp.pad(
            edge_back, ((0, 0), (span_len - (CONV - 1), 0), (0, 0))
        )
        d_mixed_low = d_mixed.astype(jnp.bfloat16)
        d_gate_low = d_gate.astype(jnp.bfloat16)
        d_raw_low = (d_raw + d_raw_tail).astype(jnp.bfloat16)
        d_inner_low = d_mixed_low[..., :inner_local]
        d_state_low = lax.dynamic_slice_in_dim(
            d_mixed_low[..., inner_local:], tensor_at * state_half, state_half, 2
        )
        statproj_own = lax.dynamic_slice_in_dim(statproj_all, tensor_at * state_half, state_half, 1)
        g_inproj = jnp.stack(
            [weight_grad(normed_low, d_gate_low), weight_grad(normed_low, d_inner_low)]
        )
        g_statproj = weight_grad(normed_low, d_state_low)
        g_stepproj = weight_grad(normed_low, d_raw_low)
        d_normed_part = (
            back_project(d_gate_low, inproj_all[0])
            + back_project(d_inner_low, inproj_all[1])
            + back_project(d_state_low, statproj_own)
            + back_project(d_raw_low, stepproj_all)
        )
        d_normed = lax.psum(d_normed_part, "tensor")
        d_rows, d_prenorm = norm_back(d_normed)
        own_rows = lax.dynamic_slice_in_dim(d_rows, tensor_at * model_half, model_half, 2)
        input_grads.append((own_rows + cotangent[batch].astype(jnp.float32)).astype(jnp.bfloat16))
        big_terms = (g_inproj, g_outproj, g_statproj, g_stepproj)
        small_terms = (
            lax.dynamic_slice_in_dim(d_prenorm, tensor_at * model_half, model_half, 0),
            d_kernel[:, :inner_local],
            lax.dynamic_slice_in_dim(
                d_kernel[:, inner_local:], tensor_at * state_half, state_half, 1
            ),
            d_param + d_param_tail,
            g_gatenorm,
        )
        shares = add_tree(
            shares,
            (
                lax.psum_scatter(big_terms[0], ("dp", "seq"), scatter_dimension=1, tiled=True),
                lax.psum_scatter(big_terms[1], ("dp", "seq"), scatter_dimension=1, tiled=True),
                lax.psum_scatter(big_terms[2], ("dp", "seq"), scatter_dimension=0, tiled=True),
                lax.psum_scatter(big_terms[3], ("dp", "seq"), scatter_dimension=0, tiled=True),
            ),
        )
        smalls = add_tree(
            smalls,
            lax.psum(
                (small_terms[0], small_terms[1], small_terms[2], small_terms[3], small_terms[4]),
                ("dp", "seq"),
            ),
        )
    big_sq = jnp.sum(jnp.stack([jnp.sum(term * term) for term in shares]))
    small_sq = jnp.sum(jnp.stack([jnp.sum(term * term) for term in smalls]))
    first_owner = jnp.where((data_at == 0) & (seq_at == 0), 1.0, 0.0)
    norm_sq = lax.psum(big_sq + first_owner * small_sq, ("dp", "seq", "tensor"))
    grad_norm = jnp.sqrt(norm_sq)
    heads_all = INNER // HEADDIM
    entries = (
        2 * D * INNER
        + 2 * D * STATE
        + D * heads_all
        + INNER * D
        + (CONV + 1) * (INNER + 2 * STATE)
        + 3 * heads_all
        + INNER
        + D
    )
    limit = CLIP_RMS * math.sqrt(entries)
    factor = limit / jnp.maximum(grad_norm, limit)
    shard_rows = shares[0].shape[1]
    row_start = seq_at * shard_rows
    big_current = (
        lax.dynamic_slice_in_dim(inproj, row_start, shard_rows, 1),
        lax.dynamic_slice_in_dim(outproj, row_start, shard_rows, 1),
        lax.dynamic_slice_in_dim(
            lax.dynamic_slice_in_dim(statproj, row_start, shard_rows, 0),
            tensor_at * state_half,
            state_half,
            1,
        ),
        lax.dynamic_slice_in_dim(stepproj, row_start, shard_rows, 0),
    )
    conv_current = (
        convinner,
        lax.dynamic_slice_in_dim(convstate, tensor_at * state_half, state_half, 1),
    )
    big_moments = (inproj_moment, outproj_moment, statproj_moment, stepproj_moment)
    small_moments = (
        prenorm_moment,
        convinner_moment,
        convstate_moment,
        headparam_moment,
        gatenorm_moment,
    )
    big_new_moments = [
        0.5 * moment_item + 0.5 * factor * grad_item
        for moment_item, grad_item in zip(big_moments, shares)
    ]
    small_new_moments = [
        0.5 * moment_item + 0.5 * factor * grad_item
        for moment_item, grad_item in zip(small_moments, smalls)
    ]
    big_new = [
        (weight_item.astype(jnp.float32) - LEARN * moment_item).astype(weight_item.dtype)
        for weight_item, moment_item in zip(big_current, big_new_moments)
    ]
    conv_new = [
        (weight_item - LEARN * moment_item).astype(weight_item.dtype)
        for weight_item, moment_item in zip(conv_current, small_new_moments[1:3])
    ]
    return (
        jnp.stack(outputs),
        jnp.stack(input_grads),
        grad_norm,
        small_new_moments[0],
        big_new_moments[0],
        big_new_moments[2],
        big_new_moments[3],
        big_new_moments[1],
        small_new_moments[1],
        small_new_moments[2],
        small_new_moments[3],
        small_new_moments[4],
        big_new[0],
        big_new[2],
        big_new[3],
        big_new[1],
        conv_new[0],
        conv_new[1],
    )


BLOCKS = 4
SPAN = 256
PART = 128
PARTS = SPAN // PART
PACKED = 48
QUARTER = 384
QHEADS = 6
BF = jnp.bfloat16
F32 = jnp.float32
ROUTE_X = [(i, i ^ 1) for i in range(BLOCKS)]
ROUTE_Y = [(i, i ^ 2) for i in range(BLOCKS)]
SWAP = [(0, 1), (1, 0)]
VMEM_LIMIT = 56 * 1024 * 1024


def dot_nn(a, b):
    return lax.dot_general(a, b, (((1,), (0,)), ((), ())), preferred_element_type=F32)


def dot_nt(a, b):
    return lax.dot_general(a, b, (((1,), (1,)), ((), ())), preferred_element_type=F32)


def dot_tn(a, b):
    return lax.dot_general(a, b, (((0,), (0,)), ((), ())), preferred_element_type=F32)


def dot_exact(a, b):
    return lax.dot_general(
        a, b, (((1,), (0,)), ((), ())), precision=HIGH, preferred_element_type=F32
    )


def sigmoid(v):
    return 1.0 / (1.0 + jnp.exp(-v))


def pair_cols(table, k, low_half):
    return jnp.where(low_half, table[:, 2 * k : 2 * k + 1], table[:, 2 * k + 1 : 2 * k + 2])


def split_sum(triangle, table):
    first = table.astype(BF)
    rest = table - first.astype(F32)
    second = rest.astype(BF)
    third = (rest - second.astype(F32)).astype(BF)
    parts = (
        first.astype(F32)
        + pltpu.roll(second.astype(F32), 8, 1)
        + pltpu.roll(third.astype(F32), 16, 1)
    )
    sums = dot_nn(triangle, parts.astype(BF))
    return sums + pltpu.roll(sums, 120, 1) + pltpu.roll(sums, 112, 1)


def head_sums(table, gather):
    first = table.astype(BF)
    second = (table - first.astype(F32)).astype(BF)
    return dot_nn(first, gather) + dot_nn(second, gather)


def rates(raw, head):
    shifted_raw = raw + head[0:1]
    step = jnp.maximum(shifted_raw, 0.0) + jnp.log1p(jnp.exp(-jnp.abs(shifted_raw)))
    lanes = lax.broadcasted_iota(jnp.int32, raw.shape, 1)
    return shifted_raw, jnp.where(lanes < QHEADS, step, 0.0)


def triangle(keep):
    rows_at = lax.broadcasted_iota(jnp.int32, (PART, PART), 0)
    cols_at = lax.broadcasted_iota(jnp.int32, (PART, PART), 1)
    return jnp.where(keep(rows_at, cols_at), 1.0, 0.0).astype(BF)


def part_terms(step, head, cols, segr):
    cum = split_sum(triangle(lambda r, c: r >= c), -step * head[1:2])
    last = cum[PART - 1 : PART]
    enter = jnp.exp(cum) * cols[:, 4:5]
    leave = jnp.exp(last - cum) * cols[:, 5:6]
    passing = jnp.exp(last) * cols[PART - 1 : PART, 4:5]
    rows_at = lax.broadcasted_iota(jnp.int32, (PART, PART), 0)
    cols_at = lax.broadcasted_iota(jnp.int32, (PART, PART), 1)
    allowed = (rows_at >= cols_at) & (cols[:, 6:7] == segr)
    return cum, enter, leave, passing, jnp.where(allowed, 0.0, -1e30)


def segment_flags(seg_ref, block):
    begin = pl.multiple_of(block * SPAN, 128)
    around = seg_ref[0, :, pl.ds(begin, SPAN + 256)]
    here = around[:, 128 : 128 + SPAN]
    flags = []
    for shift in (3, 2, 1, 0):
        flags.append(pltpu.roll(around, shift, 1)[:, 128 : 128 + SPAN] == here)
    ends = [around[:, PART * k + 127 : PART * k + 128] for k in range(PARTS + 1)]
    parts = [here[:, PART * k : PART * (k + 1)] for k in range(PARTS)]
    flags.append(jnp.concatenate([parts[k] == ends[k] for k in range(PARTS)], axis=1))
    flags.append(jnp.concatenate([parts[k] == ends[k + 1] for k in range(PARTS)], axis=1))
    for shift in (3, 2, 1, 0):
        later = pltpu.roll(around, SPAN + 256 - shift, 1) if shift else around
        flags.append(later[:, 128 : 128 + SPAN] == here)
    flags = [jnp.where(flag, 1.0, 0.0) for flag in flags]
    at = lax.broadcasted_iota(jnp.int32, (8, SPAN), 0)
    first = here
    for row in range(6):
        first = jnp.where(at == row, flags[row], first)
    second = flags[9]
    for row in range(3):
        second = jnp.where(at == row, flags[6 + row], second)
    return jnp.concatenate([first, second], axis=0)


def to_columns(rows):
    filled = jnp.concatenate([rows, jnp.zeros((128 - rows.shape[0], SPAN), F32)], axis=0)
    return filled.T


def current(own_ref, other_ref):
    return jnp.where(pl.program_id(0) == 0, own_ref[0], other_ref[0])


def current_halves(own_refs, other_refs):
    halves = [current(own, other) for own, other in zip(own_refs, other_refs)]
    return jnp.concatenate(halves, axis=0)


def fwd_kernel(
    place_ref, own_ref, other_ref, w_ref, seg_ref, taps_ref, head_ref, chan_ref, mixed_ref, raw_ref, pre_ref, y_ref, hin_ref, buf, state,
):
    @pl.when(pl.program_id(1) == 0)
    def _():
        buf[0:8] = jnp.zeros((8, buf.shape[1]), F32)
        state[...] = jnp.zeros_like(state)

    width = QUARTER + 2 * STATE
    projected = dot_nn(current(own_ref, other_ref), w_ref[...])
    raw = projected[:, width:]
    raw_ref[0, 0] = raw
    mixed_low = projected[:, :width].astype(BF)
    mixed_ref[0, 0] = mixed_low
    mixed = mixed_low.astype(F32)
    buf[8 : 8 + SPAN] = mixed
    rows = segment_flags(seg_ref, pl.program_id(1))
    cols_all = to_columns(rows)
    taps = taps_ref[...]
    head = head_ref[...]
    pre = jnp.broadcast_to(taps[CONV : CONV + 1], mixed.shape)
    for j in range(CONV):
        window = mixed if j == CONV - 1 else buf[5 + j : 5 + j + SPAN]
        pre = pre + taps[j : j + 1] * (window * cols_all[:, j : j + 1])
    buf[0:8] = mixed[SPAN - 8 :]
    pre_ref[0, 0] = pre
    act = pre * sigmoid(pre)
    _, step_all = rates(raw, head)
    skip = chan_ref[1:2]
    low_half = lax.broadcasted_iota(jnp.int32, (PART, 128), 1) < HEADDIM
    zero_low = jnp.zeros((PART, 128), BF)
    for part in range(SPAN // PART):
        at_rows = slice(part * PART, (part + 1) * PART)
        cols = cols_all[at_rows]
        values = act[at_rows, :QUARTER]
        b_low = act[at_rows, QUARTER : QUARTER + STATE].astype(BF)
        c_low = act[at_rows, QUARTER + STATE :].astype(BF)
        step = step_all[at_rows]
        cum, enter, leave, passing, block_out = part_terms(step, head, cols, rows[6:7, at_rows])
        cum_t = cum.T
        scores = dot_nt(c_low, b_low)
        held_f = state[...]
        held = held_f.astype(BF)
        hin_ref[0, 0, QUARTER * part : QUARTER * (part + 1)] = held
        carried = dot_nt(c_low, held)
        tails = []
        for k in range(QHEADS // 2):
            at = slice(128 * k, 128 * (k + 1))
            scaled = (pair_cols(step, k, low_half) * values[:, at]).astype(BF)
            weights = []
            for h in (2 * k, 2 * k + 1):
                decay = jnp.exp(cum[:, h : h + 1] - cum_t[h : h + 1] + block_out)
                weights.append((scores * decay).astype(BF))
            both = jnp.concatenate(
                [jnp.where(low_half, scaled, zero_low), jnp.where(low_half, zero_low, scaled)],
                axis=0,
            )
            own = dot_nn(jnp.concatenate(weights, axis=1), both)
            y_ref[0, 0, at_rows, at] = (
                own
                + pair_cols(enter, k, low_half) * carried[:, at]
                + skip[:, at] * values[:, at]
            )
            tails.append((pair_cols(leave, k, low_half) * scaled.astype(F32)).astype(BF))
        added = dot_tn(jnp.concatenate(tails, axis=1), b_low)
        for h in range(QHEADS):
            at = slice(HEADDIM * h, HEADDIM * (h + 1))
            state[at] = passing[:, h : h + 1] * held_f[at] + added[at]


def core_rows(place_ref):
    half = D // 2
    core = place_ref[0]
    own = pl.multiple_of(core * half, half)
    other = pl.multiple_of((1 - core) * half, half)
    return pl.ds(own, half), pl.ds(other, half)


def gate_kernel(
    place_ref, own_ref, other_ref, cot_own_0, cot_own_1, cot_other_0, cot_other_1, y_ref,
    w_gate_ref, w_out_ref, chan_ref,
    gate_ref, d_gated_ref, mine_ref, theirs_ref, stat_ref,
):
    gate = dot_nn(current(own_ref, other_ref), w_gate_ref[...])
    gate_ref[0, 0] = gate
    gated_in = y_ref[0, 0] * (gate * sigmoid(gate))
    weighted = gated_in * chan_ref[0:1]
    gun = weighted.astype(BF)
    cot = current_halves((cot_own_0, cot_own_1), (cot_other_0, cot_other_1))
    d_gated = dot_nn(cot, w_out_ref[...])
    d_gated_ref[0, 0] = d_gated
    own, other = core_rows(place_ref)
    mine_ref[0, 0] = dot_nt(gun, w_out_ref[own]).astype(BF)
    theirs_ref[0, 0] = dot_nt(gun, w_out_ref[other]).astype(BF)
    square = jnp.sum(gated_in * gated_in, axis=1, keepdims=True)
    cross = jnp.sum(d_gated * weighted, axis=1, keepdims=True)
    lanes = lax.broadcasted_iota(jnp.int32, (SPAN, 128), 1)
    table = jnp.where(lanes == 0, square, jnp.where(lanes == 1, cross, 0.0))
    stat_ref[0, 0] = table.T[0:8]


def start_sums(total, seed_ref):
    @pl.when((pl.program_id(0) == 0) & (pl.program_id(1) == 0))
    def _():
        total[...] = jnp.zeros_like(total) if seed_ref is None else seed_ref[...]


def finish_sums(total, out_ref):
    @pl.when((pl.program_id(0) == 1) & (pl.program_id(1) == BLOCKS - 1))
    def _():
        rows_of = out_ref.shape[2]
        for z in range(out_ref.shape[0]):
            out_ref[z] = total[:, z * rows_of : (z + 1) * rows_of].astype(BF)


def gate_back_first(*refs):
    gate_back_step(*refs[:12], None, *refs[12:])


def gate_back_last(*refs):
    gate_back_step(*refs[:13], *refs[13:16], refs[17])
    finish_sums(refs[17], refs[16])


def gate_back_step(
    place_ref, own_ref, other_ref, cot_own_0, cot_own_1, cot_other_0, cot_other_1, y_ref,
    gate_ref, d_gated_ref, stat_ref, chan_ref, seed_ref,
    dy_ref, d_gate_ref, g_gain_ref, g_ref,
):
    start_sums(g_ref, seed_ref)
    start_sums(g_gain_ref, None)
    stat = to_columns(stat_ref[0, 0])
    scale = lax.rsqrt(stat[:, 0:1] * (1.0 / INNER) + EPS)
    pull = stat[:, 1:2] * (1.0 / INNER) * scale * scale * scale
    gate = gate_ref[0, 0]
    y = y_ref[0, 0]
    sigma = sigmoid(gate)
    gate_act = gate * sigma
    gated_in = y * gate_act
    scaled_gain = chan_ref[0:1] * scale
    d_in = d_gated_ref[0, 0] * scaled_gain - gated_in * pull
    dy_ref[0, 0] = (d_in * gate_act).astype(BF)
    d_gate = (d_in * y * (sigma + gate_act * (1.0 - sigma))).astype(BF)
    d_gate_ref[0, 0] = d_gate
    gated = (gated_in * scaled_gain).astype(BF)
    by_gain = d_gated_ref[0, 0] * gated_in * scale
    g_gain_ref[0:1] += jnp.sum(by_gain, axis=0, keepdims=True)
    cot = current_halves((cot_own_0, cot_own_1), (cot_other_0, cot_other_1))
    g_ref[:QUARTER] += dot_tn(gated, cot)
    g_ref[QUARTER:] += dot_tn(d_gate, current(own_ref, other_ref))


def bwd_first(*refs):
    bwd_step(*refs[:16], None, refs[16], None, None, *refs[17:])


def bwd_last(*refs):
    total = refs[-1]
    bwd_step(*refs[:17], total, *refs[18:-1])
    finish_sums(total, refs[17])


def bwd_step(
    place_ref, own_ref, other_ref, mixed_ref, pre_ref, raw_ref, y_ref, hin_ref, dy_ref,
    d_gate_ref, seg_ref, taps_ref, head_ref, chan_ref, w_ref, w_gate_ref,
    seed_ref,
    g_ref, keep_ref, give_ref, slope_ref, gtap_ref, ghead_ref, mine_ref, theirs_ref,
    buf, d_state, bc_edge, slope_edge, d_late,
):
    start_sums(g_ref, seed_ref)

    @pl.when(pl.program_id(1) == 0)
    def _():
        buf[SPAN:] = jnp.zeros((8, QUARTER), F32)
        d_state[...] = jnp.zeros_like(d_state)
        bc_edge[...] = jnp.zeros_like(bc_edge)
        slope_edge[...] = jnp.zeros_like(slope_edge)

    @pl.when((pl.program_id(0) == 0) & (pl.program_id(1) == 0))
    def _():
        gtap_ref[...] = jnp.zeros_like(gtap_ref)
        ghead_ref[...] = jnp.zeros_like(ghead_ref)

    rows = segment_flags(seg_ref, BLOCKS - 1 - pl.program_id(1))
    cols_all = to_columns(rows)
    head = head_ref[...]
    taps = taps_ref[...]
    pre = pre_ref[0, 0]
    sigma = sigmoid(pre)
    act = pre * sigma
    slope = sigma * (1.0 + pre * (1.0 - sigma))
    first_core = place_ref[0] == 0

    def store(ref, first_row, rows):
        if keep_ref is not None:
            ref[0, 0, first_row : first_row + rows.shape[0]] = rows
            return
        for at in range(first_row, first_row + rows.shape[0], 16):
            group = at // PACKED
            row = SPAN + at % PACKED
            ref[0, 0, row : row + 16, 128 * group : 128 * (group + 1)] = rows[
                at - first_row : at - first_row + 16
            ]

    keep_at = mine_ref if keep_ref is None else keep_ref
    give_at = theirs_ref if give_ref is None else give_ref
    slope_half = jnp.where(
        first_core, slope[:, QUARTER : QUARTER + STATE], slope[:, QUARTER + STATE :]
    )
    slope_ref[0, 0, 0:SPAN] = slope_half
    slope_ref[0, 0, SPAN : SPAN + 16] = slope_edge[...]
    slope_edge[...] = slope_half[0:16]
    if keep_ref is None:
        for ref in (mine_ref, theirs_ref):
            ref[0, 0, SPAN + 32 :, 640:] = jnp.zeros((16, 128), BF)
    store(keep_at, SPAN, bc_edge[:, :STATE].astype(BF))
    store(give_at, SPAN, bc_edge[:, STATE:].astype(BF))
    shifted_all, step_all = rates(raw_ref[0, 0], head)
    skip = chan_ref[1:2]
    low_half = lax.broadcasted_iota(jnp.int32, (PART, 128), 1) < HEADDIM
    zero_low = jnp.zeros((PART, 128), BF)
    chan_at = lax.broadcasted_iota(jnp.int32, (QUARTER, 128), 0)
    head_at = lax.broadcasted_iota(jnp.int32, (QUARTER, 128), 1)
    gather = jnp.where(
        (chan_at >= head_at * HEADDIM) & (chan_at < (head_at + 1) * HEADDIM), 1.0, 0.0
    )
    gather_low = gather.astype(BF)
    upper = triangle(lambda r, c: r <= c)
    for part in reversed(range(SPAN // PART)):
        at_rows = slice(part * PART, (part + 1) * PART)
        cols = cols_all[at_rows]
        values = act[at_rows, :QUARTER]
        b_low = act[at_rows, QUARTER : QUARTER + STATE].astype(BF)
        c_low = act[at_rows, QUARTER + STATE :].astype(BF)
        step = step_all[at_rows]
        cum, enter, leave, passing, block_out = part_terms(step, head, cols, rows[6:7, at_rows])
        cum_t = cum.T
        scores = dot_nt(c_low, b_low)
        held = hin_ref[0, 0, QUARTER * part : QUARTER * (part + 1)]
        dy_low = dy_ref[0, 0, at_rows]
        dy = dy_low.astype(F32)
        d_after = d_state[...]
        d_after_low = d_after.astype(BF)
        from_after = dot_nt(b_low, d_after_low)
        d_scores = jnp.zeros((PART, PART), F32)
        d_scaled_all = []
        scaled_all = []
        tail_terms = []
        tails = []
        entering = []
        for k in range(QHEADS // 2):
            at = slice(128 * k, 128 * (k + 1))
            step_k = pair_cols(step, k, low_half)
            scaled = (step_k * values[:, at]).astype(BF)
            scaled_f = scaled.astype(F32)
            dy_k = dy_low[:, at]
            dy_both = jnp.concatenate(
                [jnp.where(low_half, dy_k, zero_low), jnp.where(low_half, zero_low, dy_k)],
                axis=0,
            )
            d_weights = dot_nt(dy_both, scaled)
            weights = []
            for at_h, h in enumerate((2 * k, 2 * k + 1)):
                decay = jnp.exp(cum[:, h : h + 1] - cum_t[h : h + 1] + block_out)
                weights.append((scores * decay).astype(BF))
                d_scores = d_scores + d_weights[at_h * PART : (at_h + 1) * PART] * decay
            leave_k = pair_cols(leave, k, low_half)
            tail_part = leave_k * from_after[:, at]
            d_scaled = dot_tn(jnp.concatenate(weights, axis=0), dy_both) + tail_part
            d_scaled_all.append(d_scaled)
            scaled_all.append(scaled_f)
            tail_terms.append(jnp.sum(scaled_f * tail_part, axis=0, keepdims=True))
            tails.append((leave_k * scaled_f).astype(BF))
            entering.append((pair_cols(enter, k, low_half) * dy[:, at]).astype(BF))
            d_values = step_k * d_scaled + skip[:, at] * dy[:, at]
            buf[at_rows, at] = d_values * slope[at_rows, at]
        d_scaled = jnp.concatenate(d_scaled_all, axis=1)
        scaled = jnp.concatenate(scaled_all, axis=1)
        enter_dy = jnp.concatenate(entering, axis=1)
        d_scores_low = d_scores.astype(BF)
        d_c = dot_nn(d_scores_low, b_low) + dot_nn(enter_dy, held)
        d_b = dot_tn(d_scores_low, c_low) + dot_nn(jnp.concatenate(tails, axis=1), d_after_low)
        kept_half = jnp.where(first_core, d_b, d_c)
        given_half = jnp.where(first_core, d_c, d_b)
        store(keep_at, part * PART, kept_half.astype(BF))
        store(give_at, part * PART, given_half.astype(BF))
        if part == 0:
            bc_edge[:, :STATE] = kept_half[0:16]
            bc_edge[:, STATE:] = given_half[0:16]
        by_values = head_sums(values * d_scaled, gather_low)
        y_part = y_ref[0, 0, at_rows] - skip * values
        d_cum = head_sums(dy * y_part - scaled * d_scaled, gather_low)
        tail_row = jnp.concatenate(tail_terms, axis=1)
        tail_sum = dot_exact(jnp.broadcast_to(tail_row, (8, QUARTER)), gather)[0:1]
        state_dot = jnp.sum(d_after * held.astype(F32), axis=1, keepdims=True)
        state_terms = jnp.sum(state_dot * gather, axis=0, keepdims=True)
        at_last = tail_sum + passing * state_terms
        d_rate = split_sum(upper, d_cum) + at_last
        d_step = by_values - head[1:2] * d_rate
        d_raw = d_step * sigmoid(shifted_all[at_rows])
        ghead_ref[0:1, :128] += jnp.sum(d_raw, axis=0, keepdims=True)
        ghead_ref[1:2, :128] += jnp.sum(-step * head[1:2] * d_rate, axis=0, keepdims=True)
        ghead_ref[2:3] += jnp.sum(values * dy, axis=0, keepdims=True)
        d_late[at_rows, QUARTER:] = d_raw.astype(BF)
        new_state = dot_tn(enter_dy, c_low)
        for h in range(QHEADS):
            at = slice(HEADDIM * h, HEADDIM * (h + 1))
            d_state[at] = passing[:, h : h + 1] * d_after[at] + new_state[at]
    mixed = mixed_ref[0, 0, :, :QUARTER].astype(F32)
    d_mixed = jnp.zeros((SPAN, QUARTER), F32)
    for j in range(CONV):
        ahead = CONV - 1 - j
        window = buf[ahead : ahead + SPAN] * cols_all[:, 8 + j : 9 + j]
        d_mixed = d_mixed + taps[j : j + 1, :QUARTER] * window
        gtap_ref[j : j + 1] += jnp.sum(mixed * window, axis=0, keepdims=True)
    gtap_ref[CONV : CONV + 1] += jnp.sum(buf[0:SPAN], axis=0, keepdims=True)
    buf[SPAN:] = buf[0:8]
    d_late[:, :QUARTER] = d_mixed.astype(BF)
    late = d_late[...]
    g_ref[...] += dot_tn(late, current(own_ref, other_ref))[: QUARTER + 16]
    d_gate = d_gate_ref[0, 0]
    width = QUARTER + 2 * STATE
    for rows_at, out_ref in zip(core_rows(place_ref), (mine_ref, theirs_ref)):
        total = dot_nt(late[:, :QUARTER], w_ref[rows_at, :QUARTER])
        total = total + dot_nt(late[:, QUARTER:], w_ref[rows_at, width:])
        out_ref[0, 0, :SPAN] = (total + dot_nt(d_gate, w_gate_ref[rows_at])).astype(BF)


def slot_spec(rows, width, order):
    return pl.BlockSpec((1, 1, rows, width), lambda q, j, place: (q, order(j), 0, 0))


def segment_spec():
    return pl.BlockSpec(
        (1, 8, BLOCKS * SPAN + 256), lambda q, j, place: (q, 0, 0)
    )


def fixed_spec(rows, width):
    return pl.BlockSpec((rows, width), lambda q, j, place: (0, 0))


def out_shape(rows, cols_of, kind):
    return jax.ShapeDtypeStruct((2, BLOCKS, rows, cols_of), kind)


def upward(j):
    return j


def downward(j):
    return BLOCKS - 1 - j


def own_spec(order, rows=SPAN, at=0):
    def index(q, j, place):
        return (jnp.where(q == 0, order(j), order(BLOCKS - 1)), at, 0)

    return pl.BlockSpec((1, rows, D), index)


def other_spec(order, rows=SPAN, at=0):
    def index(q, j, place):
        return (jnp.where(q == 0, order(0), order(j)), at, 0)

    return pl.BlockSpec((1, rows, D), index)


def cot_specs(cots):
    half = SPAN // 2
    second = 0 if cots[0].shape[1] == half else 1
    return [
        own_spec(upward, half),
        own_spec(upward, half, second),
        other_spec(upward, half),
        other_spec(upward, half, second),
    ]


def call_blocks(kernel, name, place, operands, in_specs, outs, scratch=()):
    return pl.pallas_call(
        kernel,
        grid_spec=pltpu.PrefetchScalarGridSpec(
            num_scalar_prefetch=1,
            grid=(2, BLOCKS),
            in_specs=in_specs,
            out_specs=[spec for spec, _ in outs],
            scratch_shapes=list(scratch),
        ),
        out_shape=[shape for _, shape in outs],
        compiler_params=pltpu.CompilerParams(vmem_limit_bytes=VMEM_LIMIT),
        cost_estimate=pl.CostEstimate(flops=1024, bytes_accessed=1024, transcendentals=0),
        name=name,
    )(place, *operands)


def slot_out(rows, width, kind, order):
    return slot_spec(rows, width, order), out_shape(rows, width, kind)


def lead_out(rows, width, order, flipped):
    def index(q, j, place):
        return (order(j), 1 - q if flipped else q, 0, 0)

    shape = jax.ShapeDtypeStruct((BLOCKS, 2, rows, width), BF)
    return pl.BlockSpec((1, 1, rows, width), index), shape


def fixed_out(rows, width):
    return fixed_spec(rows, width), jax.ShapeDtypeStruct((rows, width), F32)


def run_fwd(place, tokens, w_first, rows, taps, head, chan):
    width = QUARTER + 2 * STATE
    return call_blocks(
        fwd_kernel,
        "mix_forward",
        place,
        (*tokens, w_first, rows, taps, head, chan),
        [
            own_spec(upward),
            other_spec(upward),
            fixed_spec(D, width + 128),
            segment_spec(),
            fixed_spec(8, width),
            fixed_spec(8, 128),
            fixed_spec(8, QUARTER),
        ],
        [
            slot_out(SPAN, width, BF, upward),
            slot_out(SPAN, 128, F32, upward),
            slot_out(SPAN, width, F32, upward),
            slot_out(SPAN, QUARTER, F32, upward),
            slot_out(PARTS * QUARTER, STATE, BF, upward),
        ],
        [pltpu.VMEM((SPAN + 8, width), F32), pltpu.VMEM((QUARTER, STATE), F32)],
    )


def run_gate(place, tokens, cots, y, w_gate, w_out, chan):
    half = D // 2
    return call_blocks(
        gate_kernel,
        "gate_forward",
        place,
        (*tokens, *cots, y, w_gate, w_out, chan),
        [
            own_spec(upward),
            other_spec(upward),
            *cot_specs(cots),
            slot_spec(SPAN, QUARTER, upward),
            fixed_spec(D, QUARTER),
            fixed_spec(D, QUARTER),
            fixed_spec(8, QUARTER),
        ],
        [
            slot_out(SPAN, QUARTER, F32, upward),
            slot_out(SPAN, QUARTER, F32, upward),
            lead_out(SPAN, half, upward, False),
            lead_out(SPAN, half, upward, True),
            slot_out(8, SPAN, F32, upward),
        ],
    )


def sums_out(rows, dp_count, last):
    if not last:
        return fixed_out(rows, D), []
    share = D // dp_count
    spec = pl.BlockSpec((dp_count, rows, share), lambda q, j, place: (0, 0, 0))
    out = spec, jax.ShapeDtypeStruct((dp_count, rows, share), BF)
    return out, [pltpu.VMEM((rows, D), F32)]


def run_gate_back(place, tokens, cots, y, gate, d_gated, stat, chan, seed, dp_count):
    last = seed is not None
    total, scratch = sums_out(2 * QUARTER, dp_count, last)
    return call_blocks(
        gate_back_last if last else gate_back_first,
        "gate_backward",
        place,
        (*tokens, *cots, y, gate, d_gated, stat, chan) + ((seed,) if last else ()),
        [
            own_spec(upward),
            other_spec(upward),
            *cot_specs(cots),
            slot_spec(SPAN, QUARTER, upward),
            slot_spec(SPAN, QUARTER, upward),
            slot_spec(SPAN, QUARTER, upward),
            slot_spec(8, SPAN, upward),
            fixed_spec(8, QUARTER),
        ]
        + ([fixed_spec(2 * QUARTER, D)] if last else []),
        [
            slot_out(SPAN, QUARTER, BF, upward),
            slot_out(SPAN, QUARTER, BF, upward),
            fixed_out(8, QUARTER),
            total,
        ],
        scratch,
    )


def run_bwd(place, tokens, kept, dy, d_gate, rows, taps, head, chan, weights, seed, dp_count):
    mixed, raw, pre, y, hin = kept
    width = mixed.shape[-1]
    states = 2 * STATE
    half = D // 2
    last = seed is not None
    total, scratch = sums_out(QUARTER + 16, dp_count, last)
    rows_out = SPAN if last else SPAN + PACKED
    maps_out = [lead_out(SPAN + 16, STATE, downward, flip) for flip in (False, True)] if last else []
    return call_blocks(
        bwd_last if last else bwd_first,
        "mix_backward",
        place,
        (*tokens, mixed, pre, raw, y, hin, dy, d_gate, rows, taps, head, chan, *weights)
        + ((seed,) if last else ()),
        [
            own_spec(downward),
            other_spec(downward),
            slot_spec(SPAN, width, downward),
            slot_spec(SPAN, width, downward),
            slot_spec(SPAN, 128, downward),
            slot_spec(SPAN, QUARTER, downward),
            slot_spec(PARTS * QUARTER, STATE, downward),
            slot_spec(SPAN, QUARTER, downward),
            slot_spec(SPAN, QUARTER, downward),
            segment_spec(),
            fixed_spec(8, width),
            fixed_spec(8, 128),
            fixed_spec(8, QUARTER),
            fixed_spec(D, width + 128),
            fixed_spec(D, QUARTER),
        ]
        + ([fixed_spec(QUARTER + 16, D)] if last else []),
        [
            total,
            *maps_out,
            slot_out(SPAN + 16, STATE, F32, downward),
            fixed_out(8, QUARTER),
            fixed_out(8, QUARTER),
            lead_out(rows_out, half, downward, False),
            lead_out(rows_out, half, downward, True),
        ],
        [
            pltpu.VMEM((SPAN + 8, QUARTER), F32),
            pltpu.VMEM((QUARTER, STATE), F32),
            pltpu.VMEM((16, states), F32),
            pltpu.VMEM((16, STATE), F32),
            pltpu.VMEM((SPAN, QUARTER + 128), BF),
        ]
        + scratch,
    )


def maps_kernel(
    place_ref, packed_ref, maps_ref, slope_0, slope_1, mixed_0, mixed_1, seg_0, seg_1,
    own_0, other_0, own_1, other_1, taps_ref,
    d_maps_ref, g_ref, g_taps_ref, buf,
):
    chip = place_ref[1]
    taps = taps_ref[...]
    buf[SPAN + 16 :] = jnp.zeros((8, STATE), F32)
    sums = [jnp.zeros((1, STATE), F32) for _ in range(CONV + 1)]
    g_maps = jnp.zeros((STATE, D), F32)
    slopes, mixes, segs = (slope_0, slope_1), (mixed_0, mixed_1), (seg_0, seg_1)
    tokens = ((own_0, other_0), (own_1, other_1))
    for m in range(MB):
        for q in range(2):
            if m == 0:
                total = packed_ref[0, q].astype(F32)
                for src in range(1, BLOCKS):
                    total = total + packed_ref[src, q].astype(F32)
                groups = [total[:, 128 * k : 128 * (k + 1)] for k in range(6)]
                d_conv = jnp.concatenate(groups, axis=0)[: SPAN + 16]
            else:
                d_conv = maps_ref[0, q].astype(F32)
                for src in range(1, BLOCKS):
                    d_conv = d_conv + maps_ref[src, q].astype(F32)
            d_pre = d_conv * slopes[m][q, 0]
            buf[0 : SPAN + 16] = d_pre
            cols = to_columns(segment_flags(segs[m].at[q : q + 1], chip))
            mixed = mixes[m][q, 0].astype(F32)
            d_mixed = jnp.zeros((SPAN, STATE), F32)
            for j in range(CONV):
                ahead = CONV - 1 - j
                window = buf[ahead : ahead + SPAN] * cols[:, 8 + j : 9 + j]
                d_mixed = d_mixed + taps[j : j + 1] * window
                sums[j] = sums[j] + jnp.sum(mixed * window, axis=0, keepdims=True)
            sums[CONV] = sums[CONV] + jnp.sum(d_pre[:SPAN], axis=0, keepdims=True)
            low = d_mixed.astype(BF)
            d_maps_ref[m, q] = low
            g_maps = g_maps + dot_tn(low, tokens[m][q][0])
    g_taps_ref[...] = jnp.concatenate(sums + [jnp.zeros((3, STATE), F32)], axis=0)
    rows_of = g_ref.shape[2]
    for z in range(g_ref.shape[0]):
        g_ref[z] = g_maps[:, z * rows_of : (z + 1) * rows_of].astype(BF)


def run_maps(place, packed, maps, slopes, mixes, segs, tokens, taps, dp_count):
    def whole(shape):
        return pl.BlockSpec(shape, lambda i, place: (0,) * len(shape))

    def slope_spec():
        return pl.BlockSpec((2, 1, SPAN + 16, STATE), lambda i, place: (0, place[1], 0, 0))

    def mixed_spec():
        first = QUARTER // STATE
        return pl.BlockSpec(
            (2, 1, SPAN, STATE), lambda i, place: (0, place[1], 0, first + place[0])
        )

    def token_spec():
        return pl.BlockSpec((1, SPAN, D), lambda i, place: (place[1], 0, 0))

    share = D // dp_count
    return pl.pallas_call(
        maps_kernel,
        grid_spec=pltpu.PrefetchScalarGridSpec(
            num_scalar_prefetch=1,
            grid=(1,),
            in_specs=[
                whole(packed.shape),
                whole(maps.shape),
                slope_spec(),
                slope_spec(),
                mixed_spec(),
                mixed_spec(),
                whole(segs[0].shape),
                whole(segs[1].shape),
                token_spec(),
                token_spec(),
                token_spec(),
                token_spec(),
                whole(taps.shape),
            ],
            out_specs=[
                whole((MB, 2, SPAN, STATE)),
                whole((dp_count, STATE, share)),
                whole((8, STATE)),
            ],
            scratch_shapes=[pltpu.VMEM((SPAN + 24, STATE), F32)],
        ),
        out_shape=[
            jax.ShapeDtypeStruct((MB, 2, SPAN, STATE), BF),
            jax.ShapeDtypeStruct((dp_count, STATE, share), BF),
            jax.ShapeDtypeStruct((8, STATE), F32),
        ],
        compiler_params=pltpu.CompilerParams(vmem_limit_bytes=VMEM_LIMIT),
        cost_estimate=pl.CostEstimate(flops=1024, bytes_accessed=1024, transcendentals=0),
        name="maps_backward",
    )(place, packed, maps, *slopes, *mixes, *segs, *tokens, taps)


def norm_kernel(place_ref, mid_ref, late_ref, w_in_ref, w_state_ref, w_step_ref, step_ref, out_ref):
    rows = mid_ref.shape[1]
    squares = jnp.zeros((rows, QUARTER), F32)
    products = jnp.zeros((rows, QUARTER), F32)
    for s in range(BLOCKS):
        at = slice(s * QUARTER, (s + 1) * QUARTER)
        out = mid_ref[s, :, :QUARTER].astype(F32)
        gate = mid_ref[s, :, QUARTER:].astype(F32)
        inner = late_ref[s, :, :QUARTER].astype(F32)
        squares = squares + out * out + gate * gate + inner * inner
        products = products + gate * w_in_ref[0, :, at].astype(F32)
        products = products + inner * w_in_ref[1, :, at].astype(F32)
    state = late_ref[0, :, QUARTER : QUARTER + STATE].astype(F32)
    for s in range(1, BLOCKS):
        state = state + late_ref[s, :, QUARTER : QUARTER + STATE].astype(F32)
    step = step_ref[...]
    by_row = jnp.sum(products, axis=1, keepdims=True)
    by_row = by_row + jnp.sum(state * w_state_ref[...].astype(F32), axis=1, keepdims=True)
    by_row = by_row + jnp.sum(step * w_step_ref[...].astype(F32), axis=1, keepdims=True)
    square = jnp.sum(squares, axis=1, keepdims=True) + jnp.sum(state * state, axis=1, keepdims=True)
    square = square + jnp.sum(step * step, axis=1, keepdims=True)
    lanes = lax.broadcasted_iota(jnp.int32, (rows, 128), 1)
    table = jnp.where(lanes == 0, by_row, jnp.where(lanes == 1, square, 0.0))
    table = jnp.concatenate([table, jnp.zeros((128 - rows, 128), F32)], axis=0).T
    total = jnp.sum(table[1:2], axis=1, keepdims=True)
    at_row = lax.broadcasted_iota(jnp.int32, (8, 128), 0)
    at_lane = lax.broadcasted_iota(jnp.int32, (8, 128), 1)
    first = jnp.where((at_row == 0) & (at_lane == rows), total, table[0:8])
    out_ref[...] = jnp.where(at_row == 0, first, 0.0)


def update_kernel(
    place_ref, factor_ref, mid_ref, late_ref, step_ref, w_in_ref, w_out_ref, w_state_ref,
    w_step_ref, m_in_ref, m_out_ref, m_state_ref, m_step_ref,
    new_in_ref, new_out_ref, new_state_ref, new_step_ref,
    next_in_ref, next_out_ref, next_state_ref, next_step_ref,
):
    factor = factor_ref[0, 0]
    rows = mid_ref.shape[1]

    def write(new_ref, next_ref, at, moment, grad, weight):
        new = 0.5 * moment + (0.5 * factor) * grad
        new_ref[at] = new
        next_ref[at] = (weight.astype(F32) - LEARN * new).astype(BF)

    for s in range(BLOCKS):
        lanes = slice(s * QUARTER, (s + 1) * QUARTER)
        gate = (0, slice(None), lanes)
        write(
            new_in_ref, next_in_ref, gate, m_in_ref[gate],
            mid_ref[s, :, QUARTER:].astype(F32), w_in_ref[gate],
        )
        inner = (1, slice(None), lanes)
        write(
            new_in_ref, next_in_ref, inner, m_in_ref[inner],
            late_ref[s, :, :QUARTER].astype(F32), w_in_ref[inner],
        )
        out = mid_ref[s, :, :QUARTER].astype(F32)
        out = jnp.concatenate([out, jnp.zeros((128 - rows, QUARTER), F32)], axis=0).T
        write(
            new_out_ref, next_out_ref, lanes, m_out_ref[lanes], out[:, :rows], w_out_ref[lanes]
        )
    state = late_ref[0, :, QUARTER : QUARTER + STATE].astype(F32)
    for s in range(1, BLOCKS):
        state = state + late_ref[s, :, QUARTER : QUARTER + STATE].astype(F32)
    write(new_state_ref, next_state_ref, ..., m_state_ref[...], state, w_state_ref[...])
    write(new_step_ref, next_step_ref, ..., m_step_ref[...], step_ref[...], w_step_ref[...])


def owner_specs(rows, heads_local):
    return [
        pl.BlockSpec((2, rows, BLOCKS * QUARTER), lambda i, place: (0, place[1], 0)),
        pl.BlockSpec((rows, STATE), lambda i, place: (place[1], place[0])),
        pl.BlockSpec((rows, heads_local), lambda i, place: (place[1], 0)),
    ]


def run_owner(kernel, name, place, operands, in_specs, outs):
    return pl.pallas_call(
        kernel,
        grid_spec=pltpu.PrefetchScalarGridSpec(
            num_scalar_prefetch=1, grid=(1,), in_specs=in_specs,
            out_specs=[spec for spec, _ in outs],
        ),
        out_shape=[shape for _, shape in outs],
        compiler_params=pltpu.CompilerParams(vmem_limit_bytes=VMEM_LIMIT),
        cost_estimate=pl.CostEstimate(flops=1024, bytes_accessed=1024, transcendentals=0),
        name=name,
    )(place, *operands)


def swap_cores(block):
    return lax.ppermute(block, "tensor", SWAP)


def over_x(block):
    return lax.ppermute(block, "seq", ROUTE_X)


def over_y(block):
    return lax.ppermute(block, "seq", ROUTE_Y)


def exchange(blocks):
    return lax.all_to_all(blocks, "seq", 0, 0, tiled=True)


def gather_blocks(piece):
    return exchange(jnp.broadcast_to(piece, (BLOCKS,) + piece.shape))


def add_low(a, b):
    return (a.astype(F32) + b.astype(F32)).astype(BF)


def gather_halves(piece):
    half = piece.shape[0] // 2
    return [gather_blocks(piece[:half]), gather_blocks(piece[half:])]


def scatter(blocks):
    return jnp.sum(exchange(blocks).astype(F32), axis=0)


def after(value, *others):
    return lax.optimization_barrier((value, others))[0]


def sum_cores(table):
    return table + swap_cores(table)[::-1]


def sum_plane(table):
    table = table + over_x(table)
    return table + over_y(table)


def fast_body(
    inputs,
    segments,
    cotangent,
    prenorm,
    inproj,
    statproj,
    stepproj,
    outproj,
    convinner,
    convstate,
    headparam,
    gatenorm,
    prenorm_moment,
    inproj_moment,
    statproj_moment,
    stepproj_moment,
    outproj_moment,
    convinner_moment,
    convstate_moment,
    headparam_moment,
    gatenorm_moment,
):
    core = lax.axis_index("tensor")
    chip = lax.axis_index("seq")
    data_at = lax.axis_index("dp")
    dp_count = lax.axis_size("dp")
    heads_local = headparam.shape[1]
    rows_local = inproj.shape[1]
    shard = rows_local // BLOCKS
    half_d = D // 2
    place = jnp.stack([core, chip]).astype(jnp.int32)

    def by_core(first, second):
        return jnp.where(core == 0, first, second)

    def quarter(array, axis, width):
        return lax.dynamic_slice_in_dim(array, chip * width, width, axis)

    def all_rows(block):
        return lax.all_gather(block, "dp", axis=0, tiled=True)

    w_first = all_rows(
        jnp.concatenate(
            [
                quarter(inproj[1], 1, QUARTER),
                statproj,
                jnp.pad(quarter(stepproj, 1, QHEADS), ((0, 0), (0, 128 - QHEADS))),
            ],
            axis=1,
        )
    )
    w_gate = all_rows(quarter(inproj[0], 1, QUARTER))
    w_out = all_rows(quarter(outproj, 0, QUARTER).T)

    def whole_rows(array):
        mine = lax.dynamic_index_in_dim(array, core, 1, keepdims=False)
        theirs = lax.dynamic_index_in_dim(array, 1 - core, 1, keepdims=False)
        got = swap_cores(theirs)
        return by_core(
            jnp.concatenate([mine, got], axis=2), jnp.concatenate([got, mine], axis=2)
        )

    rows_whole = whole_rows(inputs)
    normed_own = rms_scale(rows_whole.astype(F32), prenorm).astype(BF)
    cot_own = whole_rows(cotangent)
    own_0 = gather_blocks(normed_own[0])
    segments, convinner, convstate, headparam, gatenorm = after(
        (segments, convinner, convstate, headparam, gatenorm), normed_own
    )

    seg_mine = jnp.concatenate(
        [
            lax.dynamic_index_in_dim(segments, core, 1),
            lax.dynamic_index_in_dim(segments, 1 - core, 1),
        ],
        axis=1,
    )
    seg_pad = jnp.pad(
        seg_mine.astype(F32), ((0, 0), (0, 0), (128, 128)), constant_values=-1.0
    )
    segs = jnp.broadcast_to(seg_pad[:, :, None], seg_pad.shape[:2] + (8, seg_pad.shape[2]))

    taps_inner = quarter(convinner, 1, QUARTER)
    taps = jnp.pad(jnp.concatenate([taps_inner, convstate], axis=1), ((0, 3), (0, 0)))
    head_own = quarter(headparam, 1, QHEADS)
    head = jnp.pad(
        jnp.stack([head_own[0], jnp.exp(head_own[1]), head_own[2]]),
        ((0, 5), (0, 128 - QHEADS)),
    )
    gain = quarter(gatenorm, 0, QUARTER)
    chan = jnp.pad(jnp.stack([gain, jnp.repeat(head_own[2], HEADDIM)]), ((0, 6), (0, 0)))

    def rows_dot_t(left, right):
        return lax.dot_general(left, right, (((3,), (1,)), ((), ())), preferred_element_type=F32)

    def core_sums(mine, theirs):
        return add_low(mine, swap_cores(theirs))

    def core_halves(mine, theirs):
        got = swap_cores(theirs)
        return [add_low(mine[:, q], got[:, q]) for q in range(2)]

    def over_dp(parts):
        return lax.psum_scatter(parts, "dp", scatter_dimension=0, tiled=True)[0]

    def by_place(columns):
        blocks = columns.T.reshape(BLOCKS, shard, -1)
        return lax.all_to_all(blocks, "seq", 0, 0, tiled=True)

    def forward(m, place, tokens):
        return run_fwd(place, tokens, w_first, segs[m], taps, head, chan)

    def gate_forward(m, place):
        return run_gate(place, normed[m], cots[m], kept[m][3], w_gate, w_out, chan)

    def gate_backward(m, place, gate, d_gated, sums, seed):
        return run_gate_back(
            place, normed[m], cots[m], kept[m][3], gate, d_gated, sums, chan, seed, dp_count
        )

    def backward(m, place, dy, d_gate, seed):
        return run_bwd(
            place, normed[m], kept[m], dy, d_gate, segs[m], taps, head, chan,
            (w_first, w_gate), seed, dp_count,
        )

    def token_scale(sums):
        own = lax.dynamic_index_in_dim(sums, chip, 1, keepdims=False)
        return lax.rsqrt(own[:, 0] / INNER + EPS)[..., None]

    def with_other(own):
        return own, swap_cores(own)

    own_1 = gather_blocks(after(normed_own[1], own_0))
    normed = [with_other(own_0)]
    (own_0, other_0), place = after((normed[0], place), w_first)
    kept = [forward(0, place, (own_0, other_0))]

    own_1, w_gate, piece, place = after((own_1, w_gate, cot_own[0], place), kept[0][1])
    normed.append(with_other(own_1))
    cot_0 = gather_blocks(piece)
    kept.append(forward(1, place, normed[1]))

    cot_0, w_out, piece, place = after((cot_0, w_out, cot_own[1], place), kept[1][1])
    cot_0 = with_other(cot_0)
    cots = [[cot_0[0], cot_0[0], cot_0[1], cot_0[1]]]
    half = SPAN // 2
    cot_a = gather_blocks(piece[:half])
    gate_0, d_gated_0, mine_0, theirs_0, stat_0 = gate_forward(0, place)

    cot_a, stat_0, piece, place = after((cot_a, stat_0, piece, place))
    stat_0 = sum_cores(stat_0)
    theirs_0 = after(theirs_0, stat_0)
    sums_0 = sum_plane(stat_0)
    cot_b = gather_blocks(after(piece, sums_0)[half:])
    cot_a = [cot_a, swap_cores(cot_a)]
    branch_0 = core_halves(mine_0, theirs_0)
    dy_0, d_gate_0, g_gain_0, g_mid_0 = gate_backward(0, place, gate_0, d_gated_0, sums_0, None)

    cot_a, cot_b, place, branch_0 = after((cot_a, cot_b, place, branch_0), dy_0)
    cots.append([cot_a[0], cot_b, cot_a[1], swap_cores(cot_b)])
    layer_0 = [exchange(branch_0[0])]
    gate_1, d_gated_1, mine_1, theirs_1, stat_1 = gate_forward(1, place)

    layer_0, stat_1, place = after((layer_0, stat_1, place))
    stat_1 = sum_cores(stat_1)
    theirs_1 = after(theirs_1, stat_1)
    sums_1 = sum_plane(stat_1)
    layer_0.append(exchange(after(branch_0[1], sums_1)))
    branch_1 = core_sums(mine_1, theirs_1)
    dy_1, d_gate_1, g_gain_1, mid_parts = gate_backward(1, place, gate_1, d_gated_1, sums_1, g_mid_0)

    layer_0, branch_1, place, mid_parts = after((layer_0, branch_1, place, mid_parts), dy_1)
    layer_1 = exchange(branch_1)
    mid_rows = over_dp(mid_parts)
    g_late_0, slope_0, g_taps_0, g_head_0, mine, theirs = backward(
        0, place, dy_0, d_gate_0, None
    )

    layer_1, mid_rows, theirs, place = after((layer_1, mid_rows, theirs, place), g_taps_0)
    back_0 = core_sums(mine, theirs)
    back_0, place = after((back_0, place))
    token_0 = exchange(back_0)
    late_parts, keep_1, give_1, slope_1, g_taps_1, g_head_1, mine, theirs = backward(
        1, place, dy_1, d_gate_1, g_late_0
    )

    token_0, late_parts, theirs, give_1, layer_0, layer_1, mid_rows = after(
        (token_0, late_parts, theirs, give_1, layer_0, layer_1, mid_rows)
    )
    late_rows = over_dp(late_parts)
    maps = core_sums(keep_1, give_1)
    back_1 = core_sums(mine, after(theirs, maps))
    maps = exchange(maps)
    maps, back_1 = after((maps, back_1))
    token_1 = exchange(back_1)
    taps_state = lax.dynamic_slice_in_dim(convstate, core * STATE, STATE, 1)
    d_maps, g_maps, g_state_taps = run_maps(
        place, token_0[:, :, SPAN:], maps, (slope_0, slope_1), (kept[0][0], kept[1][0]),
        segs, (*normed[0], *normed[1]), jnp.pad(taps_state, ((0, 3), (0, 0))), dp_count,
    )

    def for_dp(hop):
        at = lax.rem(data_at + hop, dp_count)
        return lax.dynamic_index_in_dim(g_maps, at, 0, keepdims=False)

    state_rows = for_dp(0).astype(F32)
    for hop in range(1, dp_count):
        route = [(i, (i + hop) % dp_count) for i in range(dp_count)]
        state_rows = state_rows + lax.ppermute(for_dp(hop), "dp", route).astype(F32)
    state_rows = state_rows.astype(BF)
    token_1, late_rows, mid_rows, state_rows = after((token_1, late_rows, mid_rows, state_rows))

    def summed(blocks):
        return jnp.sum(blocks.astype(F32), axis=0)

    layer_out = [
        jnp.stack([summed(part) for part in layer_0]) * token_scale(sums_0),
        summed(layer_1) * token_scale(sums_1),
    ]
    d_tokens = [summed(token_0[:, :, :SPAN]), summed(token_1)]
    smalls = (g_taps_0 + g_taps_1, g_head_0 + g_head_1)
    w_state = w_first[:, QUARTER : QUARTER + 2 * STATE]

    state_other = swap_cores(d_maps)[:, ::-1]
    state_mine = d_maps
    d_state_both = by_core(
        jnp.concatenate([state_mine, state_other], axis=3),
        jnp.concatenate([state_other, state_mine], axis=3),
    )
    from_state = rows_dot_t(
        d_state_both, lax.dynamic_slice_in_dim(w_state, core * half_d, half_d, 0)
    )

    def in_order(block):
        return by_core(block, block[:, ::-1])

    layer_out = in_order(jnp.stack(layer_out))
    outputs = (inputs.astype(F32) + layer_out).astype(BF)
    d_normed = in_order(jnp.stack(d_tokens) + from_state)
    rows_own = inputs.astype(F32)
    gain_own = lax.dynamic_slice_in_dim(prenorm, core * half_d, half_d, 0)
    weighted = d_normed * gain_own
    pair_sums = jnp.stack(
        [jnp.sum(rows_own * rows_own, axis=-1), jnp.sum(weighted * rows_own, axis=-1)]
    )
    pair_sums = pair_sums + swap_cores(pair_sums)
    root = lax.rsqrt(pair_sums[0] / D + EPS)[..., None]
    input_grads = (
        cotangent.astype(F32)
        + weighted * root
        - rows_own * root * root * root * (pair_sums[1] / D)[..., None]
    ).astype(BF)

    mid_share = by_place(mid_rows)
    late_share = by_place(
        jnp.concatenate([late_rows[:QUARTER], state_rows, late_rows[QUARTER:]], axis=0)
    )
    step_share = late_share[:, :, QUARTER + STATE : QUARTER + STATE + QHEADS].astype(F32)
    step_share = jnp.moveaxis(step_share, 0, 1).reshape(shard, heads_local)
    row_start = chip * shard
    in_spec, state_spec, step_spec = owner_specs(shard, heads_local)

    def whole(array):
        return pl.BlockSpec(array.shape, lambda i, place: (0,) * array.ndim)

    def whole_out(shape, kind):
        spec = pl.BlockSpec(shape, lambda i, place: (0,) * len(shape))
        return spec, jax.ShapeDtypeStruct(shape, kind)

    owner_sums = run_owner(
        norm_kernel,
        "owner_norm",
        place,
        (mid_share, late_share, inproj, statproj, stepproj, step_share),
        [whole(mid_share), whole(late_share), in_spec, state_spec, step_spec, whole(step_share)],
        [whole_out((8, 128), F32)],
    )[0]
    owner_sums = owner_sums + swap_cores(owner_sums)

    g_taps, g_head = smalls
    g_heads = jnp.concatenate(
        [g_head[:2, :QHEADS], jnp.sum(g_head[2].reshape(1, QHEADS, HEADDIM), axis=2)], axis=0
    )

    inner_local = BLOCKS * QUARTER

    def put(values, width, total):
        base = jnp.zeros(values.shape[:-1] + (total,), F32)
        return lax.dynamic_update_slice_in_dim(base, values, chip * width, values.ndim - 1)

    small_parts = [
        put(g_taps[: CONV + 1], QUARTER, inner_local),
        put(g_gain_0[0] + g_gain_1[0], QUARTER, inner_local),
        put(g_heads, QHEADS, heads_local),
        g_state_taps[: CONV + 1],
    ]
    sizes = [part.size for part in small_parts]
    vector = jnp.concatenate([part.reshape(-1) for part in small_parts])
    vector = jnp.pad(vector, (0, -vector.size % 1024)).reshape(-1, 128)

    def sum_all(value):
        value = value + over_x(value)
        value = value + over_y(value)
        hop = 1
        while hop < dp_count:
            value = value + lax.ppermute(value, "dp", [(i, i ^ hop) for i in range(dp_count)])
            hop *= 2
        return value

    vector = sum_all(vector).reshape(-1)
    small_sums = []
    start = 0
    for part, size in zip(small_parts, sizes):
        small_sums.append(vector[start : start + size].reshape(part.shape))
        start += size
    s_taps, s_gain, s_head, s_state_taps = small_sums

    small_sq = sum(jnp.sum(term * term) for term in small_sums)
    small_sq = small_sq + swap_cores(small_sq)
    owners = dp_count * BLOCKS
    owner = data_at * BLOCKS + chip
    gain_rows = lax.dynamic_slice_in_dim(prenorm, owner * shard, shard, 0)
    lanes = jnp.arange(128)
    g_prenorm = owner_sums[0] / jnp.pad(gain_rows, (0, 128 - shard), constant_values=1.0)
    g_prenorm = jnp.where(lanes < shard, g_prenorm, 0.0)
    square = owner_sums[0, shard] + jnp.sum(g_prenorm * g_prenorm)
    square = square + jnp.where(owner == 0, small_sq, 0.0)
    line = jnp.where(lanes == shard, square, g_prenorm)
    table = jnp.where(jnp.arange(owners)[:, None] == owner, line[None], 0.0)
    table = sum_all(table)
    grad_norm = jnp.sqrt(jnp.sum(table[:, shard]))
    s_prenorm = lax.dynamic_slice_in_dim(
        table[:, :shard], core * (owners // 2), owners // 2, 0
    ).reshape(half_d)

    entries = (
        2 * D * INNER
        + 2 * D * STATE
        + D * (INNER // HEADDIM)
        + INNER * D
        + (CONV + 1) * (INNER + 2 * STATE)
        + 3 * (INNER // HEADDIM)
        + INNER
        + D
    )
    limit = CLIP_RMS * math.sqrt(entries)
    factor = limit / jnp.maximum(grad_norm, limit)

    def moved(moment, grad):
        return 0.5 * moment + 0.5 * factor * grad

    def stepped(weight, moment):
        return (weight.astype(F32) - LEARN * moment).astype(weight.dtype)

    new_prenorm = moved(prenorm_moment, s_prenorm)
    outproj_own = lax.dynamic_slice_in_dim(outproj, row_start, shard, 1)
    moments = (inproj_moment, outproj_moment, statproj_moment, stepproj_moment)
    new_in, new_out, new_state, new_step, next_in, next_out, next_state, next_step = run_owner(
        update_kernel,
        "owner_update",
        place,
        (
            factor.reshape(1, 1), mid_share, late_share, step_share,
            inproj, outproj_own, statproj, stepproj, *moments,
        ),
        [
            pl.BlockSpec(memory_space=pltpu.SMEM),
            whole(mid_share), whole(late_share), whole(step_share),
            in_spec, whole(outproj_own), state_spec, step_spec,
            *[whole(moment) for moment in moments],
        ],
        [whole_out(moment.shape, kind) for kind in (F32, BF) for moment in moments],
    )
    new_taps = moved(convinner_moment, s_taps)
    new_state_taps = moved(convstate_moment, s_state_taps)
    new_head = moved(headparam_moment, s_head)
    new_gain = moved(gatenorm_moment, s_gain)
    return (
        outputs,
        input_grads,
        grad_norm,
        new_prenorm,
        new_in,
        new_state,
        new_step,
        new_out,
        new_taps,
        new_state_taps,
        new_head,
        new_gain,
        next_in,
        next_state,
        next_step,
        next_out,
        stepped(convinner, new_taps),
        stepped(lax.dynamic_slice_in_dim(convstate, core * STATE, STATE, 1), new_state_taps),
    )


def solution(mesh):
    fast = mesh.shape["seq"] == BLOCKS and mesh.shape["tensor"] == 2
    return jax.shard_map(
        fast_body if fast else general_body,
        mesh=mesh,
        in_specs=(
            P(None, "dp", "seq", "tensor"),
            P(None, "dp", None),
            P(None, "dp", "seq", "tensor"),
            P(),
            P(None, "dp", "tensor"),
            P("dp", None),
            P("dp", "tensor"),
            P("tensor", "dp"),
            P(None, "tensor"),
            P(),
            P(None, "tensor"),
            P("tensor"),
            P("tensor"),
            P(None, ("dp", "seq"), "tensor"),
            P(("dp", "seq"), "tensor"),
            P(("dp", "seq"), "tensor"),
            P("tensor", ("dp", "seq")),
            P(None, "tensor"),
            P(None, "tensor"),
            P(None, "tensor"),
            P("tensor"),
        ),
        out_specs=(
            P(None, "dp", "seq", "tensor"),
            P(None, "dp", "seq", "tensor"),
            P(),
            P("tensor"),
            P(None, ("dp", "seq"), "tensor"),
            P(("dp", "seq"), "tensor"),
            P(("dp", "seq"), "tensor"),
            P("tensor", ("dp", "seq")),
            P(None, "tensor"),
            P(None, "tensor"),
            P(None, "tensor"),
            P("tensor"),
            P(None, ("dp", "seq"), "tensor"),
            P(("dp", "seq"), "tensor"),
            P(("dp", "seq"), "tensor"),
            P("tensor", ("dp", "seq")),
            P(None, "tensor"),
            P(None, "tensor"),
        ),
        check_vma=False,
    )
```

```python
import math

import jax
import jax.numpy as jnp
from jax import lax
from jax.experimental import pallas as pl
from jax.experimental.pallas import tpu as pltpu
from jax.sharding import PartitionSpec as P

D = 1536
INNER = 3072
HEADDIM = 64
STATE = 128
CONV = 4
MB = 2


EPS = 1e-05
LEARN = 0.05
CLIP_RMS = 0.25
HIGH = lax.Precision.HIGHEST


def shifted(block, axis, distance):
    devices = range(lax.axis_size(axis))
    route = [(i - distance, i) for i in devices if i - distance in devices]
    return lax.ppermute(block, axis, route)


def prefix(array, axis, combine, identity):
    size, position = (lax.axis_size(axis), lax.axis_index(axis))
    everything = jax.tree.map(
        lambda part, kind: lax.all_gather(part.astype(kind), axis),
        array,
        (jnp.bfloat16, jnp.bfloat16),
    )
    start = jax.tree.map(
        lambda part, zero: jnp.broadcast_to(jnp.asarray(zero, part.dtype), part.shape),
        array,
        identity,
    )

    def prefix_step(k, before):
        reached = k < position
        new = combine(
            before, jax.tree.map(lambda part, own: part[k].astype(own.dtype), everything, array)
        )
        return jax.tree.map(lambda a, b: jnp.where(reached, a, b), new, before)

    return lax.fori_loop(0, size, prefix_step, start)


def entering_2(array, axis, combine, identity):
    size, position = (lax.axis_size(axis), lax.axis_index(axis))
    everything = jax.tree.map(lambda part: lax.all_gather(part, axis), array)
    start = jax.tree.map(
        lambda part, zero: jnp.broadcast_to(jnp.asarray(zero, part.dtype), part.shape),
        array,
        identity,
    )

    def entering_step(k, before):
        at = size - 1 - k
        reached = at > position
        new = combine(before, jax.tree.map(lambda part: part[at], everything))
        return jax.tree.map(lambda a, b: jnp.where(reached, a, b), new, before)

    return lax.fori_loop(0, size, entering_step, start)


def rms_scale(values, weight):
    return values * lax.rsqrt(jnp.mean(values * values, axis=-1, keepdims=True) + EPS) * weight


def conv_block(padded, seg_pad, kernel):
    length = padded.shape[0] - (CONV - 1)
    own_seg = seg_pad[CONV - 1 :]
    summed = jnp.broadcast_to(kernel[CONV], (length, kernel.shape[1]))
    for offset in range(CONV):
        window = padded[offset : offset + length]
        same_doc = (seg_pad[offset : offset + length] == own_seg)[:, None]
        summed = summed + kernel[offset] * jnp.where(same_doc, window, 0.0)
    return jax.nn.silu(summed)


def decay_table(cumulative, segids):
    row_count = segids.shape[0]
    places = jnp.arange(row_count)
    allowed = (segids[:, None] == segids[None, :]) & (places[:, None] >= places[None, :])
    allowed = allowed[:, :, None]
    gap_values = cumulative[:, None, :] - cumulative[None, :, :]
    return jnp.where(allowed, jnp.exp(jnp.where(allowed, gap_values, -60.0)), 0.0)


def head_rates(raw_step, params):
    step_sizes = jax.nn.softplus(raw_step + params[0])
    return (step_sizes, jnp.cumsum(-step_sizes * jnp.exp(params[1]), axis=0))


def mix_out(values, b_proj, c_proj, raw_step, params, segids, before, carry_in):
    step_sizes, cumulative = head_rates(raw_step, params)
    scores = jnp.dot(c_proj, b_proj.T, precision=HIGH)
    weights = scores[:, :, None] * decay_table(cumulative, segids) * step_sizes[None, :, :]
    result = jnp.einsum("tsh,shp->thp", weights, values, precision=HIGH)
    entering = jnp.where((segids == before)[:, None], jnp.exp(cumulative), 0.0)
    carried = jnp.einsum("tn,hpn->thp", c_proj, carry_in, precision=HIGH)
    return result + entering[:, :, None] * carried + params[2][None, :, None] * values


def mix_state(values, b_proj, raw_step, params, segids, before):
    step_sizes, cumulative = head_rates(raw_step, params)
    tail_weight = (
        jnp.where(
            (segids == segids[-1])[:, None], jnp.exp(cumulative[-1][None, :] - cumulative), 0.0
        )
        * step_sizes
    )
    summary = jnp.einsum("sh,shp,sn->hpn", tail_weight, values, b_proj, precision=HIGH)
    passing = jnp.where(segids[-1] == before, jnp.exp(cumulative[-1]), 0.0)
    return (summary, passing)


def chain(earlier, later):
    return (earlier[0] * later[0], later[0][..., None, None] * earlier[1] + later[1])


def add_tree(totals, terms):
    if totals is None:
        return terms
    return jax.tree.map(jnp.add, totals, terms)


def project(left_rows, matrix):
    return jnp.einsum("bld,dk->blk", left_rows, matrix, preferred_element_type=jnp.float32)


def weight_grad(left_rows, right_rows):
    return jnp.einsum("bld,blk->dk", left_rows, right_rows, preferred_element_type=jnp.float32)


def back_project(grad_rows, matrix):
    return jnp.einsum("blk,dk->bld", grad_rows, matrix, preferred_element_type=jnp.float32)


def general_body(
    inputs,
    segments,
    cotangent,
    prenorm,
    inproj,
    statproj,
    stepproj,
    outproj,
    convinner,
    convstate,
    headparam,
    gatenorm,
    prenorm_moment,
    inproj_moment,
    statproj_moment,
    stepproj_moment,
    outproj_moment,
    convinner_moment,
    convstate_moment,
    headparam_moment,
    gatenorm_moment,
):
    tensor_at = lax.axis_index("tensor")
    seq_at = lax.axis_index("seq")
    data_at = lax.axis_index("dp")
    tensor_count = lax.axis_size("tensor")
    batch_count = inputs.shape[1]
    span_len = inputs.shape[2]
    inner_local = convinner.shape[1]
    heads_local = headparam.shape[1]
    state_half = 2 * STATE // tensor_count
    model_half = D // tensor_count
    rows_full, grads_full = (
        lax.all_gather(inputs, "tensor", axis=3, tiled=True),
        lax.all_gather(cotangent, "tensor", axis=3, tiled=True),
    )
    seg_padded = jnp.pad(segments, ((0, 0), (0, 0), (CONV - 1, 0)), constant_values=-1)
    seg_local = lax.dynamic_slice_in_dim(seg_padded, seq_at * span_len, span_len + CONV - 1, 2)
    kernel = jnp.concatenate([convinner, convstate], axis=1)
    shares = None
    smalls = None
    outputs = []
    input_grads = []
    for batch in range(MB):
        inproj_all, statproj_all, stepproj_all, outproj_all = (
            lax.all_gather(inproj, "dp", axis=1, tiled=True),
            lax.all_gather(statproj, "dp", axis=0, tiled=True),
            lax.all_gather(stepproj, "dp", axis=0, tiled=True),
            lax.all_gather(outproj, "dp", axis=1, tiled=True),
        )
        rows = rows_full[batch].astype(jnp.float32)
        normed, norm_back = jax.vjp(rms_scale, rows, prenorm)
        normed_low = normed.astype(jnp.bfloat16)
        gate_pre = project(normed_low, inproj_all[0])
        inner_pre = project(normed_low, inproj_all[1])
        state_pre = project(normed_low, statproj_all)
        raw_step = project(normed_low, stepproj_all)
        mixed = jnp.concatenate([inner_pre, state_pre], axis=2).astype(jnp.bfloat16)
        edge_in = shifted(mixed[:, span_len - (CONV - 1) :, :], "seq", 1)
        padded = jnp.concatenate([edge_in, mixed], axis=1).astype(jnp.float32)
        seg_now = seg_local[batch]
        own_seg = seg_now[:, CONV - 1 :]
        before = seg_now[:, CONV - 2]
        conv_out, conv_back = jax.vjp(
            lambda pad_vals, kernel_in: jax.vmap(conv_block, in_axes=(0, 0, None))(
                pad_vals, seg_now, kernel_in
            ),
            padded,
            kernel,
        )
        values = conv_out[..., :inner_local].reshape(batch_count, span_len, heads_local, HEADDIM)
        b_proj = conv_out[..., inner_local : inner_local + STATE]
        c_proj = conv_out[..., inner_local + STATE :]
        (summary, passing), state_back = jax.vjp(
            lambda value_in, b_part, raw_part, param_in: jax.vmap(
                mix_state, in_axes=(0, 0, 0, None, 0, 0)
            )(value_in, b_part, raw_part, param_in, own_seg, before),
            values,
            b_proj,
            raw_step,
            headparam,
        )
        identity = (jnp.ones_like(passing), jnp.zeros_like(summary))
        _, carry_in = prefix((passing, summary), "seq", chain, identity)
        mixer, out_back = jax.vjp(
            lambda value_in, b_part, c_part, raw_part, param_in, state_in: jax.vmap(
                mix_out, in_axes=(0, 0, 0, 0, None, 0, 0, 0)
            )(value_in, b_part, c_part, raw_part, param_in, own_seg, before, state_in),
            values,
            b_proj,
            c_proj,
            raw_step,
            headparam,
            carry_in,
        )
        flat_mixer = mixer.reshape(batch_count, span_len, inner_local)
        gate_act = jax.nn.silu(gate_pre)
        gated_in = flat_mixer * gate_act
        total_sq = lax.psum(jnp.sum(gated_in * gated_in, axis=-1), "tensor")
        scale = lax.rsqrt(total_sq / INNER + EPS)[..., None]
        gated_low = (gated_in * scale * gatenorm).astype(jnp.bfloat16)
        branch_part = project(gated_low, outproj_all)
        branch_own = lax.psum_scatter(branch_part, "tensor", scatter_dimension=2, tiled=True)
        outputs.append((inputs[batch].astype(jnp.float32) + branch_own).astype(jnp.bfloat16))
        grad_rows = grads_full[batch]
        d_gated = back_project(grad_rows, outproj_all)
        g_outproj = jnp.einsum(
            "blk,bld->kd", gated_low, grad_rows, preferred_element_type=jnp.float32
        )
        g_gatenorm = jnp.sum(d_gated * gated_in * scale, axis=(0, 1))
        weighted = d_gated * gatenorm
        cross = lax.psum(jnp.sum(weighted * gated_in, axis=-1), "tensor")
        d_in = weighted * scale - gated_in * scale**3 * (cross / INNER)[..., None]
        d_mixer = d_in * gate_act
        sigma = jax.nn.sigmoid(gate_pre)
        d_gate = d_in * flat_mixer * sigma * (1.0 + gate_pre * (1.0 - sigma))
        d_values, d_bproj, d_cproj, d_raw, d_param, d_carry = out_back(
            d_mixer.reshape(batch_count, span_len, heads_local, HEADDIM)
        )
        _, d_after = entering_2((passing, d_carry), "seq", chain, identity)
        d_passing = jnp.sum(d_after * carry_in, axis=(2, 3))
        d_values_tail, d_bproj_tail, d_raw_tail, d_param_tail = state_back((d_after, d_passing))
        d_state = lax.psum(jnp.concatenate([d_bproj + d_bproj_tail, d_cproj], axis=2), "tensor")
        d_conv = jnp.concatenate(
            [(d_values + d_values_tail).reshape(batch_count, span_len, inner_local), d_state],
            axis=2,
        )
        d_padded, d_kernel = conv_back(d_conv)
        edge_back = shifted(d_padded[:, : CONV - 1, :].astype(jnp.bfloat16), "seq", -1).astype(
            jnp.float32
        )
        d_mixed = d_padded[:, CONV - 1 :, :] + jnp.pad(
            edge_back, ((0, 0), (span_len - (CONV - 1), 0), (0, 0))
        )
        d_mixed_low = d_mixed.astype(jnp.bfloat16)
        d_gate_low = d_gate.astype(jnp.bfloat16)
        d_raw_low = (d_raw + d_raw_tail).astype(jnp.bfloat16)
        d_inner_low = d_mixed_low[..., :inner_local]
        d_state_low = lax.dynamic_slice_in_dim(
            d_mixed_low[..., inner_local:], tensor_at * state_half, state_half, 2
        )
        statproj_own = lax.dynamic_slice_in_dim(statproj_all, tensor_at * state_half, state_half, 1)
        g_inproj = jnp.stack(
            [weight_grad(normed_low, d_gate_low), weight_grad(normed_low, d_inner_low)]
        )
        g_statproj = weight_grad(normed_low, d_state_low)
        g_stepproj = weight_grad(normed_low, d_raw_low)
        d_normed_part = (
            back_project(d_gate_low, inproj_all[0])
            + back_project(d_inner_low, inproj_all[1])
            + back_project(d_state_low, statproj_own)
            + back_project(d_raw_low, stepproj_all)
        )
        d_normed = lax.psum(d_normed_part, "tensor")
        d_rows, d_prenorm = norm_back(d_normed)
        own_rows = lax.dynamic_slice_in_dim(d_rows, tensor_at * model_half, model_half, 2)
        input_grads.append((own_rows + cotangent[batch].astype(jnp.float32)).astype(jnp.bfloat16))
        big_terms = (g_inproj, g_outproj, g_statproj, g_stepproj)
        small_terms = (
            lax.dynamic_slice_in_dim(d_prenorm, tensor_at * model_half, model_half, 0),
            d_kernel[:, :inner_local],
            lax.dynamic_slice_in_dim(
                d_kernel[:, inner_local:], tensor_at * state_half, state_half, 1
            ),
            d_param + d_param_tail,
            g_gatenorm,
        )
        shares = add_tree(
            shares,
            (
                lax.psum_scatter(big_terms[0], ("dp", "seq"), scatter_dimension=1, tiled=True),
                lax.psum_scatter(big_terms[1], ("dp", "seq"), scatter_dimension=1, tiled=True),
                lax.psum_scatter(big_terms[2], ("dp", "seq"), scatter_dimension=0, tiled=True),
                lax.psum_scatter(big_terms[3], ("dp", "seq"), scatter_dimension=0, tiled=True),
            ),
        )
        smalls = add_tree(
            smalls,
            lax.psum(
                (small_terms[0], small_terms[1], small_terms[2], small_terms[3], small_terms[4]),
                ("dp", "seq"),
            ),
        )
    big_sq = jnp.sum(jnp.stack([jnp.sum(term * term) for term in shares]))
    small_sq = jnp.sum(jnp.stack([jnp.sum(term * term) for term in smalls]))
    first_owner = jnp.where((data_at == 0) & (seq_at == 0), 1.0, 0.0)
    norm_sq = lax.psum(big_sq + first_owner * small_sq, ("dp", "seq", "tensor"))
    grad_norm = jnp.sqrt(norm_sq)
    heads_all = INNER // HEADDIM
    entries = (
        2 * D * INNER
        + 2 * D * STATE
        + D * heads_all
        + INNER * D
        + (CONV + 1) * (INNER + 2 * STATE)
        + 3 * heads_all
        + INNER
        + D
    )
    limit = CLIP_RMS * math.sqrt(entries)
    factor = limit / jnp.maximum(grad_norm, limit)
    shard_rows = shares[0].shape[1]
    row_start = seq_at * shard_rows
    big_current = (
        lax.dynamic_slice_in_dim(inproj, row_start, shard_rows, 1),
        lax.dynamic_slice_in_dim(outproj, row_start, shard_rows, 1),
        lax.dynamic_slice_in_dim(
            lax.dynamic_slice_in_dim(statproj, row_start, shard_rows, 0),
            tensor_at * state_half,
            state_half,
            1,
        ),
        lax.dynamic_slice_in_dim(stepproj, row_start, shard_rows, 0),
    )
    conv_current = (
        convinner,
        lax.dynamic_slice_in_dim(convstate, tensor_at * state_half, state_half, 1),
    )
    big_moments = (inproj_moment, outproj_moment, statproj_moment, stepproj_moment)
    small_moments = (
        prenorm_moment,
        convinner_moment,
        convstate_moment,
        headparam_moment,
        gatenorm_moment,
    )
    big_new_moments = [
        0.5 * moment_item + 0.5 * factor * grad_item
        for moment_item, grad_item in zip(big_moments, shares)
    ]
    small_new_moments = [
        0.5 * moment_item + 0.5 * factor * grad_item
        for moment_item, grad_item in zip(small_moments, smalls)
    ]
    big_new = [
        (weight_item.astype(jnp.float32) - LEARN * moment_item).astype(weight_item.dtype)
        for weight_item, moment_item in zip(big_current, big_new_moments)
    ]
    conv_new = [
        (weight_item - LEARN * moment_item).astype(weight_item.dtype)
        for weight_item, moment_item in zip(conv_current, small_new_moments[1:3])
    ]
    return (
        jnp.stack(outputs),
        jnp.stack(input_grads),
        grad_norm,
        small_new_moments[0],
        big_new_moments[0],
        big_new_moments[2],
        big_new_moments[3],
        big_new_moments[1],
        small_new_moments[1],
        small_new_moments[2],
        small_new_moments[3],
        small_new_moments[4],
        big_new[0],
        big_new[2],
        big_new[3],
        big_new[1],
        conv_new[0],
        conv_new[1],
    )


BLOCKS = 4
SPAN = 256
PART = 128
PARTS = SPAN // PART
PACKED = 48
LOG2E = 1.4426950408889634
QUARTER = 384
QHEADS = 6
MAPS_AT = 3 * QUARTER
BF = jnp.bfloat16
F32 = jnp.float32
ROUTE_X = [(i, i ^ 1) for i in range(BLOCKS)]
ROUTE_Y = [(i, i ^ 2) for i in range(BLOCKS)]
SWAP = [(0, 1), (1, 0)]
VMEM_LIMIT = 56 * 1024 * 1024


def dot_nn(a, b):
    return lax.dot_general(a, b, (((1,), (0,)), ((), ())), preferred_element_type=F32)


def dot_nt(a, b):
    return lax.dot_general(a, b, (((1,), (1,)), ((), ())), preferred_element_type=F32)


def dot_tn(a, b):
    return lax.dot_general(a, b, (((0,), (0,)), ((), ())), preferred_element_type=F32)


def dot_exact(a, b):
    return lax.dot_general(
        a, b, (((1,), (0,)), ((), ())), precision=HIGH, preferred_element_type=F32
    )


def sigmoid(v):
    return 1.0 / (1.0 + jnp.exp(-v))


def split_sum(triangle, table):
    first = table.astype(BF)
    rest = table - first.astype(F32)
    second = rest.astype(BF)
    third = (rest - second.astype(F32)).astype(BF)
    parts = (
        first.astype(F32)
        + pltpu.roll(second.astype(F32), 8, 1)
        + pltpu.roll(third.astype(F32), 16, 1)
    )
    sums = dot_nn(triangle, parts.astype(BF))
    sums = sums + pltpu.roll(sums, 120, 1) + pltpu.roll(sums, 112, 1)
    lanes = lax.broadcasted_iota(jnp.int32, sums.shape, 1)
    return jnp.where(lanes < 8, sums, 0.0)


def head_sums(table, gather):
    first = table.astype(BF)
    second = (table - first.astype(F32)).astype(BF)
    return dot_nn(first, gather) + dot_nn(second, gather)


def head_spread():
    lane = lax.broadcasted_iota(jnp.int32, (128, QUARTER), 0)
    chan = lax.broadcasted_iota(jnp.int32, (128, QUARTER), 1)
    base = jnp.where(lane < 8, lane, jnp.where(lane < 16, lane - 8, -1)) * HEADDIM
    return jnp.where((chan >= base) & (chan < base + HEADDIM) & (base >= 0), 1.0, 0.0).astype(BF)


def spread_heads(tables, spread):
    packed = []
    for table in tables:
        lanes = lax.broadcasted_iota(jnp.int32, table.shape, 1)
        table = jnp.where(lanes < 8, table, 0.0)
        first = table.astype(BF).astype(F32)
        packed.append((first + pltpu.roll(table - first, 8, 1)).astype(BF))
    wide = dot_nn(jnp.concatenate(packed, axis=0), spread)
    return [wide[PART * k : PART * (k + 1)] for k in range(len(tables))]


def rates(raw, head):
    shifted_raw = raw + head[0:1]
    step = jnp.maximum(shifted_raw, 0.0) + jnp.log1p(jnp.exp(-jnp.abs(shifted_raw)))
    lanes = lax.broadcasted_iota(jnp.int32, raw.shape, 1)
    return shifted_raw, jnp.where(lanes < QHEADS, step, 0.0)


def triangle(keep):
    rows_at = lax.broadcasted_iota(jnp.int32, (PART, PART), 0)
    cols_at = lax.broadcasted_iota(jnp.int32, (PART, PART), 1)
    return jnp.where(keep(rows_at, cols_at), 1.0, 0.0).astype(BF)


def part_terms(step, head, cols, segr, lower):
    cum = split_sum(lower, -step * head[1:2]) * LOG2E
    last = cum[PART - 1 : PART]
    enter = jnp.exp2(cum) * cols[:, 4:5]
    leave = jnp.exp2(last - cum) * cols[:, 5:6]
    passing = jnp.exp2(last) * cols[PART - 1 : PART, 4:5]
    rows_at = lax.broadcasted_iota(jnp.int32, (PART, PART), 0)
    cols_at = lax.broadcasted_iota(jnp.int32, (PART, PART), 1)
    allowed = (rows_at >= cols_at) & (cols[:, 6:7] == segr)
    return cum, enter, leave, passing, jnp.where(allowed, 0.0, -1e30)


def head_decay(cum, cum_t, h, block_out):
    return jnp.exp2(cum[:, h : h + 1] - cum_t[h : h + 1] + block_out)


def by_head(table, low_half):
    zero = jnp.zeros_like(table)
    return jnp.concatenate(
        [jnp.where(low_half, table, zero), jnp.where(low_half, zero, table)], axis=0
    )


def pass_state(passing, state, added):
    heads = [slice(HEADDIM * h, HEADDIM * (h + 1)) for h in range(QHEADS)]
    return jnp.concatenate(
        [passing[:, h : h + 1] * state[at] + added[at] for h, at in enumerate(heads)], axis=0
    )


def segment_flags(seg_ref, q, block):
    begin = pl.multiple_of(block * SPAN, 128)
    around = seg_ref[q, :, pl.ds(begin, SPAN + 256)]
    here = around[:, 128 : 128 + SPAN]
    flags = []
    for shift in (3, 2, 1, 0):
        flags.append(pltpu.roll(around, shift, 1)[:, 128 : 128 + SPAN] == here)
    ends = [around[:, PART * k + 127 : PART * k + 128] for k in range(PARTS + 1)]
    parts = [here[:, PART * k : PART * (k + 1)] for k in range(PARTS)]
    flags.append(jnp.concatenate([parts[k] == ends[k] for k in range(PARTS)], axis=1))
    flags.append(jnp.concatenate([parts[k] == ends[k + 1] for k in range(PARTS)], axis=1))
    for shift in (3, 2, 1, 0):
        later = pltpu.roll(around, SPAN + 256 - shift, 1) if shift else around
        flags.append(later[:, 128 : 128 + SPAN] == here)
    flags = [jnp.where(flag, 1.0, 0.0) for flag in flags]
    at = lax.broadcasted_iota(jnp.int32, (8, SPAN), 0)
    first = here
    for row in range(6):
        first = jnp.where(at == row, flags[row], first)
    second = flags[9]
    for row in range(3):
        second = jnp.where(at == row, flags[6 + row], second)
    return jnp.concatenate([first, second], axis=0)


def to_columns(rows):
    filled = jnp.concatenate([rows, jnp.zeros((128 - rows.shape[0], SPAN), F32)], axis=0)
    return filled.T


def both_tokens(own_ref, other_ref):
    return jnp.concatenate([own_ref[0], other_ref[0]], axis=0)


def fwd_kernel(
    place_ref, own_ref, other_ref, w_ref, seg_ref, taps_ref, head_ref, chan_ref,
    mixed_ref, raw_ref, pre_ref, y_ref, hin_ref, buf, state,
):
    block = pl.program_id(0)

    @pl.when(block == 0)
    def _():
        buf[:, 0:8] = jnp.zeros((2, 8, buf.shape[2]), F32)
        state[...] = jnp.zeros_like(state)

    width = QUARTER + 2 * STATE
    projected = dot_nn(both_tokens(own_ref, other_ref), w_ref[...])
    taps = taps_ref[...]
    head = head_ref[...]
    skip = chan_ref[1:2]
    lower = triangle(lambda r, c: r >= c)
    spread = head_spread()
    low_half = lax.broadcasted_iota(jnp.int32, (PART, 128), 1) < HEADDIM
    pieces = []
    for q in range(2):
        rows_q = slice(q * SPAN, (q + 1) * SPAN)
        raw = projected[rows_q, width:]
        raw_ref[q, 0] = raw
        mixed_low = projected[rows_q, :width].astype(BF)
        mixed_ref[q, 0] = mixed_low
        mixed = mixed_low.astype(F32)
        buf[q, 8 : 8 + SPAN] = mixed
        rows = segment_flags(seg_ref, q, block)
        cols_all = to_columns(rows)
        pre = jnp.broadcast_to(taps[CONV : CONV + 1], mixed.shape)
        for j in range(CONV):
            window = mixed if j == CONV - 1 else buf[q, 5 + j : 5 + j + SPAN]
            pre = pre + taps[j : j + 1] * (window * cols_all[:, j : j + 1])
        buf[q, 0:8] = mixed[SPAN - 8 :]
        pre_ref[q, 0] = pre
        act = pre * sigmoid(pre)
        _, step_all = rates(raw, head)
        for part in range(PARTS):
            at_rows = slice(part * PART, (part + 1) * PART)
            cols = cols_all[at_rows]
            cum, enter, leave, passing, block_out = part_terms(
                step_all[at_rows], head, cols, rows[6:7, at_rows], lower
            )
            pieces.append(
                (q, part, act[at_rows], step_all[at_rows], cum, enter, leave, passing, block_out)
            )
    work = []
    for q, part, act, step, cum, enter, leave, passing, block_out in pieces:
        values = act[:, :QUARTER]
        b_low = act[:, QUARTER : QUARTER + STATE].astype(BF)
        c_low = act[:, QUARTER + STATE :].astype(BF)
        step_w, enter_w, leave_w = spread_heads((step, enter, leave), spread)
        cum_t = cum.T
        scores = dot_nt(c_low, b_low)
        scaled = (step_w * values).astype(BF)
        tail = (leave_w * scaled.astype(F32)).astype(BF)
        added = dot_tn(tail, b_low)
        own = []
        for k in range(QHEADS // 2):
            at = slice(128 * k, 128 * (k + 1))
            weights = [
                (scores * head_decay(cum, cum_t, h, block_out)).astype(BF)
                for h in (2 * k, 2 * k + 1)
            ]
            own.append(dot_nn(jnp.concatenate(weights, axis=1), by_head(scaled[:, at], low_half)))
        own = jnp.concatenate(own, axis=1) + skip * values
        work.append((q, part, c_low, enter_w, passing, added, own))
    for q, part, c_low, enter_w, passing, added, own in sorted(work, key=lambda item: item[1]):
        held_f = state[q]
        held = held_f.astype(BF)
        hin_ref[q, 0, QUARTER * part : QUARTER * (part + 1)] = held
        y_ref[q, 0, part * PART : (part + 1) * PART] = own + enter_w * dot_nt(c_low, held)
        state[q] = pass_state(passing, held_f, added)


def core_rows(place_ref):
    half = D // 2
    core = place_ref[0]
    own = pl.multiple_of(core * half, half)
    other = pl.multiple_of((1 - core) * half, half)
    return pl.ds(own, half), pl.ds(other, half)


def gate_kernel(
    place_ref, own_ref, other_ref, cot_own_ref, cot_other_ref, y_ref, w_gate_ref, w_out_ref,
    chan_ref,
    gate_ref, d_gated_ref, mine_ref, theirs_ref, stat_ref,
):
    gate = dot_nn(both_tokens(own_ref, other_ref), w_gate_ref[...])
    d_gated = dot_nn(both_tokens(cot_own_ref, cot_other_ref), w_out_ref[...])
    guns = []
    for q in range(2):
        at = slice(q * SPAN, (q + 1) * SPAN)
        gate_q = gate[at]
        gate_ref[q, 0] = gate_q
        d_gated_ref[q, 0] = d_gated[at]
        gated_in = y_ref[q, 0] * (gate_q * sigmoid(gate_q))
        weighted = gated_in * chan_ref[0:1]
        guns.append(weighted.astype(BF))
        square = jnp.sum(gated_in * gated_in, axis=1, keepdims=True)
        cross = jnp.sum(d_gated[at] * weighted, axis=1, keepdims=True)
        lanes = lax.broadcasted_iota(jnp.int32, (SPAN, 128), 1)
        table = jnp.where(lanes == 0, square, jnp.where(lanes == 1, cross, 0.0))
        stat_ref[q, 0] = table.T[0:2]
    gun = jnp.concatenate(guns, axis=0)
    own, other = core_rows(place_ref)
    mine = dot_nt(gun, w_out_ref[own]).astype(BF)
    theirs = dot_nt(gun, w_out_ref[other]).astype(BF)
    for q in range(2):
        mine_ref[0, q] = mine[q * SPAN : (q + 1) * SPAN]
        theirs_ref[0, 1 - q] = theirs[q * SPAN : (q + 1) * SPAN]


def start_sums(total, seed_ref):
    @pl.when(pl.program_id(0) == 0)
    def _():
        total[...] = jnp.zeros_like(total) if seed_ref is None else seed_ref[...]


def finish_sums(total, out_ref):
    @pl.when(pl.program_id(0) == BLOCKS - 1)
    def _():
        rows_of = out_ref.shape[2]
        for z in range(out_ref.shape[0]):
            out_ref[z] = total[:, z * rows_of : (z + 1) * rows_of].astype(BF)


def gate_back_first(*refs):
    gate_back_step(*refs[:10], None, *refs[10:])


def gate_back_last(*refs):
    gate_back_step(*refs[:11], *refs[11:14], refs[15])
    finish_sums(refs[15], refs[14])


def gate_back_step(
    place_ref, own_ref, other_ref, cot_own_ref, cot_other_ref, y_ref, gate_ref, d_gated_ref,
    stat_ref, chan_ref, seed_ref,
    dy_ref, d_gate_ref, g_gain_ref, g_ref,
):
    start_sums(g_ref, seed_ref)
    start_sums(g_gain_ref, None)
    gateds = []
    d_gates = []
    for q in range(2):
        stat = to_columns(stat_ref[q, 0])
        scale = lax.rsqrt(stat[:, 0:1] * (1.0 / INNER) + EPS)
        pull = stat[:, 1:2] * (1.0 / INNER) * scale * scale * scale
        gate = gate_ref[q, 0]
        y = y_ref[q, 0]
        d_gated = d_gated_ref[q, 0]
        sigma = sigmoid(gate)
        gate_act = gate * sigma
        gated_in = y * gate_act
        scaled_gain = chan_ref[0:1] * scale
        d_in = d_gated * scaled_gain - gated_in * pull
        dy_ref[q, 0] = (d_in * gate_act).astype(BF)
        d_gate = (d_in * y * (sigma + gate_act * (1.0 - sigma))).astype(BF)
        d_gate_ref[q, 0] = d_gate
        d_gates.append(d_gate)
        gateds.append((gated_in * scaled_gain).astype(BF))
        g_gain_ref[0:1] += jnp.sum(d_gated * gated_in * scale, axis=0, keepdims=True)
    gated = jnp.concatenate(gateds, axis=0)
    d_gate = jnp.concatenate(d_gates, axis=0)
    g_ref[:QUARTER] += dot_tn(gated, both_tokens(cot_own_ref, cot_other_ref))
    g_ref[QUARTER:] += dot_tn(d_gate, both_tokens(own_ref, other_ref))


def bwd_first(*refs):
    bwd_step(*refs[:16], None, refs[16], None, None, *refs[17:])


def bwd_last(*refs):
    total = refs[-1]
    bwd_step(*refs[:17], total, *refs[18:-1])
    finish_sums(total, refs[17])


def bwd_step(
    place_ref, own_ref, other_ref, mixed_ref, pre_ref, raw_ref, y_ref, hin_ref, dy_ref,
    d_gate_ref, seg_ref, taps_ref, head_ref, chan_ref, w_ref, w_gate_ref,
    seed_ref,
    g_ref, keep_ref, give_ref, slope_ref, gtap_ref, ghead_ref, mine_ref, theirs_ref,
    buf, d_state, bc_edge, slope_edge, d_late,
):
    start_sums(g_ref, seed_ref)
    block = BLOCKS - 1 - pl.program_id(0)

    @pl.when(pl.program_id(0) == 0)
    def _():
        buf[:, SPAN:] = jnp.zeros((2, 8, QUARTER), F32)
        d_state[...] = jnp.zeros_like(d_state)
        bc_edge[...] = jnp.zeros_like(bc_edge)
        slope_edge[...] = jnp.zeros_like(slope_edge)
        gtap_ref[...] = jnp.zeros_like(gtap_ref)
        ghead_ref[...] = jnp.zeros_like(ghead_ref)

    head = head_ref[...]
    taps = taps_ref[...]
    skip = chan_ref[1:2]
    first_core = place_ref[0] == 0
    low_half = lax.broadcasted_iota(jnp.int32, (PART, 128), 1) < HEADDIM
    chan_at = lax.broadcasted_iota(jnp.int32, (QUARTER, 128), 0)
    head_at = lax.broadcasted_iota(jnp.int32, (QUARTER, 128), 1)
    gather = jnp.where(
        (chan_at >= head_at * HEADDIM) & (chan_at < (head_at + 1) * HEADDIM), 1.0, 0.0
    )
    gather_low = gather.astype(BF)
    lower = triangle(lambda r, c: r >= c)
    upper = triangle(lambda r, c: r <= c)
    spread = head_spread()

    def store(ref, q, first_row, rows):
        if keep_ref is not None:
            ref[0, q, first_row : first_row + rows.shape[0]] = rows
            return
        for at in range(first_row, first_row + rows.shape[0], 16):
            group = at // PACKED
            row = SPAN + at % PACKED
            ref[0, q, row : row + 16, 128 * group : 128 * (group + 1)] = rows[
                at - first_row : at - first_row + 16
            ]

    keep_at = mine_ref if keep_ref is None else keep_ref
    give_at = theirs_ref if give_ref is None else give_ref
    pieces = []
    columns = []
    slopes = []
    for q in range(2):
        rows = segment_flags(seg_ref, q, block)
        cols_all = to_columns(rows)
        columns.append(cols_all)
        pre = pre_ref[q, 0]
        sigma = sigmoid(pre)
        act = pre * sigma
        slope = sigma * (1.0 + pre * (1.0 - sigma))
        slopes.append(slope)
        slope_half = jnp.where(
            first_core, slope[:, QUARTER : QUARTER + STATE], slope[:, QUARTER + STATE :]
        )
        slope_ref[q, 0, 0:SPAN] = slope_half
        slope_ref[q, 0, SPAN : SPAN + 16] = slope_edge[q]
        slope_edge[q] = slope_half[0:16]
        if keep_ref is None:
            for ref in (mine_ref, theirs_ref):
                ref[0, q, SPAN + 32 :, 640:] = jnp.zeros((16, 128), BF)
        store(keep_at, q, SPAN, bc_edge[q, :, :STATE].astype(BF))
        store(give_at, 1 - q, SPAN, bc_edge[q, :, STATE:].astype(BF))
        shifted_all, step_all = rates(raw_ref[q, 0], head)
        for part in range(PARTS):
            at_rows = slice(part * PART, (part + 1) * PART)
            terms = part_terms(
                step_all[at_rows], head, cols_all[at_rows], rows[6:7, at_rows], lower
            )
            pieces.append((q, part, act[at_rows], shifted_all[at_rows], step_all[at_rows], terms))
    work = []
    for q, part, act, shifted_raw, step, terms in pieces:
        cum, enter, leave, passing, block_out = terms
        values = act[:, :QUARTER]
        b_low = act[:, QUARTER : QUARTER + STATE].astype(BF)
        c_low = act[:, QUARTER + STATE :].astype(BF)
        step_w, enter_w, leave_w = spread_heads((step, enter, leave), spread)
        cum_t = cum.T
        scores = dot_nt(c_low, b_low)
        dy_low = dy_ref[q, 0, part * PART : (part + 1) * PART]
        scaled = (step_w * values).astype(BF)
        tail = (leave_w * scaled.astype(F32)).astype(BF)
        enter_dy = (enter_w * dy_low.astype(F32)).astype(BF)
        d_scores = jnp.zeros((PART, PART), F32)
        own = []
        for k in range(QHEADS // 2):
            at = slice(128 * k, 128 * (k + 1))
            dy_both = by_head(dy_low[:, at], low_half)
            d_weights = dot_nt(dy_both, scaled[:, at])
            weights = []
            for half, h in enumerate((2 * k, 2 * k + 1)):
                decay = head_decay(cum, cum_t, h, block_out)
                weights.append((scores * decay).astype(BF))
                d_scores = d_scores + d_weights[half * PART : (half + 1) * PART] * decay
            own.append(dot_tn(jnp.concatenate(weights, axis=0), dy_both))
        own = jnp.concatenate(own, axis=1)
        d_scores = d_scores.astype(BF)
        new_state = dot_tn(enter_dy, c_low)
        d_c = dot_nn(d_scores, b_low)
        d_b = dot_tn(d_scores, c_low)
        work.append(
            (q, part, values, b_low, shifted_raw, step, step_w, leave_w, passing, dy_low, scaled,
             tail, enter_dy, own, new_state, d_b, d_c)
        )
    for item in sorted(work, key=lambda item: -item[1]):
        (q, part, values, b_low, shifted_raw, step, step_w, leave_w, passing, dy_low, scaled,
         tail, enter_dy, own, new_state, d_b, d_c) = item
        at_rows = slice(part * PART, (part + 1) * PART)
        held = hin_ref[q, 0, QUARTER * part : QUARTER * (part + 1)]
        dy = dy_low.astype(F32)
        scaled_f = scaled.astype(F32)
        d_after = d_state[q]
        d_after_low = d_after.astype(BF)
        tail_part = leave_w * dot_nt(b_low, d_after_low)
        d_scaled = own + tail_part
        d_c = d_c + dot_nn(enter_dy, held)
        d_b = d_b + dot_nn(tail, d_after_low)
        d_state[q] = pass_state(passing, d_after, new_state)
        kept_half = jnp.where(first_core, d_b, d_c)
        given_half = jnp.where(first_core, d_c, d_b)
        store(keep_at, q, part * PART, kept_half.astype(BF))
        store(give_at, 1 - q, part * PART, given_half.astype(BF))
        if part == 0:
            bc_edge[q, :, :STATE] = kept_half[0:16]
            bc_edge[q, :, STATE:] = given_half[0:16]
        d_values = step_w * d_scaled + skip * dy
        buf[q, at_rows] = d_values * slopes[q][at_rows, :QUARTER]
        by_values = dot_nn((values * d_scaled).astype(BF), gather_low)
        y_part = y_ref[q, 0, at_rows] - skip * values
        d_cum = head_sums(dy * y_part - scaled_f * d_scaled, gather_low)
        tail_row = jnp.sum(scaled_f * tail_part, axis=0, keepdims=True)
        tail_sum = dot_exact(jnp.broadcast_to(tail_row, (8, QUARTER)), gather)[0:1]
        state_dot = jnp.sum(d_after * held.astype(F32), axis=1, keepdims=True)
        state_terms = jnp.sum(state_dot * gather, axis=0, keepdims=True)
        d_rate = split_sum(upper, d_cum) + tail_sum + passing * state_terms
        d_raw = (by_values - head[1:2] * d_rate) * sigmoid(shifted_raw)
        ghead_ref[0:1, :128] += jnp.sum(d_raw, axis=0, keepdims=True)
        ghead_ref[1:2, :128] += jnp.sum(-step * head[1:2] * d_rate, axis=0, keepdims=True)
        ghead_ref[2:3] += jnp.sum(values * dy, axis=0, keepdims=True)
        d_late[q * SPAN + part * PART : q * SPAN + (part + 1) * PART, QUARTER:] = d_raw.astype(BF)
    for q in range(2):
        mixed = mixed_ref[q, 0, :, :QUARTER].astype(F32)
        d_mixed = jnp.zeros((SPAN, QUARTER), F32)
        for j in range(CONV):
            ahead = CONV - 1 - j
            window = buf[q, ahead : ahead + SPAN] * columns[q][:, 8 + j : 9 + j]
            d_mixed = d_mixed + taps[j : j + 1, :QUARTER] * window
            gtap_ref[j : j + 1] += jnp.sum(mixed * window, axis=0, keepdims=True)
        gtap_ref[CONV : CONV + 1] += jnp.sum(buf[q, 0:SPAN], axis=0, keepdims=True)
        buf[q, SPAN:] = buf[q, 0:8]
        d_late[q * SPAN : (q + 1) * SPAN, :QUARTER] = d_mixed.astype(BF)
    late = d_late[...]
    g_ref[...] += dot_tn(late, both_tokens(own_ref, other_ref))[: QUARTER + 16]
    d_gate = jnp.concatenate([d_gate_ref[0, 0], d_gate_ref[1, 0]], axis=0)
    grads = jnp.concatenate([late, d_gate], axis=1)
    width = QUARTER + 2 * STATE
    for rows_at, out_ref, flip in zip(core_rows(place_ref), (mine_ref, theirs_ref), (0, 1)):
        weights = [w_ref[rows_at, :QUARTER], w_ref[rows_at, width:], w_gate_ref[rows_at]]
        total = dot_nt(grads, jnp.concatenate(weights, axis=1)).astype(BF)
        for q in range(2):
            out_ref[0, q ^ flip, :SPAN] = total[q * SPAN : (q + 1) * SPAN]


def slot_spec(rows, width, order):
    return pl.BlockSpec((2, 1, rows, width), lambda j, place: (0, order(j), 0, 0))


def segment_spec():
    return pl.BlockSpec((2, 8, BLOCKS * SPAN + 256), lambda j, place: (0, 0, 0))


def fixed_spec(rows, width):
    return pl.BlockSpec((rows, width), lambda j, place: (0, 0))


def out_shape(rows, cols_of, kind):
    return jax.ShapeDtypeStruct((2, BLOCKS, rows, cols_of), kind)


def upward(j):
    return j


def downward(j):
    return BLOCKS - 1 - j


def token_specs(order):
    return [pl.BlockSpec((1, SPAN, D), lambda j, place: (order(j), 0, 0))] * 2


def call_blocks(kernel, name, place, operands, in_specs, outs, scratch=()):
    return pl.pallas_call(
        kernel,
        grid_spec=pltpu.PrefetchScalarGridSpec(
            num_scalar_prefetch=1,
            grid=(BLOCKS,),
            in_specs=in_specs,
            out_specs=[spec for spec, _ in outs],
            scratch_shapes=list(scratch),
        ),
        out_shape=[shape for _, shape in outs],
        compiler_params=pltpu.CompilerParams(vmem_limit_bytes=VMEM_LIMIT),
        cost_estimate=pl.CostEstimate(flops=1024, bytes_accessed=1024, transcendentals=0),
        name=name,
    )(place, *operands)


def slot_out(rows, width, kind, order):
    return slot_spec(rows, width, order), out_shape(rows, width, kind)


def lead_out(rows, width, order):
    shape = jax.ShapeDtypeStruct((BLOCKS, 2, rows, width), BF)
    return pl.BlockSpec((1, 2, rows, width), lambda j, place: (order(j), 0, 0, 0)), shape


def fixed_out(rows, width):
    return fixed_spec(rows, width), jax.ShapeDtypeStruct((rows, width), F32)


def run_fwd(place, tokens, w_first, rows, taps, head, chan):
    width = QUARTER + 2 * STATE
    return call_blocks(
        fwd_kernel,
        "mix_forward",
        place,
        (*tokens, w_first, rows, taps, head, chan),
        [
            *token_specs(upward),
            fixed_spec(D, width + 128),
            segment_spec(),
            fixed_spec(8, width),
            fixed_spec(8, 128),
            fixed_spec(8, QUARTER),
        ],
        [
            slot_out(SPAN, width, BF, upward),
            slot_out(SPAN, 128, F32, upward),
            slot_out(SPAN, width, F32, upward),
            slot_out(SPAN, QUARTER, F32, upward),
            slot_out(PARTS * QUARTER, STATE, BF, upward),
        ],
        [pltpu.VMEM((2, SPAN + 8, width), F32), pltpu.VMEM((2, QUARTER, STATE), F32)],
    )


def run_gate(place, tokens, cots, y, w_gate, w_out, chan):
    half = D // 2
    return call_blocks(
        gate_kernel,
        "gate_forward",
        place,
        (*tokens, *cots, y, w_gate, w_out, chan),
        [
            *token_specs(upward),
            *token_specs(upward),
            slot_spec(SPAN, QUARTER, upward),
            fixed_spec(D, QUARTER),
            fixed_spec(D, QUARTER),
            fixed_spec(8, QUARTER),
        ],
        [
            slot_out(SPAN, QUARTER, F32, upward),
            slot_out(SPAN, QUARTER, F32, upward),
            lead_out(SPAN, half, upward),
            lead_out(SPAN, half, upward),
            slot_out(2, SPAN, F32, upward),
        ],
    )


def sums_out(rows, dp_count, last):
    if not last:
        return fixed_out(rows, D), []
    share = D // dp_count
    spec = pl.BlockSpec((dp_count, rows, share), lambda j, place: (0, 0, 0))
    out = spec, jax.ShapeDtypeStruct((dp_count, rows, share), BF)
    return out, [pltpu.VMEM((rows, D), F32)]


def run_gate_back(place, tokens, cots, y, gate, d_gated, stat, chan, seed, dp_count):
    last = seed is not None
    total, scratch = sums_out(2 * QUARTER, dp_count, last)
    return call_blocks(
        gate_back_last if last else gate_back_first,
        "gate_backward",
        place,
        (*tokens, *cots, y, gate, d_gated, stat, chan) + ((seed,) if last else ()),
        [
            *token_specs(upward),
            *token_specs(upward),
            slot_spec(SPAN, QUARTER, upward),
            slot_spec(SPAN, QUARTER, upward),
            slot_spec(SPAN, QUARTER, upward),
            slot_spec(2, SPAN, upward),
            fixed_spec(8, QUARTER),
        ]
        + ([fixed_spec(2 * QUARTER, D)] if last else []),
        [
            slot_out(SPAN, QUARTER, BF, upward),
            slot_out(SPAN, QUARTER, BF, upward),
            fixed_out(8, QUARTER),
            total,
        ],
        scratch,
    )


def run_bwd(place, tokens, kept, dy, d_gate, rows, taps, head, chan, weights, seed, dp_count):
    mixed, raw, pre, y, hin = kept
    width = mixed.shape[-1]
    states = 2 * STATE
    half = D // 2
    last = seed is not None
    total, scratch = sums_out(QUARTER + 16, dp_count, last)
    rows_out = SPAN if last else SPAN + PACKED
    maps_out = [lead_out(SPAN + 16, STATE, downward)] * 2 if last else []
    return call_blocks(
        bwd_last if last else bwd_first,
        "mix_backward",
        place,
        (*tokens, mixed, pre, raw, y, hin, dy, d_gate, rows, taps, head, chan, *weights)
        + ((seed,) if last else ()),
        [
            *token_specs(downward),
            slot_spec(SPAN, width, downward),
            slot_spec(SPAN, width, downward),
            slot_spec(SPAN, 128, downward),
            slot_spec(SPAN, QUARTER, downward),
            slot_spec(PARTS * QUARTER, STATE, downward),
            slot_spec(SPAN, QUARTER, downward),
            slot_spec(SPAN, QUARTER, downward),
            segment_spec(),
            fixed_spec(8, width),
            fixed_spec(8, 128),
            fixed_spec(8, QUARTER),
            fixed_spec(D, width + 128),
            fixed_spec(D, QUARTER),
        ]
        + ([fixed_spec(QUARTER + 16, D)] if last else []),
        [
            total,
            *maps_out,
            slot_out(SPAN + 16, STATE, F32, downward),
            fixed_out(8, QUARTER),
            fixed_out(8, QUARTER),
            lead_out(rows_out, half, downward),
            lead_out(rows_out, half, downward),
        ],
        [
            pltpu.VMEM((2, SPAN + 8, QUARTER), F32),
            pltpu.VMEM((2, QUARTER, STATE), F32),
            pltpu.VMEM((2, 16, states), F32),
            pltpu.VMEM((2, 16, STATE), F32),
            pltpu.VMEM((2 * SPAN, QUARTER + 128), BF),
        ]
        + scratch,
    )


def maps_kernel(
    place_ref, packed_ref, maps_ref, slope_0, slope_1, mixed_0, mixed_1, seg_0, seg_1,
    own_0, other_0, own_1, other_1, taps_ref,
    d_maps_ref, g_ref, g_taps_ref, buf,
):
    chip = place_ref[1]
    taps = taps_ref[...]
    buf[SPAN + 16 :] = jnp.zeros((8, STATE), F32)
    sums = [jnp.zeros((1, STATE), F32) for _ in range(CONV + 1)]
    g_maps = jnp.zeros((STATE, D), F32)
    slopes, mixes, segs = (slope_0, slope_1), (mixed_0, mixed_1), (seg_0, seg_1)
    tokens = ((own_0, other_0), (own_1, other_1))
    for m in range(MB):
        for q in range(2):
            if m == 0:
                total = packed_ref[0, q].astype(F32)
                for src in range(1, BLOCKS):
                    total = total + packed_ref[src, q].astype(F32)
                groups = [total[:, 128 * k : 128 * (k + 1)] for k in range(6)]
                d_conv = jnp.concatenate(groups, axis=0)[: SPAN + 16]
            else:
                d_conv = maps_ref[0, q].astype(F32)
                for src in range(1, BLOCKS):
                    d_conv = d_conv + maps_ref[src, q].astype(F32)
            d_pre = d_conv * slopes[m][q, 0]
            buf[0 : SPAN + 16] = d_pre
            cols = to_columns(segment_flags(segs[m], q, chip))
            mixed = mixes[m][q, 0].astype(F32)
            d_mixed = jnp.zeros((SPAN, STATE), F32)
            for j in range(CONV):
                ahead = CONV - 1 - j
                window = buf[ahead : ahead + SPAN] * cols[:, 8 + j : 9 + j]
                d_mixed = d_mixed + taps[j : j + 1] * window
                sums[j] = sums[j] + jnp.sum(mixed * window, axis=0, keepdims=True)
            sums[CONV] = sums[CONV] + jnp.sum(d_pre[:SPAN], axis=0, keepdims=True)
            low = d_mixed.astype(BF)
            d_maps_ref[m, q] = low
            g_maps = g_maps + dot_tn(low, tokens[m][q][0])
    g_taps_ref[...] = jnp.concatenate(sums + [jnp.zeros((3, STATE), F32)], axis=0)
    rows_of = g_ref.shape[2]
    for z in range(g_ref.shape[0]):
        g_ref[z] = g_maps[:, z * rows_of : (z + 1) * rows_of].astype(BF)


def run_maps(place, packed, maps, slopes, mixes, segs, tokens, taps, dp_count):
    def whole(shape):
        return pl.BlockSpec(shape, lambda i, place: (0,) * len(shape))

    def slope_spec():
        return pl.BlockSpec((2, 1, SPAN + 16, STATE), lambda i, place: (0, place[1], 0, 0))

    def mixed_spec():
        first = QUARTER // STATE
        return pl.BlockSpec(
            (2, 1, SPAN, STATE), lambda i, place: (0, place[1], 0, first + place[0])
        )

    def token_spec():
        return pl.BlockSpec((1, SPAN, D), lambda i, place: (place[1], 0, 0))

    share = D // dp_count
    return pl.pallas_call(
        maps_kernel,
        grid_spec=pltpu.PrefetchScalarGridSpec(
            num_scalar_prefetch=1,
            grid=(1,),
            in_specs=[
                whole(packed.shape),
                whole(maps.shape),
                slope_spec(),
                slope_spec(),
                mixed_spec(),
                mixed_spec(),
                whole(segs[0].shape),
                whole(segs[1].shape),
                token_spec(),
                token_spec(),
                token_spec(),
                token_spec(),
                whole(taps.shape),
            ],
            out_specs=[
                whole((MB, 2, SPAN, STATE)),
                whole((dp_count, STATE, share)),
                whole((8, STATE)),
            ],
            scratch_shapes=[pltpu.VMEM((SPAN + 24, STATE), F32)],
        ),
        out_shape=[
            jax.ShapeDtypeStruct((MB, 2, SPAN, STATE), BF),
            jax.ShapeDtypeStruct((dp_count, STATE, share), BF),
            jax.ShapeDtypeStruct((8, STATE), F32),
        ],
        compiler_params=pltpu.CompilerParams(vmem_limit_bytes=VMEM_LIMIT),
        cost_estimate=pl.CostEstimate(flops=1024, bytes_accessed=1024, transcendentals=0),
        name="maps_backward",
    )(place, packed, maps, *slopes, *mixes, *segs, *tokens, taps)


def norm_kernel(place_ref, share_ref, w_in_ref, w_state_ref, w_step_ref, step_ref, out_ref):
    rows = share_ref.shape[1]
    squares = jnp.zeros((rows, QUARTER), F32)
    products = jnp.zeros((rows, QUARTER), F32)
    for s in range(BLOCKS):
        at = slice(s * QUARTER, (s + 1) * QUARTER)
        out = share_ref[s, :, :QUARTER].astype(F32)
        gate = share_ref[s, :, QUARTER : 2 * QUARTER].astype(F32)
        inner = share_ref[s, :, 2 * QUARTER : 3 * QUARTER].astype(F32)
        squares = squares + out * out + gate * gate + inner * inner
        products = products + gate * w_in_ref[0, :, at].astype(F32)
        products = products + inner * w_in_ref[1, :, at].astype(F32)
    state = share_ref[0, :, MAPS_AT : MAPS_AT + STATE].astype(F32)
    for s in range(1, BLOCKS):
        state = state + share_ref[s, :, MAPS_AT : MAPS_AT + STATE].astype(F32)
    step = step_ref[...]
    by_row = jnp.sum(products, axis=1, keepdims=True)
    by_row = by_row + jnp.sum(state * w_state_ref[...].astype(F32), axis=1, keepdims=True)
    square = jnp.sum(squares, axis=1, keepdims=True) + jnp.sum(state * state, axis=1, keepdims=True)
    lanes = lax.broadcasted_iota(jnp.int32, (rows, 128), 1)
    table = jnp.where(lanes == 0, by_row, jnp.where(lanes == 1, square, 0.0))
    table = jnp.concatenate([table, jnp.zeros((128 - rows, 128), F32)], axis=0).T
    total = jnp.sum(table[1:2], axis=1, keepdims=True)
    total = total + jnp.sum(jnp.sum(step * step, axis=0, keepdims=True), axis=1, keepdims=True)
    by_step = jnp.sum(step * w_step_ref[...].astype(F32), axis=0, keepdims=True)
    by_step = jnp.concatenate([by_step, jnp.zeros((1, 128 - rows), F32)], axis=1)
    at_row = lax.broadcasted_iota(jnp.int32, (8, 128), 0)
    at_lane = lax.broadcasted_iota(jnp.int32, (8, 128), 1)
    first = jnp.where((at_row == 0) & (at_lane == rows), total, table[0:8] + by_step)
    out_ref[...] = jnp.where(at_row == 0, first, 0.0)


def update_kernel(
    place_ref, factor_ref, share_ref, step_ref, w_in_ref, w_out_ref, w_state_ref,
    w_step_ref, m_in_ref, m_out_ref, m_state_ref, m_step_ref,
    new_in_ref, new_out_ref, new_state_ref, new_step_ref,
    next_in_ref, next_out_ref, next_state_ref, next_step_ref,
):
    factor = factor_ref[0, 0]

    def write(new_ref, next_ref, at, moment, grad, weight):
        new = 0.5 * moment + (0.5 * factor) * grad
        new_ref[at] = new
        next_ref[at] = (weight.astype(F32) - LEARN * new).astype(BF)

    for s in range(BLOCKS):
        lanes = slice(s * QUARTER, (s + 1) * QUARTER)
        gate = (0, slice(None), lanes)
        write(
            new_in_ref, next_in_ref, gate, m_in_ref[gate],
            share_ref[s, :, QUARTER : 2 * QUARTER].astype(F32), w_in_ref[gate],
        )
        inner = (1, slice(None), lanes)
        write(
            new_in_ref, next_in_ref, inner, m_in_ref[inner],
            share_ref[s, :, 2 * QUARTER : 3 * QUARTER].astype(F32), w_in_ref[inner],
        )
        out = (slice(None), lanes)
        write(
            new_out_ref, next_out_ref, out, m_out_ref[out],
            share_ref[s, :, :QUARTER].astype(F32), w_out_ref[out],
        )
    state = share_ref[0, :, MAPS_AT : MAPS_AT + STATE].astype(F32)
    for s in range(1, BLOCKS):
        state = state + share_ref[s, :, MAPS_AT : MAPS_AT + STATE].astype(F32)
    write(new_state_ref, next_state_ref, ..., m_state_ref[...], state, w_state_ref[...])
    write(new_step_ref, next_step_ref, ..., m_step_ref[...], step_ref[...], w_step_ref[...])


def owner_specs(rows):
    return [
        pl.BlockSpec((2, rows, BLOCKS * QUARTER), lambda i, place: (0, place[1], 0)),
        pl.BlockSpec((rows, STATE), lambda i, place: (place[1], place[0])),
    ]


def run_owner(kernel, name, place, operands, in_specs, outs):
    return pl.pallas_call(
        kernel,
        grid_spec=pltpu.PrefetchScalarGridSpec(
            num_scalar_prefetch=1, grid=(1,), in_specs=in_specs,
            out_specs=[spec for spec, _ in outs],
        ),
        out_shape=[shape for _, shape in outs],
        compiler_params=pltpu.CompilerParams(vmem_limit_bytes=VMEM_LIMIT),
        cost_estimate=pl.CostEstimate(flops=1024, bytes_accessed=1024, transcendentals=0),
        name=name,
    )(place, *operands)


def swap_cores(block):
    return lax.ppermute(block, "tensor", SWAP)


def over_x(block):
    return lax.ppermute(block, "seq", ROUTE_X)


def over_y(block):
    return lax.ppermute(block, "seq", ROUTE_Y)


def exchange(blocks):
    return lax.all_to_all(blocks, "seq", 0, 0, tiled=True)


def copies(piece):
    return jnp.broadcast_to(piece, (BLOCKS,) + piece.shape)


def add_low(a, b):
    return (a.astype(F32) + b.astype(F32)).astype(BF)


def scatter(blocks):
    return jnp.sum(exchange(blocks).astype(F32), axis=0)


def after(value, *others):
    return lax.optimization_barrier((value, others))[0]


def fast_body(
    inputs,
    segments,
    cotangent,
    prenorm,
    inproj,
    statproj,
    stepproj,
    outproj,
    convinner,
    convstate,
    headparam,
    gatenorm,
    prenorm_moment,
    inproj_moment,
    statproj_moment,
    stepproj_moment,
    outproj_moment,
    convinner_moment,
    convstate_moment,
    headparam_moment,
    gatenorm_moment,
):
    core = lax.axis_index("tensor")
    chip = lax.axis_index("seq")
    data_at = lax.axis_index("dp")
    dp_count = lax.axis_size("dp")
    heads_local = headparam.shape[1]
    rows_local = inproj.shape[1]
    shard = rows_local // BLOCKS
    half_d = D // 2
    place = jnp.stack([core, chip]).astype(jnp.int32)

    def by_core(first, second):
        return jnp.where(core == 0, first, second)

    def quarter(array, axis, width):
        return lax.dynamic_slice_in_dim(array, chip * width, width, axis)

    def all_rows(block):
        return lax.all_gather(block, "dp", axis=0, tiled=True)

    first_block = (
        jnp.concatenate(
            [
                quarter(inproj[1], 1, QUARTER),
                statproj,
                jnp.pad(quarter(stepproj, 1, QHEADS), ((0, 0), (0, 128 - QHEADS))),
            ],
            axis=1,
        )
    )
    inputs, first_block = after((inputs, first_block))
    w_first = all_rows(first_block)
    w_gate = all_rows(quarter(inproj[0], 1, QUARTER))
    w_out = all_rows(quarter(outproj, 0, QUARTER).T)

    def whole_rows(array):
        mine = lax.dynamic_index_in_dim(array, core, 1, keepdims=False)
        theirs = lax.dynamic_index_in_dim(array, 1 - core, 1, keepdims=False)
        got = swap_cores(theirs)
        return by_core(
            jnp.concatenate([mine, got], axis=2), jnp.concatenate([got, mine], axis=2)
        )

    rows_whole = whole_rows(inputs)
    normed_own = rms_scale(rows_whole.astype(F32), prenorm).astype(BF)
    cot_own = whole_rows(cotangent)
    first_copies, second_copies = after((copies(normed_own[0]), copies(normed_own[1])))
    own_0 = exchange(first_copies)

    seg_mine = jnp.concatenate(
        [
            lax.dynamic_index_in_dim(segments, core, 1),
            lax.dynamic_index_in_dim(segments, 1 - core, 1),
        ],
        axis=1,
    )
    seg_pad = jnp.pad(
        seg_mine.astype(F32), ((0, 0), (0, 0), (128, 128)), constant_values=-1.0
    )
    segs = jnp.broadcast_to(seg_pad[:, :, None], seg_pad.shape[:2] + (8, seg_pad.shape[2]))

    taps_inner = quarter(convinner, 1, QUARTER)
    taps = jnp.pad(jnp.concatenate([taps_inner, convstate], axis=1), ((0, 3), (0, 0)))
    head_own = quarter(headparam, 1, QHEADS)
    head = jnp.pad(
        jnp.stack([head_own[0], jnp.exp(head_own[1]), head_own[2]]),
        ((0, 5), (0, 128 - QHEADS)),
    )
    gain = quarter(gatenorm, 0, QUARTER)
    chan = jnp.pad(jnp.stack([gain, jnp.repeat(head_own[2], HEADDIM)]), ((0, 6), (0, 0)))

    def rows_dot_t(left, right):
        return lax.dot_general(left, right, (((3,), (1,)), ((), ())), preferred_element_type=F32)

    def core_sums(mine, theirs):
        return add_low(mine, swap_cores(theirs))

    def over_dp(parts):
        return lax.psum_scatter(parts, "dp", scatter_dimension=0, tiled=True)[0]

    def by_place(columns):
        blocks = columns.T.reshape(BLOCKS, shard, -1)
        return lax.all_to_all(blocks, "seq", 0, 0, tiled=True)

    def forward(m, place, tokens):
        return run_fwd(place, tokens, w_first, segs[m], taps, head, chan)

    def gate_forward(m, place):
        return run_gate(place, normed[m], cots[m], kept[m][3], w_gate, w_out, chan)

    def gate_backward(m, place, gate, d_gated, sums, seed):
        return run_gate_back(
            place, normed[m], cots[m], kept[m][3], gate, d_gated, sums, chan, seed, dp_count
        )

    def backward(m, place, dy, d_gate, seed):
        return run_bwd(
            place, normed[m], kept[m], dy, d_gate, segs[m], taps, head, chan,
            (w_first, w_gate), seed, dp_count,
        )

    def summed(blocks):
        return jnp.sum(blocks.astype(F32), axis=0)

    def in_order(block):
        return by_core(block, block[:, ::-1])

    def token_scale(sums):
        own = lax.dynamic_index_in_dim(sums, chip, 1, keepdims=False)
        return lax.rsqrt(own[:, 0] / INNER + EPS)[..., None]

    def sum_dp(value):
        hop = 1
        while hop < dp_count:
            value = value + lax.ppermute(value, "dp", [(i, i ^ hop) for i in range(dp_count)])
            hop *= 2
        return value

    def sum_seq(value):
        value = value + over_x(value)
        return value + over_y(value)

    def with_other(own):
        return own, swap_cores(own)

    stepproj_own = lax.dynamic_slice_in_dim(stepproj.T, chip * shard, shard, 1)
    outproj_own = lax.dynamic_slice_in_dim(outproj, chip * shard, shard, 1).T
    own_0, w_first, second_copies, cot_own, segs, taps, head, chan, stepproj_own, outproj_own = (
        after(
            (
                own_0, w_first, second_copies, cot_own, segs, taps, head, chan, stepproj_own,
                outproj_own,
            )
        )
    )
    own_1 = exchange(second_copies)
    normed = [with_other(own_0)]
    place, cot_copies = after((place, [copies(cot) for cot in (cot_own[0], cot_own[1])]))
    kept = [forward(0, place, normed[0])]

    own_1, w_gate, piece, place = after((own_1, w_gate, cot_copies[0], place), kept[0][1])
    normed.append(with_other(own_1))
    cot_0 = exchange(piece)
    kept.append(forward(1, place, normed[1]))

    cot_0, w_out, piece, place = after((cot_0, w_out, cot_copies[1], place), kept[1][1])
    cots = [with_other(cot_0)]
    cot_1 = exchange(piece)
    gate_0, d_gated_0, mine_0, theirs_0, stat_0 = gate_forward(0, place)

    cot_1, place, theirs_0 = after((cot_1, place, theirs_0), stat_0)
    cots.append(with_other(cot_1))
    branch_0 = core_sums(mine_0, after(theirs_0, cots[1][1]))
    gate_1, d_gated_1, mine_1, theirs_1, stat_1 = gate_forward(1, place)

    stats = jnp.stack([stat_0, after(stat_1, branch_0)])
    stats = stats + swap_cores(stats)[:, ::-1]
    theirs_1 = after(theirs_1, stats)
    sums_0, sums_1 = sum_seq(stats)
    branch_0 = after(branch_0, sums_0)
    layer_0 = exchange(branch_0)
    dy_0, d_gate_0, g_gain_0, g_mid_0 = gate_backward(0, place, gate_0, d_gated_0, sums_0, None)
    branch_1 = core_sums(mine_1, theirs_1)
    place = after(place, dy_0)
    dy_1, d_gate_1, g_gain_1, mid_parts = gate_backward(
        1, place, gate_1, d_gated_1, sums_1, g_mid_0
    )

    layer_0, branch_1, place, mid_parts = after((layer_0, branch_1, place, mid_parts), dy_1)
    layer_1 = exchange(branch_1)
    mid_rows = over_dp(mid_parts)
    g_late_0, slope_0, g_taps_0, g_head_0, mine, theirs = backward(0, place, dy_0, d_gate_0, None)

    layer_1, mid_rows, theirs, place = after((layer_1, mid_rows, theirs, place), g_taps_0)
    back_0 = core_sums(mine, theirs)
    layer_out = [
        summed(layer_0) * token_scale(sums_0), summed(layer_1) * token_scale(sums_1)
    ]
    layer_out = (inputs.astype(F32) + in_order(jnp.stack(layer_out))).astype(BF)
    back_0, place, layer_out = after((back_0, place, layer_out))
    token_0 = exchange(back_0)
    late_parts, keep_1, give_1, slope_1, g_taps_1, g_head_1, mine, theirs = backward(
        1, place, dy_1, d_gate_1, g_late_0
    )

    token_0, late_parts, theirs, give_1 = after((token_0, late_parts, theirs, give_1))
    late_rows = over_dp(late_parts)
    maps = core_sums(keep_1, give_1)
    back_1 = core_sums(mine, after(theirs, maps))
    maps = exchange(maps)
    maps, back_1, token_0, mid_rows, g_taps_1 = after(
        (maps, back_1, token_0, mid_rows, g_taps_1)
    )
    token_1 = exchange(back_1)
    taps_state = lax.dynamic_slice_in_dim(convstate, core * STATE, STATE, 1)
    d_maps, g_maps, g_state_taps = run_maps(
        place, token_0[:, :, SPAN:], maps, (slope_0, slope_1), (kept[0][0], kept[1][0]),
        segs, (*normed[0], *normed[1]), jnp.pad(taps_state, ((0, 3), (0, 0))), dp_count,
    )

    def for_dp(hop):
        at = lax.rem(data_at + hop, dp_count)
        return lax.dynamic_index_in_dim(g_maps, at, 0, keepdims=False)

    state_rows = for_dp(0).astype(F32)
    for hop in range(1, dp_count):
        route = [(i, (i + hop) % dp_count) for i in range(dp_count)]
        state_rows = state_rows + lax.ppermute(for_dp(hop), "dp", route).astype(F32)
    state_rows = state_rows.astype(BF)

    inner_local = BLOCKS * QUARTER

    def put(values, width, total):
        base = jnp.zeros(values.shape[:-1] + (total,), F32)
        return lax.dynamic_update_slice_in_dim(base, values, chip * width, values.ndim - 1)

    g_taps, g_head = g_taps_0 + g_taps_1, g_head_0 + g_head_1
    g_heads = jnp.concatenate(
        [g_head[:2, :QHEADS], jnp.sum(g_head[2].reshape(1, QHEADS, HEADDIM), axis=2)], axis=0
    )
    small_parts = [
        put(g_taps[: CONV + 1], QUARTER, inner_local),
        put(g_gain_0[0] + g_gain_1[0], QUARTER, inner_local),
        put(g_heads, QHEADS, heads_local),
        g_state_taps[: CONV + 1],
    ]
    small_shapes = [small.shape for small in small_parts]
    vector = jnp.concatenate([small.reshape(-1) for small in small_parts])
    vector = jnp.pad(vector, (0, -vector.size % 1024)).reshape(-1, 128)

    token_1, mid_rows, late_rows, state_rows = after(
        (token_1, mid_rows, late_rows, state_rows), vector
    )
    shares = jnp.concatenate(
        [mid_rows, late_rows[:QUARTER], state_rows, late_rows[QUARTER:]], axis=0
    )
    share = by_place(shares)
    d_tokens = [summed(token_0[:, :, :SPAN]), summed(token_1)]
    w_state = w_first[:, QUARTER : QUARTER + 2 * STATE]

    state_other = swap_cores(d_maps)[:, ::-1]
    state_mine = d_maps
    d_state_both = by_core(
        jnp.concatenate([state_mine, state_other], axis=3),
        jnp.concatenate([state_other, state_mine], axis=3),
    )
    from_state = rows_dot_t(
        d_state_both, lax.dynamic_slice_in_dim(w_state, core * half_d, half_d, 0)
    )

    outputs = layer_out
    d_normed = in_order(jnp.stack(d_tokens) + from_state)
    rows_own = inputs.astype(F32)
    gain_own = lax.dynamic_slice_in_dim(prenorm, core * half_d, half_d, 0)
    weighted = d_normed * gain_own
    pair_sums = jnp.stack(
        [jnp.sum(rows_own * rows_own, axis=-1), jnp.sum(weighted * rows_own, axis=-1)]
    )
    pair_sums = pair_sums + swap_cores(pair_sums)
    root = lax.rsqrt(pair_sums[0] / D + EPS)[..., None]
    input_grads = (
        cotangent.astype(F32)
        + weighted * root
        - rows_own * root * root * root * (pair_sums[1] / D)[..., None]
    ).astype(BF)

    step_at = MAPS_AT + STATE
    step_share = share[:, :, step_at : step_at + QHEADS].astype(F32)
    step_share = jnp.moveaxis(step_share, 1, 2).reshape(heads_local, shard)
    in_spec, state_spec = owner_specs(shard)

    def whole(array):
        return pl.BlockSpec(array.shape, lambda i, place: (0,) * array.ndim)

    def whole_out(shape, kind):
        spec = pl.BlockSpec(shape, lambda i, place: (0,) * len(shape))
        return spec, jax.ShapeDtypeStruct(shape, kind)

    owner_sums = run_owner(
        norm_kernel,
        "owner_norm",
        place,
        (share, inproj, statproj, stepproj_own, step_share),
        [whole(share), in_spec, state_spec, whole(stepproj_own), whole(step_share)],
        [whole_out((8, 128), F32)],
    )[0]
    owner_sums = owner_sums + swap_cores(owner_sums)

    owners = dp_count * BLOCKS
    owner = data_at * BLOCKS + chip
    gain_rows = lax.dynamic_slice_in_dim(prenorm, owner * shard, shard, 0)
    lanes = jnp.arange(128)
    g_prenorm = owner_sums[0] / jnp.pad(gain_rows, (0, 128 - shard), constant_values=1.0)
    g_prenorm = jnp.where(lanes < shard, g_prenorm, 0.0)
    square = owner_sums[0, shard] + jnp.sum(g_prenorm * g_prenorm)
    line = jnp.where(lanes == shard, square, g_prenorm)
    table = jnp.where(jnp.arange(owners)[:, None] == owner, line[None], 0.0)
    table = sum_seq(sum_dp(jnp.concatenate([table, vector], axis=0)))
    small_sums = []
    start = 0
    vector = table[owners:].reshape(-1)
    for shape in small_shapes:
        size = math.prod(shape)
        small_sums.append(vector[start : start + size].reshape(shape))
        start += size
    s_taps, s_gain, s_head, s_state_taps = small_sums

    small_sq = sum(jnp.sum(term * term) for term in small_sums)
    small_sq = small_sq + swap_cores(small_sq)
    grad_norm = jnp.sqrt(jnp.sum(table[:owners, shard]) + small_sq)
    s_prenorm = lax.dynamic_slice_in_dim(
        table[:owners, :shard], core * (owners // 2), owners // 2, 0
    ).reshape(half_d)

    entries = (
        2 * D * INNER
        + 2 * D * STATE
        + D * (INNER // HEADDIM)
        + INNER * D
        + (CONV + 1) * (INNER + 2 * STATE)
        + 3 * (INNER // HEADDIM)
        + INNER
        + D
    )
    limit = CLIP_RMS * math.sqrt(entries)
    factor = limit / jnp.maximum(grad_norm, limit)

    def moved(moment, grad):
        return 0.5 * moment + 0.5 * factor * grad

    def stepped(weight, moment):
        return (weight.astype(F32) - LEARN * moment).astype(weight.dtype)

    new_prenorm = moved(prenorm_moment, s_prenorm)
    moments = (inproj_moment, outproj_moment.T, statproj_moment, stepproj_moment.T)
    new_in, new_out, new_state, new_step, next_in, next_out, next_state, next_step = run_owner(
        update_kernel,
        "owner_update",
        place,
        (
            factor.reshape(1, 1), share, step_share,
            inproj, outproj_own, statproj, stepproj_own, *moments,
        ),
        [
            pl.BlockSpec(memory_space=pltpu.SMEM),
            whole(share), whole(step_share),
            in_spec, whole(outproj_own), state_spec, whole(stepproj_own),
            *[whole(moment) for moment in moments],
        ],
        [whole_out(moment.shape, kind) for kind in (F32, BF) for moment in moments],
    )
    new_taps = moved(convinner_moment, s_taps)
    new_state_taps = moved(convstate_moment, s_state_taps)
    new_head = moved(headparam_moment, s_head)
    new_gain = moved(gatenorm_moment, s_gain)
    return (
        outputs,
        input_grads,
        grad_norm,
        new_prenorm,
        new_in,
        new_state,
        new_step.T,
        new_out.T,
        new_taps,
        new_state_taps,
        new_head,
        new_gain,
        next_in,
        next_state,
        next_step.T,
        next_out.T,
        stepped(convinner, new_taps),
        stepped(lax.dynamic_slice_in_dim(convstate, core * STATE, STATE, 1), new_state_taps),
    )


def solution(mesh):
    fast = mesh.shape["seq"] == BLOCKS and mesh.shape["tensor"] == 2
    return jax.shard_map(
        fast_body if fast else general_body,
        mesh=mesh,
        in_specs=(
            P(None, "dp", "seq", "tensor"),
            P(None, "dp", None),
            P(None, "dp", "seq", "tensor"),
            P(),
            P(None, "dp", "tensor"),
            P("dp", None),
            P("dp", "tensor"),
            P("tensor", "dp"),
            P(None, "tensor"),
            P(),
            P(None, "tensor"),
            P("tensor"),
            P("tensor"),
            P(None, ("dp", "seq"), "tensor"),
            P(("dp", "seq"), "tensor"),
            P(("dp", "seq"), "tensor"),
            P("tensor", ("dp", "seq")),
            P(None, "tensor"),
            P(None, "tensor"),
            P(None, "tensor"),
            P("tensor"),
        ),
        out_specs=(
            P(None, "dp", "seq", "tensor"),
            P(None, "dp", "seq", "tensor"),
            P(),
            P("tensor"),
            P(None, ("dp", "seq"), "tensor"),
            P(("dp", "seq"), "tensor"),
            P(("dp", "seq"), "tensor"),
            P("tensor", ("dp", "seq")),
            P(None, "tensor"),
            P(None, "tensor"),
            P(None, "tensor"),
            P("tensor"),
            P(None, ("dp", "seq"), "tensor"),
            P(("dp", "seq"), "tensor"),
            P(("dp", "seq"), "tensor"),
            P("tensor", ("dp", "seq")),
            P(None, "tensor"),
            P(None, "tensor"),
        ),
        check_vma=False,
    )
```

```python
import functools
import math

import jax
import jax.numpy as jnp
from jax import lax
from jax.experimental import pallas as pl
from jax.experimental.pallas import tpu as pltpu
from jax.sharding import PartitionSpec as P

D = 1536
INNER = 3072
HEADDIM = 64
STATE = 128
CONV = 4
MB = 2


EPS = 1e-05
LEARN = 0.05
CLIP_RMS = 0.25
HIGH = lax.Precision.HIGHEST


def shifted(block, axis, distance):
    devices = range(lax.axis_size(axis))
    route = [(i - distance, i) for i in devices if i - distance in devices]
    return lax.ppermute(block, axis, route)


def prefix(array, axis, combine, identity):
    size, position = (lax.axis_size(axis), lax.axis_index(axis))
    everything = jax.tree.map(
        lambda part, kind: lax.all_gather(part.astype(kind), axis),
        array,
        (jnp.bfloat16, jnp.bfloat16),
    )
    start = jax.tree.map(
        lambda part, zero: jnp.broadcast_to(jnp.asarray(zero, part.dtype), part.shape),
        array,
        identity,
    )

    def prefix_step(k, before):
        reached = k < position
        new = combine(
            before, jax.tree.map(lambda part, own: part[k].astype(own.dtype), everything, array)
        )
        return jax.tree.map(lambda a, b: jnp.where(reached, a, b), new, before)

    return lax.fori_loop(0, size, prefix_step, start)


def entering_2(array, axis, combine, identity):
    size, position = (lax.axis_size(axis), lax.axis_index(axis))
    everything = jax.tree.map(lambda part: lax.all_gather(part, axis), array)
    start = jax.tree.map(
        lambda part, zero: jnp.broadcast_to(jnp.asarray(zero, part.dtype), part.shape),
        array,
        identity,
    )

    def entering_step(k, before):
        at = size - 1 - k
        reached = at > position
        new = combine(before, jax.tree.map(lambda part: part[at], everything))
        return jax.tree.map(lambda a, b: jnp.where(reached, a, b), new, before)

    return lax.fori_loop(0, size, entering_step, start)


def rms_scale(values, weight):
    return values * lax.rsqrt(jnp.mean(values * values, axis=-1, keepdims=True) + EPS) * weight


def conv_block(padded, seg_pad, kernel):
    length = padded.shape[0] - (CONV - 1)
    own_seg = seg_pad[CONV - 1 :]
    summed = jnp.broadcast_to(kernel[CONV], (length, kernel.shape[1]))
    for offset in range(CONV):
        window = padded[offset : offset + length]
        same_doc = (seg_pad[offset : offset + length] == own_seg)[:, None]
        summed = summed + kernel[offset] * jnp.where(same_doc, window, 0.0)
    return jax.nn.silu(summed)


def decay_table(cumulative, segids):
    row_count = segids.shape[0]
    places = jnp.arange(row_count)
    allowed = (segids[:, None] == segids[None, :]) & (places[:, None] >= places[None, :])
    allowed = allowed[:, :, None]
    gap_values = cumulative[:, None, :] - cumulative[None, :, :]
    return jnp.where(allowed, jnp.exp(jnp.where(allowed, gap_values, -60.0)), 0.0)


def head_rates(raw_step, params):
    step_sizes = jax.nn.softplus(raw_step + params[0])
    return (step_sizes, jnp.cumsum(-step_sizes * jnp.exp(params[1]), axis=0))


def mix_out(values, b_proj, c_proj, raw_step, params, segids, before, carry_in):
    step_sizes, cumulative = head_rates(raw_step, params)
    scores = jnp.dot(c_proj, b_proj.T, precision=HIGH)
    weights = scores[:, :, None] * decay_table(cumulative, segids) * step_sizes[None, :, :]
    result = jnp.einsum("tsh,shp->thp", weights, values, precision=HIGH)
    entering = jnp.where((segids == before)[:, None], jnp.exp(cumulative), 0.0)
    carried = jnp.einsum("tn,hpn->thp", c_proj, carry_in, precision=HIGH)
    return result + entering[:, :, None] * carried + params[2][None, :, None] * values


def mix_state(values, b_proj, raw_step, params, segids, before):
    step_sizes, cumulative = head_rates(raw_step, params)
    tail_weight = (
        jnp.where(
            (segids == segids[-1])[:, None], jnp.exp(cumulative[-1][None, :] - cumulative), 0.0
        )
        * step_sizes
    )
    summary = jnp.einsum("sh,shp,sn->hpn", tail_weight, values, b_proj, precision=HIGH)
    passing = jnp.where(segids[-1] == before, jnp.exp(cumulative[-1]), 0.0)
    return (summary, passing)


def chain(earlier, later):
    return (earlier[0] * later[0], later[0][..., None, None] * earlier[1] + later[1])


def add_tree(totals, terms):
    if totals is None:
        return terms
    return jax.tree.map(jnp.add, totals, terms)


def project(left_rows, matrix):
    return jnp.einsum("bld,dk->blk", left_rows, matrix, preferred_element_type=jnp.float32)


def weight_grad(left_rows, right_rows):
    return jnp.einsum("bld,blk->dk", left_rows, right_rows, preferred_element_type=jnp.float32)


def back_project(grad_rows, matrix):
    return jnp.einsum("blk,dk->bld", grad_rows, matrix, preferred_element_type=jnp.float32)


def general_body(
    inputs,
    segments,
    cotangent,
    prenorm,
    inproj,
    statproj,
    stepproj,
    outproj,
    convinner,
    convstate,
    headparam,
    gatenorm,
    prenorm_moment,
    inproj_moment,
    statproj_moment,
    stepproj_moment,
    outproj_moment,
    convinner_moment,
    convstate_moment,
    headparam_moment,
    gatenorm_moment,
):
    tensor_at = lax.axis_index("tensor")
    seq_at = lax.axis_index("seq")
    data_at = lax.axis_index("dp")
    tensor_count = lax.axis_size("tensor")
    batch_count = inputs.shape[1]
    span_len = inputs.shape[2]
    inner_local = convinner.shape[1]
    heads_local = headparam.shape[1]
    state_half = 2 * STATE // tensor_count
    model_half = D // tensor_count
    rows_full, grads_full = (
        lax.all_gather(inputs, "tensor", axis=3, tiled=True),
        lax.all_gather(cotangent, "tensor", axis=3, tiled=True),
    )
    seg_padded = jnp.pad(segments, ((0, 0), (0, 0), (CONV - 1, 0)), constant_values=-1)
    seg_local = lax.dynamic_slice_in_dim(seg_padded, seq_at * span_len, span_len + CONV - 1, 2)
    kernel = jnp.concatenate([convinner, convstate], axis=1)
    shares = None
    smalls = None
    outputs = []
    input_grads = []
    for batch in range(MB):
        inproj_all, statproj_all, stepproj_all, outproj_all = (
            lax.all_gather(inproj, "dp", axis=1, tiled=True),
            lax.all_gather(statproj, "dp", axis=0, tiled=True),
            lax.all_gather(stepproj, "dp", axis=0, tiled=True),
            lax.all_gather(outproj, "dp", axis=1, tiled=True),
        )
        rows = rows_full[batch].astype(jnp.float32)
        normed, norm_back = jax.vjp(rms_scale, rows, prenorm)
        normed_low = normed.astype(jnp.bfloat16)
        gate_pre = project(normed_low, inproj_all[0])
        inner_pre = project(normed_low, inproj_all[1])
        state_pre = project(normed_low, statproj_all)
        raw_step = project(normed_low, stepproj_all)
        mixed = jnp.concatenate([inner_pre, state_pre], axis=2).astype(jnp.bfloat16)
        edge_in = shifted(mixed[:, span_len - (CONV - 1) :, :], "seq", 1)
        padded = jnp.concatenate([edge_in, mixed], axis=1).astype(jnp.float32)
        seg_now = seg_local[batch]
        own_seg = seg_now[:, CONV - 1 :]
        before = seg_now[:, CONV - 2]
        conv_out, conv_back = jax.vjp(
            lambda pad_vals, kernel_in: jax.vmap(conv_block, in_axes=(0, 0, None))(
                pad_vals, seg_now, kernel_in
            ),
            padded,
            kernel,
        )
        values = conv_out[..., :inner_local].reshape(batch_count, span_len, heads_local, HEADDIM)
        b_proj = conv_out[..., inner_local : inner_local + STATE]
        c_proj = conv_out[..., inner_local + STATE :]
        (summary, passing), state_back = jax.vjp(
            lambda value_in, b_part, raw_part, param_in: jax.vmap(
                mix_state, in_axes=(0, 0, 0, None, 0, 0)
            )(value_in, b_part, raw_part, param_in, own_seg, before),
            values,
            b_proj,
            raw_step,
            headparam,
        )
        identity = (jnp.ones_like(passing), jnp.zeros_like(summary))
        _, carry_in = prefix((passing, summary), "seq", chain, identity)
        mixer, out_back = jax.vjp(
            lambda value_in, b_part, c_part, raw_part, param_in, state_in: jax.vmap(
                mix_out, in_axes=(0, 0, 0, 0, None, 0, 0, 0)
            )(value_in, b_part, c_part, raw_part, param_in, own_seg, before, state_in),
            values,
            b_proj,
            c_proj,
            raw_step,
            headparam,
            carry_in,
        )
        flat_mixer = mixer.reshape(batch_count, span_len, inner_local)
        gate_act = jax.nn.silu(gate_pre)
        gated_in = flat_mixer * gate_act
        total_sq = lax.psum(jnp.sum(gated_in * gated_in, axis=-1), "tensor")
        scale = lax.rsqrt(total_sq / INNER + EPS)[..., None]
        gated_low = (gated_in * scale * gatenorm).astype(jnp.bfloat16)
        branch_part = project(gated_low, outproj_all)
        branch_own = lax.psum_scatter(branch_part, "tensor", scatter_dimension=2, tiled=True)
        outputs.append((inputs[batch].astype(jnp.float32) + branch_own).astype(jnp.bfloat16))
        grad_rows = grads_full[batch]
        d_gated = back_project(grad_rows, outproj_all)
        g_outproj = jnp.einsum(
            "blk,bld->kd", gated_low, grad_rows, preferred_element_type=jnp.float32
        )
        g_gatenorm = jnp.sum(d_gated * gated_in * scale, axis=(0, 1))
        weighted = d_gated * gatenorm
        cross = lax.psum(jnp.sum(weighted * gated_in, axis=-1), "tensor")
        d_in = weighted * scale - gated_in * scale**3 * (cross / INNER)[..., None]
        d_mixer = d_in * gate_act
        sigma = jax.nn.sigmoid(gate_pre)
        d_gate = d_in * flat_mixer * sigma * (1.0 + gate_pre * (1.0 - sigma))
        d_values, d_bproj, d_cproj, d_raw, d_param, d_carry = out_back(
            d_mixer.reshape(batch_count, span_len, heads_local, HEADDIM)
        )
        _, d_after = entering_2((passing, d_carry), "seq", chain, identity)
        d_passing = jnp.sum(d_after * carry_in, axis=(2, 3))
        d_values_tail, d_bproj_tail, d_raw_tail, d_param_tail = state_back((d_after, d_passing))
        d_state = lax.psum(jnp.concatenate([d_bproj + d_bproj_tail, d_cproj], axis=2), "tensor")
        d_conv = jnp.concatenate(
            [(d_values + d_values_tail).reshape(batch_count, span_len, inner_local), d_state],
            axis=2,
        )
        d_padded, d_kernel = conv_back(d_conv)
        edge_back = shifted(d_padded[:, : CONV - 1, :].astype(jnp.bfloat16), "seq", -1).astype(
            jnp.float32
        )
        d_mixed = d_padded[:, CONV - 1 :, :] + jnp.pad(
            edge_back, ((0, 0), (span_len - (CONV - 1), 0), (0, 0))
        )
        d_mixed_low = d_mixed.astype(jnp.bfloat16)
        d_gate_low = d_gate.astype(jnp.bfloat16)
        d_raw_low = (d_raw + d_raw_tail).astype(jnp.bfloat16)
        d_inner_low = d_mixed_low[..., :inner_local]
        d_state_low = lax.dynamic_slice_in_dim(
            d_mixed_low[..., inner_local:], tensor_at * state_half, state_half, 2
        )
        statproj_own = lax.dynamic_slice_in_dim(statproj_all, tensor_at * state_half, state_half, 1)
        g_inproj = jnp.stack(
            [weight_grad(normed_low, d_gate_low), weight_grad(normed_low, d_inner_low)]
        )
        g_statproj = weight_grad(normed_low, d_state_low)
        g_stepproj = weight_grad(normed_low, d_raw_low)
        d_normed_part = (
            back_project(d_gate_low, inproj_all[0])
            + back_project(d_inner_low, inproj_all[1])
            + back_project(d_state_low, statproj_own)
            + back_project(d_raw_low, stepproj_all)
        )
        d_normed = lax.psum(d_normed_part, "tensor")
        d_rows, d_prenorm = norm_back(d_normed)
        own_rows = lax.dynamic_slice_in_dim(d_rows, tensor_at * model_half, model_half, 2)
        input_grads.append((own_rows + cotangent[batch].astype(jnp.float32)).astype(jnp.bfloat16))
        big_terms = (g_inproj, g_outproj, g_statproj, g_stepproj)
        small_terms = (
            lax.dynamic_slice_in_dim(d_prenorm, tensor_at * model_half, model_half, 0),
            d_kernel[:, :inner_local],
            lax.dynamic_slice_in_dim(
                d_kernel[:, inner_local:], tensor_at * state_half, state_half, 1
            ),
            d_param + d_param_tail,
            g_gatenorm,
        )
        shares = add_tree(
            shares,
            (
                lax.psum_scatter(big_terms[0], ("dp", "seq"), scatter_dimension=1, tiled=True),
                lax.psum_scatter(big_terms[1], ("dp", "seq"), scatter_dimension=1, tiled=True),
                lax.psum_scatter(big_terms[2], ("dp", "seq"), scatter_dimension=0, tiled=True),
                lax.psum_scatter(big_terms[3], ("dp", "seq"), scatter_dimension=0, tiled=True),
            ),
        )
        smalls = add_tree(
            smalls,
            lax.psum(
                (small_terms[0], small_terms[1], small_terms[2], small_terms[3], small_terms[4]),
                ("dp", "seq"),
            ),
        )
    big_sq = jnp.sum(jnp.stack([jnp.sum(term * term) for term in shares]))
    small_sq = jnp.sum(jnp.stack([jnp.sum(term * term) for term in smalls]))
    first_owner = jnp.where((data_at == 0) & (seq_at == 0), 1.0, 0.0)
    norm_sq = lax.psum(big_sq + first_owner * small_sq, ("dp", "seq", "tensor"))
    grad_norm = jnp.sqrt(norm_sq)
    heads_all = INNER // HEADDIM
    entries = (
        2 * D * INNER
        + 2 * D * STATE
        + D * heads_all
        + INNER * D
        + (CONV + 1) * (INNER + 2 * STATE)
        + 3 * heads_all
        + INNER
        + D
    )
    limit = CLIP_RMS * math.sqrt(entries)
    factor = limit / jnp.maximum(grad_norm, limit)
    shard_rows = shares[0].shape[1]
    row_start = seq_at * shard_rows
    big_current = (
        lax.dynamic_slice_in_dim(inproj, row_start, shard_rows, 1),
        lax.dynamic_slice_in_dim(outproj, row_start, shard_rows, 1),
        lax.dynamic_slice_in_dim(
            lax.dynamic_slice_in_dim(statproj, row_start, shard_rows, 0),
            tensor_at * state_half,
            state_half,
            1,
        ),
        lax.dynamic_slice_in_dim(stepproj, row_start, shard_rows, 0),
    )
    conv_current = (
        convinner,
        lax.dynamic_slice_in_dim(convstate, tensor_at * state_half, state_half, 1),
    )
    big_moments = (inproj_moment, outproj_moment, statproj_moment, stepproj_moment)
    small_moments = (
        prenorm_moment,
        convinner_moment,
        convstate_moment,
        headparam_moment,
        gatenorm_moment,
    )
    big_new_moments = [
        0.5 * moment_item + 0.5 * factor * grad_item
        for moment_item, grad_item in zip(big_moments, shares)
    ]
    small_new_moments = [
        0.5 * moment_item + 0.5 * factor * grad_item
        for moment_item, grad_item in zip(small_moments, smalls)
    ]
    big_new = [
        (weight_item.astype(jnp.float32) - LEARN * moment_item).astype(weight_item.dtype)
        for weight_item, moment_item in zip(big_current, big_new_moments)
    ]
    conv_new = [
        (weight_item - LEARN * moment_item).astype(weight_item.dtype)
        for weight_item, moment_item in zip(conv_current, small_new_moments[1:3])
    ]
    return (
        jnp.stack(outputs),
        jnp.stack(input_grads),
        grad_norm,
        small_new_moments[0],
        big_new_moments[0],
        big_new_moments[2],
        big_new_moments[3],
        big_new_moments[1],
        small_new_moments[1],
        small_new_moments[2],
        small_new_moments[3],
        small_new_moments[4],
        big_new[0],
        big_new[2],
        big_new[3],
        big_new[1],
        conv_new[0],
        conv_new[1],
    )


BLOCKS = 4
SPAN = 256
PART = 128
PARTS = SPAN // PART
PACKED = 48
LOG2E = 1.4426950408889634
QUARTER = 384
QHEADS = 6
MAPS_AT = 3 * QUARTER
BF = jnp.bfloat16
F32 = jnp.float32
ROUTE_X = [(i, i ^ 1) for i in range(BLOCKS)]
ROUTE_Y = [(i, i ^ 2) for i in range(BLOCKS)]
SWAP = [(0, 1), (1, 0)]
VMEM_LIMIT = 56 * 1024 * 1024


def dot_nn(a, b):
    return lax.dot_general(a, b, (((1,), (0,)), ((), ())), preferred_element_type=F32)


def dot_nt(a, b):
    return lax.dot_general(a, b, (((1,), (1,)), ((), ())), preferred_element_type=F32)


def dot_tn(a, b):
    return lax.dot_general(a, b, (((0,), (0,)), ((), ())), preferred_element_type=F32)


def dot_exact(a, b):
    return lax.dot_general(
        a, b, (((1,), (0,)), ((), ())), precision=HIGH, preferred_element_type=F32
    )


def sigmoid(v):
    return 1.0 / (1.0 + jnp.exp(-v))


def split_sum(triangle, table):
    first = table.astype(BF)
    rest = table - first.astype(F32)
    second = rest.astype(BF)
    third = (rest - second.astype(F32)).astype(BF)
    parts = (
        first.astype(F32)
        + pltpu.roll(second.astype(F32), 8, 1)
        + pltpu.roll(third.astype(F32), 16, 1)
    )
    sums = dot_nn(triangle, parts.astype(BF))
    sums = sums + pltpu.roll(sums, 120, 1) + pltpu.roll(sums, 112, 1)
    lanes = lax.broadcasted_iota(jnp.int32, sums.shape, 1)
    return jnp.where(lanes < 8, sums, 0.0)


def head_sums(table, gather):
    first = table.astype(BF)
    second = (table - first.astype(F32)).astype(BF)
    return dot_nn(first, gather) + dot_nn(second, gather)


def head_spread():
    lane = lax.broadcasted_iota(jnp.int32, (128, QUARTER), 0)
    chan = lax.broadcasted_iota(jnp.int32, (128, QUARTER), 1)
    base = jnp.where(lane < 8, lane, jnp.where(lane < 16, lane - 8, -1)) * HEADDIM
    return jnp.where((chan >= base) & (chan < base + HEADDIM) & (base >= 0), 1.0, 0.0).astype(BF)


def spread_heads(tables, spread):
    packed = []
    for table in tables:
        lanes = lax.broadcasted_iota(jnp.int32, table.shape, 1)
        table = jnp.where(lanes < 8, table, 0.0)
        first = table.astype(BF).astype(F32)
        packed.append((first + pltpu.roll(table - first, 8, 1)).astype(BF))
    wide = dot_nn(jnp.concatenate(packed, axis=0), spread)
    return [wide[PART * k : PART * (k + 1)] for k in range(len(tables))]


def rates(raw, head):
    shifted_raw = raw + head[0:1]
    step = jnp.maximum(shifted_raw, 0.0) + jnp.log1p(jnp.exp(-jnp.abs(shifted_raw)))
    lanes = lax.broadcasted_iota(jnp.int32, raw.shape, 1)
    return shifted_raw, jnp.where(lanes < QHEADS, step, 0.0)


def triangle(keep):
    rows_at = lax.broadcasted_iota(jnp.int32, (PART, PART), 0)
    cols_at = lax.broadcasted_iota(jnp.int32, (PART, PART), 1)
    return jnp.where(keep(rows_at, cols_at), 1.0, 0.0).astype(BF)


def part_terms(step, head, cols, segr, lower):
    cum = split_sum(lower, -step * head[1:2]) * LOG2E
    last = cum[PART - 1 : PART]
    enter = jnp.exp2(cum) * cols[:, 4:5]
    leave = jnp.exp2(last - cum) * cols[:, 5:6]
    passing = jnp.exp2(last) * cols[PART - 1 : PART, 4:5]
    rows_at = lax.broadcasted_iota(jnp.int32, (PART, PART), 0)
    cols_at = lax.broadcasted_iota(jnp.int32, (PART, PART), 1)
    allowed = (rows_at >= cols_at) & (cols[:, 6:7] == segr)
    return cum, enter, leave, passing, jnp.where(allowed, 0.0, -1e30)


def head_decay(cum, cum_t, h, block_out):
    return jnp.exp2(cum[:, h : h + 1] - cum_t[h : h + 1] + block_out)


def by_head(table, low_half):
    zero = jnp.zeros_like(table)
    return jnp.concatenate(
        [jnp.where(low_half, table, zero), jnp.where(low_half, zero, table)], axis=0
    )


def pass_state(passing, state, added):
    heads = [slice(HEADDIM * h, HEADDIM * (h + 1)) for h in range(QHEADS)]
    return jnp.concatenate(
        [passing[:, h : h + 1] * state[at] + added[at] for h, at in enumerate(heads)], axis=0
    )


def segment_flags(seg_ref, q, block):
    begin = pl.multiple_of(block * SPAN, 128)
    around = seg_ref[q, :, pl.ds(begin, SPAN + 256)]
    here = around[:, 128 : 128 + SPAN]
    flags = []
    for shift in (3, 2, 1, 0):
        flags.append(pltpu.roll(around, shift, 1)[:, 128 : 128 + SPAN] == here)
    ends = [around[:, PART * k + 127 : PART * k + 128] for k in range(PARTS + 1)]
    parts = [here[:, PART * k : PART * (k + 1)] for k in range(PARTS)]
    flags.append(jnp.concatenate([parts[k] == ends[k] for k in range(PARTS)], axis=1))
    flags.append(jnp.concatenate([parts[k] == ends[k + 1] for k in range(PARTS)], axis=1))
    for shift in (3, 2, 1, 0):
        later = pltpu.roll(around, SPAN + 256 - shift, 1) if shift else around
        flags.append(later[:, 128 : 128 + SPAN] == here)
    flags = [jnp.where(flag, 1.0, 0.0) for flag in flags]
    at = lax.broadcasted_iota(jnp.int32, (8, SPAN), 0)
    first = here
    for row in range(6):
        first = jnp.where(at == row, flags[row], first)
    second = flags[9]
    for row in range(3):
        second = jnp.where(at == row, flags[6 + row], second)
    return jnp.concatenate([first, second], axis=0)


def to_columns(rows):
    filled = jnp.concatenate([rows, jnp.zeros((128 - rows.shape[0], SPAN), F32)], axis=0)
    return filled.T


def both_tokens(own_ref, other_ref):
    return jnp.concatenate([own_ref[0], other_ref[0]], axis=0)


def fwd_pieces(place_ref, *refs):
    own_out, other_out, held, sems = refs[20:24]
    tokens = block_rows(refs[:10], place_ref, held, sems)
    own_out[0] = tokens[:SPAN]
    other_out[0] = tokens[SPAN:]
    fwd_step(tokens, *refs[10:20], *refs[24:])


def fwd_blocks(place_ref, own_ref, other_ref, *refs):
    fwd_step(both_tokens(own_ref, other_ref), *refs)


def fwd_step(
    tokens, w_ref, seg_ref, taps_ref, head_ref, chan_ref,
    mixed_ref, raw_ref, pre_ref, y_ref, hin_ref, *more,
):
    buf, state = more[-2:]
    block = pl.program_id(0)

    @pl.when(block == 0)
    def _():
        buf[:, 0:8] = jnp.zeros((2, 8, buf.shape[2]), F32)
        state[...] = jnp.zeros_like(state)

    width = QUARTER + 2 * STATE
    projected = dot_nn(tokens, w_ref[...])
    taps = taps_ref[...]
    head = head_ref[...]
    skip = chan_ref[1:2]
    lower = triangle(lambda r, c: r >= c)
    spread = head_spread()
    low_half = lax.broadcasted_iota(jnp.int32, (PART, 128), 1) < HEADDIM
    pieces = []
    for q in range(2):
        rows_q = slice(q * SPAN, (q + 1) * SPAN)
        raw = projected[rows_q, width:]
        raw_ref[q, 0] = raw
        mixed_low = projected[rows_q, :width].astype(BF)
        mixed_ref[q, 0] = mixed_low
        mixed = mixed_low.astype(F32)
        buf[q, 8 : 8 + SPAN] = mixed
        rows = segment_flags(seg_ref, q, block)
        cols_all = to_columns(rows)
        pre = jnp.broadcast_to(taps[CONV : CONV + 1], mixed.shape)
        for j in range(CONV):
            window = mixed if j == CONV - 1 else buf[q, 5 + j : 5 + j + SPAN]
            pre = pre + taps[j : j + 1] * (window * cols_all[:, j : j + 1])
        buf[q, 0:8] = mixed[SPAN - 8 :]
        pre_ref[q, 0] = pre
        act = pre * sigmoid(pre)
        _, step_all = rates(raw, head)
        for part in range(PARTS):
            at_rows = slice(part * PART, (part + 1) * PART)
            cols = cols_all[at_rows]
            cum, enter, leave, passing, block_out = part_terms(
                step_all[at_rows], head, cols, rows[6:7, at_rows], lower
            )
            pieces.append(
                (q, part, act[at_rows], step_all[at_rows], cum, enter, leave, passing, block_out)
            )
    work = []
    for q, part, act, step, cum, enter, leave, passing, block_out in pieces:
        values = act[:, :QUARTER]
        b_low = act[:, QUARTER : QUARTER + STATE].astype(BF)
        c_low = act[:, QUARTER + STATE :].astype(BF)
        step_w, enter_w, leave_w = spread_heads((step, enter, leave), spread)
        cum_t = cum.T
        scores = dot_nt(c_low, b_low)
        scaled = (step_w * values).astype(BF)
        tail = (leave_w * scaled.astype(F32)).astype(BF)
        added = dot_tn(tail, b_low)
        own = []
        for k in range(QHEADS // 2):
            at = slice(128 * k, 128 * (k + 1))
            weights = [
                (scores * head_decay(cum, cum_t, h, block_out)).astype(BF)
                for h in (2 * k, 2 * k + 1)
            ]
            own.append(dot_nn(jnp.concatenate(weights, axis=1), by_head(scaled[:, at], low_half)))
        own = jnp.concatenate(own, axis=1) + skip * values
        work.append((q, part, c_low, enter_w, passing, added, own))
    for q, part, c_low, enter_w, passing, added, own in sorted(work, key=lambda item: item[1]):
        held_f = state[q]
        held = held_f.astype(BF)
        hin_ref[q, 0, QUARTER * part : QUARTER * (part + 1)] = held
        y_ref[q, 0, part * PART : (part + 1) * PART] = own + enter_w * dot_nt(c_low, held)
        state[q] = pass_state(passing, held_f, added)


def piece_copies(refs, m, slot, held, sems):
    half = SPAN // 2
    for q in range(2):
        own, by_x, by_y, far_a, far_b = refs[5 * q : 5 * (q + 1)]
        if slot < 3:
            at = pl.ds(q * SPAN, SPAN)
            source = (own, by_x, by_y)[slot]
            source = source if m is None else source.at[m]
            yield pltpu.make_async_copy(source, held.at[slot, at], sems.at[slot, q, 0])
        else:
            for part, source in enumerate((far_a, far_b)):
                at = pl.ds(q * SPAN + part * half, half)
                yield pltpu.make_async_copy(source, held.at[slot, at], sems.at[slot, q, part])


def start_pieces(refs, m, held, sems):
    @pl.when(pl.program_id(0) == 0)
    def _():
        for slot in range(BLOCKS):
            for copy in piece_copies(refs, m, slot, held, sems):
                copy.start()


def slot_rows(refs, m, held, sems):
    start_pieces(refs, m, held, sems)
    for slot in range(BLOCKS):
        @pl.when(pl.program_id(0) == slot)
        def _():
            for copy in piece_copies(refs, m, slot, held, sems):
                copy.wait()

    return held[pl.program_id(0)]


def block_rows(refs, place_ref, held, sems):
    start_pieces(refs, None, held, sems)

    @pl.when(pl.program_id(0) == 0)
    def _():
        for slot in range(BLOCKS):
            for copy in piece_copies(refs, None, slot, held, sems):
                copy.wait()

    return held[pl.program_id(0) ^ place_ref[1]]


def cot_scratch():
    return [pltpu.VMEM((BLOCKS, 2 * SPAN, D), BF), pltpu.SemaphoreType.DMA((BLOCKS, 2, 2))]


def core_rows(place_ref):
    half = D // 2
    core = place_ref[0]
    own = pl.multiple_of(core * half, half)
    other = pl.multiple_of((1 - core) * half, half)
    return pl.ds(own, half), pl.ds(other, half)


def gate_kernel(m, place_ref, own_ref, other_ref, *refs):
    cots = refs[:10]
    (y_ref, w_gate_ref, w_out_ref, chan_ref, gate_ref, d_gated_ref, mine_ref, theirs_ref,
     stat_ref, held, sems) = refs[10:]
    gate = dot_nn(both_tokens(own_ref, other_ref), w_gate_ref[...])
    d_gated = dot_nn(slot_rows(cots, m, held, sems), w_out_ref[...])
    guns = []
    for q in range(2):
        at = slice(q * SPAN, (q + 1) * SPAN)
        gate_q = gate[at]
        gate_ref[q, 0] = gate_q
        d_gated_ref[q, 0] = d_gated[at]
        gated_in = y_ref[q, 0] * (gate_q * sigmoid(gate_q))
        weighted = gated_in * chan_ref[0:1]
        guns.append(weighted.astype(BF))
        square = jnp.sum(gated_in * gated_in, axis=1, keepdims=True)
        cross = jnp.sum(d_gated[at] * weighted, axis=1, keepdims=True)
        lanes = lax.broadcasted_iota(jnp.int32, (SPAN, 128), 1)
        table = jnp.where(lanes == 0, square, jnp.where(lanes == 1, cross, 0.0))
        stat_ref[q, 0] = table.T[0:2]
    gun = jnp.concatenate(guns, axis=0)
    own, other = core_rows(place_ref)
    mine = dot_nt(gun, w_out_ref[own]).astype(BF)
    theirs = dot_nt(gun, w_out_ref[other]).astype(BF)
    for q in range(2):
        mine_ref[0, q] = mine[q * SPAN : (q + 1) * SPAN]
        theirs_ref[0, 1 - q] = theirs[q * SPAN : (q + 1) * SPAN]


def start_sums(total, seed_ref):
    @pl.when(pl.program_id(0) == 0)
    def _():
        total[...] = jnp.zeros_like(total) if seed_ref is None else seed_ref[...]


def finish_sums(total, out_ref):
    @pl.when(pl.program_id(0) == BLOCKS - 1)
    def _():
        rows_of = out_ref.shape[2]
        for z in range(out_ref.shape[0]):
            out_ref[z] = total[:, z * rows_of : (z + 1) * rows_of].astype(BF)


def gate_back_first(*refs):
    gate_back_step(0, refs, None, *refs[18:])


def gate_back_last(*refs):
    dy_ref, d_gate_ref, g_gain_ref, parts_ref, held, sems, total = refs[19:]
    gate_back_step(1, refs, refs[18], dy_ref, d_gate_ref, g_gain_ref, total, held, sems)
    finish_sums(total, parts_ref)


def gate_back_step(m, refs, seed_ref, dy_ref, d_gate_ref, g_gain_ref, g_ref, held, sems):
    own_ref, other_ref = refs[1:3]
    cots = refs[3:13]
    y_ref, gate_ref, d_gated_ref, stat_ref, chan_ref = refs[13:18]
    start_sums(g_ref, seed_ref)
    start_sums(g_gain_ref, None)
    cot = slot_rows(cots, m, held, sems)
    gateds = []
    d_gates = []
    for q in range(2):
        stat = to_columns(stat_ref[q, 0])
        scale = lax.rsqrt(stat[:, 0:1] * (1.0 / INNER) + EPS)
        pull = stat[:, 1:2] * (1.0 / INNER) * scale * scale * scale
        gate = gate_ref[q, 0]
        y = y_ref[q, 0]
        d_gated = d_gated_ref[q, 0]
        sigma = sigmoid(gate)
        gate_act = gate * sigma
        gated_in = y * gate_act
        scaled_gain = chan_ref[0:1] * scale
        d_in = d_gated * scaled_gain - gated_in * pull
        dy_ref[q, 0] = (d_in * gate_act).astype(BF)
        d_gate = (d_in * y * (sigma + gate_act * (1.0 - sigma))).astype(BF)
        d_gate_ref[q, 0] = d_gate
        d_gates.append(d_gate)
        gateds.append((gated_in * scaled_gain).astype(BF))
        g_gain_ref[0:1] += jnp.sum(d_gated * gated_in * scale, axis=0, keepdims=True)
    gated = jnp.concatenate(gateds, axis=0)
    d_gate = jnp.concatenate(d_gates, axis=0)
    g_ref[:QUARTER] += dot_tn(gated, cot)
    g_ref[QUARTER:] += dot_tn(d_gate, both_tokens(own_ref, other_ref))


def bwd_first(*refs):
    bwd_step(*refs[:16], None, refs[16], None, None, *refs[17:])


def bwd_last(*refs):
    total = refs[-1]
    bwd_step(*refs[:17], total, *refs[18:-1])
    finish_sums(total, refs[17])


def bwd_step(
    place_ref, own_ref, other_ref, mixed_ref, pre_ref, raw_ref, y_ref, hin_ref, dy_ref,
    d_gate_ref, seg_ref, taps_ref, head_ref, chan_ref, w_ref, w_gate_ref,
    seed_ref,
    g_ref, keep_ref, give_ref, slope_ref, gtap_ref, ghead_ref, mine_ref, theirs_ref,
    buf, d_state, bc_edge, slope_edge, d_late,
):
    start_sums(g_ref, seed_ref)
    block = BLOCKS - 1 - pl.program_id(0)

    @pl.when(pl.program_id(0) == 0)
    def _():
        buf[:, SPAN:] = jnp.zeros((2, 8, QUARTER), F32)
        d_state[...] = jnp.zeros_like(d_state)
        bc_edge[...] = jnp.zeros_like(bc_edge)
        slope_edge[...] = jnp.zeros_like(slope_edge)
        gtap_ref[...] = jnp.zeros_like(gtap_ref)
        ghead_ref[...] = jnp.zeros_like(ghead_ref)

    head = head_ref[...]
    taps = taps_ref[...]
    skip = chan_ref[1:2]
    first_core = place_ref[0] == 0
    low_half = lax.broadcasted_iota(jnp.int32, (PART, 128), 1) < HEADDIM
    chan_at = lax.broadcasted_iota(jnp.int32, (QUARTER, 128), 0)
    head_at = lax.broadcasted_iota(jnp.int32, (QUARTER, 128), 1)
    gather = jnp.where(
        (chan_at >= head_at * HEADDIM) & (chan_at < (head_at + 1) * HEADDIM), 1.0, 0.0
    )
    gather_low = gather.astype(BF)
    lower = triangle(lambda r, c: r >= c)
    upper = triangle(lambda r, c: r <= c)
    spread = head_spread()

    def store(ref, q, first_row, rows):
        if keep_ref is not None:
            ref[0, q, first_row : first_row + rows.shape[0]] = rows
            return
        for at in range(first_row, first_row + rows.shape[0], 16):
            group = at // PACKED
            row = SPAN + at % PACKED
            ref[0, q, row : row + 16, 128 * group : 128 * (group + 1)] = rows[
                at - first_row : at - first_row + 16
            ]

    keep_at = mine_ref if keep_ref is None else keep_ref
    give_at = theirs_ref if give_ref is None else give_ref
    pieces = []
    columns = []
    slopes = []
    for q in range(2):
        rows = segment_flags(seg_ref, q, block)
        cols_all = to_columns(rows)
        columns.append(cols_all)
        pre = pre_ref[q, 0]
        sigma = sigmoid(pre)
        act = pre * sigma
        slope = sigma * (1.0 + pre * (1.0 - sigma))
        slopes.append(slope)
        slope_half = jnp.where(
            first_core, slope[:, QUARTER : QUARTER + STATE], slope[:, QUARTER + STATE :]
        )
        slope_ref[q, 0, 0:SPAN] = slope_half
        slope_ref[q, 0, SPAN : SPAN + 16] = slope_edge[q]
        slope_edge[q] = slope_half[0:16]
        if keep_ref is None:
            for ref in (mine_ref, theirs_ref):
                ref[0, q, SPAN + 32 :, 640:] = jnp.zeros((16, 128), BF)
        store(keep_at, q, SPAN, bc_edge[q, :, :STATE].astype(BF))
        store(give_at, 1 - q, SPAN, bc_edge[q, :, STATE:].astype(BF))
        shifted_all, step_all = rates(raw_ref[q, 0], head)
        for part in range(PARTS):
            at_rows = slice(part * PART, (part + 1) * PART)
            terms = part_terms(
                step_all[at_rows], head, cols_all[at_rows], rows[6:7, at_rows], lower
            )
            pieces.append((q, part, act[at_rows], shifted_all[at_rows], step_all[at_rows], terms))
    work = []
    for q, part, act, shifted_raw, step, terms in pieces:
        cum, enter, leave, passing, block_out = terms
        values = act[:, :QUARTER]
        b_low = act[:, QUARTER : QUARTER + STATE].astype(BF)
        c_low = act[:, QUARTER + STATE :].astype(BF)
        step_w, enter_w, leave_w = spread_heads((step, enter, leave), spread)
        cum_t = cum.T
        scores = dot_nt(c_low, b_low)
        dy_low = dy_ref[q, 0, part * PART : (part + 1) * PART]
        scaled = (step_w * values).astype(BF)
        tail = (leave_w * scaled.astype(F32)).astype(BF)
        enter_dy = (enter_w * dy_low.astype(F32)).astype(BF)
        d_scores = jnp.zeros((PART, PART), F32)
        own = []
        for k in range(QHEADS // 2):
            at = slice(128 * k, 128 * (k + 1))
            dy_both = by_head(dy_low[:, at], low_half)
            d_weights = dot_nt(dy_both, scaled[:, at])
            weights = []
            for half, h in enumerate((2 * k, 2 * k + 1)):
                decay = head_decay(cum, cum_t, h, block_out)
                weights.append((scores * decay).astype(BF))
                d_scores = d_scores + d_weights[half * PART : (half + 1) * PART] * decay
            own.append(dot_tn(jnp.concatenate(weights, axis=0), dy_both))
        own = jnp.concatenate(own, axis=1)
        d_scores = d_scores.astype(BF)
        new_state = dot_tn(enter_dy, c_low)
        d_c = dot_nn(d_scores, b_low)
        d_b = dot_tn(d_scores, c_low)
        work.append(
            (q, part, values, b_low, shifted_raw, step, step_w, leave_w, passing, dy_low, scaled,
             tail, enter_dy, own, new_state, d_b, d_c)
        )
    for item in sorted(work, key=lambda item: -item[1]):
        (q, part, values, b_low, shifted_raw, step, step_w, leave_w, passing, dy_low, scaled,
         tail, enter_dy, own, new_state, d_b, d_c) = item
        at_rows = slice(part * PART, (part + 1) * PART)
        held = hin_ref[q, 0, QUARTER * part : QUARTER * (part + 1)]
        dy = dy_low.astype(F32)
        scaled_f = scaled.astype(F32)
        d_after = d_state[q]
        d_after_low = d_after.astype(BF)
        tail_part = leave_w * dot_nt(b_low, d_after_low)
        d_scaled = own + tail_part
        d_c = d_c + dot_nn(enter_dy, held)
        d_b = d_b + dot_nn(tail, d_after_low)
        d_state[q] = pass_state(passing, d_after, new_state)
        kept_half = jnp.where(first_core, d_b, d_c)
        given_half = jnp.where(first_core, d_c, d_b)
        store(keep_at, q, part * PART, kept_half.astype(BF))
        store(give_at, 1 - q, part * PART, given_half.astype(BF))
        if part == 0:
            bc_edge[q, :, :STATE] = kept_half[0:16]
            bc_edge[q, :, STATE:] = given_half[0:16]
        d_values = step_w * d_scaled + skip * dy
        buf[q, at_rows] = d_values * slopes[q][at_rows, :QUARTER]
        by_values = dot_nn((values * d_scaled).astype(BF), gather_low)
        y_part = y_ref[q, 0, at_rows] - skip * values
        d_cum = head_sums(dy * y_part - scaled_f * d_scaled, gather_low)
        tail_row = jnp.sum(scaled_f * tail_part, axis=0, keepdims=True)
        tail_sum = dot_exact(jnp.broadcast_to(tail_row, (8, QUARTER)), gather)[0:1]
        state_dot = jnp.sum(d_after * held.astype(F32), axis=1, keepdims=True)
        state_terms = jnp.sum(state_dot * gather, axis=0, keepdims=True)
        d_rate = split_sum(upper, d_cum) + tail_sum + passing * state_terms
        d_raw = (by_values - head[1:2] * d_rate) * sigmoid(shifted_raw)
        ghead_ref[0:1, :128] += jnp.sum(d_raw, axis=0, keepdims=True)
        ghead_ref[1:2, :128] += jnp.sum(-step * head[1:2] * d_rate, axis=0, keepdims=True)
        ghead_ref[2:3] += jnp.sum(values * dy, axis=0, keepdims=True)
        d_late[q * SPAN + part * PART : q * SPAN + (part + 1) * PART, QUARTER:] = d_raw.astype(BF)
    for q in range(2):
        mixed = mixed_ref[q, 0, :, :QUARTER].astype(F32)
        d_mixed = jnp.zeros((SPAN, QUARTER), F32)
        for j in range(CONV):
            ahead = CONV - 1 - j
            window = buf[q, ahead : ahead + SPAN] * columns[q][:, 8 + j : 9 + j]
            d_mixed = d_mixed + taps[j : j + 1, :QUARTER] * window
            gtap_ref[j : j + 1] += jnp.sum(mixed * window, axis=0, keepdims=True)
        gtap_ref[CONV : CONV + 1] += jnp.sum(buf[q, 0:SPAN], axis=0, keepdims=True)
        buf[q, SPAN:] = buf[q, 0:8]
        d_late[q * SPAN : (q + 1) * SPAN, :QUARTER] = d_mixed.astype(BF)
    late = d_late[...]
    g_ref[...] += dot_tn(late, both_tokens(own_ref, other_ref))[: QUARTER + 16]
    d_gate = jnp.concatenate([d_gate_ref[0, 0], d_gate_ref[1, 0]], axis=0)
    grads = jnp.concatenate([late, d_gate], axis=1)
    width = QUARTER + 2 * STATE
    for rows_at, out_ref, flip in zip(core_rows(place_ref), (mine_ref, theirs_ref), (0, 1)):
        weights = [w_ref[rows_at, :QUARTER], w_ref[rows_at, width:], w_gate_ref[rows_at]]
        total = dot_nt(grads, jnp.concatenate(weights, axis=1)).astype(BF)
        for q in range(2):
            out_ref[0, q ^ flip, :SPAN] = total[q * SPAN : (q + 1) * SPAN]


def slot_spec(rows, width, order):
    return pl.BlockSpec((2, 1, rows, width), lambda j, place: (0, order(j), 0, 0))


def segment_spec():
    return pl.BlockSpec((2, 8, BLOCKS * SPAN + 256), lambda j, place: (0, 0, 0))


def fixed_spec(rows, width):
    return pl.BlockSpec((rows, width), lambda j, place: (0, 0))


def out_shape(rows, cols_of, kind):
    return jax.ShapeDtypeStruct((2, BLOCKS, rows, cols_of), kind)


def upward(j):
    return j


def downward(j):
    return BLOCKS - 1 - j


def token_specs(order):
    return [pl.BlockSpec((1, SPAN, D), lambda j, place: (order(j), 0, 0))] * 2


def call_blocks(kernel, name, place, operands, in_specs, outs, scratch=()):
    return pl.pallas_call(
        kernel,
        grid_spec=pltpu.PrefetchScalarGridSpec(
            num_scalar_prefetch=1,
            grid=(BLOCKS,),
            in_specs=in_specs,
            out_specs=[spec for spec, _ in outs],
            scratch_shapes=list(scratch),
        ),
        out_shape=[shape for _, shape in outs],
        compiler_params=pltpu.CompilerParams(vmem_limit_bytes=VMEM_LIMIT),
        cost_estimate=pl.CostEstimate(flops=1024, bytes_accessed=1024, transcendentals=0),
        name=name,
    )(place, *operands)


def slot_out(rows, width, kind, order):
    return slot_spec(rows, width, order), out_shape(rows, width, kind)


def lead_out(rows, width, order):
    shape = jax.ShapeDtypeStruct((BLOCKS, 2, rows, width), BF)
    return pl.BlockSpec((1, 2, rows, width), lambda j, place: (order(j), 0, 0, 0)), shape


def fixed_out(rows, width):
    return fixed_spec(rows, width), jax.ShapeDtypeStruct((rows, width), F32)


def run_fwd(place, tokens, w_first, segs, taps, head, chan):
    width = QUARTER + 2 * STATE
    pieces = len(tokens) > 2
    outs = [
        slot_out(SPAN, width, BF, upward),
        slot_out(SPAN, 128, F32, upward),
        slot_out(SPAN, width, F32, upward),
        slot_out(SPAN, QUARTER, F32, upward),
        slot_out(PARTS * QUARTER, STATE, BF, upward),
    ]
    if pieces:
        shape = jax.ShapeDtypeStruct((BLOCKS, SPAN, D), BF)
        outs += [(spec, shape) for spec in token_specs(upward)]
    return call_blocks(
        fwd_pieces if pieces else fwd_blocks,
        "mix_forward",
        place,
        (*tokens, w_first, segs, taps, head, chan),
        [
            *(cot_specs() if pieces else token_specs(upward)),
            fixed_spec(D, width + 128),
            segment_spec(),
            fixed_spec(8, width),
            fixed_spec(8, 128),
            fixed_spec(8, QUARTER),
        ],
        outs,
        (cot_scratch() if pieces else [])
        + [pltpu.VMEM((2, SPAN + 8, width), F32), pltpu.VMEM((2, QUARTER, STATE), F32)],
    )


def by_slot(spec):
    def index(j, place):
        return spec.index_map(j ^ place[1], place)

    return pl.BlockSpec(spec.block_shape, index)


def cot_specs():
    return [pl.BlockSpec(memory_space=pl.ANY)] * 10


def by_slot_outs(outs):
    return [(by_slot(spec), shape) for spec, shape in outs]


def run_gate(m, place, tokens, cots, y, w_gate, w_out, chan):
    half = D // 2
    return call_blocks(
        functools.partial(gate_kernel, m),
        "gate_forward",
        place,
        (*tokens, *cots, y, w_gate, w_out, chan),
        [
            *[by_slot(spec) for spec in token_specs(upward)],
            *cot_specs(),
            by_slot(slot_spec(SPAN, QUARTER, upward)),
            fixed_spec(D, QUARTER),
            fixed_spec(D, QUARTER),
            fixed_spec(8, QUARTER),
        ],
        by_slot_outs(
            [
                slot_out(SPAN, QUARTER, F32, upward),
                slot_out(SPAN, QUARTER, F32, upward),
                lead_out(SPAN, half, upward),
                lead_out(SPAN, half, upward),
                slot_out(2, SPAN, F32, upward),
            ]
        ),
        cot_scratch(),
    )


def sums_out(rows, dp_count, last):
    if not last:
        return fixed_out(rows, D), []
    share = D // dp_count
    spec = pl.BlockSpec((dp_count, rows, share), lambda j, place: (0, 0, 0))
    out = spec, jax.ShapeDtypeStruct((dp_count, rows, share), BF)
    return out, [pltpu.VMEM((rows, D), F32)]


def run_gate_back(place, tokens, cots, y, gate, d_gated, stat, chan, seed, dp_count):
    last = seed is not None
    total, scratch = sums_out(2 * QUARTER, dp_count, last)
    return call_blocks(
        gate_back_last if last else gate_back_first,
        "gate_backward",
        place,
        (*tokens, *cots, y, gate, d_gated, stat, chan) + ((seed,) if last else ()),
        [
            *[by_slot(spec) for spec in token_specs(upward)],
            *cot_specs(),
            *[by_slot(slot_spec(SPAN, QUARTER, upward))] * 3,
            by_slot(slot_spec(2, SPAN, upward)),
            fixed_spec(8, QUARTER),
        ]
        + ([fixed_spec(2 * QUARTER, D)] if last else []),
        by_slot_outs([slot_out(SPAN, QUARTER, BF, upward), slot_out(SPAN, QUARTER, BF, upward)])
        + [fixed_out(8, QUARTER), total],
        cot_scratch() + scratch,
    )


def run_bwd(place, tokens, kept, dy, d_gate, rows, taps, head, chan, weights, seed, dp_count):
    mixed, raw, pre, y, hin = kept
    width = mixed.shape[-1]
    states = 2 * STATE
    half = D // 2
    last = seed is not None
    total, scratch = sums_out(QUARTER + 16, dp_count, last)
    rows_out = SPAN if last else SPAN + PACKED
    maps_out = [lead_out(SPAN + 16, STATE, downward)] * 2 if last else []
    return call_blocks(
        bwd_last if last else bwd_first,
        "mix_backward",
        place,
        (*tokens, mixed, pre, raw, y, hin, dy, d_gate, rows, taps, head, chan, *weights)
        + ((seed,) if last else ()),
        [
            *token_specs(downward),
            slot_spec(SPAN, width, downward),
            slot_spec(SPAN, width, downward),
            slot_spec(SPAN, 128, downward),
            slot_spec(SPAN, QUARTER, downward),
            slot_spec(PARTS * QUARTER, STATE, downward),
            slot_spec(SPAN, QUARTER, downward),
            slot_spec(SPAN, QUARTER, downward),
            segment_spec(),
            fixed_spec(8, width),
            fixed_spec(8, 128),
            fixed_spec(8, QUARTER),
            fixed_spec(D, width + 128),
            fixed_spec(D, QUARTER),
        ]
        + ([fixed_spec(QUARTER + 16, D)] if last else []),
        [
            total,
            *maps_out,
            slot_out(SPAN + 16, STATE, F32, downward),
            fixed_out(8, QUARTER),
            fixed_out(8, QUARTER),
            lead_out(rows_out, half, downward),
            lead_out(rows_out, half, downward),
        ],
        [
            pltpu.VMEM((2, SPAN + 8, QUARTER), F32),
            pltpu.VMEM((2, QUARTER, STATE), F32),
            pltpu.VMEM((2, 16, states), F32),
            pltpu.VMEM((2, 16, STATE), F32),
            pltpu.VMEM((2 * SPAN, QUARTER + 128), BF),
        ]
        + scratch,
    )


def maps_kernel(
    place_ref, packed_ref, maps_ref, slope_0, slope_1, mixed_0, mixed_1, seg_0, seg_1,
    own_0, other_0, own_1, other_1, taps_ref,
    d_maps_ref, g_ref, g_taps_ref, buf,
):
    chip = place_ref[1]
    taps = taps_ref[...]
    buf[SPAN + 16 :] = jnp.zeros((8, STATE), F32)
    sums = [jnp.zeros((1, STATE), F32) for _ in range(CONV + 1)]
    g_maps = jnp.zeros((STATE, D), F32)
    slopes, mixes, segs = (slope_0, slope_1), (mixed_0, mixed_1), (seg_0, seg_1)
    tokens = ((own_0, other_0), (own_1, other_1))
    for m in range(MB):
        for q in range(2):
            if m == 0:
                total = packed_ref[0, q].astype(F32)
                for src in range(1, BLOCKS):
                    total = total + packed_ref[src, q].astype(F32)
                groups = [total[:, 128 * k : 128 * (k + 1)] for k in range(6)]
                d_conv = jnp.concatenate(groups, axis=0)[: SPAN + 16]
            else:
                d_conv = maps_ref[0, q].astype(F32)
                for src in range(1, BLOCKS):
                    d_conv = d_conv + maps_ref[src, q].astype(F32)
            d_pre = d_conv * slopes[m][q, 0]
            buf[0 : SPAN + 16] = d_pre
            cols = to_columns(segment_flags(segs[m], q, chip))
            mixed = mixes[m][q, 0].astype(F32)
            d_mixed = jnp.zeros((SPAN, STATE), F32)
            for j in range(CONV):
                ahead = CONV - 1 - j
                window = buf[ahead : ahead + SPAN] * cols[:, 8 + j : 9 + j]
                d_mixed = d_mixed + taps[j : j + 1] * window
                sums[j] = sums[j] + jnp.sum(mixed * window, axis=0, keepdims=True)
            sums[CONV] = sums[CONV] + jnp.sum(d_pre[:SPAN], axis=0, keepdims=True)
            low = d_mixed.astype(BF)
            d_maps_ref[m, q] = low
            g_maps = g_maps + dot_tn(low, tokens[m][q][0])
    g_taps_ref[...] = jnp.concatenate(sums + [jnp.zeros((3, STATE), F32)], axis=0)
    rows_of = g_ref.shape[2]
    for z in range(g_ref.shape[0]):
        g_ref[z] = g_maps[:, z * rows_of : (z + 1) * rows_of].astype(BF)


def run_maps(place, packed, maps, slopes, mixes, segs, tokens, taps, dp_count):
    def whole(shape):
        return pl.BlockSpec(shape, lambda i, place: (0,) * len(shape))

    def slope_spec():
        return pl.BlockSpec((2, 1, SPAN + 16, STATE), lambda i, place: (0, place[1], 0, 0))

    def mixed_spec():
        first = QUARTER // STATE
        return pl.BlockSpec(
            (2, 1, SPAN, STATE), lambda i, place: (0, place[1], 0, first + place[0])
        )

    def token_spec():
        return pl.BlockSpec((1, SPAN, D), lambda i, place: (place[1], 0, 0))

    share = D // dp_count
    return pl.pallas_call(
        maps_kernel,
        grid_spec=pltpu.PrefetchScalarGridSpec(
            num_scalar_prefetch=1,
            grid=(1,),
            in_specs=[
                whole(packed.shape),
                whole(maps.shape),
                slope_spec(),
                slope_spec(),
                mixed_spec(),
                mixed_spec(),
                whole(segs[0].shape),
                whole(segs[1].shape),
                token_spec(),
                token_spec(),
                token_spec(),
                token_spec(),
                whole(taps.shape),
            ],
            out_specs=[
                whole((MB, 2, SPAN, STATE)),
                whole((dp_count, STATE, share)),
                whole((8, STATE)),
            ],
            scratch_shapes=[pltpu.VMEM((SPAN + 24, STATE), F32)],
        ),
        out_shape=[
            jax.ShapeDtypeStruct((MB, 2, SPAN, STATE), BF),
            jax.ShapeDtypeStruct((dp_count, STATE, share), BF),
            jax.ShapeDtypeStruct((8, STATE), F32),
        ],
        compiler_params=pltpu.CompilerParams(vmem_limit_bytes=VMEM_LIMIT),
        cost_estimate=pl.CostEstimate(flops=1024, bytes_accessed=1024, transcendentals=0),
        name="maps_backward",
    )(place, packed, maps, *slopes, *mixes, *segs, *tokens, taps)


def norm_kernel(place_ref, share_ref, w_in_ref, w_state_ref, w_step_ref, step_ref, out_ref):
    rows = share_ref.shape[1]
    squares = jnp.zeros((rows, QUARTER), F32)
    products = jnp.zeros((rows, QUARTER), F32)
    for s in range(BLOCKS):
        at = slice(s * QUARTER, (s + 1) * QUARTER)
        out = share_ref[s, :, :QUARTER].astype(F32)
        gate = share_ref[s, :, QUARTER : 2 * QUARTER].astype(F32)
        inner = share_ref[s, :, 2 * QUARTER : 3 * QUARTER].astype(F32)
        squares = squares + out * out + gate * gate + inner * inner
        products = products + gate * w_in_ref[0, :, at].astype(F32)
        products = products + inner * w_in_ref[1, :, at].astype(F32)
    state = share_ref[0, :, MAPS_AT : MAPS_AT + STATE].astype(F32)
    for s in range(1, BLOCKS):
        state = state + share_ref[s, :, MAPS_AT : MAPS_AT + STATE].astype(F32)
    step = step_ref[...]
    by_row = jnp.sum(products, axis=1, keepdims=True)
    by_row = by_row + jnp.sum(state * w_state_ref[...].astype(F32), axis=1, keepdims=True)
    square = jnp.sum(squares, axis=1, keepdims=True) + jnp.sum(state * state, axis=1, keepdims=True)
    lanes = lax.broadcasted_iota(jnp.int32, (rows, 128), 1)
    table = jnp.where(lanes == 0, by_row, jnp.where(lanes == 1, square, 0.0))
    table = jnp.concatenate([table, jnp.zeros((128 - rows, 128), F32)], axis=0).T
    total = jnp.sum(table[1:2], axis=1, keepdims=True)
    total = total + jnp.sum(jnp.sum(step * step, axis=0, keepdims=True), axis=1, keepdims=True)
    by_step = jnp.sum(step * w_step_ref[...].astype(F32), axis=0, keepdims=True)
    by_step = jnp.concatenate([by_step, jnp.zeros((1, 128 - rows), F32)], axis=1)
    at_row = lax.broadcasted_iota(jnp.int32, (8, 128), 0)
    at_lane = lax.broadcasted_iota(jnp.int32, (8, 128), 1)
    first = jnp.where((at_row == 0) & (at_lane == rows), total, table[0:8] + by_step)
    out_ref[...] = jnp.where(at_row == 0, first, 0.0)


def update_kernel(
    place_ref, factor_ref, share_ref, step_ref, w_in_ref, w_out_ref, w_state_ref,
    w_step_ref, m_in_ref, m_out_ref, m_state_ref, m_step_ref,
    new_in_ref, new_out_ref, new_state_ref, new_step_ref,
    next_in_ref, next_out_ref, next_state_ref, next_step_ref,
):
    factor = factor_ref[0, 0]

    def write(new_ref, next_ref, at, moment, grad, weight):
        new = 0.5 * moment + (0.5 * factor) * grad
        new_ref[at] = new
        next_ref[at] = (weight.astype(F32) - LEARN * new).astype(BF)

    for s in range(BLOCKS):
        lanes = slice(s * QUARTER, (s + 1) * QUARTER)
        gate = (0, slice(None), lanes)
        write(
            new_in_ref, next_in_ref, gate, m_in_ref[gate],
            share_ref[s, :, QUARTER : 2 * QUARTER].astype(F32), w_in_ref[gate],
        )
        inner = (1, slice(None), lanes)
        write(
            new_in_ref, next_in_ref, inner, m_in_ref[inner],
            share_ref[s, :, 2 * QUARTER : 3 * QUARTER].astype(F32), w_in_ref[inner],
        )
        out = (slice(None), lanes)
        write(
            new_out_ref, next_out_ref, out, m_out_ref[out],
            share_ref[s, :, :QUARTER].astype(F32), w_out_ref[out],
        )
    state = share_ref[0, :, MAPS_AT : MAPS_AT + STATE].astype(F32)
    for s in range(1, BLOCKS):
        state = state + share_ref[s, :, MAPS_AT : MAPS_AT + STATE].astype(F32)
    write(new_state_ref, next_state_ref, ..., m_state_ref[...], state, w_state_ref[...])
    write(new_step_ref, next_step_ref, ..., m_step_ref[...], step_ref[...], w_step_ref[...])


def owner_specs(rows):
    return [
        pl.BlockSpec((2, rows, BLOCKS * QUARTER), lambda i, place: (0, place[1], 0)),
        pl.BlockSpec((rows, STATE), lambda i, place: (place[1], place[0])),
    ]


def run_owner(kernel, name, place, operands, in_specs, outs):
    return pl.pallas_call(
        kernel,
        grid_spec=pltpu.PrefetchScalarGridSpec(
            num_scalar_prefetch=1, grid=(1,), in_specs=in_specs,
            out_specs=[spec for spec, _ in outs],
        ),
        out_shape=[shape for _, shape in outs],
        compiler_params=pltpu.CompilerParams(vmem_limit_bytes=VMEM_LIMIT),
        cost_estimate=pl.CostEstimate(flops=1024, bytes_accessed=1024, transcendentals=0),
        name=name,
    )(place, *operands)


def swap_cores(block):
    return lax.ppermute(block, "tensor", SWAP)


def over_x(block):
    return lax.ppermute(block, "seq", ROUTE_X)


def over_y(block):
    return lax.ppermute(block, "seq", ROUTE_Y)


def exchange(blocks):
    return lax.all_to_all(blocks, "seq", 0, 0, tiled=True)


def copies(piece):
    return jnp.broadcast_to(piece, (BLOCKS,) + piece.shape)


def add_low(a, b):
    return (a.astype(F32) + b.astype(F32)).astype(BF)


def scatter(blocks):
    return jnp.sum(exchange(blocks).astype(F32), axis=0)


def after(value, *others):
    return lax.optimization_barrier((value, others))[0]


def fast_body(
    inputs,
    segments,
    cotangent,
    prenorm,
    inproj,
    statproj,
    stepproj,
    outproj,
    convinner,
    convstate,
    headparam,
    gatenorm,
    prenorm_moment,
    inproj_moment,
    statproj_moment,
    stepproj_moment,
    outproj_moment,
    convinner_moment,
    convstate_moment,
    headparam_moment,
    gatenorm_moment,
):
    core = lax.axis_index("tensor")
    chip = lax.axis_index("seq")
    data_at = lax.axis_index("dp")
    dp_count = lax.axis_size("dp")
    heads_local = headparam.shape[1]
    rows_local = inproj.shape[1]
    shard = rows_local // BLOCKS
    half_d = D // 2
    place = jnp.stack([core, chip]).astype(jnp.int32)

    def by_core(first, second):
        return jnp.where(core == 0, first, second)

    def quarter(array, axis, width):
        return lax.dynamic_slice_in_dim(array, chip * width, width, axis)

    def all_rows(block):
        return lax.all_gather(block, "dp", axis=0, tiled=True)

    first_block = (
        jnp.concatenate(
            [
                quarter(inproj[1], 1, QUARTER),
                statproj,
                jnp.pad(quarter(stepproj, 1, QHEADS), ((0, 0), (0, 128 - QHEADS))),
            ],
            axis=1,
        )
    )
    inputs, first_block = after((inputs, first_block))
    w_first = all_rows(first_block)
    w_gate = all_rows(quarter(inproj[0], 1, QUARTER))
    w_out = all_rows(quarter(outproj, 0, QUARTER).T)

    def whole_rows(array):
        mine = lax.dynamic_index_in_dim(array, core, 1, keepdims=False)
        theirs = lax.dynamic_index_in_dim(array, 1 - core, 1, keepdims=False)
        got = swap_cores(theirs)
        return by_core(
            jnp.concatenate([mine, got], axis=2), jnp.concatenate([got, mine], axis=2)
        )

    rows_whole = whole_rows(inputs)
    normed_own = rms_scale(rows_whole.astype(F32), prenorm).astype(BF)
    cot_own = whole_rows(cotangent)
    half = SPAN // 2
    mine_0, second_copies = after((normed_own[0], copies(normed_own[1])))
    near_0 = (mine_0, over_x(mine_0), over_y(mine_0))
    own_swapped = swap_cores(mine_0)

    seg_mine = jnp.concatenate(
        [
            lax.dynamic_index_in_dim(segments, core, 1),
            lax.dynamic_index_in_dim(segments, 1 - core, 1),
        ],
        axis=1,
    )
    seg_pad = jnp.pad(
        seg_mine.astype(F32), ((0, 0), (0, 0), (128, 128)), constant_values=-1.0
    )
    segs = jnp.broadcast_to(seg_pad[:, :, None], seg_pad.shape[:2] + (8, seg_pad.shape[2]))

    taps_inner = quarter(convinner, 1, QUARTER)
    taps = jnp.pad(jnp.concatenate([taps_inner, convstate], axis=1), ((0, 3), (0, 0)))
    head_own = quarter(headparam, 1, QHEADS)
    head = jnp.pad(
        jnp.stack([head_own[0], jnp.exp(head_own[1]), head_own[2]]),
        ((0, 5), (0, 128 - QHEADS)),
    )
    gain = quarter(gatenorm, 0, QUARTER)
    chan = jnp.pad(jnp.stack([gain, jnp.repeat(head_own[2], HEADDIM)]), ((0, 6), (0, 0)))

    def rows_dot_t(left, right):
        return lax.dot_general(left, right, (((3,), (1,)), ((), ())), preferred_element_type=F32)

    def core_sums(mine, theirs):
        return add_low(mine, swap_cores(theirs))

    def over_dp(parts):
        return lax.psum_scatter(parts, "dp", scatter_dimension=0, tiled=True)[0]

    def by_place(columns):
        return columns.T.reshape(BLOCKS, shard, -1)

    def forward(m, place, tokens):
        return run_fwd(place, tokens, w_first, segs[m], taps, head, chan)

    def gate_forward(m, place):
        return run_gate(m, place, normed[m], cots[m], kept[m][3], w_gate, w_out, chan)

    def gate_backward(m, place, gate, d_gated, sums, seed):
        return run_gate_back(
            place, normed[m], cots[m], kept[m][3], gate, d_gated, sums, chan, seed, dp_count
        )

    def backward(m, place, dy, d_gate, seed):
        return run_bwd(
            place, normed[m], kept[m], dy, d_gate, segs[m], taps, head, chan,
            (w_first, w_gate), seed, dp_count,
        )

    def summed(blocks):
        return jnp.sum(blocks.astype(F32), axis=0)

    def in_order(block):
        return by_core(block, block[:, ::-1])

    def token_scale(sums):
        own = lax.dynamic_index_in_dim(sums, chip, 1, keepdims=False)
        return lax.rsqrt(own[:, 0] / INNER + EPS)[..., None]

    def sum_dp(value):
        hop = 1
        while hop < dp_count:
            value = value + lax.ppermute(value, "dp", [(i, i ^ hop) for i in range(dp_count)])
            hop *= 2
        return value

    def sum_seq(value):
        value = value + over_x(value)
        return value + over_y(value)

    def with_other(own):
        return own, swap_cores(own)

    stepproj_own = lax.dynamic_slice_in_dim(stepproj.T, chip * shard, shard, 1)
    outproj_own = lax.dynamic_slice_in_dim(outproj, chip * shard, shard, 1).T
    near_0, own_swapped, cot_own, segs, taps, head, chan, stepproj_own, outproj_own = after(
        (near_0, own_swapped, cot_own, segs, taps, head, chan, stepproj_own, outproj_own)
    )
    far = over_x(near_0[2][:half]), over_y(near_0[1][half:])
    near_swapped = [swap_cores(piece) for piece in near_0[1:]]
    far, near_swapped, second_copies = after((far, near_swapped, second_copies))
    own_1 = exchange(second_copies)
    far, w_first = after((far, w_first))
    cot_other = swap_cores(cot_own)
    first_pieces = (
        *near_0, *far, own_swapped, *near_swapped, *[swap_cores(piece) for piece in far]
    )
    *kept_0, own_0, other_0 = forward(0, place, first_pieces)
    kept = [kept_0]
    normed = [(own_0, other_0)]
    cot_own, cot_other, place = after((cot_own, cot_other, place), kept[0][1])
    by_x, by_y = over_x(cot_own), over_y(cot_own)
    own_1, w_gate, place = after((own_1, w_gate, place))
    normed.append(with_other(own_1))
    kept.append(forward(1, place, normed[1]))

    by_x, by_y, w_out, place = after((by_x, by_y, w_out, place), kept[1][1])
    def far_pieces(m, by_x, by_y):
        return over_x(by_y[m, :half]), over_y(by_x[m, half:])

    def cot_pieces(far):
        return (cot_own, by_x, by_y, *far, *near_other, *[swap_cores(piece) for piece in far])

    far_0 = far_pieces(0, by_x, by_y)
    near_other = (cot_other, swap_cores(by_x), swap_cores(by_y))
    far_0, near_other, far_from, place = after((far_0, near_other, (by_x, by_y), place))
    cots = [cot_pieces(far_0)]
    far_1 = far_pieces(1, *far_from)
    gate_0, d_gated_0, mine_0, theirs_0, stat_0 = gate_forward(0, place)
    place, theirs_0, far_1 = after((place, theirs_0, far_1), stat_0)
    cots.append(cot_pieces(far_1))
    branch_0 = core_sums(mine_0, after(theirs_0, cots[1][8:]))
    gate_1, d_gated_1, mine_1, theirs_1, stat_1 = gate_forward(1, place)

    stats = jnp.stack([stat_0, after(stat_1, branch_0)])
    stats = stats + swap_cores(stats)[:, ::-1]
    theirs_1 = after(theirs_1, stats)
    sums_0, sums_1 = sum_seq(stats)
    branch_0 = after(branch_0, sums_0)
    layer_0 = exchange(branch_0)
    dy_0, d_gate_0, g_gain_0, g_mid_0 = gate_backward(0, place, gate_0, d_gated_0, sums_0, None)
    branch_1 = core_sums(mine_1, theirs_1)
    place = after(place, dy_0)
    dy_1, d_gate_1, g_gain_1, mid_parts = gate_backward(
        1, place, gate_1, d_gated_1, sums_1, g_mid_0
    )

    layer_0, branch_1, place, mid_parts = after((layer_0, branch_1, place, mid_parts), dy_1)
    layer_1 = exchange(branch_1)
    mid_rows = over_dp(mid_parts)
    g_late_0, slope_0, g_taps_0, g_head_0, mine, theirs = backward(0, place, dy_0, d_gate_0, None)

    layer_1, mid_rows, theirs, place = after((layer_1, mid_rows, theirs, place), g_taps_0)
    back_0 = core_sums(mine, theirs)
    layer_out = [
        summed(layer_0) * token_scale(sums_0), summed(layer_1) * token_scale(sums_1)
    ]
    layer_out = (inputs.astype(F32) + in_order(jnp.stack(layer_out))).astype(BF)
    back_0, place, layer_out = after((back_0, place, layer_out))
    token_0 = exchange(back_0)
    late_parts, keep_1, give_1, slope_1, g_taps_1, g_head_1, mine, theirs = backward(
        1, place, dy_1, d_gate_1, g_late_0
    )

    token_0, late_parts, theirs, give_1 = after((token_0, late_parts, theirs, give_1))
    late_rows = over_dp(late_parts)
    maps = core_sums(keep_1, give_1)
    back_1 = core_sums(mine, after(theirs, maps))
    maps = exchange(maps)
    maps, back_1, token_0, mid_rows, g_taps_1 = after(
        (maps, back_1, token_0, mid_rows, g_taps_1)
    )
    token_1 = exchange(back_1)
    taps_state = lax.dynamic_slice_in_dim(convstate, core * STATE, STATE, 1)
    d_maps, g_maps, g_state_taps = run_maps(
        place, token_0[:, :, SPAN:], maps, (slope_0, slope_1), (kept[0][0], kept[1][0]),
        segs, (*normed[0], *normed[1]), jnp.pad(taps_state, ((0, 3), (0, 0))), dp_count,
    )

    def for_dp(hop):
        at = lax.rem(data_at + hop, dp_count)
        return lax.dynamic_index_in_dim(g_maps, at, 0, keepdims=False)

    state_rows = for_dp(0).astype(F32)
    for hop in range(1, dp_count):
        route = [(i, (i + hop) % dp_count) for i in range(dp_count)]
        state_rows = state_rows + lax.ppermute(for_dp(hop), "dp", route).astype(F32)
    state_rows = state_rows.astype(BF)

    inner_local = BLOCKS * QUARTER

    def put(values, width, total):
        base = jnp.zeros(values.shape[:-1] + (total,), F32)
        return lax.dynamic_update_slice_in_dim(base, values, chip * width, values.ndim - 1)

    g_taps, g_head = g_taps_0 + g_taps_1, g_head_0 + g_head_1
    g_heads = jnp.concatenate(
        [g_head[:2, :QHEADS], jnp.sum(g_head[2].reshape(1, QHEADS, HEADDIM), axis=2)], axis=0
    )
    small_parts = [
        put(g_taps[: CONV + 1], QUARTER, inner_local),
        put(g_gain_0[0] + g_gain_1[0], QUARTER, inner_local),
        put(g_heads, QHEADS, heads_local),
        g_state_taps[: CONV + 1],
    ]
    small_shapes = [small.shape for small in small_parts]
    vector = jnp.concatenate([small.reshape(-1) for small in small_parts])
    vector = jnp.pad(vector, (0, -vector.size % 1024)).reshape(-1, 128)

    late_rows, mid_rows, state_rows = after((late_rows, mid_rows, state_rows))
    shares = jnp.concatenate(
        [mid_rows, late_rows[:QUARTER], state_rows, late_rows[QUARTER:]], axis=0
    )
    other_vector = swap_cores(vector)
    token_1, shares, vector, other_vector = after(
        (token_1, by_place(shares), vector, other_vector)
    )
    share = exchange(shares)
    d_tokens = [summed(token_0[:, :, :SPAN]), summed(token_1)]
    w_state = w_first[:, QUARTER : QUARTER + 2 * STATE]

    state_other = swap_cores(d_maps)[:, ::-1]
    state_mine = d_maps
    d_state_both = by_core(
        jnp.concatenate([state_mine, state_other], axis=3),
        jnp.concatenate([state_other, state_mine], axis=3),
    )
    from_state = rows_dot_t(
        d_state_both, lax.dynamic_slice_in_dim(w_state, core * half_d, half_d, 0)
    )

    outputs = layer_out
    d_normed = in_order(jnp.stack(d_tokens) + from_state)
    rows_own = inputs.astype(F32)
    gain_own = lax.dynamic_slice_in_dim(prenorm, core * half_d, half_d, 0)
    weighted = d_normed * gain_own
    pair_sums = jnp.stack(
        [jnp.sum(rows_own * rows_own, axis=-1), jnp.sum(weighted * rows_own, axis=-1)]
    )
    pair_sums = pair_sums + swap_cores(pair_sums)
    root = lax.rsqrt(pair_sums[0] / D + EPS)[..., None]
    input_grads = (
        cotangent.astype(F32)
        + weighted * root
        - rows_own * root * root * root * (pair_sums[1] / D)[..., None]
    ).astype(BF)

    step_at = MAPS_AT + STATE
    step_share = share[:, :, step_at : step_at + QHEADS].astype(F32)
    step_share = jnp.moveaxis(step_share, 1, 2).reshape(heads_local, shard)
    in_spec, state_spec = owner_specs(shard)

    def whole(array):
        return pl.BlockSpec(array.shape, lambda i, place: (0,) * array.ndim)

    def whole_out(shape, kind):
        spec = pl.BlockSpec(shape, lambda i, place: (0,) * len(shape))
        return spec, jax.ShapeDtypeStruct(shape, kind)

    owner_sums = run_owner(
        norm_kernel,
        "owner_norm",
        place,
        (share, inproj, statproj, stepproj_own, step_share),
        [whole(share), in_spec, state_spec, whole(stepproj_own), whole(step_share)],
        [whole_out((8, 128), F32)],
    )[0]
    owner_sums = owner_sums + swap_cores(owner_sums)

    owners = dp_count * BLOCKS
    owner = data_at * BLOCKS + chip
    gain_rows = lax.dynamic_slice_in_dim(prenorm, owner * shard, shard, 0)
    lanes = jnp.arange(128)
    g_prenorm = owner_sums[0] / jnp.pad(gain_rows, (0, 128 - shard), constant_values=1.0)
    g_prenorm = jnp.where(lanes < shard, g_prenorm, 0.0)
    square = owner_sums[0, shard] + jnp.sum(g_prenorm * g_prenorm)
    line = jnp.where(lanes == shard, square, g_prenorm)
    table = jnp.where(jnp.arange(owners)[:, None] == owner, line[None], 0.0)
    table = sum_seq(sum_dp(jnp.concatenate([table, vector, other_vector], axis=0)))
    small_sums = []
    start = 0
    both_vectors = table[owners:].reshape(2, -1)
    vector = both_vectors[0]
    for shape in small_shapes:
        size = math.prod(shape)
        small_sums.append(vector[start : start + size].reshape(shape))
        start += size
    s_taps, s_gain, s_head, s_state_taps = small_sums

    small_sq = jnp.sum(both_vectors * both_vectors, axis=1)
    grad_norm = jnp.sqrt(jnp.sum(table[:owners, shard]) + (small_sq[0] + small_sq[1]))
    s_prenorm = lax.dynamic_slice_in_dim(
        table[:owners, :shard], core * (owners // 2), owners // 2, 0
    ).reshape(half_d)

    entries = (
        2 * D * INNER
        + 2 * D * STATE
        + D * (INNER // HEADDIM)
        + INNER * D
        + (CONV + 1) * (INNER + 2 * STATE)
        + 3 * (INNER // HEADDIM)
        + INNER
        + D
    )
    limit = CLIP_RMS * math.sqrt(entries)
    factor = limit / jnp.maximum(grad_norm, limit)

    def moved(moment, grad):
        return 0.5 * moment + 0.5 * factor * grad

    def stepped(weight, moment):
        return (weight.astype(F32) - LEARN * moment).astype(weight.dtype)

    new_prenorm = moved(prenorm_moment, s_prenorm)
    moments = (inproj_moment, outproj_moment.T, statproj_moment, stepproj_moment.T)
    new_in, new_out, new_state, new_step, next_in, next_out, next_state, next_step = run_owner(
        update_kernel,
        "owner_update",
        place,
        (
            factor.reshape(1, 1), share, step_share,
            inproj, outproj_own, statproj, stepproj_own, *moments,
        ),
        [
            pl.BlockSpec(memory_space=pltpu.SMEM),
            whole(share), whole(step_share),
            in_spec, whole(outproj_own), state_spec, whole(stepproj_own),
            *[whole(moment) for moment in moments],
        ],
        [whole_out(moment.shape, kind) for kind in (F32, BF) for moment in moments],
    )
    new_taps = moved(convinner_moment, s_taps)
    new_state_taps = moved(convstate_moment, s_state_taps)
    new_head = moved(headparam_moment, s_head)
    new_gain = moved(gatenorm_moment, s_gain)
    return (
        outputs,
        input_grads,
        grad_norm,
        new_prenorm,
        new_in,
        new_state,
        new_step.T,
        new_out.T,
        new_taps,
        new_state_taps,
        new_head,
        new_gain,
        next_in,
        next_state,
        next_step.T,
        next_out.T,
        stepped(convinner, new_taps),
        stepped(lax.dynamic_slice_in_dim(convstate, core * STATE, STATE, 1), new_state_taps),
    )


def solution(mesh):
    fast = mesh.shape["seq"] == BLOCKS and mesh.shape["tensor"] == 2
    return jax.shard_map(
        fast_body if fast else general_body,
        mesh=mesh,
        in_specs=(
            P(None, "dp", "seq", "tensor"),
            P(None, "dp", None),
            P(None, "dp", "seq", "tensor"),
            P(),
            P(None, "dp", "tensor"),
            P("dp", None),
            P("dp", "tensor"),
            P("tensor", "dp"),
            P(None, "tensor"),
            P(),
            P(None, "tensor"),
            P("tensor"),
            P("tensor"),
            P(None, ("dp", "seq"), "tensor"),
            P(("dp", "seq"), "tensor"),
            P(("dp", "seq"), "tensor"),
            P("tensor", ("dp", "seq")),
            P(None, "tensor"),
            P(None, "tensor"),
            P(None, "tensor"),
            P("tensor"),
        ),
        out_specs=(
            P(None, "dp", "seq", "tensor"),
            P(None, "dp", "seq", "tensor"),
            P(),
            P("tensor"),
            P(None, ("dp", "seq"), "tensor"),
            P(("dp", "seq"), "tensor"),
            P(("dp", "seq"), "tensor"),
            P("tensor", ("dp", "seq")),
            P(None, "tensor"),
            P(None, "tensor"),
            P(None, "tensor"),
            P("tensor"),
            P(None, ("dp", "seq"), "tensor"),
            P(("dp", "seq"), "tensor"),
            P(("dp", "seq"), "tensor"),
            P("tensor", ("dp", "seq")),
            P(None, "tensor"),
            P(None, "tensor"),
        ),
        check_vma=False,
    )
```

```python
import functools
import math

import jax
import jax.numpy as jnp
from jax import lax
from jax.experimental import pallas as pl
from jax.experimental.pallas import tpu as pltpu
from jax.sharding import PartitionSpec as P

D = 1536
INNER = 3072
HEADDIM = 64
STATE = 128
CONV = 4
MB = 2


EPS = 1e-05
LEARN = 0.05
CLIP_RMS = 0.25
HIGH = lax.Precision.HIGHEST


def shifted(block, axis, distance):
    devices = range(lax.axis_size(axis))
    route = [(i - distance, i) for i in devices if i - distance in devices]
    return lax.ppermute(block, axis, route)


def prefix(array, axis, combine, identity):
    size, position = (lax.axis_size(axis), lax.axis_index(axis))
    everything = jax.tree.map(
        lambda part, kind: lax.all_gather(part.astype(kind), axis),
        array,
        (jnp.bfloat16, jnp.bfloat16),
    )
    start = jax.tree.map(
        lambda part, zero: jnp.broadcast_to(jnp.asarray(zero, part.dtype), part.shape),
        array,
        identity,
    )

    def prefix_step(k, before):
        reached = k < position
        new = combine(
            before, jax.tree.map(lambda part, own: part[k].astype(own.dtype), everything, array)
        )
        return jax.tree.map(lambda a, b: jnp.where(reached, a, b), new, before)

    return lax.fori_loop(0, size, prefix_step, start)


def entering_2(array, axis, combine, identity):
    size, position = (lax.axis_size(axis), lax.axis_index(axis))
    everything = jax.tree.map(lambda part: lax.all_gather(part, axis), array)
    start = jax.tree.map(
        lambda part, zero: jnp.broadcast_to(jnp.asarray(zero, part.dtype), part.shape),
        array,
        identity,
    )

    def entering_step(k, before):
        at = size - 1 - k
        reached = at > position
        new = combine(before, jax.tree.map(lambda part: part[at], everything))
        return jax.tree.map(lambda a, b: jnp.where(reached, a, b), new, before)

    return lax.fori_loop(0, size, entering_step, start)


def rms_scale(values, weight):
    return values * lax.rsqrt(jnp.mean(values * values, axis=-1, keepdims=True) + EPS) * weight


def conv_block(padded, seg_pad, kernel):
    length = padded.shape[0] - (CONV - 1)
    own_seg = seg_pad[CONV - 1 :]
    summed = jnp.broadcast_to(kernel[CONV], (length, kernel.shape[1]))
    for offset in range(CONV):
        window = padded[offset : offset + length]
        same_doc = (seg_pad[offset : offset + length] == own_seg)[:, None]
        summed = summed + kernel[offset] * jnp.where(same_doc, window, 0.0)
    return jax.nn.silu(summed)


def decay_table(cumulative, segids):
    row_count = segids.shape[0]
    places = jnp.arange(row_count)
    allowed = (segids[:, None] == segids[None, :]) & (places[:, None] >= places[None, :])
    allowed = allowed[:, :, None]
    gap_values = cumulative[:, None, :] - cumulative[None, :, :]
    return jnp.where(allowed, jnp.exp(jnp.where(allowed, gap_values, -60.0)), 0.0)


def head_rates(raw_step, params):
    step_sizes = jax.nn.softplus(raw_step + params[0])
    return (step_sizes, jnp.cumsum(-step_sizes * jnp.exp(params[1]), axis=0))


def mix_out(values, b_proj, c_proj, raw_step, params, segids, before, carry_in):
    step_sizes, cumulative = head_rates(raw_step, params)
    scores = jnp.dot(c_proj, b_proj.T, precision=HIGH)
    weights = scores[:, :, None] * decay_table(cumulative, segids) * step_sizes[None, :, :]
    result = jnp.einsum("tsh,shp->thp", weights, values, precision=HIGH)
    entering = jnp.where((segids == before)[:, None], jnp.exp(cumulative), 0.0)
    carried = jnp.einsum("tn,hpn->thp", c_proj, carry_in, precision=HIGH)
    return result + entering[:, :, None] * carried + params[2][None, :, None] * values


def mix_state(values, b_proj, raw_step, params, segids, before):
    step_sizes, cumulative = head_rates(raw_step, params)
    tail_weight = (
        jnp.where(
            (segids == segids[-1])[:, None], jnp.exp(cumulative[-1][None, :] - cumulative), 0.0
        )
        * step_sizes
    )
    summary = jnp.einsum("sh,shp,sn->hpn", tail_weight, values, b_proj, precision=HIGH)
    passing = jnp.where(segids[-1] == before, jnp.exp(cumulative[-1]), 0.0)
    return (summary, passing)


def chain(earlier, later):
    return (earlier[0] * later[0], later[0][..., None, None] * earlier[1] + later[1])


def add_tree(totals, terms):
    if totals is None:
        return terms
    return jax.tree.map(jnp.add, totals, terms)


def project(left_rows, matrix):
    return jnp.einsum("bld,dk->blk", left_rows, matrix, preferred_element_type=jnp.float32)


def weight_grad(left_rows, right_rows):
    return jnp.einsum("bld,blk->dk", left_rows, right_rows, preferred_element_type=jnp.float32)


def back_project(grad_rows, matrix):
    return jnp.einsum("blk,dk->bld", grad_rows, matrix, preferred_element_type=jnp.float32)


def general_body(
    inputs,
    segments,
    cotangent,
    prenorm,
    inproj,
    statproj,
    stepproj,
    outproj,
    convinner,
    convstate,
    headparam,
    gatenorm,
    prenorm_moment,
    inproj_moment,
    statproj_moment,
    stepproj_moment,
    outproj_moment,
    convinner_moment,
    convstate_moment,
    headparam_moment,
    gatenorm_moment,
):
    tensor_at = lax.axis_index("tensor")
    seq_at = lax.axis_index("seq")
    data_at = lax.axis_index("dp")
    tensor_count = lax.axis_size("tensor")
    batch_count = inputs.shape[1]
    span_len = inputs.shape[2]
    inner_local = convinner.shape[1]
    heads_local = headparam.shape[1]
    state_half = 2 * STATE // tensor_count
    model_half = D // tensor_count
    rows_full, grads_full = (
        lax.all_gather(inputs, "tensor", axis=3, tiled=True),
        lax.all_gather(cotangent, "tensor", axis=3, tiled=True),
    )
    seg_padded = jnp.pad(segments, ((0, 0), (0, 0), (CONV - 1, 0)), constant_values=-1)
    seg_local = lax.dynamic_slice_in_dim(seg_padded, seq_at * span_len, span_len + CONV - 1, 2)
    kernel = jnp.concatenate([convinner, convstate], axis=1)
    shares = None
    smalls = None
    outputs = []
    input_grads = []
    for batch in range(MB):
        inproj_all, statproj_all, stepproj_all, outproj_all = (
            lax.all_gather(inproj, "dp", axis=1, tiled=True),
            lax.all_gather(statproj, "dp", axis=0, tiled=True),
            lax.all_gather(stepproj, "dp", axis=0, tiled=True),
            lax.all_gather(outproj, "dp", axis=1, tiled=True),
        )
        rows = rows_full[batch].astype(jnp.float32)
        normed, norm_back = jax.vjp(rms_scale, rows, prenorm)
        normed_low = normed.astype(jnp.bfloat16)
        gate_pre = project(normed_low, inproj_all[0])
        inner_pre = project(normed_low, inproj_all[1])
        state_pre = project(normed_low, statproj_all)
        raw_step = project(normed_low, stepproj_all)
        mixed = jnp.concatenate([inner_pre, state_pre], axis=2).astype(jnp.bfloat16)
        edge_in = shifted(mixed[:, span_len - (CONV - 1) :, :], "seq", 1)
        padded = jnp.concatenate([edge_in, mixed], axis=1).astype(jnp.float32)
        seg_now = seg_local[batch]
        own_seg = seg_now[:, CONV - 1 :]
        before = seg_now[:, CONV - 2]
        conv_out, conv_back = jax.vjp(
            lambda pad_vals, kernel_in: jax.vmap(conv_block, in_axes=(0, 0, None))(
                pad_vals, seg_now, kernel_in
            ),
            padded,
            kernel,
        )
        values = conv_out[..., :inner_local].reshape(batch_count, span_len, heads_local, HEADDIM)
        b_proj = conv_out[..., inner_local : inner_local + STATE]
        c_proj = conv_out[..., inner_local + STATE :]
        (summary, passing), state_back = jax.vjp(
            lambda value_in, b_part, raw_part, param_in: jax.vmap(
                mix_state, in_axes=(0, 0, 0, None, 0, 0)
            )(value_in, b_part, raw_part, param_in, own_seg, before),
            values,
            b_proj,
            raw_step,
            headparam,
        )
        identity = (jnp.ones_like(passing), jnp.zeros_like(summary))
        _, carry_in = prefix((passing, summary), "seq", chain, identity)
        mixer, out_back = jax.vjp(
            lambda value_in, b_part, c_part, raw_part, param_in, state_in: jax.vmap(
                mix_out, in_axes=(0, 0, 0, 0, None, 0, 0, 0)
            )(value_in, b_part, c_part, raw_part, param_in, own_seg, before, state_in),
            values,
            b_proj,
            c_proj,
            raw_step,
            headparam,
            carry_in,
        )
        flat_mixer = mixer.reshape(batch_count, span_len, inner_local)
        gate_act = jax.nn.silu(gate_pre)
        gated_in = flat_mixer * gate_act
        total_sq = lax.psum(jnp.sum(gated_in * gated_in, axis=-1), "tensor")
        scale = lax.rsqrt(total_sq / INNER + EPS)[..., None]
        gated_low = (gated_in * scale * gatenorm).astype(jnp.bfloat16)
        branch_part = project(gated_low, outproj_all)
        branch_own = lax.psum_scatter(branch_part, "tensor", scatter_dimension=2, tiled=True)
        outputs.append((inputs[batch].astype(jnp.float32) + branch_own).astype(jnp.bfloat16))
        grad_rows = grads_full[batch]
        d_gated = back_project(grad_rows, outproj_all)
        g_outproj = jnp.einsum(
            "blk,bld->kd", gated_low, grad_rows, preferred_element_type=jnp.float32
        )
        g_gatenorm = jnp.sum(d_gated * gated_in * scale, axis=(0, 1))
        weighted = d_gated * gatenorm
        cross = lax.psum(jnp.sum(weighted * gated_in, axis=-1), "tensor")
        d_in = weighted * scale - gated_in * scale**3 * (cross / INNER)[..., None]
        d_mixer = d_in * gate_act
        sigma = jax.nn.sigmoid(gate_pre)
        d_gate = d_in * flat_mixer * sigma * (1.0 + gate_pre * (1.0 - sigma))
        d_values, d_bproj, d_cproj, d_raw, d_param, d_carry = out_back(
            d_mixer.reshape(batch_count, span_len, heads_local, HEADDIM)
        )
        _, d_after = entering_2((passing, d_carry), "seq", chain, identity)
        d_passing = jnp.sum(d_after * carry_in, axis=(2, 3))
        d_values_tail, d_bproj_tail, d_raw_tail, d_param_tail = state_back((d_after, d_passing))
        d_state = lax.psum(jnp.concatenate([d_bproj + d_bproj_tail, d_cproj], axis=2), "tensor")
        d_conv = jnp.concatenate(
            [(d_values + d_values_tail).reshape(batch_count, span_len, inner_local), d_state],
            axis=2,
        )
        d_padded, d_kernel = conv_back(d_conv)
        edge_back = shifted(d_padded[:, : CONV - 1, :].astype(jnp.bfloat16), "seq", -1).astype(
            jnp.float32
        )
        d_mixed = d_padded[:, CONV - 1 :, :] + jnp.pad(
            edge_back, ((0, 0), (span_len - (CONV - 1), 0), (0, 0))
        )
        d_mixed_low = d_mixed.astype(jnp.bfloat16)
        d_gate_low = d_gate.astype(jnp.bfloat16)
        d_raw_low = (d_raw + d_raw_tail).astype(jnp.bfloat16)
        d_inner_low = d_mixed_low[..., :inner_local]
        d_state_low = lax.dynamic_slice_in_dim(
            d_mixed_low[..., inner_local:], tensor_at * state_half, state_half, 2
        )
        statproj_own = lax.dynamic_slice_in_dim(statproj_all, tensor_at * state_half, state_half, 1)
        g_inproj = jnp.stack(
            [weight_grad(normed_low, d_gate_low), weight_grad(normed_low, d_inner_low)]
        )
        g_statproj = weight_grad(normed_low, d_state_low)
        g_stepproj = weight_grad(normed_low, d_raw_low)
        d_normed_part = (
            back_project(d_gate_low, inproj_all[0])
            + back_project(d_inner_low, inproj_all[1])
            + back_project(d_state_low, statproj_own)
            + back_project(d_raw_low, stepproj_all)
        )
        d_normed = lax.psum(d_normed_part, "tensor")
        d_rows, d_prenorm = norm_back(d_normed)
        own_rows = lax.dynamic_slice_in_dim(d_rows, tensor_at * model_half, model_half, 2)
        input_grads.append((own_rows + cotangent[batch].astype(jnp.float32)).astype(jnp.bfloat16))
        big_terms = (g_inproj, g_outproj, g_statproj, g_stepproj)
        small_terms = (
            lax.dynamic_slice_in_dim(d_prenorm, tensor_at * model_half, model_half, 0),
            d_kernel[:, :inner_local],
            lax.dynamic_slice_in_dim(
                d_kernel[:, inner_local:], tensor_at * state_half, state_half, 1
            ),
            d_param + d_param_tail,
            g_gatenorm,
        )
        shares = add_tree(
            shares,
            (
                lax.psum_scatter(big_terms[0], ("dp", "seq"), scatter_dimension=1, tiled=True),
                lax.psum_scatter(big_terms[1], ("dp", "seq"), scatter_dimension=1, tiled=True),
                lax.psum_scatter(big_terms[2], ("dp", "seq"), scatter_dimension=0, tiled=True),
                lax.psum_scatter(big_terms[3], ("dp", "seq"), scatter_dimension=0, tiled=True),
            ),
        )
        smalls = add_tree(
            smalls,
            lax.psum(
                (small_terms[0], small_terms[1], small_terms[2], small_terms[3], small_terms[4]),
                ("dp", "seq"),
            ),
        )
    big_sq = jnp.sum(jnp.stack([jnp.sum(term * term) for term in shares]))
    small_sq = jnp.sum(jnp.stack([jnp.sum(term * term) for term in smalls]))
    first_owner = jnp.where((data_at == 0) & (seq_at == 0), 1.0, 0.0)
    norm_sq = lax.psum(big_sq + first_owner * small_sq, ("dp", "seq", "tensor"))
    grad_norm = jnp.sqrt(norm_sq)
    heads_all = INNER // HEADDIM
    entries = (
        2 * D * INNER
        + 2 * D * STATE
        + D * heads_all
        + INNER * D
        + (CONV + 1) * (INNER + 2 * STATE)
        + 3 * heads_all
        + INNER
        + D
    )
    limit = CLIP_RMS * math.sqrt(entries)
    factor = limit / jnp.maximum(grad_norm, limit)
    shard_rows = shares[0].shape[1]
    row_start = seq_at * shard_rows
    big_current = (
        lax.dynamic_slice_in_dim(inproj, row_start, shard_rows, 1),
        lax.dynamic_slice_in_dim(outproj, row_start, shard_rows, 1),
        lax.dynamic_slice_in_dim(
            lax.dynamic_slice_in_dim(statproj, row_start, shard_rows, 0),
            tensor_at * state_half,
            state_half,
            1,
        ),
        lax.dynamic_slice_in_dim(stepproj, row_start, shard_rows, 0),
    )
    conv_current = (
        convinner,
        lax.dynamic_slice_in_dim(convstate, tensor_at * state_half, state_half, 1),
    )
    big_moments = (inproj_moment, outproj_moment, statproj_moment, stepproj_moment)
    small_moments = (
        prenorm_moment,
        convinner_moment,
        convstate_moment,
        headparam_moment,
        gatenorm_moment,
    )
    big_new_moments = [
        0.5 * moment_item + 0.5 * factor * grad_item
        for moment_item, grad_item in zip(big_moments, shares)
    ]
    small_new_moments = [
        0.5 * moment_item + 0.5 * factor * grad_item
        for moment_item, grad_item in zip(small_moments, smalls)
    ]
    big_new = [
        (weight_item.astype(jnp.float32) - LEARN * moment_item).astype(weight_item.dtype)
        for weight_item, moment_item in zip(big_current, big_new_moments)
    ]
    conv_new = [
        (weight_item - LEARN * moment_item).astype(weight_item.dtype)
        for weight_item, moment_item in zip(conv_current, small_new_moments[1:3])
    ]
    return (
        jnp.stack(outputs),
        jnp.stack(input_grads),
        grad_norm,
        small_new_moments[0],
        big_new_moments[0],
        big_new_moments[2],
        big_new_moments[3],
        big_new_moments[1],
        small_new_moments[1],
        small_new_moments[2],
        small_new_moments[3],
        small_new_moments[4],
        big_new[0],
        big_new[2],
        big_new[3],
        big_new[1],
        conv_new[0],
        conv_new[1],
    )


BLOCKS = 4
SPAN = 256
PART = 128
PARTS = SPAN // PART
PACKED = 48
LOG2E = 1.4426950408889634
QUARTER = 384
QHEADS = 6
MAPS_AT = 3 * QUARTER
BF = jnp.bfloat16
F32 = jnp.float32
ROUTE_X = [(i, i ^ 1) for i in range(BLOCKS)]
ROUTE_Y = [(i, i ^ 2) for i in range(BLOCKS)]
SWAP = [(0, 1), (1, 0)]
VMEM_LIMIT = 56 * 1024 * 1024


def dot_nn(a, b):
    return lax.dot_general(a, b, (((1,), (0,)), ((), ())), preferred_element_type=F32)


def dot_nt(a, b):
    return lax.dot_general(a, b, (((1,), (1,)), ((), ())), preferred_element_type=F32)


def dot_tn(a, b):
    return lax.dot_general(a, b, (((0,), (0,)), ((), ())), preferred_element_type=F32)


def dot_exact(a, b):
    return lax.dot_general(
        a, b, (((1,), (0,)), ((), ())), precision=HIGH, preferred_element_type=F32
    )


def sigmoid(v):
    return 1.0 / (1.0 + jnp.exp(-v))


def split_sum(triangle, table):
    first = table.astype(BF)
    rest = table - first.astype(F32)
    second = rest.astype(BF)
    third = (rest - second.astype(F32)).astype(BF)
    parts = (
        first.astype(F32)
        + pltpu.roll(second.astype(F32), 8, 1)
        + pltpu.roll(third.astype(F32), 16, 1)
    )
    sums = dot_nn(triangle, parts.astype(BF))
    sums = sums + pltpu.roll(sums, 120, 1) + pltpu.roll(sums, 112, 1)
    lanes = lax.broadcasted_iota(jnp.int32, sums.shape, 1)
    return jnp.where(lanes < 8, sums, 0.0)


def head_sums(table, gather):
    first = table.astype(BF)
    second = (table - first.astype(F32)).astype(BF)
    return dot_nn(first, gather) + dot_nn(second, gather)


def head_spread():
    lane = lax.broadcasted_iota(jnp.int32, (128, QUARTER), 0)
    chan = lax.broadcasted_iota(jnp.int32, (128, QUARTER), 1)
    base = jnp.where(lane < 8, lane, jnp.where(lane < 16, lane - 8, -1)) * HEADDIM
    return jnp.where((chan >= base) & (chan < base + HEADDIM) & (base >= 0), 1.0, 0.0).astype(BF)


def spread_heads(tables, spread):
    packed = []
    for table in tables:
        lanes = lax.broadcasted_iota(jnp.int32, table.shape, 1)
        table = jnp.where(lanes < 8, table, 0.0)
        first = table.astype(BF).astype(F32)
        packed.append((first + pltpu.roll(table - first, 8, 1)).astype(BF))
    wide = dot_nn(jnp.concatenate(packed, axis=0), spread)
    return [wide[PART * k : PART * (k + 1)] for k in range(len(tables))]


def rates(raw, head):
    shifted_raw = raw + head[0:1]
    step = jnp.maximum(shifted_raw, 0.0) + jnp.log1p(jnp.exp(-jnp.abs(shifted_raw)))
    lanes = lax.broadcasted_iota(jnp.int32, raw.shape, 1)
    return shifted_raw, jnp.where(lanes < QHEADS, step, 0.0)


def triangle(keep):
    rows_at = lax.broadcasted_iota(jnp.int32, (PART, PART), 0)
    cols_at = lax.broadcasted_iota(jnp.int32, (PART, PART), 1)
    return jnp.where(keep(rows_at, cols_at), 1.0, 0.0).astype(BF)


def part_terms(step, head, cols, segr, lower):
    cum = split_sum(lower, -step * head[1:2]) * LOG2E
    last = cum[PART - 1 : PART]
    enter = jnp.exp2(cum) * cols[:, 4:5]
    leave = jnp.exp2(last - cum) * cols[:, 5:6]
    passing = jnp.exp2(last) * cols[PART - 1 : PART, 4:5]
    rows_at = lax.broadcasted_iota(jnp.int32, (PART, PART), 0)
    cols_at = lax.broadcasted_iota(jnp.int32, (PART, PART), 1)
    allowed = (rows_at >= cols_at) & (cols[:, 6:7] == segr)
    return cum, enter, leave, passing, jnp.where(allowed, 0.0, -1e30)


def head_decay(cum, cum_t, h, block_out):
    return jnp.exp2(cum[:, h : h + 1] - cum_t[h : h + 1] + block_out)


def by_head(table, low_half):
    zero = jnp.zeros_like(table)
    return jnp.concatenate(
        [jnp.where(low_half, table, zero), jnp.where(low_half, zero, table)], axis=0
    )


def pass_state(passing, state, added):
    heads = [slice(HEADDIM * h, HEADDIM * (h + 1)) for h in range(QHEADS)]
    return jnp.concatenate(
        [passing[:, h : h + 1] * state[at] + added[at] for h, at in enumerate(heads)], axis=0
    )


def segment_flags(seg_ref, q, block):
    begin = pl.multiple_of(block * SPAN, 128)
    around = seg_ref[q, :, pl.ds(begin, SPAN + 256)]
    here = around[:, 128 : 128 + SPAN]
    flags = []
    for shift in (3, 2, 1, 0):
        flags.append(pltpu.roll(around, shift, 1)[:, 128 : 128 + SPAN] == here)
    ends = [around[:, PART * k + 127 : PART * k + 128] for k in range(PARTS + 1)]
    parts = [here[:, PART * k : PART * (k + 1)] for k in range(PARTS)]
    flags.append(jnp.concatenate([parts[k] == ends[k] for k in range(PARTS)], axis=1))
    flags.append(jnp.concatenate([parts[k] == ends[k + 1] for k in range(PARTS)], axis=1))
    for shift in (3, 2, 1, 0):
        later = pltpu.roll(around, SPAN + 256 - shift, 1) if shift else around
        flags.append(later[:, 128 : 128 + SPAN] == here)
    flags = [jnp.where(flag, 1.0, 0.0) for flag in flags]
    at = lax.broadcasted_iota(jnp.int32, (8, SPAN), 0)
    first = here
    for row in range(6):
        first = jnp.where(at == row, flags[row], first)
    second = flags[9]
    for row in range(3):
        second = jnp.where(at == row, flags[6 + row], second)
    return jnp.concatenate([first, second], axis=0)


def to_columns(rows):
    filled = jnp.concatenate([rows, jnp.zeros((128 - rows.shape[0], SPAN), F32)], axis=0)
    return filled.T


def both_tokens(own_ref, other_ref):
    return jnp.concatenate([own_ref[0], other_ref[0]], axis=0)


def fwd_pieces(place_ref, *refs):
    own_out, other_out, held, sems = refs[20:24]
    tokens = block_rows(refs[:10], place_ref, held, sems)
    own_out[0] = tokens[:SPAN]
    other_out[0] = tokens[SPAN:]
    fwd_step(tokens, *refs[10:20], *refs[24:])


def fwd_blocks(place_ref, own_ref, other_ref, *refs):
    fwd_step(both_tokens(own_ref, other_ref), *refs)


def fwd_step(
    tokens, w_ref, seg_ref, taps_ref, head_ref, chan_ref,
    mixed_ref, raw_ref, pre_ref, y_ref, hin_ref, *more,
):
    buf, state = more[-2:]
    block = pl.program_id(0)

    @pl.when(block == 0)
    def _():
        buf[:, 0:8] = jnp.zeros((2, 8, buf.shape[2]), F32)
        state[...] = jnp.zeros_like(state)

    width = QUARTER + 2 * STATE
    projected = dot_nn(tokens, w_ref[...])
    taps = taps_ref[...]
    head = head_ref[...]
    skip = chan_ref[1:2]
    lower = triangle(lambda r, c: r >= c)
    spread = head_spread()
    low_half = lax.broadcasted_iota(jnp.int32, (PART, 128), 1) < HEADDIM
    pieces = []
    for q in range(2):
        rows_q = slice(q * SPAN, (q + 1) * SPAN)
        raw = projected[rows_q, width:]
        raw_ref[q, 0] = raw
        mixed_low = projected[rows_q, :width].astype(BF)
        mixed_ref[q, 0] = mixed_low
        mixed = mixed_low.astype(F32)
        buf[q, 8 : 8 + SPAN] = mixed
        rows = segment_flags(seg_ref, q, block)
        cols_all = to_columns(rows)
        pre = jnp.broadcast_to(taps[CONV : CONV + 1], mixed.shape)
        for j in range(CONV):
            window = mixed if j == CONV - 1 else buf[q, 5 + j : 5 + j + SPAN]
            pre = pre + taps[j : j + 1] * (window * cols_all[:, j : j + 1])
        buf[q, 0:8] = mixed[SPAN - 8 :]
        pre_ref[q, 0] = pre
        act = pre * sigmoid(pre)
        _, step_all = rates(raw, head)
        for part in range(PARTS):
            at_rows = slice(part * PART, (part + 1) * PART)
            cols = cols_all[at_rows]
            cum, enter, leave, passing, block_out = part_terms(
                step_all[at_rows], head, cols, rows[6:7, at_rows], lower
            )
            pieces.append(
                (q, part, act[at_rows], step_all[at_rows], cum, enter, leave, passing, block_out)
            )
    work = []
    for q, part, act, step, cum, enter, leave, passing, block_out in pieces:
        values = act[:, :QUARTER]
        b_low = act[:, QUARTER : QUARTER + STATE].astype(BF)
        c_low = act[:, QUARTER + STATE :].astype(BF)
        step_w, enter_w, leave_w = spread_heads((step, enter, leave), spread)
        cum_t = cum.T
        scores = dot_nt(c_low, b_low)
        scaled = (step_w * values).astype(BF)
        tail = (leave_w * scaled.astype(F32)).astype(BF)
        added = dot_tn(tail, b_low)
        own = []
        for k in range(QHEADS // 2):
            at = slice(128 * k, 128 * (k + 1))
            weights = [
                (scores * head_decay(cum, cum_t, h, block_out)).astype(BF)
                for h in (2 * k, 2 * k + 1)
            ]
            own.append(dot_nn(jnp.concatenate(weights, axis=1), by_head(scaled[:, at], low_half)))
        own = jnp.concatenate(own, axis=1) + skip * values
        work.append((q, part, c_low, enter_w, passing, added, own))
    for q, part, c_low, enter_w, passing, added, own in sorted(work, key=lambda item: item[1]):
        held_f = state[q]
        held = held_f.astype(BF)
        hin_ref[q, 0, QUARTER * part : QUARTER * (part + 1)] = held
        y_ref[q, 0, part * PART : (part + 1) * PART] = own + enter_w * dot_nt(c_low, held)
        state[q] = pass_state(passing, held_f, added)


def piece_copies(refs, m, slot, held, sems):
    half = SPAN // 2
    for q in range(2):
        pieces = refs[5 * q : 5 * (q + 1)]
        own, by_x, by_y, far_a, far_b = pieces if m is None else [ref.at[m] for ref in pieces]
        if slot < 3:
            at = pl.ds(q * SPAN, SPAN)
            source = (own, by_x, by_y)[slot]
            yield pltpu.make_async_copy(source, held.at[slot, at], sems.at[slot, q, 0])
        else:
            for part, source in enumerate((far_a, far_b)):
                at = pl.ds(q * SPAN + part * half, half)
                yield pltpu.make_async_copy(source, held.at[slot, at], sems.at[slot, q, part])


def start_pieces(refs, m, held, sems):
    @pl.when(pl.program_id(0) == 0)
    def _():
        for slot in range(BLOCKS):
            for copy in piece_copies(refs, m, slot, held, sems):
                copy.start()


def wait_slot(refs, m, held, sems, first_step):
    for slot in range(BLOCKS):
        @pl.when(pl.program_id(0) == first_step + slot)
        def _():
            for copy in piece_copies(refs, m, slot, held, sems):
                copy.wait()


def block_rows(refs, place_ref, held, sems):
    start_pieces(refs, None, held, sems)

    @pl.when(pl.program_id(0) == 0)
    def _():
        for slot in range(BLOCKS):
            for copy in piece_copies(refs, None, slot, held, sems):
                copy.wait()

    return held[pl.program_id(0) ^ place_ref[1]]


def cot_scratch():
    return [pltpu.VMEM((BLOCKS, 2 * SPAN, D), BF), pltpu.SemaphoreType.DMA((BLOCKS, 2, 2))]


def core_rows(place_ref):
    half = D // 2
    core = place_ref[0]
    own = pl.multiple_of(core * half, half)
    other = pl.multiple_of((1 - core) * half, half)
    return pl.ds(own, half), pl.ds(other, half)


def stat_rows(row, column):
    lanes = lax.broadcasted_iota(jnp.int32, (SPAN, 128), 1)
    return jnp.where(lanes == row, column, 0.0).T[0:2]


def gate_kernel(place_ref, *refs):
    tokens, y_refs, (w_gate_ref, w_out_ref, chan_ref) = (refs[0:2], refs[2:4]), refs[4:6], refs[6:9]
    gate_refs, gun_refs, mine_refs, theirs_refs, stat_refs = [
        refs[at : at + 2] for at in range(9, 19, 2)
    ]
    step = pl.program_id(0)

    def one_block(m):
        gate = dot_nn(both_tokens(*tokens[m]), w_gate_ref[...])
        guns = []
        for q in range(2):
            gate_q = gate[q * SPAN : (q + 1) * SPAN]
            gate_refs[m][q, 0] = gate_q
            gated_in = y_refs[m][q, 0] * (gate_q * sigmoid(gate_q))
            gun = (gated_in * chan_ref[0:1]).astype(BF)
            gun_refs[m][q, 0] = gun
            guns.append(gun)
            square = jnp.sum(gated_in * gated_in, axis=1, keepdims=True)
            stat_refs[m][q, 0] = stat_rows(0, square)
        gun = jnp.concatenate(guns, axis=0)
        own, other = core_rows(place_ref)
        mine = dot_nt(gun, w_out_ref[own]).astype(BF)
        theirs = dot_nt(gun, w_out_ref[other]).astype(BF)
        for q in range(2):
            mine_refs[m][0, q] = mine[q * SPAN : (q + 1) * SPAN]
            theirs_refs[m][0, 1 - q] = theirs[q * SPAN : (q + 1) * SPAN]

    for m in range(2):
        @pl.when((step >= m * BLOCKS) & (step < (m + 1) * BLOCKS))
        def _():
            one_block(m)


def cross_kernel(place_ref, *refs):
    cots, refs = (refs[0:10], refs[0:10]), refs[10:]
    gun_refs, w_out_ref, d_gated_refs, stat_refs = refs[0:2], refs[2], refs[3:5], refs[5:7]
    held_0, sems_0, held_1, sems_1 = refs[7:]
    step = pl.program_id(0)
    start_pieces(cots[0], 0, held_0, sems_0)
    start_pieces(cots[1], 1, held_1, sems_1)

    def one_block(m, held):
        d_gated = dot_nn(held[step - m * BLOCKS], w_out_ref[...])
        for q in range(2):
            d_gated_q = d_gated[q * SPAN : (q + 1) * SPAN]
            d_gated_refs[m][q, 0] = d_gated_q
            cross = d_gated_q * gun_refs[m][q, 0].astype(F32)
            stat_refs[m][q, 0] = stat_rows(1, jnp.sum(cross, axis=1, keepdims=True))

    for m, held, sems in ((0, held_0, sems_0), (1, held_1, sems_1)):
        wait_slot(cots[m], m, held, sems, m * BLOCKS)

        @pl.when((step >= m * BLOCKS) & (step < (m + 1) * BLOCKS))
        def _():
            one_block(m, held)


def start_sums(total, seed_ref):
    @pl.when(pl.program_id(0) == 0)
    def _():
        total[...] = jnp.zeros_like(total) if seed_ref is None else seed_ref[...]


def finish_sums(total, out_ref):
    @pl.when(pl.program_id(0) == BLOCKS - 1)
    def _():
        rows_of = out_ref.shape[2]
        for z in range(out_ref.shape[0]):
            out_ref[z] = total[:, z * rows_of : (z + 1) * rows_of].astype(BF)


def gate_back_kernel(place_ref, *refs):
    tokens, refs = (refs[0:2], refs[2:4]), refs[4:]
    cots, refs = (refs[0:10], refs[0:10]), refs[10:]
    y_refs, gate_refs, d_gated_refs, stat_refs = refs[0:2], refs[2:4], refs[4:6], refs[6:8]
    chan_ref, dy_refs, d_gate_refs = refs[8], refs[9:11], refs[11:13]
    g_gain_ref, parts_ref, held_0, sems_0, held_1, sems_1, total = refs[13:]
    step = pl.program_id(0)

    @pl.when(step == 0)
    def _():
        total[...] = jnp.zeros_like(total)
        g_gain_ref[...] = jnp.zeros_like(g_gain_ref)

    start_pieces(cots[0], 0, held_0, sems_0)
    start_pieces(cots[1], 1, held_1, sems_1)

    def one_block(m, held):
        gateds = []
        d_gates = []
        for q in range(2):
            stat = to_columns(stat_refs[m][q, 0])
            scale = lax.rsqrt(stat[:, 0:1] * (1.0 / INNER) + EPS)
            pull = stat[:, 1:2] * (1.0 / INNER) * scale * scale * scale
            gate = gate_refs[m][q, 0]
            y = y_refs[m][q, 0]
            d_gated = d_gated_refs[m][q, 0]
            sigma = sigmoid(gate)
            gate_act = gate * sigma
            gated_in = y * gate_act
            scaled_gain = chan_ref[0:1] * scale
            d_in = d_gated * scaled_gain - gated_in * pull
            dy_refs[m][q, 0] = (d_in * gate_act).astype(BF)
            d_gate = (d_in * y * (sigma + gate_act * (1.0 - sigma))).astype(BF)
            d_gate_refs[m][q, 0] = d_gate
            d_gates.append(d_gate)
            gateds.append((gated_in * scaled_gain).astype(BF))
            g_gain_ref[0:1] += jnp.sum(d_gated * gated_in * scale, axis=0, keepdims=True)
        gated = jnp.concatenate(gateds, axis=0)
        d_gate = jnp.concatenate(d_gates, axis=0)
        total[:QUARTER] += dot_tn(gated, held[step - m * BLOCKS])
        total[QUARTER:] += dot_tn(d_gate, both_tokens(*tokens[m]))

    for m, held, sems in ((0, held_0, sems_0), (1, held_1, sems_1)):
        wait_slot(cots[m], m, held, sems, m * BLOCKS)

        @pl.when((step >= m * BLOCKS) & (step < (m + 1) * BLOCKS))
        def _():
            one_block(m, held)

    @pl.when(step == 2 * BLOCKS - 1)
    def _():
        rows_of = parts_ref.shape[2]
        for z in range(parts_ref.shape[0]):
            parts_ref[z] = total[:, z * rows_of : (z + 1) * rows_of].astype(BF)


def bwd_first(*refs):
    bwd_step(*refs[:16], None, refs[16], None, None, *refs[17:])


def bwd_last(*refs):
    total = refs[-1]
    bwd_step(*refs[:17], total, *refs[18:-1])
    finish_sums(total, refs[17])


def bwd_step(
    place_ref, own_ref, other_ref, mixed_ref, pre_ref, raw_ref, y_ref, hin_ref, dy_ref,
    d_gate_ref, seg_ref, taps_ref, head_ref, chan_ref, w_ref, w_gate_ref,
    seed_ref,
    g_ref, keep_ref, give_ref, slope_ref, gtap_ref, ghead_ref, mine_ref, theirs_ref,
    buf, d_state, bc_edge, slope_edge, d_late,
):
    start_sums(g_ref, seed_ref)
    block = BLOCKS - 1 - pl.program_id(0)

    @pl.when(pl.program_id(0) == 0)
    def _():
        buf[:, SPAN:] = jnp.zeros((2, 8, QUARTER), F32)
        d_state[...] = jnp.zeros_like(d_state)
        bc_edge[...] = jnp.zeros_like(bc_edge)
        slope_edge[...] = jnp.zeros_like(slope_edge)
        gtap_ref[...] = jnp.zeros_like(gtap_ref)
        ghead_ref[...] = jnp.zeros_like(ghead_ref)

    head = head_ref[...]
    taps = taps_ref[...]
    skip = chan_ref[1:2]
    first_core = place_ref[0] == 0
    low_half = lax.broadcasted_iota(jnp.int32, (PART, 128), 1) < HEADDIM
    chan_at = lax.broadcasted_iota(jnp.int32, (QUARTER, 128), 0)
    head_at = lax.broadcasted_iota(jnp.int32, (QUARTER, 128), 1)
    gather = jnp.where(
        (chan_at >= head_at * HEADDIM) & (chan_at < (head_at + 1) * HEADDIM), 1.0, 0.0
    )
    gather_low = gather.astype(BF)
    lower = triangle(lambda r, c: r >= c)
    upper = triangle(lambda r, c: r <= c)
    spread = head_spread()

    def store(ref, q, first_row, rows):
        if keep_ref is not None:
            ref[0, q, first_row : first_row + rows.shape[0]] = rows
            return
        for at in range(first_row, first_row + rows.shape[0], 16):
            group = at // PACKED
            row = SPAN + at % PACKED
            ref[0, q, row : row + 16, 128 * group : 128 * (group + 1)] = rows[
                at - first_row : at - first_row + 16
            ]

    keep_at = mine_ref if keep_ref is None else keep_ref
    give_at = theirs_ref if give_ref is None else give_ref
    pieces = []
    columns = []
    slopes = []
    for q in range(2):
        rows = segment_flags(seg_ref, q, block)
        cols_all = to_columns(rows)
        columns.append(cols_all)
        pre = pre_ref[q, 0]
        sigma = sigmoid(pre)
        act = pre * sigma
        slope = sigma * (1.0 + pre * (1.0 - sigma))
        slopes.append(slope)
        slope_half = jnp.where(
            first_core, slope[:, QUARTER : QUARTER + STATE], slope[:, QUARTER + STATE :]
        )
        slope_ref[q, 0, 0:SPAN] = slope_half
        slope_ref[q, 0, SPAN : SPAN + 16] = slope_edge[q]
        slope_edge[q] = slope_half[0:16]
        if keep_ref is None:
            for ref in (mine_ref, theirs_ref):
                ref[0, q, SPAN + 32 :, 640:] = jnp.zeros((16, 128), BF)
        store(keep_at, q, SPAN, bc_edge[q, :, :STATE].astype(BF))
        store(give_at, 1 - q, SPAN, bc_edge[q, :, STATE:].astype(BF))
        shifted_all, step_all = rates(raw_ref[q, 0], head)
        for part in range(PARTS):
            at_rows = slice(part * PART, (part + 1) * PART)
            terms = part_terms(
                step_all[at_rows], head, cols_all[at_rows], rows[6:7, at_rows], lower
            )
            pieces.append((q, part, act[at_rows], shifted_all[at_rows], step_all[at_rows], terms))
    work = []
    for q, part, act, shifted_raw, step, terms in pieces:
        cum, enter, leave, passing, block_out = terms
        values = act[:, :QUARTER]
        b_low = act[:, QUARTER : QUARTER + STATE].astype(BF)
        c_low = act[:, QUARTER + STATE :].astype(BF)
        step_w, enter_w, leave_w = spread_heads((step, enter, leave), spread)
        cum_t = cum.T
        scores = dot_nt(c_low, b_low)
        dy_low = dy_ref[q, 0, part * PART : (part + 1) * PART]
        scaled = (step_w * values).astype(BF)
        tail = (leave_w * scaled.astype(F32)).astype(BF)
        enter_dy = (enter_w * dy_low.astype(F32)).astype(BF)
        d_scores = jnp.zeros((PART, PART), F32)
        own = []
        for k in range(QHEADS // 2):
            at = slice(128 * k, 128 * (k + 1))
            dy_both = by_head(dy_low[:, at], low_half)
            d_weights = dot_nt(dy_both, scaled[:, at])
            weights = []
            for half, h in enumerate((2 * k, 2 * k + 1)):
                decay = head_decay(cum, cum_t, h, block_out)
                weights.append((scores * decay).astype(BF))
                d_scores = d_scores + d_weights[half * PART : (half + 1) * PART] * decay
            own.append(dot_tn(jnp.concatenate(weights, axis=0), dy_both))
        own = jnp.concatenate(own, axis=1)
        d_scores = d_scores.astype(BF)
        new_state = dot_tn(enter_dy, c_low)
        d_c = dot_nn(d_scores, b_low)
        d_b = dot_tn(d_scores, c_low)
        work.append(
            (q, part, values, b_low, shifted_raw, step, step_w, leave_w, passing, dy_low, scaled,
             tail, enter_dy, own, new_state, d_b, d_c)
        )
    for item in sorted(work, key=lambda item: -item[1]):
        (q, part, values, b_low, shifted_raw, step, step_w, leave_w, passing, dy_low, scaled,
         tail, enter_dy, own, new_state, d_b, d_c) = item
        at_rows = slice(part * PART, (part + 1) * PART)
        held = hin_ref[q, 0, QUARTER * part : QUARTER * (part + 1)]
        dy = dy_low.astype(F32)
        scaled_f = scaled.astype(F32)
        d_after = d_state[q]
        d_after_low = d_after.astype(BF)
        tail_part = leave_w * dot_nt(b_low, d_after_low)
        d_scaled = own + tail_part
        d_c = d_c + dot_nn(enter_dy, held)
        d_b = d_b + dot_nn(tail, d_after_low)
        d_state[q] = pass_state(passing, d_after, new_state)
        kept_half = jnp.where(first_core, d_b, d_c)
        given_half = jnp.where(first_core, d_c, d_b)
        store(keep_at, q, part * PART, kept_half.astype(BF))
        store(give_at, 1 - q, part * PART, given_half.astype(BF))
        if part == 0:
            bc_edge[q, :, :STATE] = kept_half[0:16]
            bc_edge[q, :, STATE:] = given_half[0:16]
        d_values = step_w * d_scaled + skip * dy
        buf[q, at_rows] = d_values * slopes[q][at_rows, :QUARTER]
        by_values = dot_nn((values * d_scaled).astype(BF), gather_low)
        y_part = y_ref[q, 0, at_rows] - skip * values
        d_cum = head_sums(dy * y_part - scaled_f * d_scaled, gather_low)
        tail_row = jnp.sum(scaled_f * tail_part, axis=0, keepdims=True)
        tail_sum = dot_exact(jnp.broadcast_to(tail_row, (8, QUARTER)), gather)[0:1]
        state_dot = jnp.sum(d_after * held.astype(F32), axis=1, keepdims=True)
        state_terms = jnp.sum(state_dot * gather, axis=0, keepdims=True)
        d_rate = split_sum(upper, d_cum) + tail_sum + passing * state_terms
        d_raw = (by_values - head[1:2] * d_rate) * sigmoid(shifted_raw)
        ghead_ref[0:1, :128] += jnp.sum(d_raw, axis=0, keepdims=True)
        ghead_ref[1:2, :128] += jnp.sum(-step * head[1:2] * d_rate, axis=0, keepdims=True)
        ghead_ref[2:3] += jnp.sum(values * dy, axis=0, keepdims=True)
        d_late[q * SPAN + part * PART : q * SPAN + (part + 1) * PART, QUARTER:] = d_raw.astype(BF)
    for q in range(2):
        mixed = mixed_ref[q, 0, :, :QUARTER].astype(F32)
        d_mixed = jnp.zeros((SPAN, QUARTER), F32)
        for j in range(CONV):
            ahead = CONV - 1 - j
            window = buf[q, ahead : ahead + SPAN] * columns[q][:, 8 + j : 9 + j]
            d_mixed = d_mixed + taps[j : j + 1, :QUARTER] * window
            gtap_ref[j : j + 1] += jnp.sum(mixed * window, axis=0, keepdims=True)
        gtap_ref[CONV : CONV + 1] += jnp.sum(buf[q, 0:SPAN], axis=0, keepdims=True)
        buf[q, SPAN:] = buf[q, 0:8]
        d_late[q * SPAN : (q + 1) * SPAN, :QUARTER] = d_mixed.astype(BF)
    late = d_late[...]
    g_ref[...] += dot_tn(late, both_tokens(own_ref, other_ref))[: QUARTER + 16]
    d_gate = jnp.concatenate([d_gate_ref[0, 0], d_gate_ref[1, 0]], axis=0)
    grads = jnp.concatenate([late, d_gate], axis=1)
    width = QUARTER + 2 * STATE
    for rows_at, out_ref, flip in zip(core_rows(place_ref), (mine_ref, theirs_ref), (0, 1)):
        weights = [w_ref[rows_at, :QUARTER], w_ref[rows_at, width:], w_gate_ref[rows_at]]
        total = dot_nt(grads, jnp.concatenate(weights, axis=1)).astype(BF)
        for q in range(2):
            out_ref[0, q ^ flip, :SPAN] = total[q * SPAN : (q + 1) * SPAN]


def slot_spec(rows, width, order):
    return pl.BlockSpec((2, 1, rows, width), lambda j, place: (0, order(j), 0, 0))


def segment_spec():
    return pl.BlockSpec((2, 8, BLOCKS * SPAN + 256), lambda j, place: (0, 0, 0))


def fixed_spec(rows, width):
    return pl.BlockSpec((rows, width), lambda j, place: (0, 0))


def out_shape(rows, cols_of, kind):
    return jax.ShapeDtypeStruct((2, BLOCKS, rows, cols_of), kind)


def upward(j):
    return j


def downward(j):
    return BLOCKS - 1 - j


def token_specs(order):
    return [pl.BlockSpec((1, SPAN, D), lambda j, place: (order(j), 0, 0))] * 2


def call_blocks(kernel, name, place, operands, in_specs, outs, scratch=(), steps=BLOCKS):
    return pl.pallas_call(
        kernel,
        grid_spec=pltpu.PrefetchScalarGridSpec(
            num_scalar_prefetch=1,
            grid=(steps,),
            in_specs=in_specs,
            out_specs=[spec for spec, _ in outs],
            scratch_shapes=list(scratch),
        ),
        out_shape=[shape for _, shape in outs],
        compiler_params=pltpu.CompilerParams(vmem_limit_bytes=VMEM_LIMIT),
        cost_estimate=pl.CostEstimate(flops=1024, bytes_accessed=1024, transcendentals=0),
        name=name,
    )(place, *operands)


def slot_out(rows, width, kind, order):
    return slot_spec(rows, width, order), out_shape(rows, width, kind)


def lead_out(rows, width, order):
    shape = jax.ShapeDtypeStruct((BLOCKS, 2, rows, width), BF)
    return pl.BlockSpec((1, 2, rows, width), lambda j, place: (order(j), 0, 0, 0)), shape


def fixed_out(rows, width):
    return fixed_spec(rows, width), jax.ShapeDtypeStruct((rows, width), F32)


def run_fwd(place, tokens, w_first, segs, taps, head, chan):
    width = QUARTER + 2 * STATE
    pieces = len(tokens) > 2
    outs = [
        slot_out(SPAN, width, BF, upward),
        slot_out(SPAN, 128, F32, upward),
        slot_out(SPAN, width, F32, upward),
        slot_out(SPAN, QUARTER, F32, upward),
        slot_out(PARTS * QUARTER, STATE, BF, upward),
    ]
    if pieces:
        shape = jax.ShapeDtypeStruct((BLOCKS, SPAN, D), BF)
        outs += [(spec, shape) for spec in token_specs(upward)]
    return call_blocks(
        fwd_pieces if pieces else fwd_blocks,
        "mix_forward",
        place,
        (*tokens, w_first, segs, taps, head, chan),
        [
            *(cot_specs() if pieces else token_specs(upward)),
            fixed_spec(D, width + 128),
            segment_spec(),
            fixed_spec(8, width),
            fixed_spec(8, 128),
            fixed_spec(8, QUARTER),
        ],
        outs,
        (cot_scratch() if pieces else [])
        + [pltpu.VMEM((2, SPAN + 8, width), F32), pltpu.VMEM((2, QUARTER, STATE), F32)],
    )


def cot_specs():
    return [pl.BlockSpec(memory_space=pl.ANY)] * 10


def run_gate(place, tokens, y, w_gate, w_out, chan):
    both = range(2)
    wide = slot_spec(SPAN, QUARTER, upward)
    lead, lead_shape = lead_out(SPAN, D // 2, upward)
    rows = slot_spec(2, SPAN, upward)
    kinds = (
        (wide, out_shape(SPAN, QUARTER, F32)),
        (wide, out_shape(SPAN, QUARTER, BF)),
        (lead, lead_shape),
        (lead, lead_shape),
        (rows, out_shape(2, SPAN, F32)),
    )
    return call_blocks(
        gate_kernel,
        "gate_forward",
        place,
        (*tokens[0], *tokens[1], *y, w_gate, w_out, chan),
        [
            *[in_half(spec, m) for m in both for spec in token_specs(upward)],
            *[in_half(wide, m) for m in both],
            fixed_spec(D, QUARTER),
            fixed_spec(D, QUARTER),
            fixed_spec(8, QUARTER),
        ],
        [(in_half(spec, m), shape) for spec, shape in kinds for m in both],
        steps=2 * BLOCKS,
    )


def run_cross(place, cots, gun, w_out):
    both = range(2)
    wide = slot_spec(SPAN, QUARTER, upward)
    rows = slot_spec(2, SPAN, upward)
    return call_blocks(
        cross_kernel,
        "cross_forward",
        place,
        (*cots, *gun, w_out),
        [*cot_specs(), *[in_half(wide, m) for m in both], fixed_spec(D, QUARTER)],
        [(in_half(wide, m), out_shape(SPAN, QUARTER, F32)) for m in both]
        + [(in_half(rows, m), out_shape(2, SPAN, F32)) for m in both],
        cot_scratch() + cot_scratch(),
        steps=2 * BLOCKS,
    )


def sums_out(rows, dp_count, last):
    if not last:
        return fixed_out(rows, D), []
    share = D // dp_count
    spec = pl.BlockSpec((dp_count, rows, share), lambda j, place: (0, 0, 0))
    out = spec, jax.ShapeDtypeStruct((dp_count, rows, share), BF)
    return out, [pltpu.VMEM((rows, D), F32)]


def in_half(spec, m):
    def index(j, place):
        slot = jnp.minimum(j, BLOCKS - 1) if m == 0 else jnp.maximum(j - BLOCKS, 0)
        return spec.index_map(slot ^ place[1], place)

    return pl.BlockSpec(spec.block_shape, index)


def run_gate_back(place, tokens, cots, y, gate, d_gated, stat, chan, dp_count):
    (parts_spec, parts_shape), total = sums_out(2 * QUARTER, dp_count, True)
    both = range(2)
    wide = slot_spec(SPAN, QUARTER, upward)
    outs = [
        (in_half(wide, m), out_shape(SPAN, QUARTER, BF)) for _ in range(2) for m in both
    ]
    return call_blocks(
        gate_back_kernel,
        "gate_backward",
        place,
        (*tokens[0], *tokens[1], *cots, *y, *gate, *d_gated, *stat, chan),
        [
            *[in_half(spec, m) for m in both for spec in token_specs(upward)],
            *cot_specs(),
            *[in_half(wide, m) for _ in range(3) for m in both],
            *[in_half(slot_spec(2, SPAN, upward), m) for m in both],
            fixed_spec(8, QUARTER),
        ],
        outs + [fixed_out(8, QUARTER), (parts_spec, parts_shape)],
        cot_scratch() + cot_scratch() + total,
        steps=2 * BLOCKS,
    )


def run_bwd(place, tokens, kept, dy, d_gate, rows, taps, head, chan, weights, seed, dp_count):
    mixed, raw, pre, y, hin = kept
    width = mixed.shape[-1]
    states = 2 * STATE
    half = D // 2
    last = seed is not None
    total, scratch = sums_out(QUARTER + 16, dp_count, last)
    rows_out = SPAN if last else SPAN + PACKED
    maps_out = [lead_out(SPAN + 16, STATE, downward)] * 2 if last else []
    return call_blocks(
        bwd_last if last else bwd_first,
        "mix_backward",
        place,
        (*tokens, mixed, pre, raw, y, hin, dy, d_gate, rows, taps, head, chan, *weights)
        + ((seed,) if last else ()),
        [
            *token_specs(downward),
            slot_spec(SPAN, width, downward),
            slot_spec(SPAN, width, downward),
            slot_spec(SPAN, 128, downward),
            slot_spec(SPAN, QUARTER, downward),
            slot_spec(PARTS * QUARTER, STATE, downward),
            slot_spec(SPAN, QUARTER, downward),
            slot_spec(SPAN, QUARTER, downward),
            segment_spec(),
            fixed_spec(8, width),
            fixed_spec(8, 128),
            fixed_spec(8, QUARTER),
            fixed_spec(D, width + 128),
            fixed_spec(D, QUARTER),
        ]
        + ([fixed_spec(QUARTER + 16, D)] if last else []),
        [
            total,
            *maps_out,
            slot_out(SPAN + 16, STATE, F32, downward),
            fixed_out(8, QUARTER),
            fixed_out(8, QUARTER),
            lead_out(rows_out, half, downward),
            lead_out(rows_out, half, downward),
        ],
        [
            pltpu.VMEM((2, SPAN + 8, QUARTER), F32),
            pltpu.VMEM((2, QUARTER, STATE), F32),
            pltpu.VMEM((2, 16, states), F32),
            pltpu.VMEM((2, 16, STATE), F32),
            pltpu.VMEM((2 * SPAN, QUARTER + 128), BF),
        ]
        + scratch,
    )


def maps_kernel(
    place_ref, packed_ref, maps_ref, slope_0, slope_1, mixed_0, mixed_1, seg_0, seg_1,
    own_0, other_0, own_1, other_1, taps_ref,
    d_maps_ref, g_ref, g_taps_ref, buf,
):
    chip = place_ref[1]
    taps = taps_ref[...]
    buf[SPAN + 16 :] = jnp.zeros((8, STATE), F32)
    sums = [jnp.zeros((1, STATE), F32) for _ in range(CONV + 1)]
    g_maps = jnp.zeros((STATE, D), F32)
    slopes, mixes, segs = (slope_0, slope_1), (mixed_0, mixed_1), (seg_0, seg_1)
    tokens = ((own_0, other_0), (own_1, other_1))
    for m in range(MB):
        for q in range(2):
            if m == 0:
                total = packed_ref[0, q].astype(F32)
                for src in range(1, BLOCKS):
                    total = total + packed_ref[src, q].astype(F32)
                groups = [total[:, 128 * k : 128 * (k + 1)] for k in range(6)]
                d_conv = jnp.concatenate(groups, axis=0)[: SPAN + 16]
            else:
                d_conv = maps_ref[0, q].astype(F32)
                for src in range(1, BLOCKS):
                    d_conv = d_conv + maps_ref[src, q].astype(F32)
            d_pre = d_conv * slopes[m][q, 0]
            buf[0 : SPAN + 16] = d_pre
            cols = to_columns(segment_flags(segs[m], q, chip))
            mixed = mixes[m][q, 0].astype(F32)
            d_mixed = jnp.zeros((SPAN, STATE), F32)
            for j in range(CONV):
                ahead = CONV - 1 - j
                window = buf[ahead : ahead + SPAN] * cols[:, 8 + j : 9 + j]
                d_mixed = d_mixed + taps[j : j + 1] * window
                sums[j] = sums[j] + jnp.sum(mixed * window, axis=0, keepdims=True)
            sums[CONV] = sums[CONV] + jnp.sum(d_pre[:SPAN], axis=0, keepdims=True)
            low = d_mixed.astype(BF)
            d_maps_ref[m, q] = low
            g_maps = g_maps + dot_tn(low, tokens[m][q][0])
    g_taps_ref[...] = jnp.concatenate(sums + [jnp.zeros((3, STATE), F32)], axis=0)
    rows_of = g_ref.shape[2]
    for z in range(g_ref.shape[0]):
        g_ref[z] = g_maps[:, z * rows_of : (z + 1) * rows_of].astype(BF)


def run_maps(place, packed, maps, slopes, mixes, segs, tokens, taps, dp_count):
    def whole(shape):
        return pl.BlockSpec(shape, lambda i, place: (0,) * len(shape))

    def slope_spec():
        return pl.BlockSpec((2, 1, SPAN + 16, STATE), lambda i, place: (0, place[1], 0, 0))

    def mixed_spec():
        first = QUARTER // STATE
        return pl.BlockSpec(
            (2, 1, SPAN, STATE), lambda i, place: (0, place[1], 0, first + place[0])
        )

    def token_spec():
        return pl.BlockSpec((1, SPAN, D), lambda i, place: (place[1], 0, 0))

    share = D // dp_count
    return pl.pallas_call(
        maps_kernel,
        grid_spec=pltpu.PrefetchScalarGridSpec(
            num_scalar_prefetch=1,
            grid=(1,),
            in_specs=[
                whole(packed.shape),
                whole(maps.shape),
                slope_spec(),
                slope_spec(),
                mixed_spec(),
                mixed_spec(),
                whole(segs[0].shape),
                whole(segs[1].shape),
                token_spec(),
                token_spec(),
                token_spec(),
                token_spec(),
                whole(taps.shape),
            ],
            out_specs=[
                whole((MB, 2, SPAN, STATE)),
                whole((dp_count, STATE, share)),
                whole((8, STATE)),
            ],
            scratch_shapes=[pltpu.VMEM((SPAN + 24, STATE), F32)],
        ),
        out_shape=[
            jax.ShapeDtypeStruct((MB, 2, SPAN, STATE), BF),
            jax.ShapeDtypeStruct((dp_count, STATE, share), BF),
            jax.ShapeDtypeStruct((8, STATE), F32),
        ],
        compiler_params=pltpu.CompilerParams(vmem_limit_bytes=VMEM_LIMIT),
        cost_estimate=pl.CostEstimate(flops=1024, bytes_accessed=1024, transcendentals=0),
        name="maps_backward",
    )(place, packed, maps, *slopes, *mixes, *segs, *tokens, taps)


def norm_kernel(place_ref, share_ref, w_in_ref, w_state_ref, w_step_ref, step_ref, out_ref):
    rows = share_ref.shape[1]
    squares = jnp.zeros((rows, QUARTER), F32)
    products = jnp.zeros((rows, QUARTER), F32)
    for s in range(BLOCKS):
        at = slice(s * QUARTER, (s + 1) * QUARTER)
        out = share_ref[s, :, :QUARTER].astype(F32)
        gate = share_ref[s, :, QUARTER : 2 * QUARTER].astype(F32)
        inner = share_ref[s, :, 2 * QUARTER : 3 * QUARTER].astype(F32)
        squares = squares + out * out + gate * gate + inner * inner
        products = products + gate * w_in_ref[0, :, at].astype(F32)
        products = products + inner * w_in_ref[1, :, at].astype(F32)
    state = share_ref[0, :, MAPS_AT : MAPS_AT + STATE].astype(F32)
    for s in range(1, BLOCKS):
        state = state + share_ref[s, :, MAPS_AT : MAPS_AT + STATE].astype(F32)
    step = step_ref[...]
    by_row = jnp.sum(products, axis=1, keepdims=True)
    by_row = by_row + jnp.sum(state * w_state_ref[...].astype(F32), axis=1, keepdims=True)
    square = jnp.sum(squares, axis=1, keepdims=True) + jnp.sum(state * state, axis=1, keepdims=True)
    lanes = lax.broadcasted_iota(jnp.int32, (rows, 128), 1)
    table = jnp.where(lanes == 0, by_row, jnp.where(lanes == 1, square, 0.0))
    table = jnp.concatenate([table, jnp.zeros((128 - rows, 128), F32)], axis=0).T
    total = jnp.sum(table[1:2], axis=1, keepdims=True)
    total = total + jnp.sum(jnp.sum(step * step, axis=0, keepdims=True), axis=1, keepdims=True)
    by_step = jnp.sum(step * w_step_ref[...].astype(F32), axis=0, keepdims=True)
    by_step = jnp.concatenate([by_step, jnp.zeros((1, 128 - rows), F32)], axis=1)
    at_row = lax.broadcasted_iota(jnp.int32, (8, 128), 0)
    at_lane = lax.broadcasted_iota(jnp.int32, (8, 128), 1)
    first = jnp.where((at_row == 0) & (at_lane == rows), total, table[0:8] + by_step)
    out_ref[...] = jnp.where(at_row == 0, first, 0.0)


def update_kernel(
    place_ref, factor_ref, share_ref, step_ref, w_in_ref, w_out_ref, w_state_ref,
    w_step_ref, m_in_ref, m_out_ref, m_state_ref, m_step_ref,
    new_in_ref, new_out_ref, new_state_ref, new_step_ref,
    next_in_ref, next_out_ref, next_state_ref, next_step_ref,
):
    factor = factor_ref[0, 0]

    def write(new_ref, next_ref, at, moment, grad, weight):
        new = 0.5 * moment + (0.5 * factor) * grad
        new_ref[at] = new
        next_ref[at] = (weight.astype(F32) - LEARN * new).astype(BF)

    for s in range(BLOCKS):
        lanes = slice(s * QUARTER, (s + 1) * QUARTER)
        gate = (0, slice(None), lanes)
        write(
            new_in_ref, next_in_ref, gate, m_in_ref[gate],
            share_ref[s, :, QUARTER : 2 * QUARTER].astype(F32), w_in_ref[gate],
        )
        inner = (1, slice(None), lanes)
        write(
            new_in_ref, next_in_ref, inner, m_in_ref[inner],
            share_ref[s, :, 2 * QUARTER : 3 * QUARTER].astype(F32), w_in_ref[inner],
        )
        out = (slice(None), lanes)
        write(
            new_out_ref, next_out_ref, out, m_out_ref[out],
            share_ref[s, :, :QUARTER].astype(F32), w_out_ref[out],
        )
    state = share_ref[0, :, MAPS_AT : MAPS_AT + STATE].astype(F32)
    for s in range(1, BLOCKS):
        state = state + share_ref[s, :, MAPS_AT : MAPS_AT + STATE].astype(F32)
    write(new_state_ref, next_state_ref, ..., m_state_ref[...], state, w_state_ref[...])
    write(new_step_ref, next_step_ref, ..., m_step_ref[...], step_ref[...], w_step_ref[...])


def owner_specs(rows):
    return [
        pl.BlockSpec((2, rows, BLOCKS * QUARTER), lambda i, place: (0, place[1], 0)),
        pl.BlockSpec((rows, STATE), lambda i, place: (place[1], place[0])),
    ]


def run_owner(kernel, name, place, operands, in_specs, outs):
    return pl.pallas_call(
        kernel,
        grid_spec=pltpu.PrefetchScalarGridSpec(
            num_scalar_prefetch=1, grid=(1,), in_specs=in_specs,
            out_specs=[spec for spec, _ in outs],
        ),
        out_shape=[shape for _, shape in outs],
        compiler_params=pltpu.CompilerParams(vmem_limit_bytes=VMEM_LIMIT),
        cost_estimate=pl.CostEstimate(flops=1024, bytes_accessed=1024, transcendentals=0),
        name=name,
    )(place, *operands)


def swap_cores(block):
    return lax.ppermute(block, "tensor", SWAP)


def over_x(block):
    return lax.ppermute(block, "seq", ROUTE_X)


def over_y(block):
    return lax.ppermute(block, "seq", ROUTE_Y)


def exchange(blocks):
    return lax.all_to_all(blocks, "seq", 0, 0, tiled=True)


def copies(piece):
    return jnp.broadcast_to(piece, (BLOCKS,) + piece.shape)


def add_low(a, b):
    return (a.astype(F32) + b.astype(F32)).astype(BF)


def scatter(blocks):
    return jnp.sum(exchange(blocks).astype(F32), axis=0)


def after(value, *others):
    return lax.optimization_barrier((value, others))[0]


def fast_body(
    inputs,
    segments,
    cotangent,
    prenorm,
    inproj,
    statproj,
    stepproj,
    outproj,
    convinner,
    convstate,
    headparam,
    gatenorm,
    prenorm_moment,
    inproj_moment,
    statproj_moment,
    stepproj_moment,
    outproj_moment,
    convinner_moment,
    convstate_moment,
    headparam_moment,
    gatenorm_moment,
):
    core = lax.axis_index("tensor")
    chip = lax.axis_index("seq")
    data_at = lax.axis_index("dp")
    dp_count = lax.axis_size("dp")
    heads_local = headparam.shape[1]
    rows_local = inproj.shape[1]
    shard = rows_local // BLOCKS
    half_d = D // 2
    place = jnp.stack([core, chip]).astype(jnp.int32)

    def by_core(first, second):
        return jnp.where(core == 0, first, second)

    def quarter(array, axis, width):
        return lax.dynamic_slice_in_dim(array, chip * width, width, axis)

    def all_rows(block):
        return lax.all_gather(block, "dp", axis=0, tiled=True)

    first_block = (
        jnp.concatenate(
            [
                quarter(inproj[1], 1, QUARTER),
                statproj,
                jnp.pad(quarter(stepproj, 1, QHEADS), ((0, 0), (0, 128 - QHEADS))),
            ],
            axis=1,
        )
    )
    inputs, first_block = after((inputs, first_block))
    w_first = all_rows(first_block)
    gate_block = quarter(inproj[0], 1, QUARTER)
    out_block = quarter(outproj, 0, QUARTER).T

    def whole_rows(array):
        mine = lax.dynamic_index_in_dim(array, core, 1, keepdims=False)
        theirs = lax.dynamic_index_in_dim(array, 1 - core, 1, keepdims=False)
        got = swap_cores(theirs)
        return by_core(
            jnp.concatenate([mine, got], axis=2), jnp.concatenate([got, mine], axis=2)
        )

    rows_whole = whole_rows(inputs)
    normed_own = rms_scale(rows_whole.astype(F32), prenorm).astype(BF)
    cot_own = whole_rows(cotangent)
    half = SPAN // 2
    mine_0, second_copies = after((normed_own[0], copies(normed_own[1])))
    near_0 = (mine_0, over_x(mine_0), over_y(mine_0))
    own_swapped = swap_cores(mine_0)

    seg_mine = jnp.concatenate(
        [
            lax.dynamic_index_in_dim(segments, core, 1),
            lax.dynamic_index_in_dim(segments, 1 - core, 1),
        ],
        axis=1,
    )
    seg_pad = jnp.pad(
        seg_mine.astype(F32), ((0, 0), (0, 0), (128, 128)), constant_values=-1.0
    )
    segs = jnp.broadcast_to(seg_pad[:, :, None], seg_pad.shape[:2] + (8, seg_pad.shape[2]))

    taps_inner = quarter(convinner, 1, QUARTER)
    taps = jnp.pad(jnp.concatenate([taps_inner, convstate], axis=1), ((0, 3), (0, 0)))
    head_own = quarter(headparam, 1, QHEADS)
    head = jnp.pad(
        jnp.stack([head_own[0], jnp.exp(head_own[1]), head_own[2]]),
        ((0, 5), (0, 128 - QHEADS)),
    )
    gain = quarter(gatenorm, 0, QUARTER)
    chan = jnp.pad(jnp.stack([gain, jnp.repeat(head_own[2], HEADDIM)]), ((0, 6), (0, 0)))

    def rows_dot_t(left, right):
        return lax.dot_general(left, right, (((3,), (1,)), ((), ())), preferred_element_type=F32)

    def core_sums(mine, theirs):
        return add_low(mine, swap_cores(theirs))

    def over_dp(parts):
        return lax.psum_scatter(parts, "dp", scatter_dimension=0, tiled=True)[0]

    def by_place(columns):
        return columns.T.reshape(BLOCKS, shard, -1)

    def forward(m, place, tokens):
        return run_fwd(place, tokens, w_first, segs[m], taps, head, chan)

    def backward(m, place, dy, d_gate, seed):
        return run_bwd(
            place, normed[m], kept[m], dy, d_gate, segs[m], taps, head, chan,
            (w_first, w_gate), seed, dp_count,
        )

    def summed(blocks):
        return jnp.sum(blocks.astype(F32), axis=0)

    def in_order(block):
        return by_core(block, block[:, ::-1])

    def token_scale(sums):
        own = lax.dynamic_index_in_dim(sums, chip, 1, keepdims=False)
        return lax.rsqrt(own[:, 0] / INNER + EPS)[..., None]

    def sum_dp(value):
        hop = 1
        while hop < dp_count:
            value = value + lax.ppermute(value, "dp", [(i, i ^ hop) for i in range(dp_count)])
            hop *= 2
        return value

    def sum_seq(value):
        value = value + over_x(value)
        return value + over_y(value)

    def with_other(own):
        return own, swap_cores(own)

    stepproj_own = lax.dynamic_slice_in_dim(stepproj.T, chip * shard, shard, 1)
    outproj_own = lax.dynamic_slice_in_dim(outproj, chip * shard, shard, 1).T
    (
        near_0, own_swapped, cot_own, segs, taps, head, chan, stepproj_own, outproj_own, place,
        gate_block, out_block,
    ) = after(
        (
            near_0, own_swapped, cot_own, segs, taps, head, chan, stepproj_own, outproj_own, place,
            gate_block, out_block,
        )
    )
    w_gate = all_rows(gate_block)
    w_out = all_rows(out_block)
    far = over_x(near_0[2][:half]), over_y(near_0[1][half:])
    near_swapped = [swap_cores(piece) for piece in near_0[1:]]
    far, near_swapped, second_copies = after((far, near_swapped, second_copies))
    own_1 = exchange(second_copies)
    far, w_first = after((far, w_first))
    cot_other = swap_cores(cot_own)
    first_pieces = (
        *near_0, *far, own_swapped, *near_swapped, *[swap_cores(piece) for piece in far]
    )
    *kept_0, own_0, other_0 = forward(0, place, first_pieces)
    kept = [kept_0]
    normed = [(own_0, other_0)]
    cot_own, cot_other, place = after((cot_own, cot_other, place), kept[0][1])
    by_x, by_y = over_x(cot_own), over_y(cot_own)
    own_1, w_gate, place = after((own_1, w_gate, place))
    normed.append(with_other(own_1))
    kept.append(forward(1, place, normed[1]))

    by_x, by_y, w_out, place = after((by_x, by_y, w_out, place), kept[1][1])
    far = over_x(by_y[:, :half]), over_y(by_x[:, half:])
    near_other = (cot_other, swap_cores(by_x), swap_cores(by_y))
    gate_0, gate_1, gun_0, gun_1, mine_0, mine_1, theirs_0, theirs_1, stat_0, stat_1 = run_gate(
        place, normed, (kept[0][3], kept[1][3]), w_gate, w_out, chan
    )
    far, near_other, place = after((far, near_other, place), stat_0)
    far_other = [swap_cores(piece) for piece in far]
    far_other, place, theirs_0, theirs_1 = after((far_other, place, theirs_0, theirs_1))
    cots = (cot_own, by_x, by_y, *far, *near_other, *far_other)
    d_gated_0, d_gated_1, cross_0, cross_1 = run_cross(place, cots, (gun_0, gun_1), w_out)
    branch_0 = core_sums(mine_0, theirs_0)

    stats = jnp.stack([stat_0 + cross_0, stat_1 + cross_1])
    stats = after(stats, branch_0)
    stats = stats + swap_cores(stats)[:, ::-1]
    theirs_1 = after(theirs_1, stats)
    sums_0, sums_1 = sum_seq(stats)
    branch_0 = after(branch_0, sums_0)
    layer_0 = exchange(branch_0)
    branch_1 = core_sums(mine_1, theirs_1)
    dy_0, dy_1, d_gate_0, d_gate_1, g_gain, mid_parts = run_gate_back(
        place, normed, cots, (kept[0][3], kept[1][3]), (gate_0, gate_1), (d_gated_0, d_gated_1),
        (sums_0, sums_1), chan, dp_count,
    )

    layer_0, branch_1, place, mid_parts = after((layer_0, branch_1, place, mid_parts), dy_1)
    layer_1 = exchange(branch_1)
    mid_rows = over_dp(mid_parts)
    g_late_0, slope_0, g_taps_0, g_head_0, mine, theirs = backward(0, place, dy_0, d_gate_0, None)

    layer_1, mid_rows, theirs, place = after((layer_1, mid_rows, theirs, place), g_taps_0)
    back_0 = core_sums(mine, theirs)
    layer_out = [
        summed(layer_0) * token_scale(sums_0), summed(layer_1) * token_scale(sums_1)
    ]
    layer_out = (inputs.astype(F32) + in_order(jnp.stack(layer_out))).astype(BF)
    back_0, place, layer_out = after((back_0, place, layer_out))
    token_0 = exchange(back_0)
    late_parts, keep_1, give_1, slope_1, g_taps_1, g_head_1, mine, theirs = backward(
        1, place, dy_1, d_gate_1, g_late_0
    )

    token_0, late_parts, theirs, give_1 = after((token_0, late_parts, theirs, give_1))
    late_rows = over_dp(late_parts)
    maps = core_sums(keep_1, give_1)
    back_1 = core_sums(mine, after(theirs, maps))
    maps = exchange(maps)
    maps, back_1, token_0, mid_rows, g_taps_1 = after(
        (maps, back_1, token_0, mid_rows, g_taps_1)
    )
    token_1 = exchange(back_1)
    taps_state = lax.dynamic_slice_in_dim(convstate, core * STATE, STATE, 1)
    d_maps, g_maps, g_state_taps = run_maps(
        place, token_0[:, :, SPAN:], maps, (slope_0, slope_1), (kept[0][0], kept[1][0]),
        segs, (*normed[0], *normed[1]), jnp.pad(taps_state, ((0, 3), (0, 0))), dp_count,
    )

    def for_dp(hop):
        at = lax.rem(data_at + hop, dp_count)
        return lax.dynamic_index_in_dim(g_maps, at, 0, keepdims=False)

    state_rows = for_dp(0).astype(F32)
    for hop in range(1, dp_count):
        route = [(i, (i + hop) % dp_count) for i in range(dp_count)]
        state_rows = state_rows + lax.ppermute(for_dp(hop), "dp", route).astype(F32)
    state_rows = state_rows.astype(BF)

    inner_local = BLOCKS * QUARTER

    def put(values, width, total):
        base = jnp.zeros(values.shape[:-1] + (total,), F32)
        return lax.dynamic_update_slice_in_dim(base, values, chip * width, values.ndim - 1)

    g_taps, g_head = g_taps_0 + g_taps_1, g_head_0 + g_head_1
    g_heads = jnp.concatenate(
        [g_head[:2, :QHEADS], jnp.sum(g_head[2].reshape(1, QHEADS, HEADDIM), axis=2)], axis=0
    )
    small_parts = [
        put(g_taps[: CONV + 1], QUARTER, inner_local),
        put(g_gain[0], QUARTER, inner_local),
        put(g_heads, QHEADS, heads_local),
        g_state_taps[: CONV + 1],
    ]
    small_shapes = [small.shape for small in small_parts]
    vector = jnp.concatenate([small.reshape(-1) for small in small_parts])
    vector = jnp.pad(vector, (0, -vector.size % 1024)).reshape(-1, 128)

    late_rows, mid_rows, state_rows = after((late_rows, mid_rows, state_rows))
    shares = jnp.concatenate(
        [mid_rows, late_rows[:QUARTER], state_rows, late_rows[QUARTER:]], axis=0
    )
    vector = sum_dp(after(vector, state_rows))
    other_vector = swap_cores(vector)
    token_1, shares, vector, other_vector = after(
        (token_1, by_place(shares), vector, other_vector)
    )
    share = exchange(shares)
    d_tokens = [summed(token_0[:, :, :SPAN]), summed(token_1)]
    w_state = w_first[:, QUARTER : QUARTER + 2 * STATE]

    state_other = swap_cores(d_maps)[:, ::-1]
    state_mine = d_maps
    d_state_both = by_core(
        jnp.concatenate([state_mine, state_other], axis=3),
        jnp.concatenate([state_other, state_mine], axis=3),
    )
    from_state = rows_dot_t(
        d_state_both, lax.dynamic_slice_in_dim(w_state, core * half_d, half_d, 0)
    )

    outputs = layer_out
    d_normed = in_order(jnp.stack(d_tokens) + from_state)
    rows_own = inputs.astype(F32)
    gain_own = lax.dynamic_slice_in_dim(prenorm, core * half_d, half_d, 0)
    weighted = d_normed * gain_own
    pair_sums = jnp.stack(
        [jnp.sum(rows_own * rows_own, axis=-1), jnp.sum(weighted * rows_own, axis=-1)]
    )
    pair_sums = pair_sums + swap_cores(pair_sums)
    root = lax.rsqrt(pair_sums[0] / D + EPS)[..., None]
    input_grads = (
        cotangent.astype(F32)
        + weighted * root
        - rows_own * root * root * root * (pair_sums[1] / D)[..., None]
    ).astype(BF)

    step_at = MAPS_AT + STATE
    step_share = share[:, :, step_at : step_at + QHEADS].astype(F32)
    step_share = jnp.moveaxis(step_share, 1, 2).reshape(heads_local, shard)
    in_spec, state_spec = owner_specs(shard)

    def whole(array):
        return pl.BlockSpec(array.shape, lambda i, place: (0,) * array.ndim)

    def whole_out(shape, kind):
        spec = pl.BlockSpec(shape, lambda i, place: (0,) * len(shape))
        return spec, jax.ShapeDtypeStruct(shape, kind)

    owner_sums = run_owner(
        norm_kernel,
        "owner_norm",
        place,
        (share, inproj, statproj, stepproj_own, step_share),
        [whole(share), in_spec, state_spec, whole(stepproj_own), whole(step_share)],
        [whole_out((8, 128), F32)],
    )[0]
    owner_sums = owner_sums + swap_cores(owner_sums)

    owners = dp_count * BLOCKS
    owner = data_at * BLOCKS + chip
    gain_rows = lax.dynamic_slice_in_dim(prenorm, owner * shard, shard, 0)
    lanes = jnp.arange(128)
    g_prenorm = owner_sums[0] / jnp.pad(gain_rows, (0, 128 - shard), constant_values=1.0)
    g_prenorm = jnp.where(lanes < shard, g_prenorm, 0.0)
    square = owner_sums[0, shard] + jnp.sum(g_prenorm * g_prenorm)
    line = jnp.where(lanes == shard, square, g_prenorm)
    table = jnp.where(jnp.arange(owners)[:, None] == owner, line[None], 0.0)
    table = sum_seq(jnp.concatenate([sum_dp(table), vector, other_vector], axis=0))
    small_sums = []
    start = 0
    both_vectors = table[owners:].reshape(2, -1)
    vector = both_vectors[0]
    for shape in small_shapes:
        size = math.prod(shape)
        small_sums.append(vector[start : start + size].reshape(shape))
        start += size
    s_taps, s_gain, s_head, s_state_taps = small_sums

    small_sq = jnp.sum(both_vectors * both_vectors, axis=1)
    grad_norm = jnp.sqrt(jnp.sum(table[:owners, shard]) + (small_sq[0] + small_sq[1]))
    s_prenorm = lax.dynamic_slice_in_dim(
        table[:owners, :shard], core * (owners // 2), owners // 2, 0
    ).reshape(half_d)

    entries = (
        2 * D * INNER
        + 2 * D * STATE
        + D * (INNER // HEADDIM)
        + INNER * D
        + (CONV + 1) * (INNER + 2 * STATE)
        + 3 * (INNER // HEADDIM)
        + INNER
        + D
    )
    limit = CLIP_RMS * math.sqrt(entries)
    factor = limit / jnp.maximum(grad_norm, limit)

    def moved(moment, grad):
        return 0.5 * moment + 0.5 * factor * grad

    def stepped(weight, moment):
        return (weight.astype(F32) - LEARN * moment).astype(weight.dtype)

    new_prenorm = moved(prenorm_moment, s_prenorm)
    moments = (inproj_moment, outproj_moment.T, statproj_moment, stepproj_moment.T)
    new_in, new_out, new_state, new_step, next_in, next_out, next_state, next_step = run_owner(
        update_kernel,
        "owner_update",
        place,
        (
            factor.reshape(1, 1), share, step_share,
            inproj, outproj_own, statproj, stepproj_own, *moments,
        ),
        [
            pl.BlockSpec(memory_space=pltpu.SMEM),
            whole(share), whole(step_share),
            in_spec, whole(outproj_own), state_spec, whole(stepproj_own),
            *[whole(moment) for moment in moments],
        ],
        [whole_out(moment.shape, kind) for kind in (F32, BF) for moment in moments],
    )
    new_taps = moved(convinner_moment, s_taps)
    new_state_taps = moved(convstate_moment, s_state_taps)
    new_head = moved(headparam_moment, s_head)
    new_gain = moved(gatenorm_moment, s_gain)
    return (
        outputs,
        input_grads,
        grad_norm,
        new_prenorm,
        new_in,
        new_state,
        new_step.T,
        new_out.T,
        new_taps,
        new_state_taps,
        new_head,
        new_gain,
        next_in,
        next_state,
        next_step.T,
        next_out.T,
        stepped(convinner, new_taps),
        stepped(lax.dynamic_slice_in_dim(convstate, core * STATE, STATE, 1), new_state_taps),
    )


def solution(mesh):
    fast = mesh.shape["seq"] == BLOCKS and mesh.shape["tensor"] == 2
    return jax.shard_map(
        fast_body if fast else general_body,
        mesh=mesh,
        in_specs=(
            P(None, "dp", "seq", "tensor"),
            P(None, "dp", None),
            P(None, "dp", "seq", "tensor"),
            P(),
            P(None, "dp", "tensor"),
            P("dp", None),
            P("dp", "tensor"),
            P("tensor", "dp"),
            P(None, "tensor"),
            P(),
            P(None, "tensor"),
            P("tensor"),
            P("tensor"),
            P(None, ("dp", "seq"), "tensor"),
            P(("dp", "seq"), "tensor"),
            P(("dp", "seq"), "tensor"),
            P("tensor", ("dp", "seq")),
            P(None, "tensor"),
            P(None, "tensor"),
            P(None, "tensor"),
            P("tensor"),
        ),
        out_specs=(
            P(None, "dp", "seq", "tensor"),
            P(None, "dp", "seq", "tensor"),
            P(),
            P("tensor"),
            P(None, ("dp", "seq"), "tensor"),
            P(("dp", "seq"), "tensor"),
            P(("dp", "seq"), "tensor"),
            P("tensor", ("dp", "seq")),
            P(None, "tensor"),
            P(None, "tensor"),
            P(None, "tensor"),
            P("tensor"),
            P(None, ("dp", "seq"), "tensor"),
            P(("dp", "seq"), "tensor"),
            P(("dp", "seq"), "tensor"),
            P("tensor", ("dp", "seq")),
            P(None, "tensor"),
            P(None, "tensor"),
        ),
        check_vma=False,
    )
```

```python
import functools
import math

import jax
import jax.numpy as jnp
from jax import lax
from jax.experimental import pallas as pl
from jax.experimental.pallas import tpu as pltpu
from jax.sharding import PartitionSpec as P

D = 1536
INNER = 3072
HEADDIM = 64
STATE = 128
CONV = 4
MB = 2


EPS = 1e-05
LEARN = 0.05
CLIP_RMS = 0.25
HIGH = lax.Precision.HIGHEST


def shifted(block, axis, distance):
    devices = range(lax.axis_size(axis))
    route = [(i - distance, i) for i in devices if i - distance in devices]
    return lax.ppermute(block, axis, route)


def prefix(array, axis, combine, identity):
    size, position = (lax.axis_size(axis), lax.axis_index(axis))
    everything = jax.tree.map(
        lambda part, kind: lax.all_gather(part.astype(kind), axis),
        array,
        (jnp.bfloat16, jnp.bfloat16),
    )
    start = jax.tree.map(
        lambda part, zero: jnp.broadcast_to(jnp.asarray(zero, part.dtype), part.shape),
        array,
        identity,
    )

    def prefix_step(k, before):
        reached = k < position
        new = combine(
            before, jax.tree.map(lambda part, own: part[k].astype(own.dtype), everything, array)
        )
        return jax.tree.map(lambda a, b: jnp.where(reached, a, b), new, before)

    return lax.fori_loop(0, size, prefix_step, start)


def entering_2(array, axis, combine, identity):
    size, position = (lax.axis_size(axis), lax.axis_index(axis))
    everything = jax.tree.map(lambda part: lax.all_gather(part, axis), array)
    start = jax.tree.map(
        lambda part, zero: jnp.broadcast_to(jnp.asarray(zero, part.dtype), part.shape),
        array,
        identity,
    )

    def entering_step(k, before):
        at = size - 1 - k
        reached = at > position
        new = combine(before, jax.tree.map(lambda part: part[at], everything))
        return jax.tree.map(lambda a, b: jnp.where(reached, a, b), new, before)

    return lax.fori_loop(0, size, entering_step, start)


def rms_scale(values, weight):
    return values * lax.rsqrt(jnp.mean(values * values, axis=-1, keepdims=True) + EPS) * weight


def conv_block(padded, seg_pad, kernel):
    length = padded.shape[0] - (CONV - 1)
    own_seg = seg_pad[CONV - 1 :]
    summed = jnp.broadcast_to(kernel[CONV], (length, kernel.shape[1]))
    for offset in range(CONV):
        window = padded[offset : offset + length]
        same_doc = (seg_pad[offset : offset + length] == own_seg)[:, None]
        summed = summed + kernel[offset] * jnp.where(same_doc, window, 0.0)
    return jax.nn.silu(summed)


def decay_table(cumulative, segids):
    row_count = segids.shape[0]
    places = jnp.arange(row_count)
    allowed = (segids[:, None] == segids[None, :]) & (places[:, None] >= places[None, :])
    allowed = allowed[:, :, None]
    gap_values = cumulative[:, None, :] - cumulative[None, :, :]
    return jnp.where(allowed, jnp.exp(jnp.where(allowed, gap_values, -60.0)), 0.0)


def head_rates(raw_step, params):
    step_sizes = jax.nn.softplus(raw_step + params[0])
    return (step_sizes, jnp.cumsum(-step_sizes * jnp.exp(params[1]), axis=0))


def mix_out(values, b_proj, c_proj, raw_step, params, segids, before, carry_in):
    step_sizes, cumulative = head_rates(raw_step, params)
    scores = jnp.dot(c_proj, b_proj.T, precision=HIGH)
    weights = scores[:, :, None] * decay_table(cumulative, segids) * step_sizes[None, :, :]
    result = jnp.einsum("tsh,shp->thp", weights, values, precision=HIGH)
    entering = jnp.where((segids == before)[:, None], jnp.exp(cumulative), 0.0)
    carried = jnp.einsum("tn,hpn->thp", c_proj, carry_in, precision=HIGH)
    return result + entering[:, :, None] * carried + params[2][None, :, None] * values


def mix_state(values, b_proj, raw_step, params, segids, before):
    step_sizes, cumulative = head_rates(raw_step, params)
    tail_weight = (
        jnp.where(
            (segids == segids[-1])[:, None], jnp.exp(cumulative[-1][None, :] - cumulative), 0.0
        )
        * step_sizes
    )
    summary = jnp.einsum("sh,shp,sn->hpn", tail_weight, values, b_proj, precision=HIGH)
    passing = jnp.where(segids[-1] == before, jnp.exp(cumulative[-1]), 0.0)
    return (summary, passing)


def chain(earlier, later):
    return (earlier[0] * later[0], later[0][..., None, None] * earlier[1] + later[1])


def add_tree(totals, terms):
    if totals is None:
        return terms
    return jax.tree.map(jnp.add, totals, terms)


def project(left_rows, matrix):
    return jnp.einsum("bld,dk->blk", left_rows, matrix, preferred_element_type=jnp.float32)


def weight_grad(left_rows, right_rows):
    return jnp.einsum("bld,blk->dk", left_rows, right_rows, preferred_element_type=jnp.float32)


def back_project(grad_rows, matrix):
    return jnp.einsum("blk,dk->bld", grad_rows, matrix, preferred_element_type=jnp.float32)


def general_body(
    inputs,
    segments,
    cotangent,
    prenorm,
    inproj,
    statproj,
    stepproj,
    outproj,
    convinner,
    convstate,
    headparam,
    gatenorm,
    prenorm_moment,
    inproj_moment,
    statproj_moment,
    stepproj_moment,
    outproj_moment,
    convinner_moment,
    convstate_moment,
    headparam_moment,
    gatenorm_moment,
):
    tensor_at = lax.axis_index("tensor")
    seq_at = lax.axis_index("seq")
    data_at = lax.axis_index("dp")
    tensor_count = lax.axis_size("tensor")
    batch_count = inputs.shape[1]
    span_len = inputs.shape[2]
    inner_local = convinner.shape[1]
    heads_local = headparam.shape[1]
    state_half = 2 * STATE // tensor_count
    model_half = D // tensor_count
    rows_full, grads_full = (
        lax.all_gather(inputs, "tensor", axis=3, tiled=True),
        lax.all_gather(cotangent, "tensor", axis=3, tiled=True),
    )
    seg_padded = jnp.pad(segments, ((0, 0), (0, 0), (CONV - 1, 0)), constant_values=-1)
    seg_local = lax.dynamic_slice_in_dim(seg_padded, seq_at * span_len, span_len + CONV - 1, 2)
    kernel = jnp.concatenate([convinner, convstate], axis=1)
    shares = None
    smalls = None
    outputs = []
    input_grads = []
    for batch in range(MB):
        inproj_all, statproj_all, stepproj_all, outproj_all = (
            lax.all_gather(inproj, "dp", axis=1, tiled=True),
            lax.all_gather(statproj, "dp", axis=0, tiled=True),
            lax.all_gather(stepproj, "dp", axis=0, tiled=True),
            lax.all_gather(outproj, "dp", axis=1, tiled=True),
        )
        rows = rows_full[batch].astype(jnp.float32)
        normed, norm_back = jax.vjp(rms_scale, rows, prenorm)
        normed_low = normed.astype(jnp.bfloat16)
        gate_pre = project(normed_low, inproj_all[0])
        inner_pre = project(normed_low, inproj_all[1])
        state_pre = project(normed_low, statproj_all)
        raw_step = project(normed_low, stepproj_all)
        mixed = jnp.concatenate([inner_pre, state_pre], axis=2).astype(jnp.bfloat16)
        edge_in = shifted(mixed[:, span_len - (CONV - 1) :, :], "seq", 1)
        padded = jnp.concatenate([edge_in, mixed], axis=1).astype(jnp.float32)
        seg_now = seg_local[batch]
        own_seg = seg_now[:, CONV - 1 :]
        before = seg_now[:, CONV - 2]
        conv_out, conv_back = jax.vjp(
            lambda pad_vals, kernel_in: jax.vmap(conv_block, in_axes=(0, 0, None))(
                pad_vals, seg_now, kernel_in
            ),
            padded,
            kernel,
        )
        values = conv_out[..., :inner_local].reshape(batch_count, span_len, heads_local, HEADDIM)
        b_proj = conv_out[..., inner_local : inner_local + STATE]
        c_proj = conv_out[..., inner_local + STATE :]
        (summary, passing), state_back = jax.vjp(
            lambda value_in, b_part, raw_part, param_in: jax.vmap(
                mix_state, in_axes=(0, 0, 0, None, 0, 0)
            )(value_in, b_part, raw_part, param_in, own_seg, before),
            values,
            b_proj,
            raw_step,
            headparam,
        )
        identity = (jnp.ones_like(passing), jnp.zeros_like(summary))
        _, carry_in = prefix((passing, summary), "seq", chain, identity)
        mixer, out_back = jax.vjp(
            lambda value_in, b_part, c_part, raw_part, param_in, state_in: jax.vmap(
                mix_out, in_axes=(0, 0, 0, 0, None, 0, 0, 0)
            )(value_in, b_part, c_part, raw_part, param_in, own_seg, before, state_in),
            values,
            b_proj,
            c_proj,
            raw_step,
            headparam,
            carry_in,
        )
        flat_mixer = mixer.reshape(batch_count, span_len, inner_local)
        gate_act = jax.nn.silu(gate_pre)
        gated_in = flat_mixer * gate_act
        total_sq = lax.psum(jnp.sum(gated_in * gated_in, axis=-1), "tensor")
        scale = lax.rsqrt(total_sq / INNER + EPS)[..., None]
        gated_low = (gated_in * scale * gatenorm).astype(jnp.bfloat16)
        branch_part = project(gated_low, outproj_all)
        branch_own = lax.psum_scatter(branch_part, "tensor", scatter_dimension=2, tiled=True)
        outputs.append((inputs[batch].astype(jnp.float32) + branch_own).astype(jnp.bfloat16))
        grad_rows = grads_full[batch]
        d_gated = back_project(grad_rows, outproj_all)
        g_outproj = jnp.einsum(
            "blk,bld->kd", gated_low, grad_rows, preferred_element_type=jnp.float32
        )
        g_gatenorm = jnp.sum(d_gated * gated_in * scale, axis=(0, 1))
        weighted = d_gated * gatenorm
        cross = lax.psum(jnp.sum(weighted * gated_in, axis=-1), "tensor")
        d_in = weighted * scale - gated_in * scale**3 * (cross / INNER)[..., None]
        d_mixer = d_in * gate_act
        sigma = jax.nn.sigmoid(gate_pre)
        d_gate = d_in * flat_mixer * sigma * (1.0 + gate_pre * (1.0 - sigma))
        d_values, d_bproj, d_cproj, d_raw, d_param, d_carry = out_back(
            d_mixer.reshape(batch_count, span_len, heads_local, HEADDIM)
        )
        _, d_after = entering_2((passing, d_carry), "seq", chain, identity)
        d_passing = jnp.sum(d_after * carry_in, axis=(2, 3))
        d_values_tail, d_bproj_tail, d_raw_tail, d_param_tail = state_back((d_after, d_passing))
        d_state = lax.psum(jnp.concatenate([d_bproj + d_bproj_tail, d_cproj], axis=2), "tensor")
        d_conv = jnp.concatenate(
            [(d_values + d_values_tail).reshape(batch_count, span_len, inner_local), d_state],
            axis=2,
        )
        d_padded, d_kernel = conv_back(d_conv)
        edge_back = shifted(d_padded[:, : CONV - 1, :].astype(jnp.bfloat16), "seq", -1).astype(
            jnp.float32
        )
        d_mixed = d_padded[:, CONV - 1 :, :] + jnp.pad(
            edge_back, ((0, 0), (span_len - (CONV - 1), 0), (0, 0))
        )
        d_mixed_low = d_mixed.astype(jnp.bfloat16)
        d_gate_low = d_gate.astype(jnp.bfloat16)
        d_raw_low = (d_raw + d_raw_tail).astype(jnp.bfloat16)
        d_inner_low = d_mixed_low[..., :inner_local]
        d_state_low = lax.dynamic_slice_in_dim(
            d_mixed_low[..., inner_local:], tensor_at * state_half, state_half, 2
        )
        statproj_own = lax.dynamic_slice_in_dim(statproj_all, tensor_at * state_half, state_half, 1)
        g_inproj = jnp.stack(
            [weight_grad(normed_low, d_gate_low), weight_grad(normed_low, d_inner_low)]
        )
        g_statproj = weight_grad(normed_low, d_state_low)
        g_stepproj = weight_grad(normed_low, d_raw_low)
        d_normed_part = (
            back_project(d_gate_low, inproj_all[0])
            + back_project(d_inner_low, inproj_all[1])
            + back_project(d_state_low, statproj_own)
            + back_project(d_raw_low, stepproj_all)
        )
        d_normed = lax.psum(d_normed_part, "tensor")
        d_rows, d_prenorm = norm_back(d_normed)
        own_rows = lax.dynamic_slice_in_dim(d_rows, tensor_at * model_half, model_half, 2)
        input_grads.append((own_rows + cotangent[batch].astype(jnp.float32)).astype(jnp.bfloat16))
        big_terms = (g_inproj, g_outproj, g_statproj, g_stepproj)
        small_terms = (
            lax.dynamic_slice_in_dim(d_prenorm, tensor_at * model_half, model_half, 0),
            d_kernel[:, :inner_local],
            lax.dynamic_slice_in_dim(
                d_kernel[:, inner_local:], tensor_at * state_half, state_half, 1
            ),
            d_param + d_param_tail,
            g_gatenorm,
        )
        shares = add_tree(
            shares,
            (
                lax.psum_scatter(big_terms[0], ("dp", "seq"), scatter_dimension=1, tiled=True),
                lax.psum_scatter(big_terms[1], ("dp", "seq"), scatter_dimension=1, tiled=True),
                lax.psum_scatter(big_terms[2], ("dp", "seq"), scatter_dimension=0, tiled=True),
                lax.psum_scatter(big_terms[3], ("dp", "seq"), scatter_dimension=0, tiled=True),
            ),
        )
        smalls = add_tree(
            smalls,
            lax.psum(
                (small_terms[0], small_terms[1], small_terms[2], small_terms[3], small_terms[4]),
                ("dp", "seq"),
            ),
        )
    big_sq = jnp.sum(jnp.stack([jnp.sum(term * term) for term in shares]))
    small_sq = jnp.sum(jnp.stack([jnp.sum(term * term) for term in smalls]))
    first_owner = jnp.where((data_at == 0) & (seq_at == 0), 1.0, 0.0)
    norm_sq = lax.psum(big_sq + first_owner * small_sq, ("dp", "seq", "tensor"))
    grad_norm = jnp.sqrt(norm_sq)
    heads_all = INNER // HEADDIM
    entries = (
        2 * D * INNER
        + 2 * D * STATE
        + D * heads_all
        + INNER * D
        + (CONV + 1) * (INNER + 2 * STATE)
        + 3 * heads_all
        + INNER
        + D
    )
    limit = CLIP_RMS * math.sqrt(entries)
    factor = limit / jnp.maximum(grad_norm, limit)
    shard_rows = shares[0].shape[1]
    row_start = seq_at * shard_rows
    big_current = (
        lax.dynamic_slice_in_dim(inproj, row_start, shard_rows, 1),
        lax.dynamic_slice_in_dim(outproj, row_start, shard_rows, 1),
        lax.dynamic_slice_in_dim(
            lax.dynamic_slice_in_dim(statproj, row_start, shard_rows, 0),
            tensor_at * state_half,
            state_half,
            1,
        ),
        lax.dynamic_slice_in_dim(stepproj, row_start, shard_rows, 0),
    )
    conv_current = (
        convinner,
        lax.dynamic_slice_in_dim(convstate, tensor_at * state_half, state_half, 1),
    )
    big_moments = (inproj_moment, outproj_moment, statproj_moment, stepproj_moment)
    small_moments = (
        prenorm_moment,
        convinner_moment,
        convstate_moment,
        headparam_moment,
        gatenorm_moment,
    )
    big_new_moments = [
        0.5 * moment_item + 0.5 * factor * grad_item
        for moment_item, grad_item in zip(big_moments, shares)
    ]
    small_new_moments = [
        0.5 * moment_item + 0.5 * factor * grad_item
        for moment_item, grad_item in zip(small_moments, smalls)
    ]
    big_new = [
        (weight_item.astype(jnp.float32) - LEARN * moment_item).astype(weight_item.dtype)
        for weight_item, moment_item in zip(big_current, big_new_moments)
    ]
    conv_new = [
        (weight_item - LEARN * moment_item).astype(weight_item.dtype)
        for weight_item, moment_item in zip(conv_current, small_new_moments[1:3])
    ]
    return (
        jnp.stack(outputs),
        jnp.stack(input_grads),
        grad_norm,
        small_new_moments[0],
        big_new_moments[0],
        big_new_moments[2],
        big_new_moments[3],
        big_new_moments[1],
        small_new_moments[1],
        small_new_moments[2],
        small_new_moments[3],
        small_new_moments[4],
        big_new[0],
        big_new[2],
        big_new[3],
        big_new[1],
        conv_new[0],
        conv_new[1],
    )


BLOCKS = 4
SPAN = 256
PART = 128
PARTS = SPAN // PART
PACKED = 48
LOG2E = 1.4426950408889634
QUARTER = 384
QHEADS = 6
MAPS_AT = 3 * QUARTER
BF = jnp.bfloat16
F32 = jnp.float32
ROUTE_X = [(i, i ^ 1) for i in range(BLOCKS)]
ROUTE_Y = [(i, i ^ 2) for i in range(BLOCKS)]
SWAP = [(0, 1), (1, 0)]
VMEM_LIMIT = 56 * 1024 * 1024


def dot_nn(a, b):
    return lax.dot_general(a, b, (((1,), (0,)), ((), ())), preferred_element_type=F32)


def dot_nt(a, b):
    return lax.dot_general(a, b, (((1,), (1,)), ((), ())), preferred_element_type=F32)


def dot_tn(a, b):
    return lax.dot_general(a, b, (((0,), (0,)), ((), ())), preferred_element_type=F32)


def dot_exact(a, b):
    return lax.dot_general(
        a, b, (((1,), (0,)), ((), ())), precision=HIGH, preferred_element_type=F32
    )


def sigmoid(v):
    return 1.0 / (1.0 + jnp.exp(-v))


def split_sum(triangle, table):
    first = table.astype(BF)
    rest = table - first.astype(F32)
    second = rest.astype(BF)
    third = (rest - second.astype(F32)).astype(BF)
    parts = (
        first.astype(F32)
        + pltpu.roll(second.astype(F32), 8, 1)
        + pltpu.roll(third.astype(F32), 16, 1)
    )
    sums = dot_nn(triangle, parts.astype(BF))
    sums = sums + pltpu.roll(sums, 120, 1) + pltpu.roll(sums, 112, 1)
    lanes = lax.broadcasted_iota(jnp.int32, sums.shape, 1)
    return jnp.where(lanes < 8, sums, 0.0)


def head_sums(table, gather):
    first = table.astype(BF)
    second = (table - first.astype(F32)).astype(BF)
    return dot_nn(first, gather) + dot_nn(second, gather)


def head_spread():
    lane = lax.broadcasted_iota(jnp.int32, (128, QUARTER), 0)
    chan = lax.broadcasted_iota(jnp.int32, (128, QUARTER), 1)
    base = jnp.where(lane < 8, lane, jnp.where(lane < 16, lane - 8, -1)) * HEADDIM
    return jnp.where((chan >= base) & (chan < base + HEADDIM) & (base >= 0), 1.0, 0.0).astype(BF)


def spread_heads(tables, spread):
    packed = []
    for table in tables:
        lanes = lax.broadcasted_iota(jnp.int32, table.shape, 1)
        table = jnp.where(lanes < 8, table, 0.0)
        first = table.astype(BF).astype(F32)
        packed.append((first + pltpu.roll(table - first, 8, 1)).astype(BF))
    wide = dot_nn(jnp.concatenate(packed, axis=0), spread)
    return [wide[PART * k : PART * (k + 1)] for k in range(len(tables))]


def rates(raw, head):
    shifted_raw = raw + head[0:1]
    step = jnp.maximum(shifted_raw, 0.0) + jnp.log1p(jnp.exp(-jnp.abs(shifted_raw)))
    lanes = lax.broadcasted_iota(jnp.int32, raw.shape, 1)
    return shifted_raw, jnp.where(lanes < QHEADS, step, 0.0)


def triangle(keep):
    rows_at = lax.broadcasted_iota(jnp.int32, (PART, PART), 0)
    cols_at = lax.broadcasted_iota(jnp.int32, (PART, PART), 1)
    return jnp.where(keep(rows_at, cols_at), 1.0, 0.0).astype(BF)


def part_terms(step, head, cols, segr, lower):
    cum = split_sum(lower, -step * head[1:2]) * LOG2E
    last = cum[PART - 1 : PART]
    enter = jnp.exp2(cum) * cols[:, 4:5]
    leave = jnp.exp2(last - cum) * cols[:, 5:6]
    passing = jnp.exp2(last) * cols[PART - 1 : PART, 4:5]
    rows_at = lax.broadcasted_iota(jnp.int32, (PART, PART), 0)
    cols_at = lax.broadcasted_iota(jnp.int32, (PART, PART), 1)
    allowed = (rows_at >= cols_at) & (cols[:, 6:7] == segr)
    return cum, enter, leave, passing, jnp.where(allowed, 0.0, -1e30)


def head_decay(cum, cum_t, h, block_out):
    return jnp.exp2(cum[:, h : h + 1] - cum_t[h : h + 1] + block_out)


def by_head(table, low_half):
    zero = jnp.zeros_like(table)
    return jnp.concatenate(
        [jnp.where(low_half, table, zero), jnp.where(low_half, zero, table)], axis=0
    )


def pass_state(passing, state, added):
    heads = [slice(HEADDIM * h, HEADDIM * (h + 1)) for h in range(QHEADS)]
    return jnp.concatenate(
        [passing[:, h : h + 1] * state[at] + added[at] for h, at in enumerate(heads)], axis=0
    )


def segment_flags(seg_ref, q, block):
    begin = pl.multiple_of(block * SPAN, 128)
    around = seg_ref[q, :, pl.ds(begin, SPAN + 256)]
    here = around[:, 128 : 128 + SPAN]
    flags = []
    for shift in (3, 2, 1, 0):
        flags.append(pltpu.roll(around, shift, 1)[:, 128 : 128 + SPAN] == here)
    ends = [around[:, PART * k + 127 : PART * k + 128] for k in range(PARTS + 1)]
    parts = [here[:, PART * k : PART * (k + 1)] for k in range(PARTS)]
    flags.append(jnp.concatenate([parts[k] == ends[k] for k in range(PARTS)], axis=1))
    flags.append(jnp.concatenate([parts[k] == ends[k + 1] for k in range(PARTS)], axis=1))
    for shift in (3, 2, 1, 0):
        later = pltpu.roll(around, SPAN + 256 - shift, 1) if shift else around
        flags.append(later[:, 128 : 128 + SPAN] == here)
    flags = [jnp.where(flag, 1.0, 0.0) for flag in flags]
    at = lax.broadcasted_iota(jnp.int32, (8, SPAN), 0)
    first = here
    for row in range(6):
        first = jnp.where(at == row, flags[row], first)
    second = flags[9]
    for row in range(3):
        second = jnp.where(at == row, flags[6 + row], second)
    return jnp.concatenate([first, second], axis=0)


def to_columns(rows):
    filled = jnp.concatenate([rows, jnp.zeros((128 - rows.shape[0], SPAN), F32)], axis=0)
    return filled.T


def both_tokens(own_ref, other_ref):
    return jnp.concatenate([own_ref[0], other_ref[0]], axis=0)


def fwd_pieces(place_ref, *refs):
    own_out, other_out, held, sems = refs[20:24]
    tokens = block_rows(refs[:10], place_ref, held, sems)
    own_out[0] = tokens[:SPAN]
    other_out[0] = tokens[SPAN:]
    fwd_step(tokens, *refs[10:20], *refs[24:])


def fwd_blocks(place_ref, own_ref, other_ref, *refs):
    fwd_step(both_tokens(own_ref, other_ref), *refs)


def fwd_step(
    tokens, w_ref, seg_ref, taps_ref, head_ref, chan_ref,
    mixed_ref, raw_ref, pre_ref, y_ref, hin_ref, *more,
):
    buf, state = more[-2:]
    block = pl.program_id(0)

    @pl.when(block == 0)
    def _():
        buf[:, 0:8] = jnp.zeros((2, 8, buf.shape[2]), F32)
        state[...] = jnp.zeros_like(state)

    width = QUARTER + 2 * STATE
    projected = dot_nn(tokens, w_ref[...])
    taps = taps_ref[...]
    head = head_ref[...]
    skip = chan_ref[1:2]
    lower = triangle(lambda r, c: r >= c)
    spread = head_spread()
    low_half = lax.broadcasted_iota(jnp.int32, (PART, 128), 1) < HEADDIM
    pieces = []
    for q in range(2):
        rows_q = slice(q * SPAN, (q + 1) * SPAN)
        raw = projected[rows_q, width:]
        raw_ref[q, 0] = raw
        mixed_low = projected[rows_q, :width].astype(BF)
        mixed_ref[q, 0] = mixed_low
        mixed = mixed_low.astype(F32)
        buf[q, 8 : 8 + SPAN] = mixed
        rows = segment_flags(seg_ref, q, block)
        cols_all = to_columns(rows)
        pre = jnp.broadcast_to(taps[CONV : CONV + 1], mixed.shape)
        for j in range(CONV):
            window = mixed if j == CONV - 1 else buf[q, 5 + j : 5 + j + SPAN]
            pre = pre + taps[j : j + 1] * (window * cols_all[:, j : j + 1])
        buf[q, 0:8] = mixed[SPAN - 8 :]
        pre_ref[q, 0] = pre
        act = pre * sigmoid(pre)
        _, step_all = rates(raw, head)
        for part in range(PARTS):
            at_rows = slice(part * PART, (part + 1) * PART)
            cols = cols_all[at_rows]
            cum, enter, leave, passing, block_out = part_terms(
                step_all[at_rows], head, cols, rows[6:7, at_rows], lower
            )
            pieces.append(
                (q, part, act[at_rows], step_all[at_rows], cum, enter, leave, passing, block_out)
            )
    work = []
    for q, part, act, step, cum, enter, leave, passing, block_out in pieces:
        values = act[:, :QUARTER]
        b_low = act[:, QUARTER : QUARTER + STATE].astype(BF)
        c_low = act[:, QUARTER + STATE :].astype(BF)
        step_w, enter_w, leave_w = spread_heads((step, enter, leave), spread)
        cum_t = cum.T
        scores = dot_nt(c_low, b_low)
        scaled = (step_w * values).astype(BF)
        tail = (leave_w * scaled.astype(F32)).astype(BF)
        added = dot_tn(tail, b_low)
        own = []
        for k in range(QHEADS // 2):
            at = slice(128 * k, 128 * (k + 1))
            weights = [
                (scores * head_decay(cum, cum_t, h, block_out)).astype(BF)
                for h in (2 * k, 2 * k + 1)
            ]
            own.append(dot_nn(jnp.concatenate(weights, axis=1), by_head(scaled[:, at], low_half)))
        own = jnp.concatenate(own, axis=1) + skip * values
        work.append((q, part, c_low, enter_w, passing, added, own))
    for q, part, c_low, enter_w, passing, added, own in sorted(work, key=lambda item: item[1]):
        held_f = state[q]
        held = held_f.astype(BF)
        hin_ref[q, 0, QUARTER * part : QUARTER * (part + 1)] = held
        y_ref[q, 0, part * PART : (part + 1) * PART] = own + enter_w * dot_nt(c_low, held)
        state[q] = pass_state(passing, held_f, added)


def piece_copies(refs, m, slot, held, sems):
    half = SPAN // 2
    for q in range(2):
        pieces = refs[5 * q : 5 * (q + 1)]
        own, by_x, by_y, far_a, far_b = pieces if m is None else [ref.at[m] for ref in pieces]
        if slot < 3:
            at = pl.ds(q * SPAN, SPAN)
            source = (own, by_x, by_y)[slot]
            yield pltpu.make_async_copy(source, held.at[slot, at], sems.at[slot, q, 0])
        else:
            for part, source in enumerate((far_a, far_b)):
                at = pl.ds(q * SPAN + part * half, half)
                yield pltpu.make_async_copy(source, held.at[slot, at], sems.at[slot, q, part])


def start_pieces(refs, m, held, sems):
    @pl.when(pl.program_id(0) == 0)
    def _():
        for slot in range(BLOCKS):
            for copy in piece_copies(refs, m, slot, held, sems):
                copy.start()


def wait_slot(refs, m, held, sems, first_step):
    for slot in range(BLOCKS):
        @pl.when(pl.program_id(0) == first_step + slot)
        def _():
            for copy in piece_copies(refs, m, slot, held, sems):
                copy.wait()


def block_rows(refs, place_ref, held, sems):
    start_pieces(refs, None, held, sems)

    @pl.when(pl.program_id(0) == 0)
    def _():
        for slot in range(BLOCKS):
            for copy in piece_copies(refs, None, slot, held, sems):
                copy.wait()

    return held[pl.program_id(0) ^ place_ref[1]]


def cot_scratch():
    return [pltpu.VMEM((BLOCKS, 2 * SPAN, D), BF), pltpu.SemaphoreType.DMA((BLOCKS, 2, 2))]


def core_rows(place_ref):
    half = D // 2
    core = place_ref[0]
    own = pl.multiple_of(core * half, half)
    other = pl.multiple_of((1 - core) * half, half)
    return pl.ds(own, half), pl.ds(other, half)


def stat_rows(row, column):
    lanes = lax.broadcasted_iota(jnp.int32, (SPAN, 128), 1)
    return jnp.where(lanes == row, column, 0.0).T[0:2]


def gate_kernel(place_ref, *refs):
    tokens, y_refs, (w_gate_ref, w_out_ref, chan_ref) = (refs[0:2], refs[2:4]), refs[4:6], refs[6:9]
    gate_refs, gun_refs, mine_refs, theirs_refs, stat_refs = [
        refs[at : at + 2] for at in range(9, 19, 2)
    ]
    step = pl.program_id(0)

    def one_block(m):
        gate = dot_nn(both_tokens(*tokens[m]), w_gate_ref[...])
        guns = []
        for q in range(2):
            gate_q = gate[q * SPAN : (q + 1) * SPAN]
            gate_refs[m][q, 0] = gate_q
            gated_in = y_refs[m][q, 0] * (gate_q * sigmoid(gate_q))
            gun = (gated_in * chan_ref[0:1]).astype(BF)
            gun_refs[m][q, 0] = gun
            guns.append(gun)
            square = jnp.sum(gated_in * gated_in, axis=1, keepdims=True)
            stat_refs[m][q, 0] = stat_rows(0, square)
        gun = jnp.concatenate(guns, axis=0)
        own, other = core_rows(place_ref)
        mine = dot_nt(gun, w_out_ref[own]).astype(BF)
        theirs = dot_nt(gun, w_out_ref[other]).astype(BF)
        for q in range(2):
            mine_refs[m][0, q] = mine[q * SPAN : (q + 1) * SPAN]
            theirs_refs[m][0, 1 - q] = theirs[q * SPAN : (q + 1) * SPAN]

    for m in range(2):
        @pl.when((step >= m * BLOCKS) & (step < (m + 1) * BLOCKS))
        def _():
            one_block(m)


def cross_kernel(place_ref, *refs):
    cots, refs = (refs[0:10], refs[0:10]), refs[10:]
    gun_refs, w_out_ref, d_gated_refs, stat_refs = refs[0:2], refs[2], refs[3:5], refs[5:7]
    held_0, sems_0, held_1, sems_1 = refs[7:]
    step = pl.program_id(0)
    start_pieces(cots[0], 0, held_0, sems_0)
    start_pieces(cots[1], 1, held_1, sems_1)

    def one_block(m, held):
        d_gated = dot_nn(held[step - m * BLOCKS], w_out_ref[...])
        for q in range(2):
            d_gated_q = d_gated[q * SPAN : (q + 1) * SPAN]
            d_gated_refs[m][q, 0] = d_gated_q
            cross = d_gated_q * gun_refs[m][q, 0].astype(F32)
            stat_refs[m][q, 0] = stat_rows(1, jnp.sum(cross, axis=1, keepdims=True))

    for m, held, sems in ((0, held_0, sems_0), (1, held_1, sems_1)):
        wait_slot(cots[m], m, held, sems, m * BLOCKS)

        @pl.when((step >= m * BLOCKS) & (step < (m + 1) * BLOCKS))
        def _():
            one_block(m, held)


def start_sums(total, seed_ref):
    @pl.when(pl.program_id(0) == 0)
    def _():
        total[...] = jnp.zeros_like(total) if seed_ref is None else seed_ref[...]


def finish_sums(total, out_ref):
    @pl.when(pl.program_id(0) == BLOCKS - 1)
    def _():
        rows_of = out_ref.shape[2]
        for z in range(out_ref.shape[0]):
            out_ref[z] = total[:, z * rows_of : (z + 1) * rows_of].astype(BF)


def gate_back_kernel(place_ref, *refs):
    tokens, refs = (refs[0:2], refs[2:4]), refs[4:]
    cots, refs = (refs[0:10], refs[0:10]), refs[10:]
    y_refs, gate_refs, d_gated_refs, stat_refs = refs[0:2], refs[2:4], refs[4:6], refs[6:8]
    chan_ref, dy_refs, d_gate_refs = refs[8], refs[9:11], refs[11:13]
    g_gain_ref, parts_ref, held_0, sems_0, held_1, sems_1, total = refs[13:]
    step = pl.program_id(0)

    @pl.when(step == 0)
    def _():
        total[...] = jnp.zeros_like(total)
        g_gain_ref[...] = jnp.zeros_like(g_gain_ref)

    start_pieces(cots[0], 0, held_0, sems_0)
    start_pieces(cots[1], 1, held_1, sems_1)

    def one_block(m, held):
        gateds = []
        d_gates = []
        for q in range(2):
            stat = to_columns(stat_refs[m][q, 0])
            scale = lax.rsqrt(stat[:, 0:1] * (1.0 / INNER) + EPS)
            pull = stat[:, 1:2] * (1.0 / INNER) * scale * scale * scale
            gate = gate_refs[m][q, 0]
            y = y_refs[m][q, 0]
            d_gated = d_gated_refs[m][q, 0]
            sigma = sigmoid(gate)
            gate_act = gate * sigma
            gated_in = y * gate_act
            scaled_gain = chan_ref[0:1] * scale
            d_in = d_gated * scaled_gain - gated_in * pull
            dy_refs[m][q, 0] = (d_in * gate_act).astype(BF)
            d_gate = (d_in * y * (sigma + gate_act * (1.0 - sigma))).astype(BF)
            d_gate_refs[m][q, 0] = d_gate
            d_gates.append(d_gate)
            gateds.append((gated_in * scaled_gain).astype(BF))
            g_gain_ref[0:1] += jnp.sum(d_gated * gated_in * scale, axis=0, keepdims=True)
        gated = jnp.concatenate(gateds, axis=0)
        d_gate = jnp.concatenate(d_gates, axis=0)
        total[:QUARTER] += dot_tn(gated, held[step - m * BLOCKS])
        total[QUARTER:] += dot_tn(d_gate, both_tokens(*tokens[m]))

    for m, held, sems in ((0, held_0, sems_0), (1, held_1, sems_1)):
        wait_slot(cots[m], m, held, sems, m * BLOCKS)

        @pl.when((step >= m * BLOCKS) & (step < (m + 1) * BLOCKS))
        def _():
            one_block(m, held)

    @pl.when(step == 2 * BLOCKS - 1)
    def _():
        rows_of = parts_ref.shape[2]
        for z in range(parts_ref.shape[0]):
            parts_ref[z] = total[:, z * rows_of : (z + 1) * rows_of].astype(BF)


def bwd_first(*refs):
    bwd_step(*refs[:16], None, refs[16], None, None, *refs[17:])


def bwd_last(*refs):
    total = refs[-1]
    bwd_step(*refs[:17], total, *refs[18:-1])
    finish_sums(total, refs[17])


def bwd_step(
    place_ref, own_ref, other_ref, mixed_ref, pre_ref, raw_ref, y_ref, hin_ref, dy_ref,
    d_gate_ref, seg_ref, taps_ref, head_ref, chan_ref, w_ref, w_gate_ref,
    seed_ref,
    g_ref, keep_ref, give_ref, slope_ref, gtap_ref, ghead_ref, mine_ref, theirs_ref,
    buf, d_state, bc_edge, slope_edge, d_late,
):
    start_sums(g_ref, seed_ref)
    block = BLOCKS - 1 - pl.program_id(0)

    @pl.when(pl.program_id(0) == 0)
    def _():
        buf[:, SPAN:] = jnp.zeros((2, 8, QUARTER), F32)
        d_state[...] = jnp.zeros_like(d_state)
        bc_edge[...] = jnp.zeros_like(bc_edge)
        slope_edge[...] = jnp.zeros_like(slope_edge)
        gtap_ref[...] = jnp.zeros_like(gtap_ref)
        ghead_ref[...] = jnp.zeros_like(ghead_ref)

    head = head_ref[...]
    taps = taps_ref[...]
    skip = chan_ref[1:2]
    first_core = place_ref[0] == 0
    low_half = lax.broadcasted_iota(jnp.int32, (PART, 128), 1) < HEADDIM
    chan_at = lax.broadcasted_iota(jnp.int32, (QUARTER, 128), 0)
    head_at = lax.broadcasted_iota(jnp.int32, (QUARTER, 128), 1)
    gather = jnp.where(
        (chan_at >= head_at * HEADDIM) & (chan_at < (head_at + 1) * HEADDIM), 1.0, 0.0
    )
    gather_low = gather.astype(BF)
    lower = triangle(lambda r, c: r >= c)
    upper = triangle(lambda r, c: r <= c)
    spread = head_spread()

    def store(ref, q, first_row, rows):
        if keep_ref is not None:
            ref[0, q, first_row : first_row + rows.shape[0]] = rows
            return
        for at in range(first_row, first_row + rows.shape[0], 16):
            group = at // PACKED
            row = SPAN + at % PACKED
            ref[0, q, row : row + 16, 128 * group : 128 * (group + 1)] = rows[
                at - first_row : at - first_row + 16
            ]

    keep_at = mine_ref if keep_ref is None else keep_ref
    give_at = theirs_ref if give_ref is None else give_ref
    pieces = []
    columns = []
    slopes = []
    for q in range(2):
        rows = segment_flags(seg_ref, q, block)
        cols_all = to_columns(rows)
        columns.append(cols_all)
        pre = pre_ref[q, 0]
        sigma = sigmoid(pre)
        act = pre * sigma
        slope = sigma * (1.0 + pre * (1.0 - sigma))
        slopes.append(slope)
        slope_half = jnp.where(
            first_core, slope[:, QUARTER : QUARTER + STATE], slope[:, QUARTER + STATE :]
        )
        slope_ref[q, 0, 0:SPAN] = slope_half
        slope_ref[q, 0, SPAN : SPAN + 16] = slope_edge[q]
        slope_edge[q] = slope_half[0:16]
        if keep_ref is None:
            for ref in (mine_ref, theirs_ref):
                ref[0, q, SPAN + 32 :, 640:] = jnp.zeros((16, 128), BF)
        store(keep_at, q, SPAN, bc_edge[q, :, :STATE].astype(BF))
        store(give_at, 1 - q, SPAN, bc_edge[q, :, STATE:].astype(BF))
        shifted_all, step_all = rates(raw_ref[q, 0], head)
        for part in range(PARTS):
            at_rows = slice(part * PART, (part + 1) * PART)
            terms = part_terms(
                step_all[at_rows], head, cols_all[at_rows], rows[6:7, at_rows], lower
            )
            pieces.append((q, part, act[at_rows], shifted_all[at_rows], step_all[at_rows], terms))
    work = []
    for q, part, act, shifted_raw, step, terms in pieces:
        cum, enter, leave, passing, block_out = terms
        values = act[:, :QUARTER]
        b_low = act[:, QUARTER : QUARTER + STATE].astype(BF)
        c_low = act[:, QUARTER + STATE :].astype(BF)
        step_w, enter_w, leave_w = spread_heads((step, enter, leave), spread)
        cum_t = cum.T
        scores = dot_nt(c_low, b_low)
        dy_low = dy_ref[q, 0, part * PART : (part + 1) * PART]
        scaled = (step_w * values).astype(BF)
        tail = (leave_w * scaled.astype(F32)).astype(BF)
        enter_dy = (enter_w * dy_low.astype(F32)).astype(BF)
        d_scores = jnp.zeros((PART, PART), F32)
        own = []
        for k in range(QHEADS // 2):
            at = slice(128 * k, 128 * (k + 1))
            dy_both = by_head(dy_low[:, at], low_half)
            d_weights = dot_nt(dy_both, scaled[:, at])
            weights = []
            for half, h in enumerate((2 * k, 2 * k + 1)):
                decay = head_decay(cum, cum_t, h, block_out)
                weights.append((scores * decay).astype(BF))
                d_scores = d_scores + d_weights[half * PART : (half + 1) * PART] * decay
            own.append(dot_tn(jnp.concatenate(weights, axis=0), dy_both))
        own = jnp.concatenate(own, axis=1)
        d_scores = d_scores.astype(BF)
        new_state = dot_tn(enter_dy, c_low)
        d_c = dot_nn(d_scores, b_low)
        d_b = dot_tn(d_scores, c_low)
        work.append(
            (q, part, values, b_low, shifted_raw, step, step_w, leave_w, passing, dy_low, scaled,
             tail, enter_dy, own, new_state, d_b, d_c)
        )
    for item in sorted(work, key=lambda item: -item[1]):
        (q, part, values, b_low, shifted_raw, step, step_w, leave_w, passing, dy_low, scaled,
         tail, enter_dy, own, new_state, d_b, d_c) = item
        at_rows = slice(part * PART, (part + 1) * PART)
        held = hin_ref[q, 0, QUARTER * part : QUARTER * (part + 1)]
        dy = dy_low.astype(F32)
        scaled_f = scaled.astype(F32)
        d_after = d_state[q]
        d_after_low = d_after.astype(BF)
        tail_part = leave_w * dot_nt(b_low, d_after_low)
        d_scaled = own + tail_part
        d_c = d_c + dot_nn(enter_dy, held)
        d_b = d_b + dot_nn(tail, d_after_low)
        d_state[q] = pass_state(passing, d_after, new_state)
        kept_half = jnp.where(first_core, d_b, d_c)
        given_half = jnp.where(first_core, d_c, d_b)
        store(keep_at, q, part * PART, kept_half.astype(BF))
        store(give_at, 1 - q, part * PART, given_half.astype(BF))
        if part == 0:
            bc_edge[q, :, :STATE] = kept_half[0:16]
            bc_edge[q, :, STATE:] = given_half[0:16]
        d_values = step_w * d_scaled + skip * dy
        buf[q, at_rows] = d_values * slopes[q][at_rows, :QUARTER]
        by_values = dot_nn((values * d_scaled).astype(BF), gather_low)
        y_part = y_ref[q, 0, at_rows] - skip * values
        d_cum = head_sums(dy * y_part - scaled_f * d_scaled, gather_low)
        tail_row = jnp.sum(scaled_f * tail_part, axis=0, keepdims=True)
        tail_sum = dot_exact(jnp.broadcast_to(tail_row, (8, QUARTER)), gather)[0:1]
        state_dot = jnp.sum(d_after * held.astype(F32), axis=1, keepdims=True)
        state_terms = jnp.sum(state_dot * gather, axis=0, keepdims=True)
        d_rate = split_sum(upper, d_cum) + tail_sum + passing * state_terms
        d_raw = (by_values - head[1:2] * d_rate) * sigmoid(shifted_raw)
        ghead_ref[0:1, :128] += jnp.sum(d_raw, axis=0, keepdims=True)
        ghead_ref[1:2, :128] += jnp.sum(-step * head[1:2] * d_rate, axis=0, keepdims=True)
        ghead_ref[2:3] += jnp.sum(values * dy, axis=0, keepdims=True)
        d_late[q * SPAN + part * PART : q * SPAN + (part + 1) * PART, QUARTER:] = d_raw.astype(BF)
    for q in range(2):
        mixed = mixed_ref[q, 0, :, :QUARTER].astype(F32)
        d_mixed = jnp.zeros((SPAN, QUARTER), F32)
        for j in range(CONV):
            ahead = CONV - 1 - j
            window = buf[q, ahead : ahead + SPAN] * columns[q][:, 8 + j : 9 + j]
            d_mixed = d_mixed + taps[j : j + 1, :QUARTER] * window
            gtap_ref[j : j + 1] += jnp.sum(mixed * window, axis=0, keepdims=True)
        gtap_ref[CONV : CONV + 1] += jnp.sum(buf[q, 0:SPAN], axis=0, keepdims=True)
        buf[q, SPAN:] = buf[q, 0:8]
        d_late[q * SPAN : (q + 1) * SPAN, :QUARTER] = d_mixed.astype(BF)
    late = d_late[...]
    g_ref[...] += dot_tn(late, both_tokens(own_ref, other_ref))[: QUARTER + 16]
    d_gate = jnp.concatenate([d_gate_ref[0, 0], d_gate_ref[1, 0]], axis=0)
    grads = jnp.concatenate([late, d_gate], axis=1)
    width = QUARTER + 2 * STATE
    for rows_at, out_ref, flip in zip(core_rows(place_ref), (mine_ref, theirs_ref), (0, 1)):
        weights = [w_ref[rows_at, :QUARTER], w_ref[rows_at, width:], w_gate_ref[rows_at]]
        total = dot_nt(grads, jnp.concatenate(weights, axis=1)).astype(BF)
        for q in range(2):
            out_ref[0, q ^ flip, :SPAN] = total[q * SPAN : (q + 1) * SPAN]


def slot_spec(rows, width, order):
    return pl.BlockSpec((2, 1, rows, width), lambda j, place: (0, order(j), 0, 0))


def segment_spec():
    return pl.BlockSpec((2, 8, BLOCKS * SPAN + 256), lambda j, place: (0, 0, 0))


def fixed_spec(rows, width):
    return pl.BlockSpec((rows, width), lambda j, place: (0, 0))


def out_shape(rows, cols_of, kind):
    return jax.ShapeDtypeStruct((2, BLOCKS, rows, cols_of), kind)


def upward(j):
    return j


def downward(j):
    return BLOCKS - 1 - j


def token_specs(order):
    return [pl.BlockSpec((1, SPAN, D), lambda j, place: (order(j), 0, 0))] * 2


def call_blocks(kernel, name, place, operands, in_specs, outs, scratch=(), steps=BLOCKS):
    return pl.pallas_call(
        kernel,
        grid_spec=pltpu.PrefetchScalarGridSpec(
            num_scalar_prefetch=1,
            grid=(steps,),
            in_specs=in_specs,
            out_specs=[spec for spec, _ in outs],
            scratch_shapes=list(scratch),
        ),
        out_shape=[shape for _, shape in outs],
        compiler_params=pltpu.CompilerParams(vmem_limit_bytes=VMEM_LIMIT),
        cost_estimate=pl.CostEstimate(flops=1024, bytes_accessed=1024, transcendentals=0),
        name=name,
    )(place, *operands)


def slot_out(rows, width, kind, order):
    return slot_spec(rows, width, order), out_shape(rows, width, kind)


def lead_out(rows, width, order):
    shape = jax.ShapeDtypeStruct((BLOCKS, 2, rows, width), BF)
    return pl.BlockSpec((1, 2, rows, width), lambda j, place: (order(j), 0, 0, 0)), shape


def fixed_out(rows, width):
    return fixed_spec(rows, width), jax.ShapeDtypeStruct((rows, width), F32)


def run_fwd(place, tokens, w_first, segs, taps, head, chan):
    width = QUARTER + 2 * STATE
    pieces = len(tokens) > 2
    outs = [
        slot_out(SPAN, width, BF, upward),
        slot_out(SPAN, 128, F32, upward),
        slot_out(SPAN, width, F32, upward),
        slot_out(SPAN, QUARTER, F32, upward),
        slot_out(PARTS * QUARTER, STATE, BF, upward),
    ]
    if pieces:
        shape = jax.ShapeDtypeStruct((BLOCKS, SPAN, D), BF)
        outs += [(spec, shape) for spec in token_specs(upward)]
    return call_blocks(
        fwd_pieces if pieces else fwd_blocks,
        "mix_forward",
        place,
        (*tokens, w_first, segs, taps, head, chan),
        [
            *(cot_specs() if pieces else token_specs(upward)),
            fixed_spec(D, width + 128),
            segment_spec(),
            fixed_spec(8, width),
            fixed_spec(8, 128),
            fixed_spec(8, QUARTER),
        ],
        outs,
        (cot_scratch() if pieces else [])
        + [pltpu.VMEM((2, SPAN + 8, width), F32), pltpu.VMEM((2, QUARTER, STATE), F32)],
    )


def cot_specs():
    return [pl.BlockSpec(memory_space=pl.ANY)] * 10


def run_gate(place, tokens, y, w_gate, w_out, chan):
    both = range(2)
    wide = slot_spec(SPAN, QUARTER, upward)
    lead, lead_shape = lead_out(SPAN, D // 2, upward)
    rows = slot_spec(2, SPAN, upward)
    kinds = (
        (wide, out_shape(SPAN, QUARTER, F32)),
        (wide, out_shape(SPAN, QUARTER, BF)),
        (lead, lead_shape),
        (lead, lead_shape),
        (rows, out_shape(2, SPAN, F32)),
    )
    return call_blocks(
        gate_kernel,
        "gate_forward",
        place,
        (*tokens[0], *tokens[1], *y, w_gate, w_out, chan),
        [
            *[in_half(spec, m) for m in both for spec in token_specs(upward)],
            *[in_half(wide, m) for m in both],
            fixed_spec(D, QUARTER),
            fixed_spec(D, QUARTER),
            fixed_spec(8, QUARTER),
        ],
        [(in_half(spec, m), shape) for spec, shape in kinds for m in both],
        steps=2 * BLOCKS,
    )


def run_cross(place, cots, gun, w_out):
    both = range(2)
    wide = slot_spec(SPAN, QUARTER, upward)
    rows = slot_spec(2, SPAN, upward)
    return call_blocks(
        cross_kernel,
        "cross_forward",
        place,
        (*cots, *gun, w_out),
        [*cot_specs(), *[in_half(wide, m) for m in both], fixed_spec(D, QUARTER)],
        [(in_half(wide, m), out_shape(SPAN, QUARTER, F32)) for m in both]
        + [(in_half(rows, m), out_shape(2, SPAN, F32)) for m in both],
        cot_scratch() + cot_scratch(),
        steps=2 * BLOCKS,
    )


def sums_out(rows, dp_count, last):
    if not last:
        return fixed_out(rows, D), []
    share = D // dp_count
    spec = pl.BlockSpec((dp_count, rows, share), lambda j, place: (0, 0, 0))
    out = spec, jax.ShapeDtypeStruct((dp_count, rows, share), BF)
    return out, [pltpu.VMEM((rows, D), F32)]


def in_half(spec, m):
    def index(j, place):
        slot = jnp.minimum(j, BLOCKS - 1) if m == 0 else jnp.maximum(j - BLOCKS, 0)
        return spec.index_map(slot ^ place[1], place)

    return pl.BlockSpec(spec.block_shape, index)


def run_gate_back(place, tokens, cots, y, gate, d_gated, stat, chan, dp_count):
    (parts_spec, parts_shape), total = sums_out(2 * QUARTER, dp_count, True)
    both = range(2)
    wide = slot_spec(SPAN, QUARTER, upward)
    outs = [
        (in_half(wide, m), out_shape(SPAN, QUARTER, BF)) for _ in range(2) for m in both
    ]
    return call_blocks(
        gate_back_kernel,
        "gate_backward",
        place,
        (*tokens[0], *tokens[1], *cots, *y, *gate, *d_gated, *stat, chan),
        [
            *[in_half(spec, m) for m in both for spec in token_specs(upward)],
            *cot_specs(),
            *[in_half(wide, m) for _ in range(3) for m in both],
            *[in_half(slot_spec(2, SPAN, upward), m) for m in both],
            fixed_spec(8, QUARTER),
        ],
        outs + [fixed_out(8, QUARTER), (parts_spec, parts_shape)],
        cot_scratch() + cot_scratch() + total,
        steps=2 * BLOCKS,
    )


def run_bwd(place, tokens, kept, dy, d_gate, rows, taps, head, chan, weights, seed, dp_count):
    mixed, raw, pre, y, hin = kept
    width = mixed.shape[-1]
    states = 2 * STATE
    half = D // 2
    last = seed is not None
    total, scratch = sums_out(QUARTER + 16, dp_count, last)
    rows_out = SPAN if last else SPAN + PACKED
    maps_out = [lead_out(SPAN + 16, STATE, downward)] * 2 if last else []
    return call_blocks(
        bwd_last if last else bwd_first,
        "mix_backward",
        place,
        (*tokens, mixed, pre, raw, y, hin, dy, d_gate, rows, taps, head, chan, *weights)
        + ((seed,) if last else ()),
        [
            *token_specs(downward),
            slot_spec(SPAN, width, downward),
            slot_spec(SPAN, width, downward),
            slot_spec(SPAN, 128, downward),
            slot_spec(SPAN, QUARTER, downward),
            slot_spec(PARTS * QUARTER, STATE, downward),
            slot_spec(SPAN, QUARTER, downward),
            slot_spec(SPAN, QUARTER, downward),
            segment_spec(),
            fixed_spec(8, width),
            fixed_spec(8, 128),
            fixed_spec(8, QUARTER),
            fixed_spec(D, width + 128),
            fixed_spec(D, QUARTER),
        ]
        + ([fixed_spec(QUARTER + 16, D)] if last else []),
        [
            total,
            *maps_out,
            slot_out(SPAN + 16, STATE, F32, downward),
            fixed_out(8, QUARTER),
            fixed_out(8, QUARTER),
            lead_out(rows_out, half, downward),
            lead_out(rows_out, half, downward),
        ],
        [
            pltpu.VMEM((2, SPAN + 8, QUARTER), F32),
            pltpu.VMEM((2, QUARTER, STATE), F32),
            pltpu.VMEM((2, 16, states), F32),
            pltpu.VMEM((2, 16, STATE), F32),
            pltpu.VMEM((2 * SPAN, QUARTER + 128), BF),
        ]
        + scratch,
    )


def maps_kernel(
    place_ref, packed_ref, maps_ref, slope_0, slope_1, mixed_0, mixed_1, seg_0, seg_1,
    own_0, other_0, own_1, other_1, taps_ref,
    d_maps_ref, g_ref, g_taps_ref, buf,
):
    chip = place_ref[1]
    taps = taps_ref[...]
    buf[SPAN + 16 :] = jnp.zeros((8, STATE), F32)
    sums = [jnp.zeros((1, STATE), F32) for _ in range(CONV + 1)]
    g_maps = jnp.zeros((STATE, D), F32)
    slopes, mixes, segs = (slope_0, slope_1), (mixed_0, mixed_1), (seg_0, seg_1)
    tokens = ((own_0, other_0), (own_1, other_1))
    for m in range(MB):
        for q in range(2):
            if m == 0:
                total = packed_ref[0, q].astype(F32)
                for src in range(1, BLOCKS):
                    total = total + packed_ref[src, q].astype(F32)
                groups = [total[:, 128 * k : 128 * (k + 1)] for k in range(6)]
                d_conv = jnp.concatenate(groups, axis=0)[: SPAN + 16]
            else:
                d_conv = maps_ref[0, q].astype(F32)
                for src in range(1, BLOCKS):
                    d_conv = d_conv + maps_ref[src, q].astype(F32)
            d_pre = d_conv * slopes[m][q, 0]
            buf[0 : SPAN + 16] = d_pre
            cols = to_columns(segment_flags(segs[m], q, chip))
            mixed = mixes[m][q, 0].astype(F32)
            d_mixed = jnp.zeros((SPAN, STATE), F32)
            for j in range(CONV):
                ahead = CONV - 1 - j
                window = buf[ahead : ahead + SPAN] * cols[:, 8 + j : 9 + j]
                d_mixed = d_mixed + taps[j : j + 1] * window
                sums[j] = sums[j] + jnp.sum(mixed * window, axis=0, keepdims=True)
            sums[CONV] = sums[CONV] + jnp.sum(d_pre[:SPAN], axis=0, keepdims=True)
            low = d_mixed.astype(BF)
            d_maps_ref[m, q] = low
            g_maps = g_maps + dot_tn(low, tokens[m][q][0])
    g_taps_ref[...] = jnp.concatenate(sums + [jnp.zeros((3, STATE), F32)], axis=0)
    rows_of = g_ref.shape[2]
    for z in range(g_ref.shape[0]):
        g_ref[z] = g_maps[:, z * rows_of : (z + 1) * rows_of].astype(BF)


def run_maps(place, packed, maps, slopes, mixes, segs, tokens, taps, dp_count):
    def whole(shape):
        return pl.BlockSpec(shape, lambda i, place: (0,) * len(shape))

    def slope_spec():
        return pl.BlockSpec((2, 1, SPAN + 16, STATE), lambda i, place: (0, place[1], 0, 0))

    def mixed_spec():
        first = QUARTER // STATE
        return pl.BlockSpec(
            (2, 1, SPAN, STATE), lambda i, place: (0, place[1], 0, first + place[0])
        )

    def token_spec():
        return pl.BlockSpec((1, SPAN, D), lambda i, place: (place[1], 0, 0))

    share = D // dp_count
    return pl.pallas_call(
        maps_kernel,
        grid_spec=pltpu.PrefetchScalarGridSpec(
            num_scalar_prefetch=1,
            grid=(1,),
            in_specs=[
                whole(packed.shape),
                whole(maps.shape),
                slope_spec(),
                slope_spec(),
                mixed_spec(),
                mixed_spec(),
                whole(segs[0].shape),
                whole(segs[1].shape),
                token_spec(),
                token_spec(),
                token_spec(),
                token_spec(),
                whole(taps.shape),
            ],
            out_specs=[
                whole((MB, 2, SPAN, STATE)),
                whole((dp_count, STATE, share)),
                whole((8, STATE)),
            ],
            scratch_shapes=[pltpu.VMEM((SPAN + 24, STATE), F32)],
        ),
        out_shape=[
            jax.ShapeDtypeStruct((MB, 2, SPAN, STATE), BF),
            jax.ShapeDtypeStruct((dp_count, STATE, share), BF),
            jax.ShapeDtypeStruct((8, STATE), F32),
        ],
        compiler_params=pltpu.CompilerParams(vmem_limit_bytes=VMEM_LIMIT),
        cost_estimate=pl.CostEstimate(flops=1024, bytes_accessed=1024, transcendentals=0),
        name="maps_backward",
    )(place, packed, maps, *slopes, *mixes, *segs, *tokens, taps)


def norm_kernel(place_ref, share_ref, w_in_ref, w_state_ref, w_step_ref, step_ref, out_ref):
    rows = share_ref.shape[1]
    squares = jnp.zeros((rows, QUARTER), F32)
    products = jnp.zeros((rows, QUARTER), F32)
    for s in range(BLOCKS):
        at = slice(s * QUARTER, (s + 1) * QUARTER)
        out = share_ref[s, :, :QUARTER].astype(F32)
        gate = share_ref[s, :, QUARTER : 2 * QUARTER].astype(F32)
        inner = share_ref[s, :, 2 * QUARTER : 3 * QUARTER].astype(F32)
        squares = squares + out * out + gate * gate + inner * inner
        products = products + gate * w_in_ref[0, :, at].astype(F32)
        products = products + inner * w_in_ref[1, :, at].astype(F32)
    state = share_ref[0, :, MAPS_AT : MAPS_AT + STATE].astype(F32)
    for s in range(1, BLOCKS):
        state = state + share_ref[s, :, MAPS_AT : MAPS_AT + STATE].astype(F32)
    step = step_ref[...]
    by_row = jnp.sum(products, axis=1, keepdims=True)
    by_row = by_row + jnp.sum(state * w_state_ref[...].astype(F32), axis=1, keepdims=True)
    square = jnp.sum(squares, axis=1, keepdims=True) + jnp.sum(state * state, axis=1, keepdims=True)
    lanes = lax.broadcasted_iota(jnp.int32, (rows, 128), 1)
    table = jnp.where(lanes == 0, by_row, jnp.where(lanes == 1, square, 0.0))
    table = jnp.concatenate([table, jnp.zeros((128 - rows, 128), F32)], axis=0).T
    total = jnp.sum(table[1:2], axis=1, keepdims=True)
    total = total + jnp.sum(jnp.sum(step * step, axis=0, keepdims=True), axis=1, keepdims=True)
    by_step = jnp.sum(step * w_step_ref[...].astype(F32), axis=0, keepdims=True)
    by_step = jnp.concatenate([by_step, jnp.zeros((1, 128 - rows), F32)], axis=1)
    at_row = lax.broadcasted_iota(jnp.int32, (8, 128), 0)
    at_lane = lax.broadcasted_iota(jnp.int32, (8, 128), 1)
    first = jnp.where((at_row == 0) & (at_lane == rows), total, table[0:8] + by_step)
    out_ref[...] = jnp.where(at_row == 0, first, 0.0)


def update_kernel(
    place_ref, factor_ref, share_ref, step_ref, w_in_ref, w_out_ref, w_state_ref,
    w_step_ref, m_in_ref, m_out_ref, m_state_ref, m_step_ref,
    new_in_ref, new_out_ref, new_state_ref, new_step_ref,
    next_in_ref, next_out_ref, next_state_ref, next_step_ref,
):
    factor = factor_ref[0, 0]

    def write(new_ref, next_ref, at, moment, grad, weight):
        new = 0.5 * moment + (0.5 * factor) * grad
        new_ref[at] = new
        next_ref[at] = (weight.astype(F32) - LEARN * new).astype(BF)

    for s in range(BLOCKS):
        lanes = slice(s * QUARTER, (s + 1) * QUARTER)
        gate = (0, slice(None), lanes)
        write(
            new_in_ref, next_in_ref, gate, m_in_ref[gate],
            share_ref[s, :, QUARTER : 2 * QUARTER].astype(F32), w_in_ref[gate],
        )
        inner = (1, slice(None), lanes)
        write(
            new_in_ref, next_in_ref, inner, m_in_ref[inner],
            share_ref[s, :, 2 * QUARTER : 3 * QUARTER].astype(F32), w_in_ref[inner],
        )
        out = (slice(None), lanes)
        write(
            new_out_ref, next_out_ref, out, m_out_ref[out],
            share_ref[s, :, :QUARTER].astype(F32), w_out_ref[out],
        )
    state = share_ref[0, :, MAPS_AT : MAPS_AT + STATE].astype(F32)
    for s in range(1, BLOCKS):
        state = state + share_ref[s, :, MAPS_AT : MAPS_AT + STATE].astype(F32)
    write(new_state_ref, next_state_ref, ..., m_state_ref[...], state, w_state_ref[...])
    write(new_step_ref, next_step_ref, ..., m_step_ref[...], step_ref[...], w_step_ref[...])


def owner_specs(rows):
    return [
        pl.BlockSpec((2, rows, BLOCKS * QUARTER), lambda i, place: (0, place[1], 0)),
        pl.BlockSpec((rows, STATE), lambda i, place: (place[1], place[0])),
    ]


def run_owner(kernel, name, place, operands, in_specs, outs):
    return pl.pallas_call(
        kernel,
        grid_spec=pltpu.PrefetchScalarGridSpec(
            num_scalar_prefetch=1, grid=(1,), in_specs=in_specs,
            out_specs=[spec for spec, _ in outs],
        ),
        out_shape=[shape for _, shape in outs],
        compiler_params=pltpu.CompilerParams(vmem_limit_bytes=VMEM_LIMIT),
        cost_estimate=pl.CostEstimate(flops=1024, bytes_accessed=1024, transcendentals=0),
        name=name,
    )(place, *operands)


def swap_cores(block):
    return lax.ppermute(block, "tensor", SWAP)


def over_x(block):
    return lax.ppermute(block, "seq", ROUTE_X)


def over_y(block):
    return lax.ppermute(block, "seq", ROUTE_Y)


def exchange(blocks):
    return lax.all_to_all(blocks, "seq", 0, 0, tiled=True)


def copies(piece):
    return jnp.broadcast_to(piece, (BLOCKS,) + piece.shape)


def add_low(a, b):
    return (a.astype(F32) + b.astype(F32)).astype(BF)


def scatter(blocks):
    return jnp.sum(exchange(blocks).astype(F32), axis=0)


def after(value, *others):
    return lax.optimization_barrier((value, others))[0]


def fast_body(
    inputs,
    segments,
    cotangent,
    prenorm,
    inproj,
    statproj,
    stepproj,
    outproj,
    convinner,
    convstate,
    headparam,
    gatenorm,
    prenorm_moment,
    inproj_moment,
    statproj_moment,
    stepproj_moment,
    outproj_moment,
    convinner_moment,
    convstate_moment,
    headparam_moment,
    gatenorm_moment,
):
    core = lax.axis_index("tensor")
    chip = lax.axis_index("seq")
    data_at = lax.axis_index("dp")
    dp_count = lax.axis_size("dp")
    heads_local = headparam.shape[1]
    rows_local = inproj.shape[1]
    shard = rows_local // BLOCKS
    half_d = D // 2
    place = jnp.stack([core, chip]).astype(jnp.int32)

    def by_core(first, second):
        return jnp.where(core == 0, first, second)

    def quarter(array, axis, width):
        return lax.dynamic_slice_in_dim(array, chip * width, width, axis)

    def all_rows(block):
        return lax.all_gather(block, "dp", axis=0, tiled=True)

    first_block = (
        jnp.concatenate(
            [
                quarter(inproj[1], 1, QUARTER),
                statproj,
                jnp.pad(quarter(stepproj, 1, QHEADS), ((0, 0), (0, 128 - QHEADS))),
            ],
            axis=1,
        )
    )
    inputs, first_block = after((inputs, first_block))
    w_first = all_rows(first_block)
    gate_block = quarter(inproj[0], 1, QUARTER)
    out_block = quarter(outproj, 0, QUARTER).T

    def whole_rows(array):
        mine = lax.dynamic_index_in_dim(array, core, 1, keepdims=False)
        theirs = lax.dynamic_index_in_dim(array, 1 - core, 1, keepdims=False)
        got = swap_cores(theirs)
        return by_core(
            jnp.concatenate([mine, got], axis=2), jnp.concatenate([got, mine], axis=2)
        )

    rows_whole = whole_rows(inputs)
    normed_own = rms_scale(rows_whole.astype(F32), prenorm).astype(BF)
    cot_own = whole_rows(cotangent)
    half = SPAN // 2
    mine_0, second_copies = after((normed_own[0], copies(normed_own[1])))
    near_0 = (mine_0, over_x(mine_0), over_y(mine_0))
    own_swapped = swap_cores(mine_0)

    seg_mine = jnp.concatenate(
        [
            lax.dynamic_index_in_dim(segments, core, 1),
            lax.dynamic_index_in_dim(segments, 1 - core, 1),
        ],
        axis=1,
    )
    seg_pad = jnp.pad(
        seg_mine.astype(F32), ((0, 0), (0, 0), (128, 128)), constant_values=-1.0
    )
    segs = jnp.broadcast_to(seg_pad[:, :, None], seg_pad.shape[:2] + (8, seg_pad.shape[2]))

    taps_inner = quarter(convinner, 1, QUARTER)
    taps = jnp.pad(jnp.concatenate([taps_inner, convstate], axis=1), ((0, 3), (0, 0)))
    head_own = quarter(headparam, 1, QHEADS)
    head = jnp.pad(
        jnp.stack([head_own[0], jnp.exp(head_own[1]), head_own[2]]),
        ((0, 5), (0, 128 - QHEADS)),
    )
    gain = quarter(gatenorm, 0, QUARTER)
    chan = jnp.pad(jnp.stack([gain, jnp.repeat(head_own[2], HEADDIM)]), ((0, 6), (0, 0)))

    def rows_dot_t(left, right):
        return lax.dot_general(left, right, (((3,), (1,)), ((), ())), preferred_element_type=F32)

    def core_sums(mine, theirs):
        return add_low(mine, swap_cores(theirs))

    def over_dp(parts):
        return lax.psum_scatter(parts, "dp", scatter_dimension=0, tiled=True)[0]

    def by_place(columns):
        return columns.T.reshape(BLOCKS, shard, -1)

    def forward(m, place, tokens):
        return run_fwd(place, tokens, w_first, segs[m], taps, head, chan)

    def backward(m, place, dy, d_gate, seed):
        return run_bwd(
            place, normed[m], kept[m], dy, d_gate, segs[m], taps, head, chan,
            (w_first, w_gate), seed, dp_count,
        )

    def summed(blocks):
        return jnp.sum(blocks.astype(F32), axis=0)

    def in_order(block):
        return by_core(block, block[:, ::-1])

    def token_scale(sums):
        own = lax.dynamic_index_in_dim(sums, chip, 1, keepdims=False)
        return lax.rsqrt(own[:, 0] / INNER + EPS)[..., None]

    def sum_dp(value):
        hop = 1
        while hop < dp_count:
            value = value + lax.ppermute(value, "dp", [(i, i ^ hop) for i in range(dp_count)])
            hop *= 2
        return value

    def sum_seq(value):
        value = value + over_x(value)
        return value + over_y(value)

    def with_other(own):
        return own, swap_cores(own)

    stepproj_own = lax.dynamic_slice_in_dim(stepproj.T, chip * shard, shard, 1)
    outproj_own = lax.dynamic_slice_in_dim(outproj, chip * shard, shard, 1).T
    (
        near_0, own_swapped, cot_own, segs, taps, head, chan, stepproj_own, outproj_own, place,
        gate_block, out_block,
    ) = after(
        (
            near_0, own_swapped, cot_own, segs, taps, head, chan, stepproj_own, outproj_own, place,
            gate_block, out_block,
        )
    )
    w_gate = all_rows(gate_block)
    w_out = all_rows(out_block)
    far = over_x(near_0[2][:half]), over_y(near_0[1][half:])
    near_swapped = [swap_cores(piece) for piece in near_0[1:]]
    far, near_swapped, second_copies = after((far, near_swapped, second_copies))
    own_1 = exchange(second_copies)
    far, w_first = after((far, w_first))
    cot_other = swap_cores(cot_own)
    first_pieces = (
        *near_0, *far, own_swapped, *near_swapped, *[swap_cores(piece) for piece in far]
    )
    *kept_0, own_0, other_0 = forward(0, place, first_pieces)
    kept = [kept_0]
    normed = [(own_0, other_0)]
    cot_own, cot_other, place = after((cot_own, cot_other, place), kept[0][1])
    by_x, by_y = over_x(cot_own), over_y(cot_own)
    own_1, w_gate, place = after((own_1, w_gate, place))
    normed.append(with_other(own_1))
    kept.append(forward(1, place, normed[1]))

    by_x, by_y, w_out, place = after((by_x, by_y, w_out, place), kept[1][1])
    far = over_x(by_y[:, :half]), over_y(by_x[:, half:])
    near_other = (cot_other, swap_cores(by_x), swap_cores(by_y))
    gate_0, gate_1, gun_0, gun_1, mine_0, mine_1, theirs_0, theirs_1, stat_0, stat_1 = run_gate(
        place, normed, (kept[0][3], kept[1][3]), w_gate, w_out, chan
    )
    far, near_other, place = after((far, near_other, place), stat_0)
    far_other = [swap_cores(piece) for piece in far]
    far_other, place, theirs_0, theirs_1 = after((far_other, place, theirs_0, theirs_1))
    cots = (cot_own, by_x, by_y, *far, *near_other, *far_other)
    d_gated_0, d_gated_1, cross_0, cross_1 = run_cross(place, cots, (gun_0, gun_1), w_out)
    got_0 = swap_cores(theirs_0)

    stats = jnp.stack([stat_0 + cross_0, stat_1 + cross_1])
    got_0, stats = after((got_0, stats))
    branch_0 = add_low(mine_0, got_0)
    stats = stats + swap_cores(stats)[:, ::-1]
    theirs_1 = after(theirs_1, stats)
    sums_0, sums_1 = sum_seq(stats)
    branch_0 = after(branch_0, sums_0)
    layer_0 = exchange(branch_0)
    branch_1 = core_sums(mine_1, theirs_1)
    dy_0, dy_1, d_gate_0, d_gate_1, g_gain, mid_parts = run_gate_back(
        place, normed, cots, (kept[0][3], kept[1][3]), (gate_0, gate_1), (d_gated_0, d_gated_1),
        (sums_0, sums_1), chan, dp_count,
    )

    layer_0, branch_1, place, mid_parts = after((layer_0, branch_1, place, mid_parts), dy_1)
    layer_1 = exchange(branch_1)
    mid_rows = over_dp(mid_parts)
    g_late_0, slope_0, g_taps_0, g_head_0, mine, theirs = backward(0, place, dy_0, d_gate_0, None)

    layer_1, mid_rows, theirs, place = after((layer_1, mid_rows, theirs, place), g_taps_0)
    back_0 = core_sums(mine, theirs)
    layer_out = [
        summed(layer_0) * token_scale(sums_0), summed(layer_1) * token_scale(sums_1)
    ]
    layer_out = (inputs.astype(F32) + in_order(jnp.stack(layer_out))).astype(BF)
    back_0, place, layer_out = after((back_0, place, layer_out))
    token_0 = exchange(back_0)
    late_parts, keep_1, give_1, slope_1, g_taps_1, g_head_1, mine, theirs = backward(
        1, place, dy_1, d_gate_1, g_late_0
    )

    token_0, late_parts, theirs, give_1 = after((token_0, late_parts, theirs, give_1))
    late_rows = over_dp(late_parts)
    maps = core_sums(keep_1, give_1)
    back_1 = core_sums(mine, after(theirs, maps))
    maps = exchange(maps)
    maps, back_1, token_0, mid_rows, g_taps_1 = after(
        (maps, back_1, token_0, mid_rows, g_taps_1)
    )
    token_1 = exchange(back_1)
    taps_state = lax.dynamic_slice_in_dim(convstate, core * STATE, STATE, 1)
    d_maps, g_maps, g_state_taps = run_maps(
        place, token_0[:, :, SPAN:], maps, (slope_0, slope_1), (kept[0][0], kept[1][0]),
        segs, (*normed[0], *normed[1]), jnp.pad(taps_state, ((0, 3), (0, 0))), dp_count,
    )

    def for_dp(hop):
        at = lax.rem(data_at + hop, dp_count)
        return lax.dynamic_index_in_dim(g_maps, at, 0, keepdims=False)

    state_rows = for_dp(0).astype(F32)
    for hop in range(1, dp_count):
        route = [(i, (i + hop) % dp_count) for i in range(dp_count)]
        state_rows = state_rows + lax.ppermute(for_dp(hop), "dp", route).astype(F32)
    state_rows = state_rows.astype(BF)

    inner_local = BLOCKS * QUARTER

    def put(values, width, total):
        base = jnp.zeros(values.shape[:-1] + (total,), F32)
        return lax.dynamic_update_slice_in_dim(base, values, chip * width, values.ndim - 1)

    g_taps, g_head = g_taps_0 + g_taps_1, g_head_0 + g_head_1
    g_heads = jnp.concatenate(
        [g_head[:2, :QHEADS], jnp.sum(g_head[2].reshape(1, QHEADS, HEADDIM), axis=2)], axis=0
    )
    small_parts = [
        put(g_taps[: CONV + 1], QUARTER, inner_local),
        put(g_gain[0], QUARTER, inner_local),
        put(g_heads, QHEADS, heads_local),
        g_state_taps[: CONV + 1],
    ]
    small_shapes = [small.shape for small in small_parts]
    vector = jnp.concatenate([small.reshape(-1) for small in small_parts])
    vector = jnp.pad(vector, (0, -vector.size % 1024)).reshape(-1, 128)

    late_rows, mid_rows, state_rows = after((late_rows, mid_rows, state_rows))
    shares = jnp.concatenate(
        [mid_rows, late_rows[:QUARTER], state_rows, late_rows[QUARTER:]], axis=0
    )
    vector = sum_dp(after(vector, state_rows))
    other_vector = swap_cores(vector)
    token_1, shares, vector, other_vector = after(
        (token_1, by_place(shares), vector, other_vector)
    )
    share = exchange(shares)
    d_tokens = [summed(token_0[:, :, :SPAN]), summed(token_1)]
    w_state = w_first[:, QUARTER : QUARTER + 2 * STATE]

    state_other = swap_cores(d_maps)[:, ::-1]
    state_mine = d_maps
    d_state_both = by_core(
        jnp.concatenate([state_mine, state_other], axis=3),
        jnp.concatenate([state_other, state_mine], axis=3),
    )
    from_state = rows_dot_t(
        d_state_both, lax.dynamic_slice_in_dim(w_state, core * half_d, half_d, 0)
    )

    outputs = layer_out
    d_normed = in_order(jnp.stack(d_tokens) + from_state)
    rows_own = inputs.astype(F32)
    gain_own = lax.dynamic_slice_in_dim(prenorm, core * half_d, half_d, 0)
    weighted = d_normed * gain_own
    pair_sums = jnp.stack(
        [jnp.sum(rows_own * rows_own, axis=-1), jnp.sum(weighted * rows_own, axis=-1)]
    )
    pair_sums = pair_sums + swap_cores(pair_sums)
    root = lax.rsqrt(pair_sums[0] / D + EPS)[..., None]
    input_grads = (
        cotangent.astype(F32)
        + weighted * root
        - rows_own * root * root * root * (pair_sums[1] / D)[..., None]
    ).astype(BF)

    step_at = MAPS_AT + STATE
    step_share = share[:, :, step_at : step_at + QHEADS].astype(F32)
    step_share = jnp.moveaxis(step_share, 1, 2).reshape(heads_local, shard)
    in_spec, state_spec = owner_specs(shard)

    def whole(array):
        return pl.BlockSpec(array.shape, lambda i, place: (0,) * array.ndim)

    def whole_out(shape, kind):
        spec = pl.BlockSpec(shape, lambda i, place: (0,) * len(shape))
        return spec, jax.ShapeDtypeStruct(shape, kind)

    owner_sums = run_owner(
        norm_kernel,
        "owner_norm",
        place,
        (share, inproj, statproj, stepproj_own, step_share),
        [whole(share), in_spec, state_spec, whole(stepproj_own), whole(step_share)],
        [whole_out((8, 128), F32)],
    )[0]
    owner_sums = owner_sums + swap_cores(owner_sums)

    owners = dp_count * BLOCKS
    owner = data_at * BLOCKS + chip
    gain_rows = lax.dynamic_slice_in_dim(prenorm, owner * shard, shard, 0)
    lanes = jnp.arange(128)
    g_prenorm = owner_sums[0] / jnp.pad(gain_rows, (0, 128 - shard), constant_values=1.0)
    g_prenorm = jnp.where(lanes < shard, g_prenorm, 0.0)
    square = owner_sums[0, shard] + jnp.sum(g_prenorm * g_prenorm)
    line = jnp.where(lanes == shard, square, g_prenorm)
    table = jnp.where(jnp.arange(owners)[:, None] == owner, line[None], 0.0)
    table = sum_seq(jnp.concatenate([sum_dp(table), vector, other_vector], axis=0))
    small_sums = []
    start = 0
    both_vectors = table[owners:].reshape(2, -1)
    vector = both_vectors[0]
    for shape in small_shapes:
        size = math.prod(shape)
        small_sums.append(vector[start : start + size].reshape(shape))
        start += size
    s_taps, s_gain, s_head, s_state_taps = small_sums

    small_sq = jnp.sum(both_vectors * both_vectors, axis=1)
    grad_norm = jnp.sqrt(jnp.sum(table[:owners, shard]) + (small_sq[0] + small_sq[1]))
    s_prenorm = lax.dynamic_slice_in_dim(
        table[:owners, :shard], core * (owners // 2), owners // 2, 0
    ).reshape(half_d)

    entries = (
        2 * D * INNER
        + 2 * D * STATE
        + D * (INNER // HEADDIM)
        + INNER * D
        + (CONV + 1) * (INNER + 2 * STATE)
        + 3 * (INNER // HEADDIM)
        + INNER
        + D
    )
    limit = CLIP_RMS * math.sqrt(entries)
    factor = limit / jnp.maximum(grad_norm, limit)

    def moved(moment, grad):
        return 0.5 * moment + 0.5 * factor * grad

    def stepped(weight, moment):
        return (weight.astype(F32) - LEARN * moment).astype(weight.dtype)

    new_prenorm = moved(prenorm_moment, s_prenorm)
    moments = (inproj_moment, outproj_moment.T, statproj_moment, stepproj_moment.T)
    new_in, new_out, new_state, new_step, next_in, next_out, next_state, next_step = run_owner(
        update_kernel,
        "owner_update",
        place,
        (
            factor.reshape(1, 1), share, step_share,
            inproj, outproj_own, statproj, stepproj_own, *moments,
        ),
        [
            pl.BlockSpec(memory_space=pltpu.SMEM),
            whole(share), whole(step_share),
            in_spec, whole(outproj_own), state_spec, whole(stepproj_own),
            *[whole(moment) for moment in moments],
        ],
        [whole_out(moment.shape, kind) for kind in (F32, BF) for moment in moments],
    )
    new_taps = moved(convinner_moment, s_taps)
    new_state_taps = moved(convstate_moment, s_state_taps)
    new_head = moved(headparam_moment, s_head)
    new_gain = moved(gatenorm_moment, s_gain)
    return (
        outputs,
        input_grads,
        grad_norm,
        new_prenorm,
        new_in,
        new_state,
        new_step.T,
        new_out.T,
        new_taps,
        new_state_taps,
        new_head,
        new_gain,
        next_in,
        next_state,
        next_step.T,
        next_out.T,
        stepped(convinner, new_taps),
        stepped(lax.dynamic_slice_in_dim(convstate, core * STATE, STATE, 1), new_state_taps),
    )


def solution(mesh):
    fast = mesh.shape["seq"] == BLOCKS and mesh.shape["tensor"] == 2
    return jax.shard_map(
        fast_body if fast else general_body,
        mesh=mesh,
        in_specs=(
            P(None, "dp", "seq", "tensor"),
            P(None, "dp", None),
            P(None, "dp", "seq", "tensor"),
            P(),
            P(None, "dp", "tensor"),
            P("dp", None),
            P("dp", "tensor"),
            P("tensor", "dp"),
            P(None, "tensor"),
            P(),
            P(None, "tensor"),
            P("tensor"),
            P("tensor"),
            P(None, ("dp", "seq"), "tensor"),
            P(("dp", "seq"), "tensor"),
            P(("dp", "seq"), "tensor"),
            P("tensor", ("dp", "seq")),
            P(None, "tensor"),
            P(None, "tensor"),
            P(None, "tensor"),
            P("tensor"),
        ),
        out_specs=(
            P(None, "dp", "seq", "tensor"),
            P(None, "dp", "seq", "tensor"),
            P(),
            P("tensor"),
            P(None, ("dp", "seq"), "tensor"),
            P(("dp", "seq"), "tensor"),
            P(("dp", "seq"), "tensor"),
            P("tensor", ("dp", "seq")),
            P(None, "tensor"),
            P(None, "tensor"),
            P(None, "tensor"),
            P("tensor"),
            P(None, ("dp", "seq"), "tensor"),
            P(("dp", "seq"), "tensor"),
            P(("dp", "seq"), "tensor"),
            P("tensor", ("dp", "seq")),
            P(None, "tensor"),
            P(None, "tensor"),
        ),
        check_vma=False,
    )
```
